32 devices in a mesh: groups: 2 (over x), row: 16 (over z, y, core).
Axes of the slice: x: 2, y: 2, z: 4, core: 2. Of those that a mesh axis runs over, the one named last changes fastest.
Arguments:
- pair_state: bfloat16 [256, 128, 128], P(('groups', 'row')), parts along dimension 0, may hold values from -24 to 24
- pair_mask: int32 [256, 128], P(('groups', 'row')), parts along dimension 0, may hold values from 0 to 1, as said below
- norm_gains: float32 [2, 2, 128], replicated, may hold values from 0.1 to 1.9
- norm_biases: float32 [2, 2, 128], replicated, may hold values from -3 to 3
- proj_weights: bfloat16 [2, 128, 512], replicated, may hold values from -0.5 to 0.5
- gate_weights: bfloat16 [2, 128, 128], replicated, may hold values from -0.5 to 0.5
- out_weights: bfloat16 [2, 128, 128], replicated, may hold values from -0.5 to 0.5
Outputs:
- pair_result: bfloat16 [256, 128, 128], P(('groups', 'row')), parts along dimension 0
The draws below stay inside these ranges and needn't reach their ends.
There are 2 independent parts, one for each index of `groups`. The reference program is written for one: setup_inputs(seed, part) draws one part's arguments, and reference() takes and returns one part's arrays. A program takes and returns all parts, laid end to end along the dimension named above; an argument that names none is the same for every part. Nothing has to cross between parts.
Inputs may be any that keep to these rules, and one draw needn't show every extreme that they name: `pair_mask`: 1 where both tokens are real (not padding) and their chains may interact, 0 elsewhere.
All inputs are finite; a program needn't handle non-finite values.
Results may differ from the reference program's by a relative error of at most 0.0065.
Values may be sent and summed in bfloat16 or wider, within the bound.
No kernel may reach another device: no remote copies, remote signals or barrier semaphores. Data moves between devices by JAX's collectives and lax.ppermute only.
A program may use at most 64 MiB of HBM per device.

```python
import math
import jax
import jax.numpy as jnp
from jax import lax

C = 128
N = 128


def draw_pair_state(key, part):
    key = jax.random.fold_in(key, 5)
    subkeys = jax.random.split(key, 3)
    channel_scale = jnp.exp(jax.random.uniform(subkeys[0], (C,), jnp.float32, math.log(0.3), math.log(3.0)))
    place_scale = jnp.exp(jax.random.uniform(subkeys[1], (N, N, 1), jnp.float32, math.log(0.5), math.log(2.0)))
    entries = jnp.clip(jax.random.normal(subkeys[2], (N, N, C), jnp.float32), -4.0, 4.0)
    return (entries * channel_scale * place_scale).astype(jnp.bfloat16)


def draw_pair_mask(key, part):
    key = jax.random.fold_in(key, 9)
    subkeys = jax.random.split(key, 3)
    boundaries = jnp.sort(jax.random.randint(subkeys[0], (7,), 1, N))
    position = jnp.arange(N, dtype=jnp.int32)
    chain_ids = jnp.sum((position[:, None] >= boundaries[None, :]).astype(jnp.int32), axis=1)
    padding = jax.random.randint(subkeys[1], (), 0, N // 4 + 1)
    real_tokens = (position < N - padding).astype(jnp.int32)
    allowed = jnp.minimum(jax.random.randint(subkeys[2], (8, 8), 0, 4), 1)
    allowed = jnp.maximum(allowed, jnp.eye(8, dtype=jnp.int32))
    pair_table = allowed[chain_ids][:, chain_ids]
    return real_tokens[:, None] * real_tokens[None, :] * pair_table


def gaussian(own_key, extent, scale, reach, kind=jnp.bfloat16):
    return jnp.clip(scale * jax.random.normal(own_key, extent, jnp.float32), -reach, reach).astype(kind)


def setup_inputs(seed: int = 0, part: int = 0) -> dict:
    key_list = jax.random.split(jax.random.key(seed), 8)
    part_splits = jax.random.split(jax.random.fold_in(key_list[7], part), 8)
    pair_state = draw_pair_state(jax.random.fold_in(jax.random.fold_in(key_list[7], part), 71), part)
    pair_mask = draw_pair_mask(jax.random.fold_in(jax.random.fold_in(key_list[7], part), 71), part)
    norm_gains = jnp.clip(1.0 + 0.18 * jax.random.normal(key_list[2], (2, 2, C), jnp.float32), 0.1, 1.9)
    norm_biases = gaussian(key_list[3], (2, 2, C), 0.5, 3.0, jnp.float32)
    proj_weights = gaussian(key_list[4], (2, C, 4 * C), C ** -0.5, 0.5)
    gate_weights = gaussian(key_list[5], (2, C, C), C ** -0.5, 0.5)
    out_weights = gaussian(key_list[6], (2, C, C), C ** -0.5, 0.5)
    return {"pair_state": pair_state, "pair_mask": pair_mask, "norm_gains": norm_gains, "norm_biases": norm_biases, "proj_weights": proj_weights, "gate_weights": gate_weights, "out_weights": out_weights}


def layer_norm(values, norm_gain, norm_bias, reduce_dim):
    average = lax.optimization_barrier(jnp.mean(values, axis=reduce_dim, keepdims=True))
    centred = values - average
    spread = lax.optimization_barrier(jnp.mean(centred * centred, axis=reduce_dim, keepdims=True))
    return centred * lax.rsqrt(spread + 1e-05) * norm_gain + norm_bias

def project_block(block_pair, block_mask, norm_gain, norm_bias, weights, gate_matrix):
    channels = block_pair.shape[2]
    flat = layer_norm(block_pair.astype(jnp.float32), norm_gain, norm_bias, 2).astype(jnp.bfloat16).reshape(-1, channels)
    mask_flat = block_mask.astype(jnp.float32).reshape(-1, 1)

    def gated(offset):
        gate_part = jnp.dot(flat, weights[:, offset:offset + channels], preferred_element_type=jnp.float32)
        value_part = jnp.dot(flat, weights[:, offset + channels:offset + 2 * channels], preferred_element_type=jnp.float32)
        masked = jax.nn.sigmoid(gate_part) * value_part * mask_flat
        return masked.astype(jnp.bfloat16).reshape(block_pair.shape)
    out_gate = jax.nn.sigmoid(jnp.dot(flat, gate_matrix, preferred_element_type=jnp.float32))
    return (gated(0), gated(2 * channels), out_gate.astype(jnp.bfloat16).reshape(block_pair.shape))

def triangle(pair_now, pair_mask, which_layer, incoming, norm_gains, norm_biases, proj_weights, gate_weights, out_weights):
    tokens = pair_now.shape[0]
    channels = pair_now.shape[2]
    blocks = tokens // 16
    pair_blocks = pair_now.reshape(blocks, 16, tokens, channels)

    def project(pieces):
        return project_block(pieces[0], pieces[1], norm_gains[which_layer, 0], norm_biases[which_layer, 0], proj_weights[which_layer], gate_weights[which_layer])
    left_panel, right_panel, out_gate = lax.map(project, (pair_blocks, pair_mask.reshape(blocks, 16, tokens)))
    left_cols = jnp.moveaxis(left_panel.reshape(tokens, tokens, channels), 2, 0)
    right_cols = jnp.moveaxis(right_panel.reshape(tokens, tokens, channels), 2, 0)

    def contract(pieces):
        if incoming:
            return jnp.dot(pieces[0].T, pieces[1], preferred_element_type=jnp.float32).astype(jnp.bfloat16)
        return jnp.dot(pieces[0], pieces[1].T, preferred_element_type=jnp.float32).astype(jnp.bfloat16)
    mixed = lax.map(contract, (left_cols, right_cols))
    mixed_rows = jnp.moveaxis(mixed, 0, 2).reshape(blocks, 16, tokens, channels)

    def finish(pieces):
        block_pair, block_gate, block_mixed = pieces
        normed_out = layer_norm(block_mixed.astype(jnp.float32), norm_gains[which_layer, 1], norm_biases[which_layer, 1], 2).astype(jnp.bfloat16)
        projected = jnp.dot(normed_out.reshape(-1, channels), out_weights[which_layer], preferred_element_type=jnp.float32).reshape(block_pair.shape)
        return (block_pair.astype(jnp.float32) + block_gate.astype(jnp.float32) * projected).astype(jnp.bfloat16)
    updated = lax.map(finish, (pair_blocks, out_gate, mixed_rows))
    return updated.reshape(tokens, tokens, channels)

def reference(pair_state, pair_mask, norm_gains, norm_biases, proj_weights, gate_weights, out_weights):
    middle = triangle(pair_state, pair_mask, 0, False, norm_gains, norm_biases, proj_weights, gate_weights, out_weights)
    return triangle(middle, pair_mask, 1, True, norm_gains, norm_biases, proj_weights, gate_weights, out_weights)
```

```python
import jax
import jax.numpy as jnp
from jax import lax
from jax.sharding import PartitionSpec as P


def layer_norm(values, norm_gain, norm_bias, reduce_dim):
    average = jnp.mean(values, axis=reduce_dim, keepdims=True)
    centred = values - average
    spread = jnp.mean(centred * centred, axis=reduce_dim, keepdims=True)
    return centred * lax.rsqrt(spread + 1e-05) * norm_gain + norm_bias


def triangle(pair_rows, mask_rows, which, form, norm_gains, norm_biases, proj_weights, gate_weights, out_weights):
    groups = lax.axis_size("row")
    per_dev, tokens, channels = pair_rows.shape
    per_group = channels // groups
    normed = layer_norm(
        pair_rows.astype(jnp.float32), norm_gains[which, 0], norm_biases[which, 0], 2
    ).astype(jnp.bfloat16)
    weights = proj_weights[which]

    def gated(offset):
        gate_part = jnp.einsum(
            "rnd,de->ern", normed, weights[:, offset : offset + channels], preferred_element_type=jnp.float32
        )
        value_part = jnp.einsum(
            "rnd,de->ern",
            normed,
            weights[:, offset + channels : offset + 2 * channels],
            preferred_element_type=jnp.float32,
        )
        masked = jax.nn.sigmoid(gate_part) * value_part * mask_rows[None]
        return masked.astype(jnp.bfloat16).reshape(groups, 1, per_group, per_dev, tokens)

    both = jnp.concatenate([gated(0), gated(2 * channels)], axis=1)
    out_gate = jax.nn.sigmoid(
        jnp.einsum("rnd,de->rne", normed, gate_weights[which], preferred_element_type=jnp.float32)
    ).astype(jnp.bfloat16)
    both = lax.all_to_all(both, "row", split_axis=0, concat_axis=0, tiled=True)
    left = jnp.moveaxis(both[:, 0], 0, 1).reshape(per_group, tokens, tokens)
    right = jnp.moveaxis(both[:, 1], 0, 1).reshape(per_group, tokens, tokens)
    product = jnp.einsum(form, left, right, preferred_element_type=jnp.float32).astype(jnp.bfloat16)
    product = product.reshape(per_group, groups, per_dev, tokens)
    merged = lax.all_to_all(product, "row", split_axis=1, concat_axis=0, tiled=True)
    merged = merged.reshape(channels, per_dev, tokens)
    normed_out = layer_norm(
        merged.astype(jnp.float32),
        norm_gains[which, 1][:, None, None],
        norm_biases[which, 1][:, None, None],
        0,
    ).astype(jnp.bfloat16)
    projected = jnp.einsum("crn,cd->rnd", normed_out, out_weights[which], preferred_element_type=jnp.float32)
    return (pair_rows.astype(jnp.float32) + out_gate.astype(jnp.float32) * projected).astype(jnp.bfloat16)


def on_device(pair_state, pair_mask, *params):
    mask_rows = pair_mask.astype(jnp.float32)
    middle = triangle(pair_state, mask_rows, 0, "cik,cjk->cij", *params)
    return triangle(middle, mask_rows, 1, "cki,ckj->cij", *params)


def solution(mesh):
    rows = ("groups", "row")
    return jax.shard_map(
        on_device,
        mesh=mesh,
        in_specs=(P(rows, None, None), P(rows, None), P(), P(), P(), P(), P()),
        out_specs=P(rows, None, None),
        check_vma=False,
    )
```

```python
import jax
import jax.numpy as jnp
from jax import lax
from jax.sharding import PartitionSpec as P


def layer_norm(values, norm_gain, norm_bias, reduce_dim):
    average = jnp.mean(values, axis=reduce_dim, keepdims=True)
    centred = values - average
    spread = jnp.mean(centred * centred, axis=reduce_dim, keepdims=True)
    return centred * lax.rsqrt(spread + 1e-05) * norm_gain + norm_bias


def by_partner(blocks):
    me = lax.axis_index("row")
    count = blocks.shape[0]
    bit = 1
    while bit < count:
        split = blocks.reshape((count // (2 * bit), 2, bit) + blocks.shape[1:])
        blocks = jnp.where((me & bit) != 0, split[:, ::-1], split).reshape(blocks.shape)
        bit *= 2
    return blocks


def exchange(blocks):
    count = blocks.shape[0]
    if count & (count - 1):
        return lax.all_to_all(blocks, "row", split_axis=0, concat_axis=0, tiled=True)
    out = by_partner(blocks)
    got = [out[0]]
    for k in range(1, count):
        got.append(lax.ppermute(out[k], "row", [(d, d ^ k) for d in range(count)]))
    return by_partner(jnp.stack(got))


def triangle(pair_rows, mask_rows, which, form, norm_gains, norm_biases, proj_weights, gate_weights, out_weights):
    groups = lax.axis_size("row")
    per_dev, tokens, channels = pair_rows.shape
    per_group = channels // groups
    normed = layer_norm(
        pair_rows.astype(jnp.float32), norm_gains[which, 0], norm_biases[which, 0], 2
    ).astype(jnp.bfloat16)
    weights = proj_weights[which]

    def gated(offset):
        gate_part = jnp.einsum(
            "rnd,de->ern", normed, weights[:, offset : offset + channels], preferred_element_type=jnp.float32
        )
        value_part = jnp.einsum(
            "rnd,de->ern",
            normed,
            weights[:, offset + channels : offset + 2 * channels],
            preferred_element_type=jnp.float32,
        )
        masked = jax.nn.sigmoid(gate_part) * value_part * mask_rows[None]
        return masked.astype(jnp.bfloat16).reshape(groups, 1, per_group, per_dev, tokens)

    both = jnp.concatenate([gated(0), gated(2 * channels)], axis=1)
    out_gate = jax.nn.sigmoid(
        jnp.einsum("rnd,de->rne", normed, gate_weights[which], preferred_element_type=jnp.float32)
    ).astype(jnp.bfloat16)
    both = exchange(both)
    left = jnp.moveaxis(both[:, 0], 0, 1).reshape(per_group, tokens, tokens)
    right = jnp.moveaxis(both[:, 1], 0, 1).reshape(per_group, tokens, tokens)
    product = jnp.einsum(form, left, right, preferred_element_type=jnp.float32).astype(jnp.bfloat16)
    product = jnp.moveaxis(product.reshape(per_group, groups, per_dev, tokens), 1, 0)
    merged = exchange(product)
    merged = merged.reshape(channels, per_dev, tokens)
    normed_out = layer_norm(
        merged.astype(jnp.float32),
        norm_gains[which, 1][:, None, None],
        norm_biases[which, 1][:, None, None],
        0,
    ).astype(jnp.bfloat16)
    projected = jnp.einsum("crn,cd->rnd", normed_out, out_weights[which], preferred_element_type=jnp.float32)
    return (pair_rows.astype(jnp.float32) + out_gate.astype(jnp.float32) * projected).astype(jnp.bfloat16)


def on_device(pair_state, pair_mask, *params):
    mask_rows = pair_mask.astype(jnp.float32)
    middle = triangle(pair_state, mask_rows, 0, "cik,cjk->cij", *params)
    return triangle(middle, mask_rows, 1, "cki,ckj->cij", *params)


def solution(mesh):
    rows = ("groups", "row")
    return jax.shard_map(
        on_device,
        mesh=mesh,
        in_specs=(P(rows, None, None), P(rows, None), P(), P(), P(), P(), P()),
        out_specs=P(rows, None, None),
        check_vma=False,
    )
```

```python
import jax
import jax.numpy as jnp
from jax import lax
from jax.sharding import PartitionSpec as P


def layer_norm(values, norm_gain, norm_bias, reduce_dim):
    average = jnp.mean(values, axis=reduce_dim, keepdims=True)
    centred = values - average
    spread = jnp.mean(centred * centred, axis=reduce_dim, keepdims=True)
    return centred * lax.rsqrt(spread + 1e-05) * norm_gain + norm_bias


def exchange(blocks):
    count = blocks.shape[0]
    core = lax.axis_index("row") % 2
    split = blocks.reshape((count // 2, 2) + blocks.shape[1:])
    keep = jnp.where(core == 0, split[:, 0], split[:, 1])
    send = jnp.where(core == 0, split[:, 1], split[:, 0])
    got = lax.ppermute(send, "row", [(d, d ^ 1) for d in range(count)])
    split = jnp.where(core == 0, jnp.stack([keep, got], 1), jnp.stack([got, keep], 1))
    same_core = [list(range(c, count, 2)) for c in range(2)]
    split = lax.all_to_all(split, "row", split_axis=0, concat_axis=0, tiled=True, axis_index_groups=same_core)
    return split.reshape(blocks.shape)


def triangle(pair_rows, mask_rows, which, form, norm_gains, norm_biases, proj_weights, gate_weights, out_weights):
    groups = lax.axis_size("row")
    per_dev, tokens, channels = pair_rows.shape
    per_group = channels // groups
    normed = layer_norm(
        pair_rows.astype(jnp.float32), norm_gains[which, 0], norm_biases[which, 0], 2
    ).astype(jnp.bfloat16)
    weights = proj_weights[which]

    def gated(offset):
        gate_part = jnp.einsum(
            "rnd,de->ern", normed, weights[:, offset : offset + channels], preferred_element_type=jnp.float32
        )
        value_part = jnp.einsum(
            "rnd,de->ern",
            normed,
            weights[:, offset + channels : offset + 2 * channels],
            preferred_element_type=jnp.float32,
        )
        masked = jax.nn.sigmoid(gate_part) * value_part * mask_rows[None]
        return masked.astype(jnp.bfloat16).reshape(groups, 1, per_group, per_dev, tokens)

    both = jnp.concatenate([gated(0), gated(2 * channels)], axis=1)
    out_gate = jax.nn.sigmoid(
        jnp.einsum("rnd,de->rne", normed, gate_weights[which], preferred_element_type=jnp.float32)
    ).astype(jnp.bfloat16)
    both = exchange(both)
    left = jnp.moveaxis(both[:, 0], 0, 1).reshape(per_group, tokens, tokens)
    right = jnp.moveaxis(both[:, 1], 0, 1).reshape(per_group, tokens, tokens)
    product = jnp.einsum(form, left, right, preferred_element_type=jnp.float32).astype(jnp.bfloat16)
    product = jnp.moveaxis(product.reshape(per_group, groups, per_dev, tokens), 1, 0)
    merged = exchange(product)
    merged = merged.reshape(channels, per_dev, tokens)
    normed_out = layer_norm(
        merged.astype(jnp.float32),
        norm_gains[which, 1][:, None, None],
        norm_biases[which, 1][:, None, None],
        0,
    ).astype(jnp.bfloat16)
    projected = jnp.einsum("crn,cd->rnd", normed_out, out_weights[which], preferred_element_type=jnp.float32)
    return (pair_rows.astype(jnp.float32) + out_gate.astype(jnp.float32) * projected).astype(jnp.bfloat16)


def on_device(pair_state, pair_mask, *params):
    mask_rows = pair_mask.astype(jnp.float32)
    middle = triangle(pair_state, mask_rows, 0, "cik,cjk->cij", *params)
    return triangle(middle, mask_rows, 1, "cki,ckj->cij", *params)


def solution(mesh):
    rows = ("groups", "row")
    return jax.shard_map(
        on_device,
        mesh=mesh,
        in_specs=(P(rows, None, None), P(rows, None), P(), P(), P(), P(), P()),
        out_specs=P(rows, None, None),
        check_vma=False,
    )
```

```python
import functools

import jax
import jax.numpy as jnp
from jax import lax
from jax.experimental import pallas as pl
from jax.experimental.pallas import tpu as pltpu
from jax.sharding import PartitionSpec as P

F32 = jnp.float32
BF16 = jnp.bfloat16
NT = (((1,), (1,)), ((), ()))
NN = (((1,), (0,)), ((), ()))
TN = (((0,), (0,)), ((), ()))


def dot(a, b, dims):
    return lax.dot_general(a, b, dims, preferred_element_type=F32)


def sigmoid(values):
    return 0.5 * jnp.tanh(0.5 * values) + 0.5


def unit(values, axis):
    scale = 1.0 / values.shape[axis]
    centred = values - jnp.sum(values, axis=axis, keepdims=True) * scale
    spread = jnp.sum(centred * centred, axis=axis, keepdims=True) * scale
    return centred * lax.rsqrt(spread + 1e-05)


def project_kernel(per_group, pair_ref, mask_ref, gain_ref, bias_ref, proj_ref, gatew_ref, both_ref, gate_ref, panels):
    project_rows(per_group, 0, lambda r: pair_ref[r], mask_ref, gain_ref, bias_ref, proj_ref, gatew_ref, both_ref, gate_ref, panels)


def project_rows(per_group, which, pair_row, mask_ref, gain_ref, bias_ref, proj_ref, gatew_ref, both_ref, gate_ref, panels):
    rows = mask_ref.shape[0]
    channels = gatew_ref.shape[2]
    groups = channels // per_group
    weights_t = proj_ref[which].T
    gain = gain_ref[which, 0:1]
    bias = bias_ref[which, 0:1]
    for r in range(rows):
        normed = (unit(pair_row(r).astype(F32), 1) * gain + bias).astype(BF16)
        products = dot(weights_t, normed, NT)
        mask = mask_ref[r : r + 1].astype(F32)
        for side in range(2):
            base = 2 * side * channels
            gated = sigmoid(products[base : base + channels]) * products[base + channels : base + 2 * channels] * mask
            for g in range(groups):
                start = (2 * g + side) * per_group
                panels[start : start + per_group, r, :] = gated[g * per_group : (g + 1) * per_group]
        gate_ref[r] = sigmoid(dot(normed, gatew_ref[which], NN)).astype(BF16)
    both_ref[...] = panels[...].astype(BF16).reshape(both_ref.shape)


def finish_rows(which, store, merged_ref, pair_ref, gate_ref, gain_ref, bias_ref, outw_ref, unit_scratch):
    channels, rows, tokens = unit_scratch.shape
    unit_scratch[...] = unit(merged_ref[...].astype(F32).reshape(channels, rows, tokens), 0)
    gain = jnp.broadcast_to(gain_ref[which, 1:2], (tokens, channels)).T
    bias = jnp.broadcast_to(bias_ref[which, 1:2], (tokens, channels)).T
    for r in range(rows):
        normed = (unit_scratch[:, r, :] * gain + bias).astype(BF16)
        projected = dot(normed, outw_ref[which], TN)
        store(r, (pair_ref[r].astype(F32) + gate_ref[r].astype(F32) * projected).astype(BF16))


def mix_kernel(per_group, rows, incoming, both_ref, product_ref):
    groups, _, tokens = both_ref.shape
    step = 2 * rows

    def matrices(side, pair):
        start = (side * per_group + 2 * pair) * rows
        block = both_ref[:, start : start + step, :].astype(F32)
        return [block[:, h * rows : (h + 1) * rows].reshape(groups * rows, tokens).astype(BF16) for h in range(2)]

    for pair in range(per_group // 2):
        lefts, rights = matrices(0, pair), matrices(1, pair)
        sums = [
            dot(left, right, TN if incoming else NT).reshape(groups, rows, tokens)
            for left, right in zip(lefts, rights)
        ]
        product_ref[:, pair * step : (pair + 1) * step, :] = jnp.concatenate(sums, axis=1).astype(BF16)


def step_kernel(
    per_group, merged_ref, pair_ref, gate_ref, mask_ref, gain_ref, bias_ref, outw_ref, proj_ref,
    gatew_ref, middle_ref, both_ref, gate1_ref, unit_scratch, panels,
):
    def store(r, values):
        middle_ref[r] = values

    finish_rows(0, store, merged_ref, pair_ref, gate_ref, gain_ref, bias_ref, outw_ref, unit_scratch)
    project_rows(
        per_group, 1, lambda r: middle_ref[r], mask_ref, gain_ref, bias_ref, proj_ref, gatew_ref, both_ref, gate1_ref, panels
    )


def finish_kernel(merged_ref, pair_ref, gate_ref, gain_ref, bias_ref, outw_ref, result_ref, unit_scratch):
    def store(r, values):
        result_ref[r] = values

    finish_rows(1, store, merged_ref, pair_ref, gate_ref, gain_ref, bias_ref, outw_ref, unit_scratch)


def on_device(pair, mask, gains, biases, proj, gatew, outw):
    groups = lax.axis_size("row")
    rows, tokens, channels = pair.shape
    per_group = channels // groups
    whole = pl.BlockSpec(memory_space=pltpu.VMEM)
    params = pltpu.CompilerParams(vmem_limit_bytes=48 * 1024 * 1024)
    both_shape = jax.ShapeDtypeStruct((2 * channels * rows, tokens), BF16)
    pair_shape = jax.ShapeDtypeStruct(pair.shape, BF16)
    panels = pltpu.VMEM((2 * channels, rows, tokens), F32)
    unit_scratch = pltpu.VMEM((channels, rows, tokens), F32)

    def exchange(array):
        return lax.all_to_all(array, "row", split_axis=0, concat_axis=0, tiled=True)

    def mix(both, incoming):
        product = pl.pallas_call(
            functools.partial(mix_kernel, per_group, rows, incoming),
            out_shape=jax.ShapeDtypeStruct((groups, per_group * rows, tokens), BF16),
            in_specs=[whole],
            out_specs=whole,
            compiler_params=params,
            name="mix",
        )(both.reshape(groups, 2 * per_group * rows, tokens))
        return product.reshape(channels * rows, tokens)

    both, gate = pl.pallas_call(
        functools.partial(project_kernel, per_group),
        out_shape=(both_shape, pair_shape),
        in_specs=[whole] * 6,
        out_specs=(whole, whole),
        scratch_shapes=[panels],
        compiler_params=params,
        name="project",
    )(pair, mask, gains, biases, proj, gatew)
    merged = exchange(mix(exchange(both), False))
    middle, both, gate = pl.pallas_call(
        functools.partial(step_kernel, per_group),
        out_shape=(pair_shape, both_shape, pair_shape),
        in_specs=[whole] * 9,
        out_specs=(whole, whole, whole),
        scratch_shapes=[unit_scratch, panels],
        compiler_params=params,
        name="finish_project",
    )(merged, pair, gate, mask, gains, biases, outw, proj, gatew)
    merged = exchange(mix(exchange(both), True))
    return pl.pallas_call(
        finish_kernel,
        out_shape=pair_shape,
        in_specs=[whole] * 6,
        out_specs=whole,
        scratch_shapes=[unit_scratch],
        compiler_params=params,
        name="finish",
    )(merged, middle, gate, gains, biases, outw)


def solution(mesh):
    rows = ("groups", "row")
    return jax.shard_map(
        on_device,
        mesh=mesh,
        in_specs=(P(rows, None, None), P(rows, None), P(), P(), P(), P(), P()),
        out_specs=P(rows, None, None),
        check_vma=False,
    )
```

```python
import functools

import jax
import jax.numpy as jnp
from jax import lax
from jax.experimental import pallas as pl
from jax.experimental.pallas import tpu as pltpu
from jax.sharding import PartitionSpec as P

F32 = jnp.float32
BF16 = jnp.bfloat16
NT = (((1,), (1,)), ((), ()))
NN = (((1,), (0,)), ((), ()))
TN = (((0,), (0,)), ((), ()))


def dot(a, b, dims):
    return lax.dot_general(a, b, dims, preferred_element_type=F32)


def sigmoid(values):
    return 0.5 * jnp.tanh(0.5 * values) + 0.5


def unit(values, axis):
    scale = 1.0 / values.shape[axis]
    centred = values - jnp.sum(values, axis=axis, keepdims=True) * scale
    spread = jnp.sum(centred * centred, axis=axis, keepdims=True) * scale
    return centred * lax.rsqrt(spread + 1e-05)


def project_kernel(per_group, *refs):
    inputs, (both_ref, gate_ref), held, (panels, sems) = refs[:7], refs[7:9], refs[9:16], refs[16:]
    copies = [pltpu.make_async_copy(src, dst, sems.at[n]) for n, (src, dst) in enumerate(zip(inputs, held))]
    for copy in copies:
        copy.start()
    for copy in copies:
        copy.wait()
    pair_ref, mask_ref, gain_ref, bias_ref, proj_ref, gatew_ref, _ = held
    project_rows(per_group, 0, lambda r: pair_ref[r], mask_ref, gain_ref, bias_ref, proj_ref, gatew_ref, both_ref, gate_ref, panels)


def project_rows(per_group, which, pair_row, mask_ref, gain_ref, bias_ref, proj_ref, gatew_ref, both_ref, gate_ref, panels):
    rows = mask_ref.shape[0]
    channels = gatew_ref.shape[2]
    groups = channels // per_group
    weights_t = proj_ref[which].T
    gain = gain_ref[which, 0:1]
    bias = bias_ref[which, 0:1]
    for r in range(rows):
        normed = (unit(pair_row(r).astype(F32), 1) * gain + bias).astype(BF16)
        products = dot(weights_t, normed, NT)
        mask = mask_ref[r : r + 1].astype(F32)
        for side in range(2):
            base = 2 * side * channels
            gated = sigmoid(products[base : base + channels]) * products[base + channels : base + 2 * channels] * mask
            for g in range(groups):
                start = (2 * g + side) * per_group
                panels[start : start + per_group, r, :] = gated[g * per_group : (g + 1) * per_group]
        gate_ref[r] = sigmoid(dot(normed, gatew_ref[which], NN)).astype(BF16)
    both_ref[...] = panels[...].astype(BF16).reshape(both_ref.shape)


def finish_rows(which, store, merged_ref, pair_ref, gate_ref, gain_ref, bias_ref, outw_ref, unit_scratch):
    channels, rows, tokens = unit_scratch.shape
    unit_scratch[...] = unit(merged_ref[...].astype(F32).reshape(channels, rows, tokens), 0)
    gain = jnp.broadcast_to(gain_ref[which, 1:2], (tokens, channels)).T
    bias = jnp.broadcast_to(bias_ref[which, 1:2], (tokens, channels)).T
    for r in range(rows):
        normed = (unit_scratch[:, r, :] * gain + bias).astype(BF16)
        projected = dot(normed, outw_ref[which], TN)
        store(r, (pair_ref[r].astype(F32) + gate_ref[r].astype(F32) * projected).astype(BF16))


def mix_kernel(per_group, rows, incoming, both_ref, product_ref):
    groups, _, tokens = both_ref.shape
    step = 2 * rows

    def matrices(side, pair):
        start = (side * per_group + 2 * pair) * rows
        block = both_ref[:, start : start + step, :].astype(F32)
        return [block[:, h * rows : (h + 1) * rows].reshape(groups * rows, tokens).astype(BF16) for h in range(2)]

    for pair in range(per_group // 2):
        lefts, rights = matrices(0, pair), matrices(1, pair)
        sums = [
            dot(left, right, TN if incoming else NT).reshape(groups, rows, tokens)
            for left, right in zip(lefts, rights)
        ]
        product_ref[:, pair * step : (pair + 1) * step, :] = jnp.concatenate(sums, axis=1).astype(BF16)


def step_kernel(
    per_group, merged_ref, pair_ref, gate_ref, mask_ref, gain_ref, bias_ref, outw_ref, proj_ref,
    gatew_ref, middle_ref, both_ref, gate1_ref, unit_scratch, panels,
):
    def store(r, values):
        middle_ref[r] = values

    finish_rows(0, store, merged_ref, pair_ref, gate_ref, gain_ref, bias_ref, outw_ref, unit_scratch)
    project_rows(
        per_group, 1, lambda r: middle_ref[r], mask_ref, gain_ref, bias_ref, proj_ref, gatew_ref, both_ref, gate1_ref, panels
    )


def finish_kernel(merged_ref, pair_ref, gate_ref, gain_ref, bias_ref, outw_ref, result_ref, unit_scratch, done, sems):
    copies = []

    def store(r, values):
        done[r] = values
        copies.append(pltpu.make_async_copy(done.at[r], result_ref.at[r], sems.at[r]))
        copies[-1].start()

    finish_rows(1, store, merged_ref, pair_ref, gate_ref, gain_ref, bias_ref, outw_ref, unit_scratch)
    for copy in copies:
        copy.wait()


def on_device(pair, mask, gains, biases, proj, gatew, outw):
    groups = lax.axis_size("row")
    rows, tokens, channels = pair.shape
    per_group = channels // groups
    whole = pl.BlockSpec(memory_space=pltpu.VMEM)
    hbm = pl.BlockSpec(memory_space=pltpu.HBM)
    params = pltpu.CompilerParams(vmem_limit_bytes=48 * 1024 * 1024)
    both_shape = jax.ShapeDtypeStruct((2 * channels * rows, tokens), BF16)
    pair_shape = jax.ShapeDtypeStruct(pair.shape, BF16)
    panels = pltpu.VMEM((2 * channels, rows, tokens), F32)
    unit_scratch = pltpu.VMEM((channels, rows, tokens), F32)

    def exchange(array):
        return lax.all_to_all(array, "row", split_axis=0, concat_axis=0, tiled=True)

    def mix(both, incoming):
        product = pl.pallas_call(
            functools.partial(mix_kernel, per_group, rows, incoming),
            out_shape=jax.ShapeDtypeStruct((groups, per_group * rows, tokens), BF16),
            in_specs=[whole],
            out_specs=whole,
            compiler_params=params,
            name="mix",
        )(both.reshape(groups, 2 * per_group * rows, tokens))
        return product.reshape(channels * rows, tokens)

    inputs = (pair, mask, gains, biases, proj, gatew, outw)
    both, gate, pair, mask, gains, biases, proj, gatew, outw = pl.pallas_call(
        functools.partial(project_kernel, per_group),
        out_shape=(both_shape, pair_shape) + tuple(jax.ShapeDtypeStruct(a.shape, a.dtype) for a in inputs),
        in_specs=[hbm] * 7,
        out_specs=(whole,) * 9,
        scratch_shapes=[panels, pltpu.SemaphoreType.DMA((7,))],
        compiler_params=params,
        name="project",
    )(*(pltpu.with_memory_space_constraint(a, pltpu.HBM) for a in inputs))
    merged = exchange(mix(exchange(both), False))
    middle, both, gate = pl.pallas_call(
        functools.partial(step_kernel, per_group),
        out_shape=(pair_shape, both_shape, pair_shape),
        in_specs=[whole] * 9,
        out_specs=(whole, whole, whole),
        scratch_shapes=[unit_scratch, panels],
        compiler_params=params,
        name="finish_project",
    )(merged, pair, gate, mask, gains, biases, outw, proj, gatew)
    merged = exchange(mix(exchange(both), True))
    return pl.pallas_call(
        finish_kernel,
        out_shape=pair_shape,
        in_specs=[whole] * 6,
        out_specs=hbm,
        scratch_shapes=[unit_scratch, pltpu.VMEM(pair.shape, BF16), pltpu.SemaphoreType.DMA((rows,))],
        compiler_params=params,
        name="finish",
    )(merged, middle, gate, gains, biases, outw)


def solution(mesh):
    rows = ("groups", "row")
    return jax.shard_map(
        on_device,
        mesh=mesh,
        in_specs=(P(rows, None, None), P(rows, None), P(), P(), P(), P(), P()),
        out_specs=P(rows, None, None),
        check_vma=False,
    )
```

```python
import functools

import jax
import jax.numpy as jnp
from jax import lax
from jax.experimental import pallas as pl
from jax.experimental.pallas import tpu as pltpu
from jax.sharding import PartitionSpec as P

F32 = jnp.float32
BF16 = jnp.bfloat16
NT = (((1,), (1,)), ((), ()))
NN = (((1,), (0,)), ((), ()))
TN = (((0,), (0,)), ((), ()))


def dot(a, b, dims):
    return lax.dot_general(a, b, dims, preferred_element_type=F32)


def sigmoid(values):
    return 0.5 * jnp.tanh(0.5 * values) + 0.5


def unit(values, axis):
    scale = 1.0 / values.shape[axis]
    centred = values - jnp.sum(values, axis=axis, keepdims=True) * scale
    spread = jnp.sum(centred * centred, axis=axis, keepdims=True) * scale
    return centred * lax.rsqrt(spread + 1e-05)


def chunks(rows, tokens):
    wide = max(1, min(rows, 256 // tokens))
    return [list(range(start, min(start + wide, rows))) for start in range(0, rows, wide)]


def span(chunk, tokens):
    return slice(chunk[0] * tokens, (chunk[-1] + 1) * tokens)


def lanes(parts):
    return parts[0] if len(parts) == 1 else jnp.concatenate(parts, axis=1)


def affine(values, gain, bias, tokens):
    parts = [values[:, n : n + tokens] * gain + bias for n in range(0, values.shape[1], tokens)]
    return lanes(parts).astype(BF16)


def store_panels(panels, per_group, chunk, tokens, products, mask):
    channels = products.shape[0] // 4
    for side in range(2):
        base = 2 * side * channels
        gated = sigmoid(products[base : base + channels]) * products[base + channels : base + 2 * channels] * mask
        for h, r in enumerate(chunk):
            for g in range(channels // per_group):
                start = (2 * g + side) * per_group
                panels[start : start + per_group, r, :] = gated[
                    g * per_group : (g + 1) * per_group, h * tokens : (h + 1) * tokens
                ]


def mask_lanes(mask_ref, chunk):
    return lanes([mask_ref[r : r + 1].astype(F32) for r in chunk])


def project_kernel(per_group, *refs):
    inputs, both_ref, held, (panels, sems) = refs[:7], refs[7], refs[8:15], refs[15:]
    copies = [pltpu.make_async_copy(src, dst, sems.at[n]) for n, (src, dst) in enumerate(zip(inputs, held))]
    for copy in copies:
        copy.start()
    for copy in copies[:5]:
        copy.wait()
    pair_ref, mask_ref, gain_ref, bias_ref, proj_ref, _, _ = held
    rows, tokens, channels = pair_ref.shape
    weights_t = proj_ref[0].T
    for chunk in chunks(rows, tokens):
        pair = pair_ref[chunk[0] : chunk[-1] + 1].reshape(len(chunk) * tokens, channels)
        normed = (unit(pair.astype(F32), 1) * gain_ref[0, 0:1] + bias_ref[0, 0:1]).astype(BF16)
        products = dot(weights_t, normed, NT)
        store_panels(panels, per_group, chunk, tokens, products, mask_lanes(mask_ref, chunk))
    both_ref[...] = panels[...].astype(BF16).reshape(both_ref.shape)
    for copy in copies[5:]:
        copy.wait()


def prepare_kernel(
    pair_ref, gain_ref, bias_ref, proj_ref, gatew_ref, outw_ref,
    pair_t_ref, gate_t_ref, columns_ref, proj_t_ref, gatew_t_ref, outw_t_ref,
):
    rows, tokens, channels = pair_ref.shape

    def column(ref, which, norm):
        return jnp.broadcast_to(ref[which, norm : norm + 1], (tokens, channels)).T

    for n, (which, norm) in enumerate(((0, 1), (1, 0), (1, 1))):
        columns_ref[2 * n] = column(gain_ref, which, norm)
        columns_ref[2 * n + 1] = column(bias_ref, which, norm)
    proj_t_ref[...] = proj_ref[1].T
    gatew_t_ref[...] = gatew_ref[1].T
    outw_t_ref[0] = outw_ref[0].T
    outw_t_ref[1] = outw_ref[1].T
    first_t = gatew_ref[0].T
    gain, bias = column(gain_ref, 0, 0), column(bias_ref, 0, 0)
    for chunk in chunks(rows, tokens):
        pair_t = lanes([pair_ref[r].T for r in chunk])
        pair_t_ref[:, span(chunk, tokens)] = pair_t
        normed = affine(unit(pair_t.astype(F32), 0), gain, bias, tokens)
        gate_t_ref[:, span(chunk, tokens)] = sigmoid(dot(first_t, normed, NN)).astype(BF16)


def gate_kernel(normed_t_ref, gatew_t_ref, gate_t_ref):
    step = min(256, normed_t_ref.shape[1])
    for start in range(0, normed_t_ref.shape[1], step):
        gate = sigmoid(dot(gatew_t_ref[...], normed_t_ref[:, start : start + step], NN))
        gate_t_ref[:, start : start + step] = gate.astype(BF16)


def mix_kernel(per_group, rows, incoming, both_ref, product_ref):
    groups, _, tokens = both_ref.shape
    step = 2 * rows

    def matrices(side, pair):
        start = (side * per_group + 2 * pair) * rows
        block = both_ref[:, start : start + step, :].astype(F32)
        return [block[:, h * rows : (h + 1) * rows].reshape(groups * rows, tokens).astype(BF16) for h in range(2)]

    for pair in range(per_group // 2):
        lefts, rights = matrices(0, pair), matrices(1, pair)
        sums = [
            dot(left, right, TN if incoming else NT).reshape(groups, rows, tokens)
            for left, right in zip(lefts, rights)
        ]
        product_ref[:, pair * step : (pair + 1) * step, :] = jnp.concatenate(sums, axis=1).astype(BF16)


def finish_rows(emit, merged_ref, pair_t_ref, gate_t_ref, gain, bias, outw_t, unit_scratch):
    channels, rows, tokens = unit_scratch.shape
    unit_scratch[...] = unit(merged_ref[...].astype(F32).reshape(channels, rows, tokens), 0)
    for chunk in chunks(rows, tokens):
        normed = lanes([(unit_scratch[:, r, :] * gain + bias).astype(BF16) for r in chunk])
        part = span(chunk, tokens)
        change = gate_t_ref[:, part].astype(F32) * dot(outw_t, normed, NN)
        emit(chunk, part, (pair_t_ref[:, part].astype(F32) + change).astype(BF16))


def step_kernel(
    per_group, merged_ref, pair_t_ref, gate_t_ref, mask_ref, columns_ref, outw_t_ref, proj_t_ref,
    both_ref, middle_t_ref, normed_t_ref, unit_scratch, panels,
):
    tokens = mask_ref.shape[1]

    def emit(chunk, part, middle):
        middle_t_ref[:, part] = middle
        normed = affine(unit(middle.astype(F32), 0), columns_ref[2], columns_ref[3], tokens)
        normed_t_ref[:, part] = normed
        products = dot(proj_t_ref[...], normed, NN)
        store_panels(panels, per_group, chunk, tokens, products, mask_lanes(mask_ref, chunk))

    finish_rows(
        emit, merged_ref, pair_t_ref, gate_t_ref, columns_ref[0], columns_ref[1], outw_t_ref[0], unit_scratch
    )
    both_ref[...] = panels[...].astype(BF16).reshape(both_ref.shape)


def finish_kernel(
    merged_ref, middle_t_ref, gate_t_ref, columns_ref, outw_t_ref, result_ref, unit_scratch, done, sems
):
    tokens = unit_scratch.shape[2]
    copies = []

    def emit(chunk, part, result):
        for h, r in enumerate(chunk):
            done[r] = result[:, h * tokens : (h + 1) * tokens].T
            copies.append(pltpu.make_async_copy(done.at[r], result_ref.at[r], sems.at[r]))
            copies[-1].start()

    finish_rows(
        emit, merged_ref, middle_t_ref, gate_t_ref, columns_ref[4], columns_ref[5], outw_t_ref[1], unit_scratch
    )
    for copy in copies:
        copy.wait()


def on_device(*inputs):
    groups = lax.axis_size("row")
    rows, tokens, channels = inputs[0].shape
    per_group = channels // groups
    whole = pl.BlockSpec(memory_space=pltpu.VMEM)
    hbm = pl.BlockSpec(memory_space=pltpu.HBM)
    params = pltpu.CompilerParams(vmem_limit_bytes=48 * 1024 * 1024)
    shape = jax.ShapeDtypeStruct
    both_shape = shape((2 * channels * rows, tokens), BF16)
    flat_shape = shape((channels, rows * tokens), BF16)
    panels = pltpu.VMEM((2 * channels, rows, tokens), F32)
    unit_scratch = pltpu.VMEM((channels, rows, tokens), F32)
    beside = pl.CostEstimate(flops=10**9, bytes_accessed=4 * 2**20, transcendentals=0)

    def exchange(array):
        return lax.all_to_all(array, "row", split_axis=0, concat_axis=0, tiled=True)

    def mix(both, incoming):
        product = pl.pallas_call(
            functools.partial(mix_kernel, per_group, rows, incoming),
            out_shape=shape((groups, per_group * rows, tokens), BF16),
            in_specs=[whole],
            out_specs=whole,
            compiler_params=params,
            name="mix",
        )(both.reshape(groups, 2 * per_group * rows, tokens))
        return product.reshape(channels * rows, tokens)

    both, pair, mask, gains, biases, proj, gatew, outw = pl.pallas_call(
        functools.partial(project_kernel, per_group),
        out_shape=(both_shape,) + tuple(shape(a.shape, a.dtype) for a in inputs),
        in_specs=[hbm] * 7,
        out_specs=(whole,) * 8,
        scratch_shapes=[panels, pltpu.SemaphoreType.DMA((7,))],
        compiler_params=params,
        name="project",
    )(*(pltpu.with_memory_space_constraint(a, pltpu.HBM) for a in inputs))
    both = exchange(both)
    pair_t, gate_t, columns, proj_t, gatew_t, outw_t = pl.pallas_call(
        prepare_kernel,
        out_shape=(
            flat_shape,
            flat_shape,
            shape((6, channels, tokens), F32),
            shape((4 * channels, channels), BF16),
            shape((channels, channels), BF16),
            shape((2, channels, channels), BF16),
        ),
        in_specs=[whole] * 6,
        out_specs=(whole,) * 6,
        compiler_params=params,
        cost_estimate=beside,
        name="prepare",
    )(pair, gains, biases, proj, gatew, outw)
    merged = exchange(mix(both, False))
    both, middle_t, normed_t = pl.pallas_call(
        functools.partial(step_kernel, per_group),
        out_shape=(both_shape, flat_shape, flat_shape),
        in_specs=[whole] * 7,
        out_specs=(whole,) * 3,
        scratch_shapes=[unit_scratch, panels],
        compiler_params=params,
        name="finish_project",
    )(merged, pair_t, gate_t, mask, columns, outw_t, proj_t)
    both = exchange(both)
    gate_t = pl.pallas_call(
        gate_kernel,
        out_shape=flat_shape,
        in_specs=[whole] * 2,
        out_specs=whole,
        compiler_params=params,
        cost_estimate=beside,
        name="gate",
    )(normed_t, gatew_t)
    merged = exchange(mix(both, True))
    return pl.pallas_call(
        finish_kernel,
        out_shape=shape((rows, tokens, channels), BF16),
        in_specs=[whole] * 5,
        out_specs=hbm,
        scratch_shapes=[unit_scratch, pltpu.VMEM((rows, tokens, channels), BF16), pltpu.SemaphoreType.DMA((rows,))],
        compiler_params=params,
        name="finish",
    )(merged, middle_t, gate_t, columns, outw_t)


def solution(mesh):
    rows = ("groups", "row")
    return jax.shard_map(
        on_device,
        mesh=mesh,
        in_specs=(P(rows, None, None), P(rows, None), P(), P(), P(), P(), P()),
        out_specs=P(rows, None, None),
        check_vma=False,
    )
```

```python
import functools

import jax
import jax.numpy as jnp
from jax import lax
from jax.experimental import pallas as pl
from jax.experimental.pallas import tpu as pltpu
from jax.sharding import PartitionSpec as P

F32 = jnp.float32
BF16 = jnp.bfloat16
LANES = 128
NT = (((1,), (1,)), ((), ()))
NN = (((1,), (0,)), ((), ()))
TN = (((0,), (0,)), ((), ()))


def dot(a, b, dims):
    return lax.dot_general(a, b, dims, preferred_element_type=F32)


def sigmoid(values):
    return 0.5 * jnp.tanh(0.5 * values) + 0.5


def unit(values, axis):
    scale = 1.0 / values.shape[axis]
    centred = values - jnp.sum(values, axis=axis, keepdims=True) * scale
    spread = jnp.sum(centred * centred, axis=axis, keepdims=True) * scale
    return centred * lax.rsqrt(spread + 1e-05)


def chunks(rows, tokens):
    wide = max(1, min(rows, 256 // tokens))
    return [list(range(start, min(start + wide, rows))) for start in range(0, rows, wide)]


def span(chunk, tokens):
    return slice(chunk[0] * tokens, (chunk[-1] + 1) * tokens)


def lanes(parts):
    return parts[0] if len(parts) == 1 else jnp.concatenate(parts, axis=1)


def affine(values, gain, bias, tokens):
    parts = [values[:, n : n + tokens] * gain + bias for n in range(0, values.shape[1], tokens)]
    return lanes(parts).astype(BF16)


def store_panels(panels, per_group, rows, chunk, tokens, products, mask):
    channels = products.shape[0] // 5
    for side in range(2):
        base = 2 * side * channels
        gated = sigmoid(products[base : base + channels]) * products[base + channels : base + 2 * channels] * mask
        for h, r in enumerate(chunk):
            for g in range(channels // per_group):
                where = pl.ds((2 * g + side) * per_group * rows + r, per_group, stride=rows)
                for t in range(tokens // LANES):
                    first = h * tokens + t * LANES
                    panels[t, where, :] = gated[g * per_group : (g + 1) * per_group, first : first + LANES]
    return sigmoid(products[4 * channels :]).astype(BF16)


def mask_lanes(mask_ref, chunk):
    return lanes([mask_ref[r : r + 1].astype(F32) for r in chunk])


def column(ref, which, norm, tokens):
    row = ref[which, norm : norm + 1]
    return jnp.broadcast_to(row, (tokens, row.shape[1])).T


def project_kernel(per_group, *refs):
    inputs, refs = refs[:7], refs[7:]
    both_ref, pair_t_ref, gate_t_ref, mask_ref, columns_ref, proj_t_ref, outw_t_ref = refs[:7]
    pair_ref, gain_ref, bias_ref, proj_ref, gatew_ref, outw_ref, panels, sems = refs[7:]
    held = (pair_ref, mask_ref, gain_ref, bias_ref, proj_ref, gatew_ref, outw_ref)
    copies = [pltpu.make_async_copy(src, dst, sems.at[n]) for n, (src, dst) in enumerate(zip(inputs, held))]
    for copy in copies:
        copy.start()
    for copy in copies:
        copy.wait()
    rows, tokens, channels = pair_ref.shape
    for which in range(2):
        proj_t_ref[which, : 4 * channels] = proj_ref[which].T
        proj_t_ref[which, 4 * channels :] = gatew_ref[which].T
        outw_t_ref[which] = outw_ref[which].T
    for n, (which, norm) in enumerate(((0, 1), (1, 0), (1, 1))):
        columns_ref[2 * n] = column(gain_ref, which, norm, tokens)
        columns_ref[2 * n + 1] = column(bias_ref, which, norm, tokens)
    gain, bias = column(gain_ref, 0, 0, tokens), column(bias_ref, 0, 0, tokens)
    for chunk in chunks(rows, tokens):
        part = span(chunk, tokens)
        pair_t = lanes([pair_ref[r].T for r in chunk])
        pair_t_ref[:, part] = pair_t
        normed = affine(unit(pair_t.astype(F32), 0), gain, bias, tokens)
        products = dot(proj_t_ref[0], normed, NN)
        gate_t_ref[:, part] = store_panels(
            panels, per_group, rows, chunk, tokens, products, mask_lanes(mask_ref, chunk)
        )
    for t in range(tokens // LANES):
        both_ref[:, t * LANES : (t + 1) * LANES] = panels[t].astype(BF16)


def mix_kernel(per_group, rows, incoming, both_ref, product_ref):
    groups, _, tokens = both_ref.shape
    step = 2 * rows

    def matrices(side, pair):
        start = (side * per_group + 2 * pair) * rows
        block = both_ref[:, start : start + step, :].astype(F32)
        return [block[:, h * rows : (h + 1) * rows].reshape(groups * rows, tokens).astype(BF16) for h in range(2)]

    for pair in range(per_group // 2):
        lefts, rights = matrices(0, pair), matrices(1, pair)
        sums = [
            dot(left, right, TN if incoming else NT).reshape(groups, rows, tokens)
            for left, right in zip(lefts, rights)
        ]
        product_ref[:, pair * step : (pair + 1) * step, :] = jnp.concatenate(sums, axis=1).astype(BF16)


def finish_rows(emit, rows, merged_ref, pair_t_ref, gate_t_ref, gain, bias, outw_t, unit_scratch):
    tokens = merged_ref.shape[1]
    channels = merged_ref.shape[0] // rows
    sums = merged_ref[...].astype(F32).reshape(channels, rows, tokens)
    units = unit(sums, 0).reshape(channels * rows, tokens)
    tiles = range(tokens // LANES)
    for t in tiles:
        unit_scratch[t] = units[:, t * LANES : (t + 1) * LANES]
    for chunk in chunks(rows, tokens):
        part = span(chunk, tokens)
        units = lanes([unit_scratch[t, pl.ds(r, channels, stride=rows), :] for r in chunk for t in tiles])
        normed = affine(units, gain, bias, tokens)
        change = gate_t_ref[:, part].astype(F32) * dot(outw_t, normed, NN)
        emit(chunk, part, (pair_t_ref[:, part].astype(F32) + change).astype(BF16))


def step_kernel(
    per_group, merged_ref, pair_t_ref, gate_t_ref, mask_ref, columns_ref, outw_t_ref, proj_t_ref,
    both_ref, middle_t_ref, gate1_t_ref, unit_scratch, panels,
):
    rows, tokens = mask_ref.shape

    def emit(chunk, part, middle):
        middle_t_ref[:, part] = middle
        normed = affine(unit(middle.astype(F32), 0), columns_ref[2], columns_ref[3], tokens)
        products = dot(proj_t_ref[1], normed, NN)
        gate1_t_ref[:, part] = store_panels(
            panels, per_group, rows, chunk, tokens, products, mask_lanes(mask_ref, chunk)
        )

    finish_rows(
        emit, rows, merged_ref, pair_t_ref, gate_t_ref, columns_ref[0], columns_ref[1], outw_t_ref[0], unit_scratch
    )
    for t in range(tokens // LANES):
        both_ref[:, t * LANES : (t + 1) * LANES] = panels[t].astype(BF16)


def finish_kernel(
    merged_ref, middle_t_ref, gate_t_ref, columns_ref, outw_t_ref, result_ref, unit_scratch, done, sems
):
    rows, tokens, _ = result_ref.shape
    copies = []

    def emit(chunk, part, result):
        for h, r in enumerate(chunk):
            done[r] = result[:, h * tokens : (h + 1) * tokens].T
            copies.append(pltpu.make_async_copy(done.at[r], result_ref.at[r], sems.at[r]))
            copies[-1].start()

    finish_rows(
        emit, rows, merged_ref, middle_t_ref, gate_t_ref, columns_ref[4], columns_ref[5], outw_t_ref[1], unit_scratch
    )
    for copy in copies:
        copy.wait()


def on_device(*inputs):
    groups = lax.axis_size("row")
    rows, tokens, channels = inputs[0].shape
    per_group = channels // groups
    whole = pl.BlockSpec(memory_space=pltpu.VMEM)
    hbm = pl.BlockSpec(memory_space=pltpu.HBM)
    params = pltpu.CompilerParams(vmem_limit_bytes=48 * 1024 * 1024)
    shape = jax.ShapeDtypeStruct
    both_shape = shape((2 * channels * rows, tokens), BF16)
    flat_shape = shape((channels, rows * tokens), BF16)
    panels = pltpu.VMEM((tokens // LANES, 2 * channels * rows, LANES), F32)
    unit_scratch = pltpu.VMEM((tokens // LANES, channels * rows, LANES), F32)

    def exchange(array):
        return lax.all_to_all(array, "row", split_axis=0, concat_axis=0, tiled=True)

    def mix(both, incoming):
        product = pl.pallas_call(
            functools.partial(mix_kernel, per_group, rows, incoming),
            out_shape=shape((groups, per_group * rows, tokens), BF16),
            in_specs=[whole],
            out_specs=whole,
            compiler_params=params,
            name="mix",
        )(both.reshape(groups, 2 * per_group * rows, tokens))
        return product.reshape(channels * rows, tokens)

    both, pair_t, gate_t, mask, columns, proj_t, outw_t = pl.pallas_call(
        functools.partial(project_kernel, per_group),
        out_shape=(
            both_shape,
            flat_shape,
            flat_shape,
            shape((rows, tokens), inputs[1].dtype),
            shape((6, channels, tokens), F32),
            shape((2, 5 * channels, channels), BF16),
            shape((2, channels, channels), BF16),
        ),
        in_specs=[hbm] * 7,
        out_specs=(whole,) * 7,
        scratch_shapes=[pltpu.VMEM(inputs[n].shape, inputs[n].dtype) for n in (0, 2, 3, 4, 5, 6)]
        + [panels, pltpu.SemaphoreType.DMA((7,))],
        compiler_params=params,
        name="project",
    )(*(pltpu.with_memory_space_constraint(a, pltpu.HBM) for a in inputs))
    merged = exchange(mix(exchange(both), False))
    both, middle_t, gate_t = pl.pallas_call(
        functools.partial(step_kernel, per_group),
        out_shape=(both_shape, flat_shape, flat_shape),
        in_specs=[whole] * 7,
        out_specs=(whole,) * 3,
        scratch_shapes=[unit_scratch, panels],
        compiler_params=params,
        name="finish_project",
    )(merged, pair_t, gate_t, mask, columns, outw_t, proj_t)
    merged = exchange(mix(exchange(both), True))
    return pl.pallas_call(
        finish_kernel,
        out_shape=shape((rows, tokens, channels), BF16),
        in_specs=[whole] * 5,
        out_specs=hbm,
        scratch_shapes=[unit_scratch, pltpu.VMEM((rows, tokens, channels), BF16), pltpu.SemaphoreType.DMA((rows,))],
        compiler_params=params,
        name="finish",
    )(merged, middle_t, gate_t, columns, outw_t)


def solution(mesh):
    rows = ("groups", "row")
    return jax.shard_map(
        on_device,
        mesh=mesh,
        in_specs=(P(rows, None, None), P(rows, None), P(), P(), P(), P(), P()),
        out_specs=P(rows, None, None),
        check_vma=False,
    )
```

```python
import functools

import jax
import jax.numpy as jnp
from jax import lax
from jax.experimental import pallas as pl
from jax.experimental.pallas import tpu as pltpu
from jax.sharding import PartitionSpec as P

F32 = jnp.float32
BF16 = jnp.bfloat16
LANES = 128
NT = (((1,), (1,)), ((), ()))
NN = (((1,), (0,)), ((), ()))
TN = (((0,), (0,)), ((), ()))


def dot(a, b, dims):
    return lax.dot_general(a, b, dims, preferred_element_type=F32)


def sigmoid(values):
    return 0.5 * jnp.tanh(0.5 * values) + 0.5


def unit(values, axis):
    scale = 1.0 / values.shape[axis]
    centred = values - jnp.sum(values, axis=axis, keepdims=True) * scale
    spread = jnp.sum(centred * centred, axis=axis, keepdims=True) * scale
    return centred * lax.rsqrt(spread + 1e-05)


def chunks(rows, tokens):
    wide = max(1, min(rows, 256 // tokens))
    return [list(range(start, min(start + wide, rows))) for start in range(0, rows, wide)]


def span(chunk, tokens):
    return slice(chunk[0] * tokens, (chunk[-1] + 1) * tokens)


def lanes(parts):
    return parts[0] if len(parts) == 1 else jnp.concatenate(parts, axis=1)


def affine(values, gain, bias, tokens):
    parts = [values[:, n : n + tokens] * gain + bias for n in range(0, values.shape[1], tokens)]
    return lanes(parts).astype(BF16)


def store_panels(panels, per_group, rows, chunk, tokens, products, mask):
    channels = products.shape[0] // 5
    for side in range(2):
        base = 2 * side * channels
        gated = sigmoid(products[base : base + channels]) * products[base + channels : base + 2 * channels] * mask
        for h, r in enumerate(chunk):
            for g in range(channels // per_group):
                where = pl.ds((2 * g + side) * per_group * rows + r, per_group, stride=rows)
                for t in range(tokens // LANES):
                    first = h * tokens + t * LANES
                    panels[t, where, :] = gated[g * per_group : (g + 1) * per_group, first : first + LANES]
    return sigmoid(products[4 * channels :]).astype(BF16)


def mask_lanes(mask_ref, chunk):
    return lanes([mask_ref[r : r + 1].astype(F32) for r in chunk])


def column(ref, which, norm, tokens):
    row = ref[which, norm : norm + 1]
    return jnp.broadcast_to(row, (tokens, row.shape[1])).T


def fetch(copies):
    for copy in copies:
        copy.start()
    for copy in copies:
        copy.wait()


def weights_kernel(
    gain_hbm, bias_hbm, proj_hbm, gatew_hbm, outw_hbm, columns_ref, proj_t_ref, outw_t_ref,
    gain_ref, bias_ref, proj_ref, gatew_ref, outw_ref, sems,
):
    pairs = (
        (gain_hbm, gain_ref), (bias_hbm, bias_ref), (proj_hbm, proj_ref), (gatew_hbm, gatew_ref), (outw_hbm, outw_ref)
    )
    fetch([pltpu.make_async_copy(src, dst, sems.at[n]) for n, (src, dst) in enumerate(pairs)])
    tokens = columns_ref.shape[2]
    channels = outw_ref.shape[1]
    for which in range(2):
        proj_t_ref[which, : 4 * channels] = proj_ref[which].T
        proj_t_ref[which, 4 * channels :] = gatew_ref[which].T
        outw_t_ref[which] = outw_ref[which].T
        for norm in range(2):
            columns_ref[4 * which + 2 * norm] = column(gain_ref, which, norm, tokens)
            columns_ref[4 * which + 2 * norm + 1] = column(bias_ref, which, norm, tokens)


def project_kernel(per_group, rows, pair_rows, mask_rows, refs):
    columns_ref, proj_t_ref, both_ref, pair_t_ref, gate_t_ref, mask_ref, panels = refs
    tokens = mask_ref.shape[1]
    for r in range(rows):
        mask_ref[r : r + 1] = mask_rows(r)
    for chunk in chunks(rows, tokens):
        part = span(chunk, tokens)
        pair_t = lanes([pair_rows(r).T for r in chunk])
        pair_t_ref[:, part] = pair_t
        normed = affine(unit(pair_t.astype(F32), 0), columns_ref[0], columns_ref[1], tokens)
        products = dot(proj_t_ref[0], normed, NN)
        gate_t_ref[:, part] = store_panels(
            panels, per_group, rows, chunk, tokens, products, mask_lanes(mask_ref, chunk)
        )
    for t in range(tokens // LANES):
        both_ref[:, t * LANES : (t + 1) * LANES] = panels[t].astype(BF16)


def project_own(per_group, pair_hbm, mask_hbm, *refs):
    refs, (pair_ref, mask_ref, sems) = refs[:-3], refs[-3:]
    pairs = ((pair_hbm, pair_ref), (mask_hbm, mask_ref))
    fetch([pltpu.make_async_copy(src, dst, sems.at[n]) for n, (src, dst) in enumerate(pairs)])
    project_kernel(
        per_group, pair_ref.shape[0], lambda r: pair_ref[r], lambda r: mask_ref[r : r + 1].astype(F32), refs
    )


def project_moved(per_group, stay_ref, kept_ref, first_ref, second_ref, *refs):
    half, tokens = kept_ref.shape[0], kept_ref.shape[1] - 1
    stay = jnp.full((tokens, kept_ref.shape[2]), stay_ref[0]) != 0

    def pair_rows(r):
        if r >= half:
            return second_ref[r - half, :tokens]
        return jnp.where(stay, kept_ref[r, :tokens].astype(F32), first_ref[r, :tokens].astype(F32)).astype(BF16)

    def mask_rows(r):
        if r >= half:
            return second_ref[r - half, tokens:].astype(F32)
        return jnp.where(stay[:1], kept_ref[r, tokens:].astype(F32), first_ref[r, tokens:].astype(F32))

    project_kernel(per_group, 2 * half, pair_rows, mask_rows, refs)


def regroup(blocks):
    count, rows, _ = blocks.shape
    swapped = jnp.concatenate([blocks[count // 2 :], blocks[: count // 2]], axis=0)
    return jnp.where(lax.broadcasted_iota(jnp.int32, blocks.shape, 1) < rows // 2, blocks, swapped)


def mix_kernel(per_group, rows, incoming, moved, both_ref, product_ref):
    groups, _, tokens = both_ref.shape
    step = 2 * rows

    def matrices(side, pair):
        start = (side * per_group + 2 * pair) * rows
        block = both_ref[:, start : start + step, :].astype(F32)
        blocks = [block[:, h * rows : (h + 1) * rows] for h in range(2)]
        if moved and side == 1 and not incoming:
            blocks = [regroup(b) for b in blocks]
        return [b.reshape(groups * rows, tokens).astype(BF16) for b in blocks]

    for pair in range(per_group // 2):
        lefts, rights = matrices(0, pair), matrices(1, pair)
        sums = [
            dot(left, right, TN if incoming else NT).reshape(groups, rows, tokens)
            for left, right in zip(lefts, rights)
        ]
        if moved and incoming:
            sums = [regroup(b) for b in sums]
        product_ref[:, pair * step : (pair + 1) * step, :] = jnp.concatenate(sums, axis=1).astype(BF16)


def finish_rows(emit, rows, merged_ref, pair_t_ref, gate_t_ref, gain, bias, outw_t, unit_scratch):
    tokens = merged_ref.shape[1]
    channels = merged_ref.shape[0] // rows
    sums = merged_ref[...].astype(F32).reshape(channels, rows, tokens)
    units = unit(sums, 0).reshape(channels * rows, tokens)
    tiles = range(tokens // LANES)
    for t in tiles:
        unit_scratch[t] = units[:, t * LANES : (t + 1) * LANES]
    for chunk in chunks(rows, tokens):
        part = span(chunk, tokens)
        units = lanes([unit_scratch[t, pl.ds(r, channels, stride=rows), :] for r in chunk for t in tiles])
        normed = affine(units, gain, bias, tokens)
        change = gate_t_ref[:, part].astype(F32) * dot(outw_t, normed, NN)
        emit(chunk, part, (pair_t_ref[:, part].astype(F32) + change).astype(BF16))


def step_kernel(
    per_group, merged_ref, pair_t_ref, gate_t_ref, mask_ref, columns_ref, outw_t_ref, proj_t_ref,
    both_ref, middle_t_ref, gate1_t_ref, unit_scratch, panels,
):
    rows, tokens = mask_ref.shape

    def emit(chunk, part, middle):
        middle_t_ref[:, part] = middle
        normed = affine(unit(middle.astype(F32), 0), columns_ref[4], columns_ref[5], tokens)
        products = dot(proj_t_ref[1], normed, NN)
        gate1_t_ref[:, part] = store_panels(
            panels, per_group, rows, chunk, tokens, products, mask_lanes(mask_ref, chunk)
        )

    finish_rows(
        emit, rows, merged_ref, pair_t_ref, gate_t_ref, columns_ref[2], columns_ref[3], outw_t_ref[0], unit_scratch
    )
    for t in range(tokens // LANES):
        both_ref[:, t * LANES : (t + 1) * LANES] = panels[t].astype(BF16)


def finish_kernel(
    rows, merged_ref, middle_t_ref, gate_t_ref, columns_ref, outw_t_ref, result_ref, unit_scratch, done, sems
):
    tokens = merged_ref.shape[1]
    copies = []

    def emit(chunk, part, result):
        for h, r in enumerate(chunk):
            done[r] = result[:, h * tokens : (h + 1) * tokens].T
            copies.append(pltpu.make_async_copy(done.at[r], result_ref.at[r], sems.at[r]))
            copies[-1].start()

    finish_rows(
        emit, rows, merged_ref, middle_t_ref, gate_t_ref, columns_ref[6], columns_ref[7], outw_t_ref[1], unit_scratch
    )
    for copy in copies:
        copy.wait()


def finish_moved(
    rows, merged_ref, middle_t_ref, gate_t_ref, columns_ref, outw_t_ref, first_ref, second_ref, unit_scratch
):
    tokens = merged_ref.shape[1]

    def emit(chunk, part, result):
        for h, r in enumerate(chunk):
            half, place = ((first_ref, r), (second_ref, r - rows // 2))[r >= rows // 2]
            half[place] = result[:, h * tokens : (h + 1) * tokens].T

    finish_rows(
        emit, rows, merged_ref, middle_t_ref, gate_t_ref, columns_ref[6], columns_ref[7], outw_t_ref[1], unit_scratch
    )


def cube_moves(count):
    half = count // 2
    seconds, firsts = [], []
    for group in range(2):
        for d in range(count):
            here = group * count + d
            stays = (d >= half) == (group == 1)
            near = (1 - group) * count + d
            along = group * count + (d + half) % count
            seconds.append((here, near if stays else along))
            if not stays:
                firsts.append((here, (1 - group) * count + (d + half) % count))
    cubes = [list(range(c * half, (c + 1) * half)) + list(range(count + c * half, count + (c + 1) * half)) for c in range(2)]
    return firsts, seconds, cubes


def on_device(pair, mask, gains, biases, proj, gatew, outw):
    axes = ("groups", "row")
    groups = lax.axis_size("row")
    rows, tokens, channels = pair.shape
    per_group = channels // groups
    whole = pl.BlockSpec(memory_space=pltpu.VMEM)
    hbm = pl.BlockSpec(memory_space=pltpu.HBM)
    params = pltpu.CompilerParams(vmem_limit_bytes=48 * 1024 * 1024)
    shape = jax.ShapeDtypeStruct
    both_shape = shape((2 * channels * rows, tokens), BF16)
    flat_shape = shape((channels, rows * tokens), BF16)
    panels = pltpu.VMEM((tokens // LANES, 2 * channels * rows, LANES), F32)
    unit_scratch = pltpu.VMEM((tokens // LANES, channels * rows, LANES), F32)
    moved = lax.axis_size("groups") == 2 and groups == 16 and rows == 8
    firsts, seconds, cubes = cube_moves(groups)

    def kernel(body, out_shape, operands, name, in_specs=None, out_specs=whole, scratch=(), cost=None):
        return pl.pallas_call(
            body,
            out_shape=out_shape,
            in_specs=in_specs or [whole] * len(operands),
            out_specs=jax.tree.map(lambda _: out_specs, out_shape),
            scratch_shapes=scratch,
            compiler_params=params,
            cost_estimate=cost,
            name=name,
        )(*operands)

    def from_hbm(arrays):
        return [pltpu.with_memory_space_constraint(a, pltpu.HBM) for a in arrays]

    def held(arrays):
        return [pltpu.VMEM(a.shape, a.dtype) for a in arrays] + [pltpu.SemaphoreType.DMA((len(arrays),))]

    def exchange(array):
        if moved:
            return lax.all_to_all(array, axes, split_axis=0, concat_axis=0, tiled=True, axis_index_groups=cubes)
        return lax.all_to_all(array, "row", split_axis=0, concat_axis=0, tiled=True)

    def mix(both, incoming):
        product = kernel(
            functools.partial(mix_kernel, per_group, rows, incoming, moved),
            shape((groups, per_group * rows, tokens), BF16),
            [both.reshape(groups, 2 * per_group * rows, tokens)],
            "mix",
        )
        return product.reshape(channels * rows, tokens)

    params_in = (gains, biases, proj, gatew, outw)
    columns, proj_t, outw_t = kernel(
        weights_kernel,
        (shape((8, channels, tokens), F32), shape((2, 5 * channels, channels), BF16), shape((2, channels, channels), BF16)),
        from_hbm(params_in),
        "weights",
        in_specs=[hbm] * 5,
        scratch=held(params_in),
        cost=pl.CostEstimate(flops=10**9, bytes_accessed=4 * 2**20, transcendentals=0),
    )
    project_out = (both_shape, flat_shape, flat_shape, shape((rows, tokens), F32))
    if moved:
        half = rows // 2
        with_mask = jnp.concatenate([pair, mask.astype(BF16)[:, :, None].swapaxes(1, 2)], axis=1)
        kept = with_mask[:half]
        second = lax.ppermute(with_mask[half:], axes, seconds)
        first = lax.ppermute(kept, axes, firsts)
        stays = (lax.axis_index("row") >= groups // 2) == (lax.axis_index("groups") == 1)
        both, pair_t, gate_t, mask_rows = kernel(
            functools.partial(project_moved, per_group),
            project_out,
            [stays.astype(jnp.int32).reshape(1), kept, first, second, columns, proj_t],
            "project",
            in_specs=[pl.BlockSpec(memory_space=pltpu.SMEM)] + [whole] * 5,
            scratch=[panels],
        )
    else:
        both, pair_t, gate_t, mask_rows = kernel(
            functools.partial(project_own, per_group),
            project_out,
            from_hbm((pair, mask)) + [columns, proj_t],
            "project",
            in_specs=[hbm] * 2 + [whole] * 2,
            scratch=[panels] + held((pair, mask)),
        )
    merged = exchange(mix(exchange(both), False))
    both, middle_t, gate_t = kernel(
        functools.partial(step_kernel, per_group),
        (both_shape, flat_shape, flat_shape),
        [merged, pair_t, gate_t, mask_rows, columns, outw_t, proj_t],
        "finish_project",
        scratch=[unit_scratch, panels],
    )
    merged = exchange(mix(exchange(both), True))
    operands = [merged, middle_t, gate_t, columns, outw_t]
    if not moved:
        return kernel(
            functools.partial(finish_kernel, rows),
            shape(pair.shape, BF16),
            operands,
            "finish",
            out_specs=hbm,
            scratch=[unit_scratch, pltpu.VMEM(pair.shape, BF16), pltpu.SemaphoreType.DMA((rows,))],
        )
    half_shape = shape((half, tokens, channels), BF16)
    first, second = kernel(
        functools.partial(finish_moved, rows), (half_shape, half_shape), operands, "finish", scratch=[unit_scratch]
    )
    second = lax.ppermute(second, axes, [(b, a) for a, b in seconds])
    back = lax.ppermute(first, axes, [(b, a) for a, b in firsts])
    return jnp.concatenate([jnp.where(stays, first, back), second], axis=0)


def solution(mesh):
    rows = ("groups", "row")
    return jax.shard_map(
        on_device,
        mesh=mesh,
        in_specs=(P(rows, None, None), P(rows, None), P(), P(), P(), P(), P()),
        out_specs=P(rows, None, None),
        check_vma=False,
    )
```

```python
import functools

import jax
import jax.numpy as jnp
from jax import lax
from jax.experimental import pallas as pl
from jax.experimental.pallas import tpu as pltpu
from jax.sharding import PartitionSpec as P

F32 = jnp.float32
BF16 = jnp.bfloat16
LANES = 128
NT = (((1,), (1,)), ((), ()))
NN = (((1,), (0,)), ((), ()))
TN = (((0,), (0,)), ((), ()))


def dot(a, b, dims):
    return lax.dot_general(a, b, dims, preferred_element_type=F32)


def sigmoid(values):
    return 0.5 * jnp.tanh(0.5 * values) + 0.5


def unit(values, axis):
    scale = 1.0 / values.shape[axis]
    centred = values - jnp.sum(values, axis=axis, keepdims=True) * scale
    spread = jnp.sum(centred * centred, axis=axis, keepdims=True) * scale
    return centred * lax.rsqrt(spread + 1e-05)


def chunks(rows, tokens):
    wide = max(1, min(rows, 256 // tokens))
    return [list(range(start, min(start + wide, rows))) for start in range(0, rows, wide)]


def span(chunk, tokens):
    return slice(chunk[0] * tokens, (chunk[-1] + 1) * tokens)


def lanes(parts):
    return parts[0] if len(parts) == 1 else jnp.concatenate(parts, axis=1)


def affine(values, gain, bias, tokens):
    parts = [values[:, n : n + tokens] * gain + bias for n in range(0, values.shape[1], tokens)]
    return lanes(parts).astype(BF16)


def store_panels(panels, per_group, rows, chunk, tokens, products, mask):
    channels = products.shape[0] // 5
    for side in range(2):
        base = 2 * side * channels
        gated = sigmoid(products[base : base + channels]) * products[base + channels : base + 2 * channels] * mask
        for h, r in enumerate(chunk):
            for g in range(channels // per_group):
                where = pl.ds((2 * g + side) * per_group * rows + r, per_group, stride=rows)
                for t in range(tokens // LANES):
                    first = h * tokens + t * LANES
                    panels[t, where, :] = gated[g * per_group : (g + 1) * per_group, first : first + LANES]
    return sigmoid(products[4 * channels :]).astype(BF16)


def mask_lanes(mask_ref, chunk):
    return lanes([mask_ref[r : r + 1].astype(F32) for r in chunk])


def column(ref, which, norm, tokens):
    row = ref[which, norm : norm + 1]
    return jnp.broadcast_to(row, (tokens, row.shape[1])).T


def project_kernel(per_group, *refs):
    inputs, refs = refs[:7], refs[7:]
    both_ref, pair_t_ref, gate_t_ref, mask_ref, columns_ref, proj_t_ref, outw_t_ref = refs[:7]
    pair_ref, gain_ref, bias_ref, proj_ref, gatew_ref, outw_ref, panels, sems = refs[7:]
    held = (pair_ref, mask_ref, gain_ref, bias_ref, proj_ref, gatew_ref, outw_ref)
    copies = [pltpu.make_async_copy(src, dst, sems.at[n]) for n, (src, dst) in enumerate(zip(inputs, held))]
    for copy in copies:
        copy.start()
    for copy in copies:
        copy.wait()
    rows, tokens, channels = pair_ref.shape
    for which in range(2):
        proj_t_ref[which, : 4 * channels] = proj_ref[which].T
        proj_t_ref[which, 4 * channels :] = gatew_ref[which].T
        outw_t_ref[which] = outw_ref[which].T
    for n, (which, norm) in enumerate(((0, 1), (1, 0), (1, 1))):
        columns_ref[2 * n] = column(gain_ref, which, norm, tokens)
        columns_ref[2 * n + 1] = column(bias_ref, which, norm, tokens)
    gain, bias = column(gain_ref, 0, 0, tokens), column(bias_ref, 0, 0, tokens)
    for chunk in chunks(rows, tokens):
        part = span(chunk, tokens)
        pair_t = lanes([pair_ref[r].T for r in chunk])
        pair_t_ref[:, part] = pair_t
        normed = affine(unit(pair_t.astype(F32), 0), gain, bias, tokens)
        products = dot(proj_t_ref[0], normed, NN)
        gate_t_ref[:, part] = store_panels(
            panels, per_group, rows, chunk, tokens, products, mask_lanes(mask_ref, chunk)
        )
    for t in range(tokens // LANES):
        both_ref[:, t * LANES : (t + 1) * LANES] = panels[t].astype(BF16)


def rank_order(count):
    parts = 4 if count % 4 == 0 else 1
    return [(rank % parts) * (count // parts) + rank // parts for rank in range(count)]


def take(blocks, places):
    return jnp.concatenate([blocks[n : n + 1] for n in places], axis=0)


def mix_kernel(per_group, rows, incoming, both_ref, product_ref):
    groups, _, tokens = both_ref.shape
    step = 2 * rows
    order = rank_order(groups)
    ranks = [order.index(device) for device in range(groups)]

    def matrices(side, pair):
        start = (side * per_group + 2 * pair) * rows
        block = both_ref[:, start : start + step, :].astype(F32)
        if side == 1 and not incoming:
            block = take(block, ranks)
        return [block[:, h * rows : (h + 1) * rows].reshape(groups * rows, tokens).astype(BF16) for h in range(2)]

    for pair in range(per_group // 2):
        lefts, rights = matrices(0, pair), matrices(1, pair)
        sums = [
            dot(left, right, TN if incoming else NT).reshape(groups, rows, tokens)
            for left, right in zip(lefts, rights)
        ]
        sums = jnp.concatenate(sums, axis=1)
        if incoming:
            sums = take(sums, order)
        product_ref[:, pair * step : (pair + 1) * step, :] = sums.astype(BF16)


def finish_rows(emit, rows, merged_ref, pair_t_ref, gate_t_ref, gain, bias, outw_t, unit_scratch):
    tokens = merged_ref.shape[1]
    channels = merged_ref.shape[0] // rows
    sums = merged_ref[...].astype(F32).reshape(channels, rows, tokens)
    units = unit(sums, 0).reshape(channels * rows, tokens)
    tiles = range(tokens // LANES)
    for t in tiles:
        unit_scratch[t] = units[:, t * LANES : (t + 1) * LANES]
    for chunk in chunks(rows, tokens):
        part = span(chunk, tokens)
        units = lanes([unit_scratch[t, pl.ds(r, channels, stride=rows), :] for r in chunk for t in tiles])
        normed = affine(units, gain, bias, tokens)
        change = gate_t_ref[:, part].astype(F32) * dot(outw_t, normed, NN)
        emit(chunk, part, (pair_t_ref[:, part].astype(F32) + change).astype(BF16))


def step_kernel(
    per_group, merged_ref, pair_t_ref, gate_t_ref, mask_ref, columns_ref, outw_t_ref, proj_t_ref,
    both_ref, middle_t_ref, gate1_t_ref, unit_scratch, panels,
):
    rows, tokens = mask_ref.shape

    def emit(chunk, part, middle):
        middle_t_ref[:, part] = middle
        normed = affine(unit(middle.astype(F32), 0), columns_ref[2], columns_ref[3], tokens)
        products = dot(proj_t_ref[1], normed, NN)
        gate1_t_ref[:, part] = store_panels(
            panels, per_group, rows, chunk, tokens, products, mask_lanes(mask_ref, chunk)
        )

    finish_rows(
        emit, rows, merged_ref, pair_t_ref, gate_t_ref, columns_ref[0], columns_ref[1], outw_t_ref[0], unit_scratch
    )
    for t in range(tokens // LANES):
        both_ref[:, t * LANES : (t + 1) * LANES] = panels[t].astype(BF16)


def finish_kernel(
    merged_ref, middle_t_ref, gate_t_ref, columns_ref, outw_t_ref, result_ref, unit_scratch, done, sems
):
    rows, tokens, _ = result_ref.shape
    copies = []

    def emit(chunk, part, result):
        for h, r in enumerate(chunk):
            done[r] = result[:, h * tokens : (h + 1) * tokens].T
            copies.append(pltpu.make_async_copy(done.at[r], result_ref.at[r], sems.at[r]))
            copies[-1].start()

    finish_rows(
        emit, rows, merged_ref, middle_t_ref, gate_t_ref, columns_ref[4], columns_ref[5], outw_t_ref[1], unit_scratch
    )
    for copy in copies:
        copy.wait()


def on_device(*inputs):
    groups = lax.axis_size("row")
    rows, tokens, channels = inputs[0].shape
    per_group = channels // groups
    whole = pl.BlockSpec(memory_space=pltpu.VMEM)
    hbm = pl.BlockSpec(memory_space=pltpu.HBM)
    params = pltpu.CompilerParams(vmem_limit_bytes=48 * 1024 * 1024)
    shape = jax.ShapeDtypeStruct
    both_shape = shape((2 * channels * rows, tokens), BF16)
    flat_shape = shape((channels, rows * tokens), BF16)
    panels = pltpu.VMEM((tokens // LANES, 2 * channels * rows, LANES), F32)
    unit_scratch = pltpu.VMEM((tokens // LANES, channels * rows, LANES), F32)

    def exchange(array):
        return lax.all_to_all(
            array, "row", split_axis=0, concat_axis=0, tiled=True, axis_index_groups=[rank_order(groups)]
        )

    def mix(both, incoming):
        product = pl.pallas_call(
            functools.partial(mix_kernel, per_group, rows, incoming),
            out_shape=shape((groups, per_group * rows, tokens), BF16),
            in_specs=[whole],
            out_specs=whole,
            compiler_params=params,
            name="mix",
        )(both.reshape(groups, 2 * per_group * rows, tokens))
        return product.reshape(channels * rows, tokens)

    both, pair_t, gate_t, mask, columns, proj_t, outw_t = pl.pallas_call(
        functools.partial(project_kernel, per_group),
        out_shape=(
            both_shape,
            flat_shape,
            flat_shape,
            shape((rows, tokens), inputs[1].dtype),
            shape((6, channels, tokens), F32),
            shape((2, 5 * channels, channels), BF16),
            shape((2, channels, channels), BF16),
        ),
        in_specs=[hbm] * 7,
        out_specs=(whole,) * 7,
        scratch_shapes=[pltpu.VMEM(inputs[n].shape, inputs[n].dtype) for n in (0, 2, 3, 4, 5, 6)]
        + [panels, pltpu.SemaphoreType.DMA((7,))],
        compiler_params=params,
        name="project",
    )(*(pltpu.with_memory_space_constraint(a, pltpu.HBM) for a in inputs))
    merged = exchange(mix(exchange(both), False))
    both, middle_t, gate_t = pl.pallas_call(
        functools.partial(step_kernel, per_group),
        out_shape=(both_shape, flat_shape, flat_shape),
        in_specs=[whole] * 7,
        out_specs=(whole,) * 3,
        scratch_shapes=[unit_scratch, panels],
        compiler_params=params,
        name="finish_project",
    )(merged, pair_t, gate_t, mask, columns, outw_t, proj_t)
    merged = exchange(mix(exchange(both), True))
    return pl.pallas_call(
        finish_kernel,
        out_shape=shape((rows, tokens, channels), BF16),
        in_specs=[whole] * 5,
        out_specs=hbm,
        scratch_shapes=[unit_scratch, pltpu.VMEM((rows, tokens, channels), BF16), pltpu.SemaphoreType.DMA((rows,))],
        compiler_params=params,
        name="finish",
    )(merged, middle_t, gate_t, columns, outw_t)


def solution(mesh):
    rows = ("groups", "row")
    return jax.shard_map(
        on_device,
        mesh=mesh,
        in_specs=(P(rows, None, None), P(rows, None), P(), P(), P(), P(), P()),
        out_specs=P(rows, None, None),
        check_vma=False,
    )
```

```python
import functools

import jax
import jax.numpy as jnp
from jax import lax
from jax.experimental import pallas as pl
from jax.experimental.pallas import tpu as pltpu
from jax.sharding import PartitionSpec as P

F32 = jnp.float32
BF16 = jnp.bfloat16
LANES = 128
NT = (((1,), (1,)), ((), ()))
NN = (((1,), (0,)), ((), ()))
TN = (((0,), (0,)), ((), ()))


def dot(a, b, dims):
    return lax.dot_general(a, b, dims, preferred_element_type=F32)


def sigmoid(values):
    return 0.5 * jnp.tanh(0.5 * values) + 0.5


def unit(values, axis):
    scale = 1.0 / values.shape[axis]
    centred = values - jnp.sum(values, axis=axis, keepdims=True) * scale
    spread = jnp.sum(centred * centred, axis=axis, keepdims=True) * scale
    return centred * lax.rsqrt(spread + 1e-05)


def chunks(rows, tokens):
    wide = max(1, min(rows, 256 // tokens))
    return [list(range(start, min(start + wide, rows))) for start in range(0, rows, wide)]


def span(chunk, tokens):
    return slice(chunk[0] * tokens, (chunk[-1] + 1) * tokens)


def lanes(parts):
    return parts[0] if len(parts) == 1 else jnp.concatenate(parts, axis=1)


def affine(values, gain, bias, tokens):
    parts = [values[:, n : n + tokens] * gain + bias for n in range(0, values.shape[1], tokens)]
    return lanes(parts).astype(BF16)


def store_panels(panels, per_group, rows, chunk, tokens, products, mask):
    channels = products.shape[0] // 5
    for side in range(2):
        base = 2 * side * channels
        gated = sigmoid(products[base : base + channels]) * products[base + channels : base + 2 * channels] * mask
        for h, r in enumerate(chunk):
            for g in range(channels // per_group):
                where = pl.ds((2 * g + side) * per_group * rows + r, per_group, stride=rows)
                for t in range(tokens // LANES):
                    first = h * tokens + t * LANES
                    panels[t, where, :] = gated[g * per_group : (g + 1) * per_group, first : first + LANES]
    return sigmoid(products[4 * channels :]).astype(BF16)


def mask_lanes(mask_ref, chunk):
    return lanes([mask_ref[r : r + 1].astype(F32) for r in chunk])


def column(ref, which, norm, tokens):
    row = ref[which, norm : norm + 1]
    return jnp.broadcast_to(row, (tokens, row.shape[1])).T


def project_kernel(per_group, *refs):
    inputs, refs = refs[:7], refs[7:]
    both_ref, pair_t_ref, gate_t_ref, mask_ref, columns_ref, proj_t_ref, outw_t_ref = refs[:7]
    pair_ref, gain_ref, bias_ref, proj_ref, gatew_ref, outw_ref, panels, sems = refs[7:]
    held = (pair_ref, mask_ref, gain_ref, bias_ref, proj_ref, gatew_ref, outw_ref)
    copies = [pltpu.make_async_copy(src, dst, sems.at[n]) for n, (src, dst) in enumerate(zip(inputs, held))]
    for copy in copies:
        copy.start()
    for copy in copies:
        copy.wait()
    rows, tokens, channels = pair_ref.shape
    for which in range(2):
        proj_t_ref[which, : 4 * channels] = proj_ref[which].T
        proj_t_ref[which, 4 * channels :] = gatew_ref[which].T
        outw_t_ref[which] = outw_ref[which].T
    for n, (which, norm) in enumerate(((0, 1), (1, 0), (1, 1))):
        columns_ref[2 * n] = column(gain_ref, which, norm, tokens)
        columns_ref[2 * n + 1] = column(bias_ref, which, norm, tokens)
    gain, bias = column(gain_ref, 0, 0, tokens), column(bias_ref, 0, 0, tokens)
    for chunk in chunks(rows, tokens):
        part = span(chunk, tokens)
        pair_t = lanes([pair_ref[r].T for r in chunk])
        pair_t_ref[:, part] = pair_t
        normed = affine(unit(pair_t.astype(F32), 0), gain, bias, tokens)
        products = dot(proj_t_ref[0], normed, NN)
        gate_t_ref[:, part] = store_panels(
            panels, per_group, rows, chunk, tokens, products, mask_lanes(mask_ref, chunk)
        )
    for t in range(tokens // LANES):
        both_ref[:, t * LANES : (t + 1) * LANES] = panels[t].astype(BF16)


def rank_order(count):
    if count % 4:
        return list(range(count))
    quarter = count // 4
    return [part * quarter + n for part in (0, 1, 3, 2) for n in range(quarter)]


def take(blocks, places):
    return jnp.concatenate([blocks[n : n + 1] for n in places], axis=0)


def mix_kernel(per_group, rows, incoming, both_ref, product_ref):
    groups, _, tokens = both_ref.shape
    step = 2 * rows
    order = rank_order(groups)
    ranks = [order.index(device) for device in range(groups)]

    def matrices(side, pair):
        start = (side * per_group + 2 * pair) * rows
        block = both_ref[:, start : start + step, :].astype(F32)
        if side == 1 and not incoming:
            block = take(block, ranks)
        return [block[:, h * rows : (h + 1) * rows].reshape(groups * rows, tokens).astype(BF16) for h in range(2)]

    for pair in range(per_group // 2):
        lefts, rights = matrices(0, pair), matrices(1, pair)
        sums = [
            dot(left, right, TN if incoming else NT).reshape(groups, rows, tokens)
            for left, right in zip(lefts, rights)
        ]
        sums = jnp.concatenate(sums, axis=1)
        if incoming:
            sums = take(sums, order)
        product_ref[:, pair * step : (pair + 1) * step, :] = sums.astype(BF16)


def finish_rows(emit, rows, merged_ref, pair_t_ref, gate_t_ref, gain, bias, outw_t, unit_scratch):
    tokens = merged_ref.shape[1]
    channels = merged_ref.shape[0] // rows
    sums = merged_ref[...].astype(F32).reshape(channels, rows, tokens)
    units = unit(sums, 0).reshape(channels * rows, tokens)
    tiles = range(tokens // LANES)
    for t in tiles:
        unit_scratch[t] = units[:, t * LANES : (t + 1) * LANES]
    for chunk in chunks(rows, tokens):
        part = span(chunk, tokens)
        units = lanes([unit_scratch[t, pl.ds(r, channels, stride=rows), :] for r in chunk for t in tiles])
        normed = affine(units, gain, bias, tokens)
        change = gate_t_ref[:, part].astype(F32) * dot(outw_t, normed, NN)
        emit(chunk, part, (pair_t_ref[:, part].astype(F32) + change).astype(BF16))


def step_kernel(
    per_group, merged_ref, pair_t_ref, gate_t_ref, mask_ref, columns_ref, outw_t_ref, proj_t_ref,
    both_ref, middle_t_ref, gate1_t_ref, unit_scratch, panels,
):
    rows, tokens = mask_ref.shape

    def emit(chunk, part, middle):
        middle_t_ref[:, part] = middle
        normed = affine(unit(middle.astype(F32), 0), columns_ref[2], columns_ref[3], tokens)
        products = dot(proj_t_ref[1], normed, NN)
        gate1_t_ref[:, part] = store_panels(
            panels, per_group, rows, chunk, tokens, products, mask_lanes(mask_ref, chunk)
        )

    finish_rows(
        emit, rows, merged_ref, pair_t_ref, gate_t_ref, columns_ref[0], columns_ref[1], outw_t_ref[0], unit_scratch
    )
    for t in range(tokens // LANES):
        both_ref[:, t * LANES : (t + 1) * LANES] = panels[t].astype(BF16)


def finish_kernel(
    merged_ref, middle_t_ref, gate_t_ref, columns_ref, outw_t_ref, result_ref, unit_scratch, done, sems
):
    rows, tokens, _ = result_ref.shape
    copies = []

    def emit(chunk, part, result):
        for h, r in enumerate(chunk):
            done[r] = result[:, h * tokens : (h + 1) * tokens].T
            copies.append(pltpu.make_async_copy(done.at[r], result_ref.at[r], sems.at[r]))
            copies[-1].start()

    finish_rows(
        emit, rows, merged_ref, middle_t_ref, gate_t_ref, columns_ref[4], columns_ref[5], outw_t_ref[1], unit_scratch
    )
    for copy in copies:
        copy.wait()


def on_device(*inputs):
    groups = lax.axis_size("row")
    rows, tokens, channels = inputs[0].shape
    per_group = channels // groups
    whole = pl.BlockSpec(memory_space=pltpu.VMEM)
    hbm = pl.BlockSpec(memory_space=pltpu.HBM)
    params = pltpu.CompilerParams(vmem_limit_bytes=48 * 1024 * 1024)
    shape = jax.ShapeDtypeStruct
    both_shape = shape((2 * channels * rows, tokens), BF16)
    flat_shape = shape((channels, rows * tokens), BF16)
    panels = pltpu.VMEM((tokens // LANES, 2 * channels * rows, LANES), F32)
    unit_scratch = pltpu.VMEM((tokens // LANES, channels * rows, LANES), F32)

    def exchange(array):
        return lax.all_to_all(
            array, "row", split_axis=0, concat_axis=0, tiled=True, axis_index_groups=[rank_order(groups)]
        )

    def mix(both, incoming):
        product = pl.pallas_call(
            functools.partial(mix_kernel, per_group, rows, incoming),
            out_shape=shape((groups, per_group * rows, tokens), BF16),
            in_specs=[whole],
            out_specs=whole,
            compiler_params=params,
            name="mix",
        )(both.reshape(groups, 2 * per_group * rows, tokens))
        return product.reshape(channels * rows, tokens)

    both, pair_t, gate_t, mask, columns, proj_t, outw_t = pl.pallas_call(
        functools.partial(project_kernel, per_group),
        out_shape=(
            both_shape,
            flat_shape,
            flat_shape,
            shape((rows, tokens), inputs[1].dtype),
            shape((6, channels, tokens), F32),
            shape((2, 5 * channels, channels), BF16),
            shape((2, channels, channels), BF16),
        ),
        in_specs=[hbm] * 7,
        out_specs=(whole,) * 7,
        scratch_shapes=[pltpu.VMEM(inputs[n].shape, inputs[n].dtype) for n in (0, 2, 3, 4, 5, 6)]
        + [panels, pltpu.SemaphoreType.DMA((7,))],
        compiler_params=params,
        name="project",
    )(*(pltpu.with_memory_space_constraint(a, pltpu.HBM) for a in inputs))
    merged = exchange(mix(exchange(both), False))
    both, middle_t, gate_t = pl.pallas_call(
        functools.partial(step_kernel, per_group),
        out_shape=(both_shape, flat_shape, flat_shape),
        in_specs=[whole] * 7,
        out_specs=(whole,) * 3,
        scratch_shapes=[unit_scratch, panels],
        compiler_params=params,
        name="finish_project",
    )(merged, pair_t, gate_t, mask, columns, outw_t, proj_t)
    merged = exchange(mix(exchange(both), True))
    return pl.pallas_call(
        finish_kernel,
        out_shape=shape((rows, tokens, channels), BF16),
        in_specs=[whole] * 5,
        out_specs=hbm,
        scratch_shapes=[unit_scratch, pltpu.VMEM((rows, tokens, channels), BF16), pltpu.SemaphoreType.DMA((rows,))],
        compiler_params=params,
        name="finish",
    )(merged, middle_t, gate_t, columns, outw_t)


def solution(mesh):
    rows = ("groups", "row")
    return jax.shard_map(
        on_device,
        mesh=mesh,
        in_specs=(P(rows, None, None), P(rows, None), P(), P(), P(), P(), P()),
        out_specs=P(rows, None, None),
        check_vma=False,
    )
```

```python
import functools

import jax
import jax.numpy as jnp
from jax import lax
from jax.experimental import pallas as pl
from jax.experimental.pallas import tpu as pltpu
from jax.sharding import PartitionSpec as P

F32 = jnp.float32
BF16 = jnp.bfloat16
LANES = 128
NT = (((1,), (1,)), ((), ()))
NN = (((1,), (0,)), ((), ()))
TN = (((0,), (0,)), ((), ()))


def dot(a, b, dims):
    return lax.dot_general(a, b, dims, preferred_element_type=F32)


def sigmoid(values):
    return 0.5 * jnp.tanh(0.5 * values) + 0.5


def unit(values, axis):
    scale = 1.0 / values.shape[axis]
    centred = values - jnp.sum(values, axis=axis, keepdims=True) * scale
    spread = jnp.sum(centred * centred, axis=axis, keepdims=True) * scale
    return centred * lax.rsqrt(spread + 1e-05)


def chunks(rows, tokens):
    wide = max(1, min(rows, 256 // tokens))
    return [list(range(start, min(start + wide, rows))) for start in range(0, rows, wide)]


def span(chunk, tokens):
    return slice(chunk[0] * tokens, (chunk[-1] + 1) * tokens)


def lanes(parts):
    return parts[0] if len(parts) == 1 else jnp.concatenate(parts, axis=1)


def affine(values, gain, bias, tokens):
    parts = [values[:, n : n + tokens] * gain + bias for n in range(0, values.shape[1], tokens)]
    return lanes(parts).astype(BF16)


def store_panels(panels, per_group, rows, chunk, tokens, products, mask):
    channels = products.shape[0] // 5
    for side in range(2):
        base = 2 * side * channels
        gated = sigmoid(products[base : base + channels]) * products[base + channels : base + 2 * channels] * mask
        for h, r in enumerate(chunk):
            for g in range(channels // per_group):
                where = pl.ds((2 * g + side) * per_group * rows + r, per_group, stride=rows)
                for t in range(tokens // LANES):
                    first = h * tokens + t * LANES
                    panels[t, where, :] = gated[g * per_group : (g + 1) * per_group, first : first + LANES]
    return sigmoid(products[4 * channels :]).astype(BF16)


def mask_lanes(mask_ref, chunk):
    return lanes([mask_ref[r : r + 1].astype(F32) for r in chunk])


def column(ref, which, norm, tokens):
    row = ref[which, norm : norm + 1]
    return jnp.broadcast_to(row, (tokens, row.shape[1])).T


def project_kernel(per_group, *refs):
    inputs, refs = refs[:7], refs[7:]
    both_ref, pair_t_ref, gate_t_ref, mask_ref, columns_ref, proj_t_ref, outw_t_ref = refs[:7]
    pair_ref, gain_ref, bias_ref, proj_ref, gatew_ref, outw_ref, panels, sems = refs[7:]
    held = (pair_ref, mask_ref, gain_ref, bias_ref, proj_ref, gatew_ref, outw_ref)
    copies = [pltpu.make_async_copy(src, dst, sems.at[n]) for n, (src, dst) in enumerate(zip(inputs, held))]
    for copy in copies:
        copy.start()
    for copy in copies:
        copy.wait()
    rows, tokens, channels = pair_ref.shape
    for which in range(2):
        proj_t_ref[which, : 4 * channels] = proj_ref[which].T
        proj_t_ref[which, 4 * channels :] = gatew_ref[which].T
        outw_t_ref[which] = outw_ref[which].T
    for n, (which, norm) in enumerate(((0, 1), (1, 0), (1, 1))):
        columns_ref[2 * n] = column(gain_ref, which, norm, tokens)
        columns_ref[2 * n + 1] = column(bias_ref, which, norm, tokens)
    gain, bias = column(gain_ref, 0, 0, tokens), column(bias_ref, 0, 0, tokens)
    for chunk in chunks(rows, tokens):
        part = span(chunk, tokens)
        pair_t = lanes([pair_ref[r].T for r in chunk])
        pair_t_ref[:, part] = pair_t
        normed = affine(unit(pair_t.astype(F32), 0), gain, bias, tokens)
        products = dot(proj_t_ref[0], normed, NN)
        gate_t_ref[:, part] = store_panels(
            panels, per_group, rows, chunk, tokens, products, mask_lanes(mask_ref, chunk)
        )
    for t in range(tokens // LANES):
        both_ref[:, t * LANES : (t + 1) * LANES] = panels[t].astype(BF16)


def rank_order(count):
    if count % 4:
        return list(range(count))
    quarter = count // 4
    return [part * quarter + n for part in (0, 2, 1, 3) for n in range(quarter)]


def take(blocks, places):
    return jnp.concatenate([blocks[n : n + 1] for n in places], axis=0)


def mix_kernel(per_group, rows, incoming, both_ref, product_ref):
    groups, _, tokens = both_ref.shape
    step = 2 * rows
    order = rank_order(groups)
    ranks = [order.index(device) for device in range(groups)]

    def matrices(side, pair):
        start = (side * per_group + 2 * pair) * rows
        block = both_ref[:, start : start + step, :].astype(F32)
        if side == 1 and not incoming:
            block = take(block, ranks)
        return [block[:, h * rows : (h + 1) * rows].reshape(groups * rows, tokens).astype(BF16) for h in range(2)]

    for pair in range(per_group // 2):
        lefts, rights = matrices(0, pair), matrices(1, pair)
        sums = [
            dot(left, right, TN if incoming else NT).reshape(groups, rows, tokens)
            for left, right in zip(lefts, rights)
        ]
        sums = jnp.concatenate(sums, axis=1)
        if incoming:
            sums = take(sums, order)
        product_ref[:, pair * step : (pair + 1) * step, :] = sums.astype(BF16)


def finish_rows(emit, rows, merged_ref, pair_t_ref, gate_t_ref, gain, bias, outw_t, unit_scratch):
    tokens = merged_ref.shape[1]
    channels = merged_ref.shape[0] // rows
    sums = merged_ref[...].astype(F32).reshape(channels, rows, tokens)
    units = unit(sums, 0).reshape(channels * rows, tokens)
    tiles = range(tokens // LANES)
    for t in tiles:
        unit_scratch[t] = units[:, t * LANES : (t + 1) * LANES]
    for chunk in chunks(rows, tokens):
        part = span(chunk, tokens)
        units = lanes([unit_scratch[t, pl.ds(r, channels, stride=rows), :] for r in chunk for t in tiles])
        normed = affine(units, gain, bias, tokens)
        change = gate_t_ref[:, part].astype(F32) * dot(outw_t, normed, NN)
        emit(chunk, part, (pair_t_ref[:, part].astype(F32) + change).astype(BF16))


def step_kernel(
    per_group, merged_ref, pair_t_ref, gate_t_ref, mask_ref, columns_ref, outw_t_ref, proj_t_ref,
    both_ref, middle_t_ref, gate1_t_ref, unit_scratch, panels,
):
    rows, tokens = mask_ref.shape

    def emit(chunk, part, middle):
        middle_t_ref[:, part] = middle
        normed = affine(unit(middle.astype(F32), 0), columns_ref[2], columns_ref[3], tokens)
        products = dot(proj_t_ref[1], normed, NN)
        gate1_t_ref[:, part] = store_panels(
            panels, per_group, rows, chunk, tokens, products, mask_lanes(mask_ref, chunk)
        )

    finish_rows(
        emit, rows, merged_ref, pair_t_ref, gate_t_ref, columns_ref[0], columns_ref[1], outw_t_ref[0], unit_scratch
    )
    for t in range(tokens // LANES):
        both_ref[:, t * LANES : (t + 1) * LANES] = panels[t].astype(BF16)


def finish_kernel(
    merged_ref, middle_t_ref, gate_t_ref, columns_ref, outw_t_ref, result_ref, unit_scratch, done, sems
):
    rows, tokens, _ = result_ref.shape
    copies = []

    def emit(chunk, part, result):
        for h, r in enumerate(chunk):
            done[r] = result[:, h * tokens : (h + 1) * tokens].T
            copies.append(pltpu.make_async_copy(done.at[r], result_ref.at[r], sems.at[r]))
            copies[-1].start()

    finish_rows(
        emit, rows, merged_ref, middle_t_ref, gate_t_ref, columns_ref[4], columns_ref[5], outw_t_ref[1], unit_scratch
    )
    for copy in copies:
        copy.wait()


def on_device(*inputs):
    groups = lax.axis_size("row")
    rows, tokens, channels = inputs[0].shape
    per_group = channels // groups
    whole = pl.BlockSpec(memory_space=pltpu.VMEM)
    hbm = pl.BlockSpec(memory_space=pltpu.HBM)
    params = pltpu.CompilerParams(vmem_limit_bytes=48 * 1024 * 1024)
    shape = jax.ShapeDtypeStruct
    both_shape = shape((2 * channels * rows, tokens), BF16)
    flat_shape = shape((channels, rows * tokens), BF16)
    panels = pltpu.VMEM((tokens // LANES, 2 * channels * rows, LANES), F32)
    unit_scratch = pltpu.VMEM((tokens // LANES, channels * rows, LANES), F32)

    def exchange(array):
        return lax.all_to_all(
            array, "row", split_axis=0, concat_axis=0, tiled=True, axis_index_groups=[rank_order(groups)]
        )

    def mix(both, incoming):
        product = pl.pallas_call(
            functools.partial(mix_kernel, per_group, rows, incoming),
            out_shape=shape((groups, per_group * rows, tokens), BF16),
            in_specs=[whole],
            out_specs=whole,
            compiler_params=params,
            name="mix",
        )(both.reshape(groups, 2 * per_group * rows, tokens))
        return product.reshape(channels * rows, tokens)

    both, pair_t, gate_t, mask, columns, proj_t, outw_t = pl.pallas_call(
        functools.partial(project_kernel, per_group),
        out_shape=(
            both_shape,
            flat_shape,
            flat_shape,
            shape((rows, tokens), inputs[1].dtype),
            shape((6, channels, tokens), F32),
            shape((2, 5 * channels, channels), BF16),
            shape((2, channels, channels), BF16),
        ),
        in_specs=[hbm] * 7,
        out_specs=(whole,) * 7,
        scratch_shapes=[pltpu.VMEM(inputs[n].shape, inputs[n].dtype) for n in (0, 2, 3, 4, 5, 6)]
        + [panels, pltpu.SemaphoreType.DMA((7,))],
        compiler_params=params,
        name="project",
    )(*(pltpu.with_memory_space_constraint(a, pltpu.HBM) for a in inputs))
    merged = exchange(mix(exchange(both), False))
    both, middle_t, gate_t = pl.pallas_call(
        functools.partial(step_kernel, per_group),
        out_shape=(both_shape, flat_shape, flat_shape),
        in_specs=[whole] * 7,
        out_specs=(whole,) * 3,
        scratch_shapes=[unit_scratch, panels],
        compiler_params=params,
        name="finish_project",
    )(merged, pair_t, gate_t, mask, columns, outw_t, proj_t)
    merged = exchange(mix(exchange(both), True))
    return pl.pallas_call(
        finish_kernel,
        out_shape=shape((rows, tokens, channels), BF16),
        in_specs=[whole] * 5,
        out_specs=hbm,
        scratch_shapes=[unit_scratch, pltpu.VMEM((rows, tokens, channels), BF16), pltpu.SemaphoreType.DMA((rows,))],
        compiler_params=params,
        name="finish",
    )(merged, middle_t, gate_t, columns, outw_t)


def solution(mesh):
    rows = ("groups", "row")
    return jax.shard_map(
        on_device,
        mesh=mesh,
        in_specs=(P(rows, None, None), P(rows, None), P(), P(), P(), P(), P()),
        out_specs=P(rows, None, None),
        check_vma=False,
    )
```

```python
import functools

import jax
import jax.numpy as jnp
from jax import lax
from jax.experimental import pallas as pl
from jax.experimental.pallas import tpu as pltpu
from jax.sharding import PartitionSpec as P

F32 = jnp.float32
BF16 = jnp.bfloat16
LANES = 128
NT = (((1,), (1,)), ((), ()))
NN = (((1,), (0,)), ((), ()))
TN = (((0,), (0,)), ((), ()))


def dot(a, b, dims):
    return lax.dot_general(a, b, dims, preferred_element_type=F32)


def unit(values, axis):
    scale = 1.0 / values.shape[axis]
    centred = values - jnp.sum(values, axis=axis, keepdims=True) * scale
    spread = jnp.sum(centred * centred, axis=axis, keepdims=True) * scale
    return centred * lax.rsqrt(spread + 1e-05)


def chunks(rows, tokens, limit):
    wide = max(1, min(rows, limit // tokens))
    return [list(range(start, min(start + wide, rows))) for start in range(0, rows, wide)]


def span(chunk, tokens):
    return slice(chunk[0] * tokens, (chunk[-1] + 1) * tokens)


def lanes(parts):
    return parts[0] if len(parts) == 1 else jnp.concatenate(parts, axis=1)


def affine(values, gain, bias, tokens):
    parts = [values[:, n : n + tokens] * gain + bias for n in range(0, values.shape[1], tokens)]
    return lanes(parts).astype(BF16)


def store_panels(panels, per_group, rows, chunk, tokens, products, half_mask):
    channels = products.shape[0] // 5
    for side in range(2):
        base = 2 * side * channels
        gate, value = products[base : base + channels], products[base + channels : base + 2 * channels]
        gated = (jnp.tanh(gate) + 1.0) * (value * half_mask)
        for h, r in enumerate(chunk):
            for g in range(channels // per_group):
                where = pl.ds((2 * g + side) * per_group * rows + r, per_group, stride=rows)
                for t in range(tokens // LANES):
                    first = h * tokens + t * LANES
                    panels[t, where, :] = gated[g * per_group : (g + 1) * per_group, first : first + LANES]
    return (0.5 * jnp.tanh(products[4 * channels :]) + 0.5).astype(BF16)


def half_lanes(mask_ref, chunk):
    return lanes([mask_ref[r : r + 1].astype(F32) * 0.5 for r in chunk])


def project_kernel(per_group, *refs):
    inputs, refs = refs[:7], refs[7:]
    both_ref, pair_t_ref, gate_t_ref, mask_ref, columns_ref, proj_t_ref, outw_t_ref = refs[:7]
    pair_ref, gain_ref, bias_ref, proj_ref, gatew_ref, outw_ref, panels, sems = refs[7:]
    held = (pair_ref, mask_ref, gain_ref, bias_ref, proj_ref, gatew_ref, outw_ref)
    copies = [pltpu.make_async_copy(src, dst, sems.at[n]) for n, (src, dst) in enumerate(zip(inputs, held))]
    for copy in copies:
        copy.start()
    for copy in copies:
        copy.wait()
    rows, tokens, channels = pair_ref.shape
    small = jnp.concatenate([ref[which] for ref in (gain_ref, bias_ref) for which in range(2)], axis=0).T
    for n in range(4):
        for side in range(2):
            place = 4 * side + n
            columns_ref[2 * n + side] = jnp.broadcast_to(small[:, place : place + 1], (channels, tokens))
    for which in range(2):
        for part in range(4):
            block = proj_ref[which, :, part * channels : (part + 1) * channels].T
            proj_t_ref[which, part * channels : (part + 1) * channels] = block if part % 2 else block * 0.5
        proj_t_ref[which, 4 * channels :] = gatew_ref[which].T * 0.5
        outw_t_ref[which] = outw_ref[which].T
    for chunk in chunks(rows, tokens, 1024):
        part = span(chunk, tokens)
        pair_t = lanes([pair_ref[r].T for r in chunk])
        pair_t_ref[:, part] = pair_t
        normed = affine(unit(pair_t.astype(F32), 0), columns_ref[0], columns_ref[1], tokens)
        products = dot(proj_t_ref[0], normed, NN)
        gate_t_ref[:, part] = store_panels(
            panels, per_group, rows, chunk, tokens, products, half_lanes(mask_ref, chunk)
        )
    for t in range(tokens // LANES):
        both_ref[:, t * LANES : (t + 1) * LANES] = panels[t].astype(BF16)


def mix_kernel(per_group, rows, incoming, both_ref, product_ref):
    groups, _, tokens = both_ref.shape
    step = 2 * rows

    def matrices(side, pair):
        start = (side * per_group + 2 * pair) * rows
        block = both_ref[:, start : start + step, :].astype(F32)
        return [block[:, h * rows : (h + 1) * rows].reshape(groups * rows, tokens).astype(BF16) for h in range(2)]

    for pair in range(per_group // 2):
        lefts, rights = matrices(0, pair), matrices(1, pair)
        sums = [
            dot(left, right, TN if incoming else NT).reshape(groups, rows, tokens)
            for left, right in zip(lefts, rights)
        ]
        product_ref[:, pair * step : (pair + 1) * step, :] = jnp.concatenate(sums, axis=1).astype(BF16)


def finish_rows(emit, rows, merged_ref, pair_t_ref, gate_t_ref, gain, bias, outw_t, unit_scratch):
    tokens = merged_ref.shape[1]
    channels = merged_ref.shape[0] // rows
    sums = merged_ref[...].astype(F32).reshape(channels, rows, tokens)
    units = unit(sums, 0).reshape(channels * rows, tokens)
    tiles = range(tokens // LANES)
    for t in tiles:
        unit_scratch[t] = units[:, t * LANES : (t + 1) * LANES]
    for chunk in chunks(rows, tokens, 512):
        part = span(chunk, tokens)
        units = lanes([unit_scratch[t, pl.ds(r, channels, stride=rows), :] for r in chunk for t in tiles])
        normed = affine(units, gain, bias, tokens)
        change = gate_t_ref[:, part].astype(F32) * dot(outw_t, normed, NN)
        emit(chunk, part, (pair_t_ref[:, part].astype(F32) + change).astype(BF16))


def step_kernel(
    per_group, merged_ref, pair_t_ref, gate_t_ref, mask_ref, columns_ref, outw_t_ref, proj_t_ref,
    both_ref, middle_t_ref, gate1_t_ref, unit_scratch, panels,
):
    rows, tokens = mask_ref.shape

    def emit(chunk, part, middle):
        middle_t_ref[:, part] = middle
        normed = affine(unit(middle.astype(F32), 0), columns_ref[4], columns_ref[5], tokens)
        products = dot(proj_t_ref[1], normed, NN)
        gate1_t_ref[:, part] = store_panels(
            panels, per_group, rows, chunk, tokens, products, half_lanes(mask_ref, chunk)
        )

    finish_rows(
        emit, rows, merged_ref, pair_t_ref, gate_t_ref, columns_ref[2], columns_ref[3], outw_t_ref[0], unit_scratch
    )
    for t in range(tokens // LANES):
        both_ref[:, t * LANES : (t + 1) * LANES] = panels[t].astype(BF16)


def finish_kernel(
    merged_ref, middle_t_ref, gate_t_ref, columns_ref, outw_t_ref, result_ref, unit_scratch, done, sems
):
    rows, tokens, _ = result_ref.shape
    copies = []

    def emit(chunk, part, result):
        for h, r in enumerate(chunk):
            done[r] = result[:, h * tokens : (h + 1) * tokens].T
            copies.append(pltpu.make_async_copy(done.at[r], result_ref.at[r], sems.at[r]))
            copies[-1].start()

    finish_rows(
        emit, rows, merged_ref, middle_t_ref, gate_t_ref, columns_ref[6], columns_ref[7], outw_t_ref[1], unit_scratch
    )
    for copy in copies:
        copy.wait()


def on_device(*inputs):
    groups = lax.axis_size("row")
    rows, tokens, channels = inputs[0].shape
    per_group = channels // groups
    whole = pl.BlockSpec(memory_space=pltpu.VMEM)
    hbm = pl.BlockSpec(memory_space=pltpu.HBM)
    params = pltpu.CompilerParams(vmem_limit_bytes=48 * 1024 * 1024)
    shape = jax.ShapeDtypeStruct
    both_shape = shape((2 * channels * rows, tokens), BF16)
    flat_shape = shape((channels, rows * tokens), BF16)
    panels = pltpu.VMEM((tokens // LANES, 2 * channels * rows, LANES), F32)
    unit_scratch = pltpu.VMEM((tokens // LANES, channels * rows, LANES), F32)

    def exchange(array):
        return lax.all_to_all(array, "row", split_axis=0, concat_axis=0, tiled=True)

    def mix(both, incoming):
        product = pl.pallas_call(
            functools.partial(mix_kernel, per_group, rows, incoming),
            out_shape=shape((groups, per_group * rows, tokens), BF16),
            in_specs=[whole],
            out_specs=whole,
            compiler_params=params,
            name="mix",
        )(both.reshape(groups, 2 * per_group * rows, tokens))
        return product.reshape(channels * rows, tokens)

    both, pair_t, gate_t, mask, columns, proj_t, outw_t = pl.pallas_call(
        functools.partial(project_kernel, per_group),
        out_shape=(
            both_shape,
            flat_shape,
            flat_shape,
            shape((rows, tokens), inputs[1].dtype),
            shape((8, channels, tokens), F32),
            shape((2, 5 * channels, channels), BF16),
            shape((2, channels, channels), BF16),
        ),
        in_specs=[hbm] * 7,
        out_specs=(whole,) * 7,
        scratch_shapes=[pltpu.VMEM(inputs[n].shape, inputs[n].dtype) for n in (0, 2, 3, 4, 5, 6)]
        + [panels, pltpu.SemaphoreType.DMA((7,))],
        compiler_params=params,
        name="project",
    )(*(pltpu.with_memory_space_constraint(a, pltpu.HBM) for a in inputs))
    merged = exchange(mix(exchange(both), False))
    both, middle_t, gate_t = pl.pallas_call(
        functools.partial(step_kernel, per_group),
        out_shape=(both_shape, flat_shape, flat_shape),
        in_specs=[whole] * 7,
        out_specs=(whole,) * 3,
        scratch_shapes=[unit_scratch, panels],
        compiler_params=params,
        name="finish_project",
    )(merged, pair_t, gate_t, mask, columns, outw_t, proj_t)
    merged = exchange(mix(exchange(both), True))
    return pl.pallas_call(
        finish_kernel,
        out_shape=shape((rows, tokens, channels), BF16),
        in_specs=[whole] * 5,
        out_specs=hbm,
        scratch_shapes=[unit_scratch, pltpu.VMEM((rows, tokens, channels), BF16), pltpu.SemaphoreType.DMA((rows,))],
        compiler_params=params,
        name="finish",
    )(merged, middle_t, gate_t, columns, outw_t)


def solution(mesh):
    rows = ("groups", "row")
    return jax.shard_map(
        on_device,
        mesh=mesh,
        in_specs=(P(rows, None, None), P(rows, None), P(), P(), P(), P(), P()),
        out_specs=P(rows, None, None),
        check_vma=False,
    )
```

```python
import functools

import jax
import jax.numpy as jnp
from jax import lax
from jax.experimental import pallas as pl
from jax.experimental.pallas import tpu as pltpu
from jax.sharding import PartitionSpec as P

F32 = jnp.float32
BF16 = jnp.bfloat16
LANES = 128
NT = (((1,), (1,)), ((), ()))
NN = (((1,), (0,)), ((), ()))
TN = (((0,), (0,)), ((), ()))


def dot(a, b, dims):
    return lax.dot_general(a, b, dims, preferred_element_type=F32)


def unit(values, axis):
    scale = 1.0 / values.shape[axis]
    centred = values - jnp.sum(values, axis=axis, keepdims=True) * scale
    spread = jnp.sum(centred * centred, axis=axis, keepdims=True) * scale
    return centred * lax.rsqrt(spread + 1e-05)


def chunks(rows, tokens, limit):
    wide = max(1, min(rows, limit // tokens))
    return [list(range(start, min(start + wide, rows))) for start in range(0, rows, wide)]


def span(chunk, tokens):
    return slice(chunk[0] * tokens, (chunk[-1] + 1) * tokens)


def lanes(parts):
    return parts[0] if len(parts) == 1 else jnp.concatenate(parts, axis=1)


def affine(values, gain, bias, tokens):
    parts = [values[:, n : n + tokens] * gain + bias for n in range(0, values.shape[1], tokens)]
    return lanes(parts).astype(BF16)


def project_chunk(panels, per_group, rows, chunk, tokens, weights_t, normed, half_mask):
    channels = normed.shape[0]
    size = channels // 2
    for block in range(4):
        side, first = block // 2, block % 2 * size
        products = dot(weights_t[2 * size * block : 2 * size * (block + 1)], normed, NN)
        gated = (jnp.tanh(products[:size]) + 1.0) * (products[size:] * half_mask)
        for h, r in enumerate(chunk):
            for c in range(0, size, per_group):
                where = pl.ds((2 * (first + c) + side * per_group) * rows + r, per_group, stride=rows)
                for t in range(tokens // LANES):
                    lane = h * tokens + t * LANES
                    panels[t, where, :] = gated[c : c + per_group, lane : lane + LANES]
    return (0.5 * jnp.tanh(dot(weights_t[4 * channels :], normed, NN)) + 0.5).astype(BF16)


def half_lanes(mask_ref, chunk):
    return lanes([mask_ref[r : r + 1].astype(F32) * 0.5 for r in chunk])


def project_kernel(per_group, *refs):
    inputs, refs = refs[:7], refs[7:]
    both_ref, pair_t_ref, gate_t_ref, mask_ref, columns_ref, proj_t_ref, outw_t_ref = refs[:7]
    pair_ref, gain_ref, bias_ref, proj_ref, gatew_ref, outw_ref, panels, sems = refs[7:]
    held = (pair_ref, mask_ref, gain_ref, bias_ref, proj_ref, gatew_ref, outw_ref)
    copies = [pltpu.make_async_copy(src, dst, sems.at[n]) for n, (src, dst) in enumerate(zip(inputs, held))]
    for copy in copies:
        copy.start()
    for copy in copies:
        copy.wait()
    rows, tokens, channels = pair_ref.shape
    small = jnp.concatenate([ref[which] for ref in (gain_ref, bias_ref) for which in range(2)], axis=0).T
    for n in range(4):
        for side in range(2):
            place = 4 * side + n
            columns_ref[2 * n + side] = jnp.broadcast_to(small[:, place : place + 1], (channels, tokens))
    for which in range(2):
        size = channels // 2
        for part in range(4):
            block = proj_ref[which, :, part * channels : (part + 1) * channels].T
            block = block if part % 2 else block * 0.5
            for h in range(2):
                start = (part // 2 * 4 + h * 2 + part % 2) * size
                proj_t_ref[which, start : start + size] = block[h * size : (h + 1) * size]
        proj_t_ref[which, 4 * channels :] = gatew_ref[which].T * 0.5
        outw_t_ref[which] = outw_ref[which].T
    for chunk in chunks(rows, tokens, 256):
        part = span(chunk, tokens)
        pair_t = lanes([pair_ref[r].T for r in chunk])
        pair_t_ref[:, part] = pair_t
        normed = affine(unit(pair_t.astype(F32), 0), columns_ref[0], columns_ref[1], tokens)
        gate_t_ref[:, part] = project_chunk(
            panels, per_group, rows, chunk, tokens, proj_t_ref.at[0], normed, half_lanes(mask_ref, chunk)
        )
    for t in range(tokens // LANES):
        both_ref[:, t * LANES : (t + 1) * LANES] = panels[t].astype(BF16)


def mix_kernel(per_group, rows, incoming, both_ref, product_ref):
    groups, _, tokens = both_ref.shape
    step = 2 * rows

    def matrices(side, pair):
        start = (side * per_group + 2 * pair) * rows
        block = both_ref[:, start : start + step, :].astype(F32)
        return [block[:, h * rows : (h + 1) * rows].reshape(groups * rows, tokens).astype(BF16) for h in range(2)]

    for pair in range(per_group // 2):
        lefts, rights = matrices(0, pair), matrices(1, pair)
        sums = [
            dot(left, right, TN if incoming else NT).reshape(groups, rows, tokens)
            for left, right in zip(lefts, rights)
        ]
        product_ref[:, pair * step : (pair + 1) * step, :] = jnp.concatenate(sums, axis=1).astype(BF16)


def finish_rows(emit, rows, merged_ref, pair_t_ref, gate_t_ref, gain, bias, outw_t, unit_scratch):
    tokens = merged_ref.shape[1]
    channels = merged_ref.shape[0] // rows
    tiles = range(tokens // LANES)
    parts = [slice(first * rows, (first + 16) * rows) for first in range(0, channels, 16)]

    def sums(part):
        return merged_ref[part].astype(F32).reshape(16, rows, tokens)

    average = sum(jnp.sum(sums(part), axis=0) for part in parts) * (1.0 / channels)
    spread = sum(jnp.sum(jnp.square(sums(part) - average), axis=0) for part in parts) * (1.0 / channels)
    inverse = lax.rsqrt(spread + 1e-05)
    for part in parts:
        units = ((sums(part) - average) * inverse).reshape(16 * rows, tokens)
        for t in tiles:
            unit_scratch[t, part, :] = units[:, t * LANES : (t + 1) * LANES]
    for chunk in chunks(rows, tokens, 256):
        part = span(chunk, tokens)
        units = lanes([unit_scratch[t, pl.ds(r, channels, stride=rows), :] for r in chunk for t in tiles])
        normed = affine(units, gain, bias, tokens)
        change = gate_t_ref[:, part].astype(F32) * dot(outw_t, normed, NN)
        emit(chunk, part, (pair_t_ref[:, part].astype(F32) + change).astype(BF16))


def step_kernel(
    per_group, merged_ref, pair_t_ref, gate_t_ref, mask_ref, columns_ref, outw_t_ref, proj_t_ref,
    both_ref, middle_t_ref, gate1_t_ref, unit_scratch, panels,
):
    rows, tokens = mask_ref.shape

    def emit(chunk, part, middle):
        middle_t_ref[:, part] = middle
        normed = affine(unit(middle.astype(F32), 0), columns_ref[4], columns_ref[5], tokens)
        gate1_t_ref[:, part] = project_chunk(
            panels, per_group, rows, chunk, tokens, proj_t_ref.at[1], normed, half_lanes(mask_ref, chunk)
        )

    finish_rows(
        emit, rows, merged_ref, pair_t_ref, gate_t_ref, columns_ref[2], columns_ref[3], outw_t_ref[0], unit_scratch
    )
    for t in range(tokens // LANES):
        both_ref[:, t * LANES : (t + 1) * LANES] = panels[t].astype(BF16)


def finish_kernel(
    merged_ref, middle_t_ref, gate_t_ref, columns_ref, outw_t_ref, result_ref, unit_scratch, done, sems
):
    rows, tokens, _ = result_ref.shape
    copies = []

    def emit(chunk, part, result):
        for h, r in enumerate(chunk):
            done[r] = result[:, h * tokens : (h + 1) * tokens].T
            copies.append(pltpu.make_async_copy(done.at[r], result_ref.at[r], sems.at[r]))
            copies[-1].start()

    finish_rows(
        emit, rows, merged_ref, middle_t_ref, gate_t_ref, columns_ref[6], columns_ref[7], outw_t_ref[1], unit_scratch
    )
    for copy in copies:
        copy.wait()


def on_device(*inputs):
    groups = lax.axis_size("row")
    rows, tokens, channels = inputs[0].shape
    per_group = channels // groups
    whole = pl.BlockSpec(memory_space=pltpu.VMEM)
    hbm = pl.BlockSpec(memory_space=pltpu.HBM)
    params = pltpu.CompilerParams(vmem_limit_bytes=48 * 1024 * 1024)
    shape = jax.ShapeDtypeStruct
    both_shape = shape((2 * channels * rows, tokens), BF16)
    flat_shape = shape((channels, rows * tokens), BF16)
    panels = pltpu.VMEM((tokens // LANES, 2 * channels * rows, LANES), F32)
    unit_scratch = pltpu.VMEM((tokens // LANES, channels * rows, LANES), F32)

    def exchange(array):
        return lax.all_to_all(array, "row", split_axis=0, concat_axis=0, tiled=True)

    def mix(both, incoming):
        product = pl.pallas_call(
            functools.partial(mix_kernel, per_group, rows, incoming),
            out_shape=shape((groups, per_group * rows, tokens), BF16),
            in_specs=[whole],
            out_specs=whole,
            compiler_params=params,
            name="mix",
        )(both.reshape(groups, 2 * per_group * rows, tokens))
        return product.reshape(channels * rows, tokens)

    both, pair_t, gate_t, mask, columns, proj_t, outw_t = pl.pallas_call(
        functools.partial(project_kernel, per_group),
        out_shape=(
            both_shape,
            flat_shape,
            flat_shape,
            shape((rows, tokens), inputs[1].dtype),
            shape((8, channels, tokens), F32),
            shape((2, 5 * channels, channels), BF16),
            shape((2, channels, channels), BF16),
        ),
        in_specs=[hbm] * 7,
        out_specs=(whole,) * 7,
        scratch_shapes=[pltpu.VMEM(inputs[n].shape, inputs[n].dtype) for n in (0, 2, 3, 4, 5, 6)]
        + [panels, pltpu.SemaphoreType.DMA((7,))],
        compiler_params=params,
        name="project",
    )(*(pltpu.with_memory_space_constraint(a, pltpu.HBM) for a in inputs))
    merged = exchange(mix(exchange(both), False))
    both, middle_t, gate_t = pl.pallas_call(
        functools.partial(step_kernel, per_group),
        out_shape=(both_shape, flat_shape, flat_shape),
        in_specs=[whole] * 7,
        out_specs=(whole,) * 3,
        scratch_shapes=[unit_scratch, panels],
        compiler_params=params,
        name="finish_project",
    )(merged, pair_t, gate_t, mask, columns, outw_t, proj_t)
    merged = exchange(mix(exchange(both), True))
    return pl.pallas_call(
        finish_kernel,
        out_shape=shape((rows, tokens, channels), BF16),
        in_specs=[whole] * 5,
        out_specs=hbm,
        scratch_shapes=[unit_scratch, pltpu.VMEM((rows, tokens, channels), BF16), pltpu.SemaphoreType.DMA((rows,))],
        compiler_params=params,
        name="finish",
    )(merged, middle_t, gate_t, columns, outw_t)


def solution(mesh):
    rows = ("groups", "row")
    return jax.shard_map(
        on_device,
        mesh=mesh,
        in_specs=(P(rows, None, None), P(rows, None), P(), P(), P(), P(), P()),
        out_specs=P(rows, None, None),
        check_vma=False,
    )
```

```python
import functools

import jax
import jax.numpy as jnp
from jax import lax
from jax.experimental import pallas as pl
from jax.experimental.pallas import tpu as pltpu
from jax.sharding import PartitionSpec as P

F32 = jnp.float32
BF16 = jnp.bfloat16
LANES = 128
NT = (((1,), (1,)), ((), ()))
NN = (((1,), (0,)), ((), ()))
TN = (((0,), (0,)), ((), ()))


def dot(a, b, dims):
    return lax.dot_general(a, b, dims, preferred_element_type=F32)


def unit(values, axis):
    scale = 1.0 / values.shape[axis]
    centred = values - jnp.sum(values, axis=axis, keepdims=True) * scale
    spread = jnp.sum(centred * centred, axis=axis, keepdims=True) * scale
    return centred * lax.rsqrt(spread + 1e-05)


def chunks(rows, tokens, limit):
    wide = max(1, min(rows, limit // tokens))
    return [list(range(start, min(start + wide, rows))) for start in range(0, rows, wide)]


def span(chunk, tokens):
    return slice(chunk[0] * tokens, (chunk[-1] + 1) * tokens)


def lanes(parts):
    return parts[0] if len(parts) == 1 else jnp.concatenate(parts, axis=1)


def affine(values, gain, bias, tokens):
    parts = [values[:, n : n + tokens] * gain + bias for n in range(0, values.shape[1], tokens)]
    return lanes(parts).astype(BF16)


def store_panels(panels, per_group, rows, chunk, tokens, products, half_mask):
    channels = products.shape[0] // 5
    for side in range(2):
        base = 2 * side * channels
        gate, value = products[base : base + channels], products[base + channels : base + 2 * channels]
        gated = (jnp.tanh(gate) + 1.0) * (value * half_mask)
        for h, r in enumerate(chunk):
            for g in range(channels // per_group):
                where = pl.ds((2 * g + side) * per_group * (rows + 1) + r, per_group, stride=rows + 1)
                for t in range(tokens // LANES):
                    first = h * tokens + t * LANES
                    panels[t, where, :] = gated[g * per_group : (g + 1) * per_group, first : first + LANES]
    return (0.5 * jnp.tanh(products[4 * channels :]) + 0.5).astype(BF16)


def pack_panels(panels, both_ref, rows):
    for t in range(both_ref.shape[1] // LANES):
        for first in range(0, both_ref.shape[0] // rows, 16):
            parts = [panels[t, pl.ds(c * (rows + 1), rows), :] for c in range(first, first + 16)]
            packed = jnp.concatenate(parts, axis=0).astype(BF16)
            both_ref[first * rows : (first + 16) * rows, t * LANES : (t + 1) * LANES] = packed


def half_lanes(mask_ref, chunk):
    return lanes([mask_ref[r : r + 1].astype(F32) * 0.5 for r in chunk])


def project_kernel(per_group, *refs):
    inputs, refs = refs[:7], refs[7:]
    both_ref, pair_t_ref, gate_t_ref, mask_ref, columns_ref, proj_t_ref, outw_t_ref = refs[:7]
    pair_ref, gain_ref, bias_ref, proj_ref, gatew_ref, outw_ref, panels, sems = refs[7:]
    held = (pair_ref, mask_ref, gain_ref, bias_ref, proj_ref, gatew_ref, outw_ref)
    copies = [pltpu.make_async_copy(src, dst, sems.at[n]) for n, (src, dst) in enumerate(zip(inputs, held))]
    for copy in copies:
        copy.start()
    for copy in copies:
        copy.wait()
    rows, tokens, channels = pair_ref.shape
    small = jnp.concatenate([ref[which] for ref in (gain_ref, bias_ref) for which in range(2)], axis=0).T
    for n in range(4):
        for side in range(2):
            place = 4 * side + n
            columns_ref[2 * n + side] = jnp.broadcast_to(small[:, place : place + 1], (channels, tokens))
    for which in range(2):
        for part in range(4):
            block = proj_ref[which, :, part * channels : (part + 1) * channels].T
            proj_t_ref[which, part * channels : (part + 1) * channels] = block if part % 2 else block * 0.5
        proj_t_ref[which, 4 * channels :] = gatew_ref[which].T * 0.5
        outw_t_ref[which] = outw_ref[which].T
    for chunk in chunks(rows, tokens, 256):
        part = span(chunk, tokens)
        pair_t = lanes([pair_ref[r].T for r in chunk])
        pair_t_ref[:, part] = pair_t
        normed = affine(unit(pair_t.astype(F32), 0), columns_ref[0], columns_ref[1], tokens)
        products = dot(proj_t_ref[0], normed, NN)
        gate_t_ref[:, part] = store_panels(
            panels, per_group, rows, chunk, tokens, products, half_lanes(mask_ref, chunk)
        )
    pack_panels(panels, both_ref, rows)


def mix_kernel(per_group, rows, incoming, both_ref, product_ref):
    groups, _, tokens = both_ref.shape
    step = 2 * rows

    def matrices(side, pair):
        start = (side * per_group + 2 * pair) * rows
        block = both_ref[:, start : start + step, :].astype(F32)
        return [block[:, h * rows : (h + 1) * rows].reshape(groups * rows, tokens).astype(BF16) for h in range(2)]

    for pair in range(per_group // 2):
        lefts, rights = matrices(0, pair), matrices(1, pair)
        sums = [
            dot(left, right, TN if incoming else NT).reshape(groups, rows, tokens)
            for left, right in zip(lefts, rights)
        ]
        product_ref[:, pair * step : (pair + 1) * step, :] = jnp.concatenate(sums, axis=1).astype(BF16)


def finish_rows(emit, rows, merged_ref, pair_t_ref, gate_t_ref, gain, bias, outw_t, unit_scratch):
    tokens = merged_ref.shape[1]
    channels = merged_ref.shape[0] // rows
    tiles = range(tokens // LANES)
    parts = [slice(first * rows, (first + 16) * rows) for first in range(0, channels, 16)]

    def sums(part):
        return merged_ref[part].astype(F32).reshape(16, rows, tokens)

    average = sum(jnp.sum(sums(part), axis=0) for part in parts) * (1.0 / channels)
    spread = sum(jnp.sum(jnp.square(sums(part) - average), axis=0) for part in parts) * (1.0 / channels)
    inverse = lax.rsqrt(spread + 1e-05)
    for part in parts:
        units = (sums(part) - average) * inverse
        for t in tiles:
            for n in range(16):
                where = pl.ds((part.start // rows + n) * (rows + 1), rows)
                unit_scratch[t, where, :] = units[n, :, t * LANES : (t + 1) * LANES]
    for chunk in chunks(rows, tokens, 256):
        part = span(chunk, tokens)
        units = lanes([unit_scratch[t, pl.ds(r, channels, stride=rows + 1), :] for r in chunk for t in tiles])
        normed = affine(units, gain, bias, tokens)
        change = gate_t_ref[:, part].astype(F32) * dot(outw_t, normed, NN)
        emit(chunk, part, (pair_t_ref[:, part].astype(F32) + change).astype(BF16))


def step_kernel(
    per_group, merged_ref, pair_t_ref, gate_t_ref, mask_ref, columns_ref, outw_t_ref, proj_t_ref,
    both_ref, middle_t_ref, gate1_t_ref, unit_scratch, panels,
):
    rows, tokens = mask_ref.shape

    def emit(chunk, part, middle):
        middle_t_ref[:, part] = middle
        normed = affine(unit(middle.astype(F32), 0), columns_ref[4], columns_ref[5], tokens)
        products = dot(proj_t_ref[1], normed, NN)
        gate1_t_ref[:, part] = store_panels(
            panels, per_group, rows, chunk, tokens, products, half_lanes(mask_ref, chunk)
        )

    finish_rows(
        emit, rows, merged_ref, pair_t_ref, gate_t_ref, columns_ref[2], columns_ref[3], outw_t_ref[0], unit_scratch
    )
    pack_panels(panels, both_ref, rows)


def finish_kernel(
    merged_ref, middle_t_ref, gate_t_ref, columns_ref, outw_t_ref, result_ref, unit_scratch, done, sems
):
    rows, tokens, _ = result_ref.shape
    copies = []

    def emit(chunk, part, result):
        for h, r in enumerate(chunk):
            done[r] = result[:, h * tokens : (h + 1) * tokens].T
            copies.append(pltpu.make_async_copy(done.at[r], result_ref.at[r], sems.at[r]))
            copies[-1].start()

    finish_rows(
        emit, rows, merged_ref, middle_t_ref, gate_t_ref, columns_ref[6], columns_ref[7], outw_t_ref[1], unit_scratch
    )
    for copy in copies:
        copy.wait()


def on_device(*inputs):
    groups = lax.axis_size("row")
    rows, tokens, channels = inputs[0].shape
    per_group = channels // groups
    whole = pl.BlockSpec(memory_space=pltpu.VMEM)
    hbm = pl.BlockSpec(memory_space=pltpu.HBM)
    params = pltpu.CompilerParams(vmem_limit_bytes=48 * 1024 * 1024)
    shape = jax.ShapeDtypeStruct
    both_shape = shape((2 * channels * rows, tokens), BF16)
    flat_shape = shape((channels, rows * tokens), BF16)
    panels = pltpu.VMEM((tokens // LANES, 2 * channels * (rows + 1), LANES), F32)
    unit_scratch = pltpu.VMEM((tokens // LANES, channels * (rows + 1), LANES), F32)

    def exchange(array):
        return lax.all_to_all(array, "row", split_axis=0, concat_axis=0, tiled=True)

    def mix(both, incoming):
        product = pl.pallas_call(
            functools.partial(mix_kernel, per_group, rows, incoming),
            out_shape=shape((groups, per_group * rows, tokens), BF16),
            in_specs=[whole],
            out_specs=whole,
            compiler_params=params,
            name="mix",
        )(both.reshape(groups, 2 * per_group * rows, tokens))
        return product.reshape(channels * rows, tokens)

    both, pair_t, gate_t, mask, columns, proj_t, outw_t = pl.pallas_call(
        functools.partial(project_kernel, per_group),
        out_shape=(
            both_shape,
            flat_shape,
            flat_shape,
            shape((rows, tokens), inputs[1].dtype),
            shape((8, channels, tokens), F32),
            shape((2, 5 * channels, channels), BF16),
            shape((2, channels, channels), BF16),
        ),
        in_specs=[hbm] * 7,
        out_specs=(whole,) * 7,
        scratch_shapes=[pltpu.VMEM(inputs[n].shape, inputs[n].dtype) for n in (0, 2, 3, 4, 5, 6)]
        + [panels, pltpu.SemaphoreType.DMA((7,))],
        compiler_params=params,
        name="project",
    )(*(pltpu.with_memory_space_constraint(a, pltpu.HBM) for a in inputs))
    merged = exchange(mix(exchange(both), False))
    both, middle_t, gate_t = pl.pallas_call(
        functools.partial(step_kernel, per_group),
        out_shape=(both_shape, flat_shape, flat_shape),
        in_specs=[whole] * 7,
        out_specs=(whole,) * 3,
        scratch_shapes=[unit_scratch, panels],
        compiler_params=params,
        name="finish_project",
    )(merged, pair_t, gate_t, mask, columns, outw_t, proj_t)
    merged = exchange(mix(exchange(both), True))
    return pl.pallas_call(
        finish_kernel,
        out_shape=shape((rows, tokens, channels), BF16),
        in_specs=[whole] * 5,
        out_specs=hbm,
        scratch_shapes=[unit_scratch, pltpu.VMEM((rows, tokens, channels), BF16), pltpu.SemaphoreType.DMA((rows,))],
        compiler_params=params,
        name="finish",
    )(merged, middle_t, gate_t, columns, outw_t)


def solution(mesh):
    rows = ("groups", "row")
    return jax.shard_map(
        on_device,
        mesh=mesh,
        in_specs=(P(rows, None, None), P(rows, None), P(), P(), P(), P(), P()),
        out_specs=P(rows, None, None),
        check_vma=False,
    )
```

```python
import functools

import jax
import jax.numpy as jnp
from jax import lax
from jax.experimental import pallas as pl
from jax.experimental.pallas import tpu as pltpu
from jax.sharding import PartitionSpec as P

F32 = jnp.float32
BF16 = jnp.bfloat16
LANES = 128
NT = (((1,), (1,)), ((), ()))
NN = (((1,), (0,)), ((), ()))
TN = (((0,), (0,)), ((), ()))


def dot(a, b, dims):
    return lax.dot_general(a, b, dims, preferred_element_type=F32)


def unit(values, axis):
    scale = 1.0 / values.shape[axis]
    centred = values - jnp.sum(values, axis=axis, keepdims=True) * scale
    spread = jnp.sum(centred * centred, axis=axis, keepdims=True) * scale
    return centred * lax.rsqrt(spread + 1e-05)


def chunks(rows, tokens, limit):
    wide = max(1, min(rows, limit // tokens))
    return [list(range(start, min(start + wide, rows))) for start in range(0, rows, wide)]


def span(chunk, tokens):
    return slice(chunk[0] * tokens, (chunk[-1] + 1) * tokens)


def lanes(parts):
    return parts[0] if len(parts) == 1 else jnp.concatenate(parts, axis=1)


def affine(values, gain, bias, tokens):
    parts = [values[:, n : n + tokens] * gain + bias for n in range(0, values.shape[1], tokens)]
    return lanes(parts).astype(BF16)


def store_panels(panels, per_group, rows, chunk, tokens, products, half_mask):
    channels = products.shape[0] // 5
    for side in range(2):
        base = 2 * side * channels
        gate, value = products[base : base + channels], products[base + channels : base + 2 * channels]
        gated = (jnp.tanh(gate) + 1.0) * (value * half_mask)
        for h, r in enumerate(chunk):
            for g in range(channels // per_group):
                where = pl.ds((2 * g + side) * per_group * (rows + 1) + r, per_group, stride=rows + 1)
                for t in range(tokens // LANES):
                    first = h * tokens + t * LANES
                    panels[t, where, :] = gated[g * per_group : (g + 1) * per_group, first : first + LANES]
    return (0.5 * jnp.tanh(products[4 * channels :]) + 0.5).astype(BF16)


def pack_panels(panels, both_ref, rows):
    for t in range(both_ref.shape[1] // LANES):
        for first in range(0, both_ref.shape[0] // rows, 16):
            parts = [panels[t, pl.ds(c * (rows + 1), rows), :] for c in range(first, first + 16)]
            packed = jnp.concatenate(parts, axis=0).astype(BF16)
            both_ref[first * rows : (first + 16) * rows, t * LANES : (t + 1) * LANES] = packed


def split_panels(panels, core_ref, left_ref, right_ref, other_ref, rows):
    size = left_ref.shape[0]
    for t in range(left_ref.shape[1] // LANES):
        for first in range(0, size // rows, 16):
            first_core = jnp.full((16 * rows, LANES), core_ref[0]) == 0
            for side, own_ref in enumerate((left_ref, right_ref)):
                mine, others = [
                    jnp.concatenate(
                        [
                            panels[t, pl.ds(((2 * g + side) * (size // rows) + c) * (rows + 1), rows), :]
                            for c in range(first, first + 16)
                        ],
                        axis=0,
                    )
                    for g in range(2)
                ]
                lane = slice(t * LANES, (t + 1) * LANES)
                part = slice(first * rows, (first + 16) * rows)
                own_ref[part, lane] = jnp.where(first_core, mine, others).astype(BF16)
                part = slice(side * size + first * rows, side * size + (first + 16) * rows)
                other_ref[part, lane] = jnp.where(first_core, others, mine).astype(BF16)


def half_lanes(mask_ref, chunk):
    return lanes([mask_ref[r : r + 1].astype(F32) * 0.5 for r in chunk])


def project_kernel(per_group, by_core, *refs):
    core_ref, refs = (refs[0], refs[1:]) if by_core else (None, refs)
    inputs, refs = refs[:7], refs[7:]
    if by_core:
        outs, refs = refs[:3], refs[3:]
        both_ref = None
    else:
        both_ref, refs = refs[0], refs[1:]
    pair_t_ref, gate_t_ref, mask_ref, columns_ref, proj_t_ref, outw_t_ref = refs[:6]
    pair_ref, gain_ref, bias_ref, proj_ref, gatew_ref, outw_ref, panels, sems = refs[6:]
    held = (pair_ref, mask_ref, gain_ref, bias_ref, proj_ref, gatew_ref, outw_ref)
    copies = [pltpu.make_async_copy(src, dst, sems.at[n]) for n, (src, dst) in enumerate(zip(inputs, held))]
    for copy in copies:
        copy.start()
    for copy in copies:
        copy.wait()
    rows, tokens, channels = pair_ref.shape
    small = jnp.concatenate([ref[which] for ref in (gain_ref, bias_ref) for which in range(2)], axis=0).T
    for n in range(4):
        for side in range(2):
            place = 4 * side + n
            columns_ref[2 * n + side] = jnp.broadcast_to(small[:, place : place + 1], (channels, tokens))
    for which in range(2):
        for part in range(4):
            block = proj_ref[which, :, part * channels : (part + 1) * channels].T
            proj_t_ref[which, part * channels : (part + 1) * channels] = block if part % 2 else block * 0.5
        proj_t_ref[which, 4 * channels :] = gatew_ref[which].T * 0.5
        outw_t_ref[which] = outw_ref[which].T
    for chunk in chunks(rows, tokens, 256):
        part = span(chunk, tokens)
        pair_t = lanes([pair_ref[r].T for r in chunk])
        pair_t_ref[:, part] = pair_t
        normed = affine(unit(pair_t.astype(F32), 0), columns_ref[0], columns_ref[1], tokens)
        products = dot(proj_t_ref[0], normed, NN)
        gate_t_ref[:, part] = store_panels(
            panels, per_group, rows, chunk, tokens, products, half_lanes(mask_ref, chunk)
        )
    if by_core:
        split_panels(panels, core_ref, *outs, rows)
    else:
        pack_panels(panels, both_ref, rows)


def mix_kernel(per_group, rows, incoming, both_ref, product_ref):
    groups, _, tokens = both_ref.shape
    step = 2 * rows

    def matrices(side, pair):
        start = (side * per_group + 2 * pair) * rows
        block = both_ref[:, start : start + step, :].astype(F32)
        return [block[:, h * rows : (h + 1) * rows].reshape(groups * rows, tokens).astype(BF16) for h in range(2)]

    for pair in range(per_group // 2):
        lefts, rights = matrices(0, pair), matrices(1, pair)
        sums = [
            dot(left, right, TN if incoming else NT).reshape(groups, rows, tokens)
            for left, right in zip(lefts, rights)
        ]
        product_ref[:, pair * step : (pair + 1) * step, :] = jnp.concatenate(sums, axis=1).astype(BF16)


def mix_gathered(rows, core_ref, own_ref, got_ref, right_ref, keep_ref, send_ref):
    chips, _, count, _, tokens = right_ref.shape
    first_core = jnp.full((chips, rows, tokens), core_ref[0]) == 0
    for c in range(count):
        mine, others = right_ref[:, 0, c].astype(F32), right_ref[:, 1, c].astype(F32)
        halves = [jnp.where(first_core, mine, others), jnp.where(first_core, others, mine)]
        right = jnp.concatenate(halves, axis=1).reshape(2 * chips * rows, tokens).astype(BF16)
        left = jnp.concatenate([own_ref[c].astype(F32), got_ref[c].astype(F32)], axis=0).astype(BF16)
        sums = dot(left, right, NT)
        keep_ref[c] = sums[:rows].astype(BF16)
        send_ref[c] = sums[rows:].astype(BF16)


def finish_rows(emit, rows, channels, tokens, load, pair_t_ref, gate_t_ref, gain, bias, outw_t, unit_scratch):
    tiles = range(tokens // LANES)
    parts = [slice(first * rows, (first + 16) * rows) for first in range(0, channels, 16)]

    def sums(part):
        return load(part).reshape(16, rows, tokens)

    average = sum(jnp.sum(sums(part), axis=0) for part in parts) * (1.0 / channels)
    spread = sum(jnp.sum(jnp.square(sums(part) - average), axis=0) for part in parts) * (1.0 / channels)
    inverse = lax.rsqrt(spread + 1e-05)
    for part in parts:
        units = (sums(part) - average) * inverse
        for t in tiles:
            for n in range(16):
                where = pl.ds((part.start // rows + n) * (rows + 1), rows)
                unit_scratch[t, where, :] = units[n, :, t * LANES : (t + 1) * LANES]
    for chunk in chunks(rows, tokens, 256):
        part = span(chunk, tokens)
        units = lanes([unit_scratch[t, pl.ds(r, channels, stride=rows + 1), :] for r in chunk for t in tiles])
        normed = affine(units, gain, bias, tokens)
        change = gate_t_ref[:, part].astype(F32) * dot(outw_t, normed, NN)
        emit(chunk, part, (pair_t_ref[:, part].astype(F32) + change).astype(BF16))


def step_kernel(per_group, by_core, *refs):
    if not by_core:
        merged_ref, refs = refs[0], refs[1:]
        return step_rows(per_group, lambda part: merged_ref[part].astype(F32), *refs)
    core_ref, keep_ref, got_ref, refs = refs[0], refs[1], refs[2], refs[3:]
    size = keep_ref.shape[0]

    def load(part):
        late = part.start >= size
        part = slice(part.start - size, part.stop - size) if late else part
        keep, got = keep_ref[part].astype(F32), got_ref[part].astype(F32)
        return jnp.where(jnp.full(keep.shape, core_ref[0]) == int(late), keep, got)

    step_rows(per_group, load, *refs)


def step_rows(
    per_group, load, pair_t_ref, gate_t_ref, mask_ref, columns_ref, outw_t_ref, proj_t_ref,
    both_ref, middle_t_ref, gate1_t_ref, unit_scratch, panels,
):
    rows, tokens = mask_ref.shape

    def emit(chunk, part, middle):
        middle_t_ref[:, part] = middle
        normed = affine(unit(middle.astype(F32), 0), columns_ref[4], columns_ref[5], tokens)
        products = dot(proj_t_ref[1], normed, NN)
        gate1_t_ref[:, part] = store_panels(
            panels, per_group, rows, chunk, tokens, products, half_lanes(mask_ref, chunk)
        )

    finish_rows(
        emit, rows, pair_t_ref.shape[0], tokens, load, pair_t_ref, gate_t_ref, columns_ref[2], columns_ref[3],
        outw_t_ref[0], unit_scratch,
    )
    pack_panels(panels, both_ref, rows)


def finish_kernel(
    merged_ref, middle_t_ref, gate_t_ref, columns_ref, outw_t_ref, result_ref, unit_scratch, done, sems
):
    rows, tokens, _ = result_ref.shape
    copies = []

    def emit(chunk, part, result):
        for h, r in enumerate(chunk):
            done[r] = result[:, h * tokens : (h + 1) * tokens].T
            copies.append(pltpu.make_async_copy(done.at[r], result_ref.at[r], sems.at[r]))
            copies[-1].start()

    finish_rows(
        emit, rows, middle_t_ref.shape[0], tokens, lambda part: merged_ref[part].astype(F32), middle_t_ref, gate_t_ref,
        columns_ref[6], columns_ref[7], outw_t_ref[1], unit_scratch,
    )
    for copy in copies:
        copy.wait()


def on_device(*inputs):
    groups = lax.axis_size("row")
    rows, tokens, channels = inputs[0].shape
    per_group = channels // groups
    whole = pl.BlockSpec(memory_space=pltpu.VMEM)
    hbm = pl.BlockSpec(memory_space=pltpu.HBM)
    params = pltpu.CompilerParams(vmem_limit_bytes=48 * 1024 * 1024)
    shape = jax.ShapeDtypeStruct
    both_shape = shape((2 * channels * rows, tokens), BF16)
    flat_shape = shape((channels, rows * tokens), BF16)
    panels = pltpu.VMEM((tokens // LANES, 2 * channels * (rows + 1), LANES), F32)
    unit_scratch = pltpu.VMEM((tokens // LANES, channels * (rows + 1), LANES), F32)

    def exchange(array):
        return lax.all_to_all(array, "row", split_axis=0, concat_axis=0, tiled=True)

    def mix(both, incoming):
        product = pl.pallas_call(
            functools.partial(mix_kernel, per_group, rows, incoming),
            out_shape=shape((groups, per_group * rows, tokens), BF16),
            in_specs=[whole],
            out_specs=whole,
            compiler_params=params,
            name="mix",
        )(both.reshape(groups, 2 * per_group * rows, tokens))
        return product.reshape(channels * rows, tokens)

    half = channels // 2
    by_core = groups % 2 == 0 and groups * rows * tokens * half * 2 <= 4 * 2**20
    smem = pl.BlockSpec(memory_space=pltpu.SMEM)
    core = (lax.axis_index("row") % 2).astype(jnp.int32).reshape(1)
    half_shape = shape((half * rows, tokens), BF16)
    projected = (half_shape, half_shape, shape((2 * half * rows, tokens), BF16)) if by_core else (both_shape,)
    results = pl.pallas_call(
        functools.partial(project_kernel, half if by_core else per_group, by_core),
        out_shape=projected
        + (
            flat_shape,
            flat_shape,
            shape((rows, tokens), inputs[1].dtype),
            shape((8, channels, tokens), F32),
            shape((2, 5 * channels, channels), BF16),
            shape((2, channels, channels), BF16),
        ),
        in_specs=[smem] * by_core + [hbm] * 7,
        out_specs=(whole,) * (len(projected) + 6),
        scratch_shapes=[pltpu.VMEM(inputs[n].shape, inputs[n].dtype) for n in (0, 2, 3, 4, 5, 6)]
        + [panels, pltpu.SemaphoreType.DMA((7,))],
        compiler_params=params,
        name="project",
    )(*[core] * by_core, *(pltpu.with_memory_space_constraint(a, pltpu.HBM) for a in inputs))
    pair_t, gate_t, mask, columns, proj_t, outw_t = results[-6:]
    if by_core:
        left, right, other = results[:3]
        swap = [(d, d ^ 1) for d in range(groups)]
        got = lax.ppermute(other, "row", swap)
        gathered = lax.all_gather(
            jnp.concatenate([right, got[half * rows :]], axis=0),
            "row",
            axis_index_groups=[list(range(c, groups, 2)) for c in range(2)],
        )
        block = half // 4
        keep, send = pl.pallas_call(
            functools.partial(mix_gathered, rows),
            grid=(4,),
            out_shape=(shape((half, rows, tokens), BF16),) * 2,
            in_specs=[smem]
            + [pl.BlockSpec((block, rows, tokens), lambda n: (n, 0, 0))] * 2
            + [pl.BlockSpec((groups // 2, 2, block, rows, tokens), lambda n: (0, 0, n, 0, 0))],
            out_specs=(pl.BlockSpec((block, rows, tokens), lambda n: (n, 0, 0)),) * 2,
            compiler_params=params,
            name="mix_gathered",
        )(
            core,
            left.reshape(half, rows, tokens),
            got.reshape(2 * half, rows, tokens),
            gathered.reshape(groups // 2, 2, half, rows, tokens),
        )
        merged = (core, keep.reshape(half * rows, tokens), lax.ppermute(send, "row", swap).reshape(half * rows, tokens))
    else:
        merged = (exchange(mix(exchange(results[0]), False)),)
    both, middle_t, gate_t = pl.pallas_call(
        functools.partial(step_kernel, per_group, by_core),
        out_shape=(both_shape, flat_shape, flat_shape),
        in_specs=[smem] * by_core + [whole] * (len(merged) - by_core + 6),
        out_specs=(whole,) * 3,
        scratch_shapes=[unit_scratch, panels],
        compiler_params=params,
        name="finish_project",
    )(*merged, pair_t, gate_t, mask, columns, outw_t, proj_t)
    merged = exchange(mix(exchange(both), True))
    return pl.pallas_call(
        finish_kernel,
        out_shape=shape((rows, tokens, channels), BF16),
        in_specs=[whole] * 5,
        out_specs=hbm,
        scratch_shapes=[unit_scratch, pltpu.VMEM((rows, tokens, channels), BF16), pltpu.SemaphoreType.DMA((rows,))],
        compiler_params=params,
        name="finish",
    )(merged, middle_t, gate_t, columns, outw_t)


def solution(mesh):
    rows = ("groups", "row")
    return jax.shard_map(
        on_device,
        mesh=mesh,
        in_specs=(P(rows, None, None), P(rows, None), P(), P(), P(), P(), P()),
        out_specs=P(rows, None, None),
        check_vma=False,
    )
```

```python
import functools

import jax
import jax.numpy as jnp
from jax import lax
from jax.experimental import pallas as pl
from jax.experimental.pallas import tpu as pltpu
from jax.sharding import PartitionSpec as P

F32 = jnp.float32
BF16 = jnp.bfloat16
LANES = 128
NT = (((1,), (1,)), ((), ()))
NN = (((1,), (0,)), ((), ()))
TN = (((0,), (0,)), ((), ()))


def dot(a, b, dims):
    return lax.dot_general(a, b, dims, preferred_element_type=F32)


def unit(values, axis):
    scale = 1.0 / values.shape[axis]
    centred = values - jnp.sum(values, axis=axis, keepdims=True) * scale
    spread = jnp.sum(centred * centred, axis=axis, keepdims=True) * scale
    return centred * lax.rsqrt(spread + 1e-05)


def chunks(rows, tokens, limit):
    wide = max(1, min(rows, limit // tokens))
    return [list(range(start, min(start + wide, rows))) for start in range(0, rows, wide)]


def span(chunk, tokens):
    return slice(chunk[0] * tokens, (chunk[-1] + 1) * tokens)


def lanes(parts):
    return parts[0] if len(parts) == 1 else jnp.concatenate(parts, axis=1)


def affine(values, gain, bias, tokens):
    parts = [values[:, n : n + tokens] * gain + bias for n in range(0, values.shape[1], tokens)]
    return lanes(parts).astype(BF16)


def store_panels(panels, per_group, rows, chunk, tokens, products, half_mask):
    channels = products.shape[0] // 5
    for side in range(2):
        base = 2 * side * channels
        gate, value = products[base : base + channels], products[base + channels : base + 2 * channels]
        gated = (jnp.tanh(gate) + 1.0) * (value * half_mask)
        for h, r in enumerate(chunk):
            for g in range(channels // per_group):
                where = pl.ds((2 * g + side) * per_group * (rows + 1) + r, per_group, stride=rows + 1)
                for t in range(tokens // LANES):
                    first = h * tokens + t * LANES
                    panels[t, where, :] = gated[g * per_group : (g + 1) * per_group, first : first + LANES]
    return (0.5 * jnp.tanh(products[4 * channels :]) + 0.5).astype(BF16)


def pack_panels(panels, both_ref, rows):
    for t in range(both_ref.shape[1] // LANES):
        for first in range(0, both_ref.shape[0] // rows, 16):
            parts = [panels[t, pl.ds(c * (rows + 1), rows), :] for c in range(first, first + 16)]
            packed = jnp.concatenate(parts, axis=0).astype(BF16)
            both_ref[first * rows : (first + 16) * rows, t * LANES : (t + 1) * LANES] = packed


def split_panels(panels, core_ref, left_ref, right_ref, other_left_ref, other_right_ref, rows):
    size = left_ref.shape[0]
    for t in range(left_ref.shape[1] // LANES):
        for first in range(0, size // rows, 16):
            first_core = jnp.full((16 * rows, LANES), core_ref[0]) == 0
            for side, (own_ref, other_ref) in enumerate(((left_ref, other_left_ref), (right_ref, other_right_ref))):
                mine, others = [
                    jnp.concatenate(
                        [
                            panels[t, pl.ds(((2 * g + side) * (size // rows) + c) * (rows + 1), rows), :]
                            for c in range(first, first + 16)
                        ],
                        axis=0,
                    )
                    for g in range(2)
                ]
                lane = slice(t * LANES, (t + 1) * LANES)
                part = slice(first * rows, (first + 16) * rows)
                own_ref[part, lane] = jnp.where(first_core, mine, others).astype(BF16)
                other_ref[part, lane] = jnp.where(first_core, others, mine).astype(BF16)


def half_lanes(mask_ref, chunk):
    return lanes([mask_ref[r : r + 1].astype(F32) * 0.5 for r in chunk])


def project_kernel(per_group, by_core, *refs):
    core_ref, refs = (refs[0], refs[1:]) if by_core else (None, refs)
    inputs, refs = refs[:7], refs[7:]
    if by_core:
        outs, refs = refs[:4], refs[4:]
        both_ref = None
    else:
        both_ref, refs = refs[0], refs[1:]
    pair_t_ref, gate_t_ref, mask_ref, columns_ref, proj_t_ref, outw_t_ref = refs[:6]
    pair_ref, gain_ref, bias_ref, proj_ref, gatew_ref, outw_ref, panels, sems = refs[6:]
    held = (pair_ref, mask_ref, gain_ref, bias_ref, proj_ref, gatew_ref, outw_ref)
    copies = [pltpu.make_async_copy(src, dst, sems.at[n]) for n, (src, dst) in enumerate(zip(inputs, held))]
    for copy in copies:
        copy.start()
    for copy in copies:
        copy.wait()
    rows, tokens, channels = pair_ref.shape
    small = jnp.concatenate([ref[which] for ref in (gain_ref, bias_ref) for which in range(2)], axis=0).T
    for n in range(4):
        for side in range(2):
            place = 4 * side + n
            columns_ref[2 * n + side] = jnp.broadcast_to(small[:, place : place + 1], (channels, tokens))
    for which in range(2):
        for part in range(4):
            block = proj_ref[which, :, part * channels : (part + 1) * channels].T
            proj_t_ref[which, part * channels : (part + 1) * channels] = block if part % 2 else block * 0.5
        proj_t_ref[which, 4 * channels :] = gatew_ref[which].T * 0.5
        outw_t_ref[which] = outw_ref[which].T
    for chunk in chunks(rows, tokens, 256):
        part = span(chunk, tokens)
        pair_t = lanes([pair_ref[r].T for r in chunk])
        pair_t_ref[:, part] = pair_t
        normed = affine(unit(pair_t.astype(F32), 0), columns_ref[0], columns_ref[1], tokens)
        products = dot(proj_t_ref[0], normed, NN)
        gate_t_ref[:, part] = store_panels(
            panels, per_group, rows, chunk, tokens, products, half_lanes(mask_ref, chunk)
        )
    if by_core:
        split_panels(panels, core_ref, *outs, rows)
    else:
        pack_panels(panels, both_ref, rows)


def mix_kernel(per_group, rows, incoming, both_ref, product_ref):
    groups, _, tokens = both_ref.shape
    step = 2 * rows

    def matrices(side, pair):
        start = (side * per_group + 2 * pair) * rows
        block = both_ref[:, start : start + step, :].astype(F32)
        return [block[:, h * rows : (h + 1) * rows].reshape(groups * rows, tokens).astype(BF16) for h in range(2)]

    for pair in range(per_group // 2):
        lefts, rights = matrices(0, pair), matrices(1, pair)
        sums = [
            dot(left, right, TN if incoming else NT).reshape(groups, rows, tokens)
            for left, right in zip(lefts, rights)
        ]
        product_ref[:, pair * step : (pair + 1) * step, :] = jnp.concatenate(sums, axis=1).astype(BF16)


def ring_chips(count):
    return list(range(0, count, 2)) + list(range(count - 1, 0, -2))


def token_order(place_ref, chips, rows, tokens):
    shape = (tokens, tokens)
    lane, token = (lax.broadcasted_iota(jnp.int32, shape, axis) for axis in range(2))
    core, place = jnp.full(shape, place_ref[0]), jnp.full(shape, place_ref[1])
    device = token // rows
    chip, source_core = device // 2, device % 2
    source = jnp.where(chip % 2 == 0, chip // 2, chips - 1 - chip // 2)
    distance = (place - source + chips) % chips
    slot = 2 * distance + jnp.where(source_core == core, 0, 1)
    return jnp.where(lane == slot * rows + token % rows, 1.0, 0.0).astype(BF16)


def mix_gathered(place_ref, own_ref, got_ref, *refs):
    rights, (keep_ref, send_ref) = refs[:-2], refs[-2:]
    count, rows, tokens = own_ref.shape
    order = token_order(place_ref, len(rights) // 2, rows, tokens)
    group = 8

    def body(n, carry):
        part = pl.ds(n * group, group)
        lefts = jnp.concatenate([own_ref[part].astype(F32), got_ref[part].astype(F32)], axis=1).astype(BF16)
        blocks = [ref[part].astype(F32) for ref in rights]
        sums = []
        for c in range(group):
            right = jnp.concatenate([block[c] for block in blocks], axis=0).astype(BF16)
            sums.append(dot(lefts[c], right, NT).astype(BF16))
        sums = dot(jnp.concatenate(sums, axis=0), order, NN).reshape(group, 2 * rows, tokens)
        keep_ref[part] = sums[:, :rows].astype(BF16)
        send_ref[part] = sums[:, rows:].astype(BF16)
        return carry

    lax.fori_loop(0, count // group, body, 0)


def finish_rows(emit, rows, channels, tokens, load, pair_t_ref, gate_t_ref, gain, bias, outw_t, unit_scratch):
    tiles = range(tokens // LANES)
    parts = [slice(first * rows, (first + 16) * rows) for first in range(0, channels, 16)]

    def sums(part):
        return load(part).reshape(16, rows, tokens)

    average = sum(jnp.sum(sums(part), axis=0) for part in parts) * (1.0 / channels)
    spread = sum(jnp.sum(jnp.square(sums(part) - average), axis=0) for part in parts) * (1.0 / channels)
    inverse = lax.rsqrt(spread + 1e-05)
    for part in parts:
        units = (sums(part) - average) * inverse
        for t in tiles:
            for n in range(16):
                where = pl.ds((part.start // rows + n) * (rows + 1), rows)
                unit_scratch[t, where, :] = units[n, :, t * LANES : (t + 1) * LANES]
    for chunk in chunks(rows, tokens, 256):
        part = span(chunk, tokens)
        units = lanes([unit_scratch[t, pl.ds(r, channels, stride=rows + 1), :] for r in chunk for t in tiles])
        normed = affine(units, gain, bias, tokens)
        change = gate_t_ref[:, part].astype(F32) * dot(outw_t, normed, NN)
        emit(chunk, part, (pair_t_ref[:, part].astype(F32) + change).astype(BF16))


def step_kernel(per_group, by_core, *refs):
    if not by_core:
        merged_ref, refs = refs[0], refs[1:]
        return step_rows(per_group, lambda part: merged_ref[part].astype(F32), *refs)
    core_ref, keep_ref, got_ref, refs = refs[0], refs[1], refs[2], refs[3:]
    size = keep_ref.shape[0]

    def load(part):
        late = part.start >= size
        part = slice(part.start - size, part.stop - size) if late else part
        keep, got = keep_ref[part].astype(F32), got_ref[part].astype(F32)
        return jnp.where(jnp.full(keep.shape, core_ref[0]) == int(late), keep, got)

    step_rows(per_group, load, *refs)


def step_rows(
    per_group, load, pair_t_ref, gate_t_ref, mask_ref, columns_ref, outw_t_ref, proj_t_ref,
    both_ref, middle_t_ref, gate1_t_ref, unit_scratch, panels,
):
    rows, tokens = mask_ref.shape

    def emit(chunk, part, middle):
        middle_t_ref[:, part] = middle
        normed = affine(unit(middle.astype(F32), 0), columns_ref[4], columns_ref[5], tokens)
        products = dot(proj_t_ref[1], normed, NN)
        gate1_t_ref[:, part] = store_panels(
            panels, per_group, rows, chunk, tokens, products, half_lanes(mask_ref, chunk)
        )

    finish_rows(
        emit, rows, pair_t_ref.shape[0], tokens, load, pair_t_ref, gate_t_ref, columns_ref[2], columns_ref[3],
        outw_t_ref[0], unit_scratch,
    )
    pack_panels(panels, both_ref, rows)


def finish_kernel(
    merged_ref, middle_t_ref, gate_t_ref, columns_ref, outw_t_ref, result_ref, unit_scratch, done, sems
):
    rows, tokens, _ = result_ref.shape
    copies = []

    def emit(chunk, part, result):
        for h, r in enumerate(chunk):
            done[r] = result[:, h * tokens : (h + 1) * tokens].T
            copies.append(pltpu.make_async_copy(done.at[r], result_ref.at[r], sems.at[r]))
            copies[-1].start()

    finish_rows(
        emit, rows, middle_t_ref.shape[0], tokens, lambda part: merged_ref[part].astype(F32), middle_t_ref, gate_t_ref,
        columns_ref[6], columns_ref[7], outw_t_ref[1], unit_scratch,
    )
    for copy in copies:
        copy.wait()


def on_device(*inputs):
    groups = lax.axis_size("row")
    rows, tokens, channels = inputs[0].shape
    per_group = channels // groups
    whole = pl.BlockSpec(memory_space=pltpu.VMEM)
    hbm = pl.BlockSpec(memory_space=pltpu.HBM)
    params = pltpu.CompilerParams(vmem_limit_bytes=48 * 1024 * 1024)
    shape = jax.ShapeDtypeStruct
    both_shape = shape((2 * channels * rows, tokens), BF16)
    flat_shape = shape((channels, rows * tokens), BF16)
    panels = pltpu.VMEM((tokens // LANES, 2 * channels * (rows + 1), LANES), F32)
    unit_scratch = pltpu.VMEM((tokens // LANES, channels * (rows + 1), LANES), F32)

    def exchange(array):
        return lax.all_to_all(array, "row", split_axis=0, concat_axis=0, tiled=True)

    def mix(both, incoming):
        product = pl.pallas_call(
            functools.partial(mix_kernel, per_group, rows, incoming),
            out_shape=shape((groups, per_group * rows, tokens), BF16),
            in_specs=[whole],
            out_specs=whole,
            compiler_params=params,
            name="mix",
        )(both.reshape(groups, 2 * per_group * rows, tokens))
        return product.reshape(channels * rows, tokens)

    half = channels // 2
    by_core = groups % 4 == 0 and groups * rows * tokens * half * 2 <= 4 * 2**20
    smem = pl.BlockSpec(memory_space=pltpu.SMEM)
    core = (lax.axis_index("row") % 2).astype(jnp.int32).reshape(1)
    half_shape = shape((half * rows, tokens), BF16)
    projected = (half_shape,) * 4 if by_core else (both_shape,)
    results = pl.pallas_call(
        functools.partial(project_kernel, half if by_core else per_group, by_core),
        out_shape=projected
        + (
            flat_shape,
            flat_shape,
            shape((rows, tokens), inputs[1].dtype),
            shape((8, channels, tokens), F32),
            shape((2, 5 * channels, channels), BF16),
            shape((2, channels, channels), BF16),
        ),
        in_specs=[smem] * by_core + [hbm] * 7,
        out_specs=(whole,) * (len(projected) + 6),
        scratch_shapes=[pltpu.VMEM(inputs[n].shape, inputs[n].dtype) for n in (0, 2, 3, 4, 5, 6)]
        + [panels, pltpu.SemaphoreType.DMA((7,))],
        compiler_params=params,
        name="project",
    )(*[core] * by_core, *(pltpu.with_memory_space_constraint(a, pltpu.HBM) for a in inputs))
    pair_t, gate_t, mask, columns, proj_t, outw_t = results[-6:]
    if by_core:
        left, right, other_left, other_right = results[:4]
        chips = groups // 2
        ring = ring_chips(chips)

        def along(array, step):
            pairs = [(2 * q + c, 2 * ring[(p + step) % chips] + c) for p, q in enumerate(ring) for c in range(2)]
            return lax.ppermute(array, "row", pairs)

        def rounds(array, step, count):
            arrays = [array]
            for _ in range(count):
                arrays.append(along(arrays[-1], step))
            return arrays

        swap = [(d, d ^ 1) for d in range(groups)]
        got_right = lax.ppermute(other_right, "row", swap)
        got_left = lax.ppermute(other_left, "row", swap)
        middle = chips // 2
        ups = [rounds(right, 1, middle), rounds(got_right, 1, middle - 1)]
        downs = [rounds(right, -1, middle - 1), rounds(got_right, -1, middle)]
        rights = [
            ups[piece][distance] if distance < len(ups[piece]) else downs[piece][chips - distance]
            for distance in range(chips)
            for piece in range(2)
        ]
        chip = lax.axis_index("row") // 2
        place = jnp.where(chip % 2 == 0, chip // 2, chips - 1 - chip // 2).astype(jnp.int32)
        keep, send = pl.pallas_call(
            mix_gathered,
            out_shape=(shape((half, rows, tokens), BF16),) * 2,
            in_specs=[smem] + [whole] * (2 + len(rights)),
            out_specs=(whole,) * 2,
            compiler_params=params,
            name="mix_gathered",
        )(
            jnp.concatenate([core, place.reshape(1)]),
            *(array.reshape(half, rows, tokens) for array in (left, got_left, *rights)),
        )
        merged = (core, keep.reshape(half * rows, tokens), lax.ppermute(send, "row", swap).reshape(half * rows, tokens))
    else:
        merged = (exchange(mix(exchange(results[0]), False)),)
    both, middle_t, gate_t = pl.pallas_call(
        functools.partial(step_kernel, per_group, by_core),
        out_shape=(both_shape, flat_shape, flat_shape),
        in_specs=[smem] * by_core + [whole] * (len(merged) - by_core + 6),
        out_specs=(whole,) * 3,
        scratch_shapes=[unit_scratch, panels],
        compiler_params=params,
        name="finish_project",
    )(*merged, pair_t, gate_t, mask, columns, outw_t, proj_t)
    merged = exchange(mix(exchange(both), True))
    return pl.pallas_call(
        finish_kernel,
        out_shape=shape((rows, tokens, channels), BF16),
        in_specs=[whole] * 5,
        out_specs=hbm,
        scratch_shapes=[unit_scratch, pltpu.VMEM((rows, tokens, channels), BF16), pltpu.SemaphoreType.DMA((rows,))],
        compiler_params=params,
        name="finish",
    )(merged, middle_t, gate_t, columns, outw_t)


def solution(mesh):
    rows = ("groups", "row")
    return jax.shard_map(
        on_device,
        mesh=mesh,
        in_specs=(P(rows, None, None), P(rows, None), P(), P(), P(), P(), P()),
        out_specs=P(rows, None, None),
        check_vma=False,
    )
```

```python
import functools

import jax
import jax.numpy as jnp
from jax import lax
from jax.experimental import pallas as pl
from jax.experimental.pallas import tpu as pltpu
from jax.sharding import PartitionSpec as P

F32 = jnp.float32
BF16 = jnp.bfloat16
LANES = 128
NT = (((1,), (1,)), ((), ()))
NN = (((1,), (0,)), ((), ()))
TN = (((0,), (0,)), ((), ()))


def dot(a, b, dims):
    return lax.dot_general(a, b, dims, preferred_element_type=F32)


def unit(values, axis):
    scale = 1.0 / values.shape[axis]
    centred = values - jnp.sum(values, axis=axis, keepdims=True) * scale
    spread = jnp.sum(centred * centred, axis=axis, keepdims=True) * scale
    return centred * lax.rsqrt(spread + 1e-05)


def chunks(rows, tokens, limit):
    wide = max(1, min(rows, limit // tokens))
    return [list(range(start, min(start + wide, rows))) for start in range(0, rows, wide)]


def span(chunk, tokens):
    return slice(chunk[0] * tokens, (chunk[-1] + 1) * tokens)


def lanes(parts):
    return parts[0] if len(parts) == 1 else jnp.concatenate(parts, axis=1)


def affine(values, gain, bias, tokens):
    parts = [values[:, n : n + tokens] * gain + bias for n in range(0, values.shape[1], tokens)]
    return lanes(parts).astype(BF16)


def store_panels(panels, per_group, rows, chunk, tokens, products, half_mask):
    channels = products.shape[0] // 5
    for side in range(2):
        base = 2 * side * channels
        gate, value = products[base : base + channels], products[base + channels : base + 2 * channels]
        gated = (jnp.tanh(gate) + 1.0) * (value * half_mask)
        for h, r in enumerate(chunk):
            for g in range(channels // per_group):
                where = pl.ds((2 * g + side) * per_group * rows + r, per_group, stride=rows)
                for t in range(tokens // LANES):
                    first = h * tokens + t * LANES
                    panels[t, where, :] = gated[g * per_group : (g + 1) * per_group, first : first + LANES]
    return (0.5 * jnp.tanh(products[4 * channels :]) + 0.5).astype(BF16)


def pack_panels(panels, both_ref):
    for t in range(both_ref.shape[1] // LANES):
        both_ref[:, t * LANES : (t + 1) * LANES] = panels[t].astype(BF16)


def split_panels(panels, core_ref, left_ref, right_ref, other_left_ref, other_right_ref):
    size = left_ref.shape[0]
    core = core_ref[0]
    for t in range(left_ref.shape[1] // LANES):
        for side, (own_ref, other_ref) in enumerate(((left_ref, other_left_ref), (right_ref, other_right_ref))):
            for group, ref in ((core, own_ref), (1 - core, other_ref)):
                start = pl.multiple_of((2 * group + side) * size, size)
                ref[:, t * LANES : (t + 1) * LANES] = panels[t, pl.ds(start, size), :].astype(BF16)


def half_lanes(mask_ref, chunk):
    return lanes([mask_ref[r : r + 1].astype(F32) * 0.5 for r in chunk])


def project_kernel(per_group, by_core, *refs):
    core_ref, refs = (refs[0], refs[1:]) if by_core else (None, refs)
    inputs, refs = refs[:7], refs[7:]
    if by_core:
        outs, refs = refs[:4], refs[4:]
        both_ref = None
    else:
        both_ref, refs = refs[0], refs[1:]
    pair_t_ref, gate_t_ref, mask_ref, columns_ref, proj_t_ref, outw_t_ref = refs[:6]
    pair_ref, gain_ref, bias_ref, proj_ref, gatew_ref, outw_ref, panels, sems = refs[6:]
    held = (pair_ref, mask_ref, gain_ref, bias_ref, proj_ref, gatew_ref, outw_ref)
    copies = [pltpu.make_async_copy(src, dst, sems.at[n]) for n, (src, dst) in enumerate(zip(inputs, held))]
    for copy in copies:
        copy.start()
    for copy in copies:
        copy.wait()
    rows, tokens, channels = pair_ref.shape
    small = jnp.concatenate([ref[which] for ref in (gain_ref, bias_ref) for which in range(2)], axis=0).T
    for n in range(4):
        for side in range(2):
            place = 4 * side + n
            columns_ref[2 * n + side] = jnp.broadcast_to(small[:, place : place + 1], (channels, tokens))
    for which in range(2):
        for part in range(4):
            block = proj_ref[which, :, part * channels : (part + 1) * channels].T
            proj_t_ref[which, part * channels : (part + 1) * channels] = block if part % 2 else block * 0.5
        proj_t_ref[which, 4 * channels :] = gatew_ref[which].T * 0.5
        outw_t_ref[which] = outw_ref[which].T
    for chunk in chunks(rows, tokens, 256):
        part = span(chunk, tokens)
        pair_t = lanes([pair_ref[r].T for r in chunk])
        pair_t_ref[:, part] = pair_t
        normed = affine(unit(pair_t.astype(F32), 0), columns_ref[0], columns_ref[1], tokens)
        products = dot(proj_t_ref[0], normed, NN)
        gate_t_ref[:, part] = store_panels(
            panels, per_group, rows, chunk, tokens, products, half_lanes(mask_ref, chunk)
        )
    if by_core:
        split_panels(panels, core_ref, *outs)
    else:
        pack_panels(panels, both_ref)


def mix_kernel(per_group, rows, incoming, both_ref, product_ref):
    groups, _, tokens = both_ref.shape
    step = 2 * rows

    def matrices(side, pair):
        start = (side * per_group + 2 * pair) * rows
        block = both_ref[:, start : start + step, :].astype(F32)
        return [block[:, h * rows : (h + 1) * rows].reshape(groups * rows, tokens).astype(BF16) for h in range(2)]

    for pair in range(per_group // 2):
        lefts, rights = matrices(0, pair), matrices(1, pair)
        sums = [
            dot(left, right, TN if incoming else NT).reshape(groups, rows, tokens)
            for left, right in zip(lefts, rights)
        ]
        product_ref[:, pair * step : (pair + 1) * step, :] = jnp.concatenate(sums, axis=1).astype(BF16)


def ring_chips(count):
    return list(range(0, count, 2)) + list(range(count - 1, 0, -2))


def token_order(place_ref, distances, rows, tokens):
    chips = len(distances)
    shape = (tokens, tokens)
    lane, token = (lax.broadcasted_iota(jnp.int32, shape, axis) for axis in range(2))
    core, place = jnp.full(shape, place_ref[0]), jnp.full(shape, place_ref[1])
    device = token // rows
    chip, source_core = device // 2, device % 2
    source = jnp.where(chip % 2 == 0, chip // 2, chips - 1 - chip // 2)
    distance = (place - source + chips) % chips
    place_of = sum(jnp.where(distance == d, n, 0) for n, d in enumerate(distances))
    slot = 2 * place_of + jnp.where(source_core == core, 0, 1)
    return jnp.where(lane == slot * rows + token % rows, 1.0, 0.0).astype(BF16)


def gathered_sums(own_ref, got_ref, rights, first_lane, c):
    _, rows, tokens = own_ref.shape
    left = jnp.concatenate([own_ref[c].astype(F32), got_ref[c].astype(F32)], axis=0).astype(BF16)
    blocks = [ref[c].astype(F32) for ref in rights]
    last = first_lane + len(blocks) * rows
    empty = [jnp.zeros((n, tokens), F32) for n in (first_lane, tokens - last)]
    blocks = [block for block in (empty[0], *blocks, empty[1]) if block.shape[0]]
    return dot(left, jnp.concatenate(blocks, axis=0).astype(BF16), NT)


def mix_early(own_ref, got_ref, *refs):
    rights, early_ref = refs[:-1], refs[-1]
    for c in range(own_ref.shape[0]):
        early_ref[c] = gathered_sums(own_ref, got_ref, rights, 0, c).astype(BF16)


def mix_late(distances, early, place_ref, own_ref, got_ref, early_ref, *refs):
    rights, (keep_ref, send_ref) = refs[:-2], refs[-2:]
    count, rows, tokens = own_ref.shape
    order = token_order(place_ref, distances, rows, tokens)
    group = 8
    for first in range(0, count, group):
        sums = [
            (gathered_sums(own_ref, got_ref, rights, early * rows, c) + early_ref[c].astype(F32)).astype(BF16)
            for c in range(first, first + group)
        ]
        sums = dot(jnp.concatenate(sums, axis=0), order, NN).reshape(group, 2 * rows, tokens)
        keep_ref[first : first + group] = sums[:, :rows].astype(BF16)
        send_ref[first : first + group] = sums[:, rows:].astype(BF16)


def finish_rows(emit, rows, channels, tokens, load, pair_t_ref, gate_t_ref, gain, bias, outw_t, unit_scratch):
    tiles = range(tokens // LANES)
    parts = [slice(first * rows, (first + 16) * rows) for first in range(0, channels, 16)]

    def sums(part):
        return load(part).reshape(16, rows, tokens)

    average = sum(jnp.sum(sums(part), axis=0) for part in parts) * (1.0 / channels)
    spread = sum(jnp.sum(jnp.square(sums(part) - average), axis=0) for part in parts) * (1.0 / channels)
    inverse = lax.rsqrt(spread + 1e-05)
    for part in parts:
        units = ((sums(part) - average) * inverse).reshape(16 * rows, tokens)
        for t in tiles:
            unit_scratch[t, part, :] = units[:, t * LANES : (t + 1) * LANES]
    for chunk in chunks(rows, tokens, 256):
        part = span(chunk, tokens)
        units = lanes([unit_scratch[t, pl.ds(r, channels, stride=rows), :] for r in chunk for t in tiles])
        normed = affine(units, gain, bias, tokens)
        change = gate_t_ref[:, part].astype(F32) * dot(outw_t, normed, NN)
        emit(chunk, part, (pair_t_ref[:, part].astype(F32) + change).astype(BF16))


def step_kernel(per_group, by_core, *refs):
    if not by_core:
        merged_ref, refs = refs[0], refs[1:]
        return step_rows(per_group, lambda part: merged_ref[part].astype(F32), *refs)
    core_ref, keep_ref, got_ref, refs = refs[0], refs[1], refs[2], refs[3:]
    size = keep_ref.shape[0]

    def load(part):
        late = part.start >= size
        part = slice(part.start - size, part.stop - size) if late else part
        keep, got = keep_ref[part].astype(F32), got_ref[part].astype(F32)
        return jnp.where(jnp.full(keep.shape, core_ref[0]) == int(late), keep, got)

    step_rows(per_group, load, *refs)


def step_rows(
    per_group, load, pair_t_ref, gate_t_ref, mask_ref, columns_ref, outw_t_ref, proj_t_ref,
    both_ref, middle_t_ref, gate1_t_ref, unit_scratch, panels,
):
    rows, tokens = mask_ref.shape

    def emit(chunk, part, middle):
        middle_t_ref[:, part] = middle
        normed = affine(unit(middle.astype(F32), 0), columns_ref[4], columns_ref[5], tokens)
        products = dot(proj_t_ref[1], normed, NN)
        gate1_t_ref[:, part] = store_panels(
            panels, per_group, rows, chunk, tokens, products, half_lanes(mask_ref, chunk)
        )

    finish_rows(
        emit, rows, pair_t_ref.shape[0], tokens, load, pair_t_ref, gate_t_ref, columns_ref[2], columns_ref[3],
        outw_t_ref[0], unit_scratch,
    )
    pack_panels(panels, both_ref)


def finish_kernel(
    merged_ref, middle_t_ref, gate_t_ref, columns_ref, outw_t_ref, result_ref, unit_scratch, done, sems
):
    rows, tokens, _ = result_ref.shape
    copies = []

    def emit(chunk, part, result):
        for h, r in enumerate(chunk):
            done[r] = result[:, h * tokens : (h + 1) * tokens].T
            copies.append(pltpu.make_async_copy(done.at[r], result_ref.at[r], sems.at[r]))
            copies[-1].start()

    finish_rows(
        emit, rows, middle_t_ref.shape[0], tokens, lambda part: merged_ref[part].astype(F32), middle_t_ref, gate_t_ref,
        columns_ref[6], columns_ref[7], outw_t_ref[1], unit_scratch,
    )
    for copy in copies:
        copy.wait()


def on_device(*inputs):
    groups = lax.axis_size("row")
    rows, tokens, channels = inputs[0].shape
    per_group = channels // groups
    whole = pl.BlockSpec(memory_space=pltpu.VMEM)
    hbm = pl.BlockSpec(memory_space=pltpu.HBM)
    params = pltpu.CompilerParams(vmem_limit_bytes=48 * 1024 * 1024)
    shape = jax.ShapeDtypeStruct
    both_shape = shape((2 * channels * rows, tokens), BF16)
    flat_shape = shape((channels, rows * tokens), BF16)
    panels = pltpu.VMEM((tokens // LANES, 2 * channels * rows, LANES), F32)
    unit_scratch = pltpu.VMEM((tokens // LANES, channels * rows, LANES), F32)

    def exchange(array):
        return lax.all_to_all(array, "row", split_axis=0, concat_axis=0, tiled=True)

    def mix(both, incoming):
        product = pl.pallas_call(
            functools.partial(mix_kernel, per_group, rows, incoming),
            out_shape=shape((groups, per_group * rows, tokens), BF16),
            in_specs=[whole],
            out_specs=whole,
            compiler_params=params,
            name="mix",
        )(both.reshape(groups, 2 * per_group * rows, tokens))
        return product.reshape(channels * rows, tokens)

    half = channels // 2
    by_core = groups % 4 == 0 and groups * rows * tokens * half * 2 <= 4 * 2**20
    smem = pl.BlockSpec(memory_space=pltpu.SMEM)
    core = (lax.axis_index("row") % 2).astype(jnp.int32).reshape(1)
    half_shape = shape((half * rows, tokens), BF16)
    projected = (half_shape,) * 4 if by_core else (both_shape,)
    results = pl.pallas_call(
        functools.partial(project_kernel, half if by_core else per_group, by_core),
        out_shape=projected
        + (
            flat_shape,
            flat_shape,
            shape((rows, tokens), inputs[1].dtype),
            shape((8, channels, tokens), F32),
            shape((2, 5 * channels, channels), BF16),
            shape((2, channels, channels), BF16),
        ),
        in_specs=[smem] * by_core + [hbm] * 7,
        out_specs=(whole,) * (len(projected) + 6),
        scratch_shapes=[pltpu.VMEM(inputs[n].shape, inputs[n].dtype) for n in (0, 2, 3, 4, 5, 6)]
        + [panels, pltpu.SemaphoreType.DMA((7,))],
        compiler_params=params,
        name="project",
    )(*[core] * by_core, *(pltpu.with_memory_space_constraint(a, pltpu.HBM) for a in inputs))
    pair_t, gate_t, mask, columns, proj_t, outw_t = results[-6:]
    if by_core:
        left, right, other_left, other_right = results[:4]
        chips = groups // 2
        ring = ring_chips(chips)

        def along(array, step):
            pairs = [(2 * q + c, 2 * ring[(p + step) % chips] + c) for p, q in enumerate(ring) for c in range(2)]
            return lax.ppermute(array, "row", pairs)

        def rounds(array, step, count):
            arrays = [array]
            for _ in range(count):
                arrays.append(along(arrays[-1], step))
            return arrays

        swap = [(d, d ^ 1) for d in range(groups)]
        got_right = lax.ppermute(other_right, "row", swap)
        got_left = lax.ppermute(other_left, "row", swap)
        middle = chips // 2
        ups = [rounds(right, 1, middle), rounds(got_right, 1, middle - 1)]
        downs = [rounds(right, -1, middle - 1), rounds(got_right, -1, middle)]
        distances = sorted(range(chips), key=lambda d: min(d, chips - d))
        early = 2 * (chips // 2 + 1)
        rights = [
            ups[piece][d] if d < len(ups[piece]) else downs[piece][chips - d] for d in distances for piece in range(2)
        ]
        rights = [array.reshape(half, rows, tokens) for array in rights]
        lefts = [array.reshape(half, rows, tokens) for array in (left, got_left)]
        chip = lax.axis_index("row") // 2
        place = jnp.where(chip % 2 == 0, chip // 2, chips - 1 - chip // 2).astype(jnp.int32)
        first_sums = pl.pallas_call(
            mix_early,
            out_shape=shape((half, 2 * rows, tokens), BF16),
            in_specs=[whole] * (2 + early),
            out_specs=whole,
            compiler_params=params,
            cost_estimate=pl.CostEstimate(flops=10**9, bytes_accessed=4 * 2**20, transcendentals=0),
            name="mix_early",
        )(*lefts, *rights[:early])
        keep, send = pl.pallas_call(
            functools.partial(mix_late, distances, early),
            out_shape=(shape((half, rows, tokens), BF16),) * 2,
            in_specs=[smem] + [whole] * (3 + len(rights) - early),
            out_specs=(whole,) * 2,
            compiler_params=params,
            name="mix_late",
        )(jnp.concatenate([core, place.reshape(1)]), *lefts, first_sums, *rights[early:])
        merged = (core, keep.reshape(half * rows, tokens), lax.ppermute(send, "row", swap).reshape(half * rows, tokens))
    else:
        merged = (exchange(mix(exchange(results[0]), False)),)
    both, middle_t, gate_t = pl.pallas_call(
        functools.partial(step_kernel, per_group, by_core),
        out_shape=(both_shape, flat_shape, flat_shape),
        in_specs=[smem] * by_core + [whole] * (len(merged) - by_core + 6),
        out_specs=(whole,) * 3,
        scratch_shapes=[unit_scratch, panels],
        compiler_params=params,
        name="finish_project",
    )(*merged, pair_t, gate_t, mask, columns, outw_t, proj_t)
    merged = exchange(mix(exchange(both), True))
    return pl.pallas_call(
        finish_kernel,
        out_shape=shape((rows, tokens, channels), BF16),
        in_specs=[whole] * 5,
        out_specs=hbm,
        scratch_shapes=[unit_scratch, pltpu.VMEM((rows, tokens, channels), BF16), pltpu.SemaphoreType.DMA((rows,))],
        compiler_params=params,
        name="finish",
    )(merged, middle_t, gate_t, columns, outw_t)


def solution(mesh):
    rows = ("groups", "row")
    return jax.shard_map(
        on_device,
        mesh=mesh,
        in_specs=(P(rows, None, None), P(rows, None), P(), P(), P(), P(), P()),
        out_specs=P(rows, None, None),
        check_vma=False,
    )
```

```python
import functools

import jax
import jax.numpy as jnp
from jax import lax
from jax.experimental import pallas as pl
from jax.experimental.pallas import tpu as pltpu
from jax.sharding import PartitionSpec as P

F32 = jnp.float32
BF16 = jnp.bfloat16
LANES = 128
NT = (((1,), (1,)), ((), ()))
NN = (((1,), (0,)), ((), ()))
TN = (((0,), (0,)), ((), ()))


def dot(a, b, dims):
    return lax.dot_general(a, b, dims, preferred_element_type=F32)


def unit(values, axis):
    scale = 1.0 / values.shape[axis]
    centred = values - jnp.sum(values, axis=axis, keepdims=True) * scale
    spread = jnp.sum(centred * centred, axis=axis, keepdims=True) * scale
    return centred * lax.rsqrt(spread + 1e-05)


def chunks(rows, tokens, limit):
    wide = max(1, min(rows, limit // tokens))
    return [list(range(start, min(start + wide, rows))) for start in range(0, rows, wide)]


def span(chunk, tokens):
    return slice(chunk[0] * tokens, (chunk[-1] + 1) * tokens)


def lanes(parts):
    return parts[0] if len(parts) == 1 else jnp.concatenate(parts, axis=1)


def affine(values, gain, bias, tokens):
    parts = [values[:, n : n + tokens] * gain + bias for n in range(0, values.shape[1], tokens)]
    return lanes(parts).astype(BF16)


def store_panels(panels, per_group, rows, chunk, tokens, products, half_mask):
    channels = products.shape[0] // 5
    for side in range(2):
        base = 2 * side * channels
        gate, value = products[base : base + channels], products[base + channels : base + 2 * channels]
        gated = (jnp.tanh(gate) + 1.0) * (value * half_mask)
        for h, r in enumerate(chunk):
            for g in range(channels // per_group):
                where = pl.ds((2 * g + side) * per_group * rows + r, per_group, stride=rows)
                for t in range(tokens // LANES):
                    first = h * tokens + t * LANES
                    panels[t, where, :] = gated[g * per_group : (g + 1) * per_group, first : first + LANES]
    return (0.5 * jnp.tanh(products[4 * channels :]) + 0.5).astype(BF16)


def pack_panels(panels, both_ref):
    for t in range(both_ref.shape[1] // LANES):
        both_ref[:, t * LANES : (t + 1) * LANES] = panels[t].astype(BF16)


def split_panels(panels, core_ref, left_ref, right_ref, other_left_ref, other_right_ref):
    size = left_ref.shape[0]
    core = core_ref[0]
    for t in range(left_ref.shape[1] // LANES):
        for side, (own_ref, other_ref) in enumerate(((left_ref, other_left_ref), (right_ref, other_right_ref))):
            for group, ref in ((core, own_ref), (1 - core, other_ref)):
                start = pl.multiple_of((2 * group + side) * size, size)
                ref[:, t * LANES : (t + 1) * LANES] = panels[t, pl.ds(start, size), :].astype(BF16)


def half_lanes(mask_ref, chunk):
    return lanes([mask_ref[r : r + 1].astype(F32) * 0.5 for r in chunk])


def project_kernel(per_group, by_core, *refs):
    core_ref, refs = (refs[0], refs[1:]) if by_core else (None, refs)
    inputs, refs = refs[:7], refs[7:]
    if by_core:
        outs, refs = refs[:4], refs[4:]
        both_ref = None
    else:
        both_ref, refs = refs[0], refs[1:]
    pair_t_ref, gate_t_ref, mask_ref, columns_ref, proj_t_ref, outw_t_ref = refs[:6]
    pair_ref, gain_ref, bias_ref, proj_ref, gatew_ref, outw_ref, panels, sems = refs[6:]
    held = (pair_ref, mask_ref, gain_ref, bias_ref, proj_ref, gatew_ref, outw_ref)
    copies = [pltpu.make_async_copy(src, dst, sems.at[n]) for n, (src, dst) in enumerate(zip(inputs, held))]
    for copy in copies:
        copy.start()
    for copy in copies:
        copy.wait()
    rows, tokens, channels = pair_ref.shape
    small = jnp.concatenate([ref[which] for ref in (gain_ref, bias_ref) for which in range(2)], axis=0).T
    for n in range(4):
        for side in range(2):
            place = 4 * side + n
            columns_ref[2 * n + side] = jnp.broadcast_to(small[:, place : place + 1], (channels, tokens))
    for which in range(2):
        for part in range(4):
            block = proj_ref[which, :, part * channels : (part + 1) * channels].T
            proj_t_ref[which, part * channels : (part + 1) * channels] = block if part % 2 else block * 0.5
        proj_t_ref[which, 4 * channels :] = gatew_ref[which].T * 0.5
        outw_t_ref[which] = outw_ref[which].T
    for chunk in chunks(rows, tokens, 256):
        part = span(chunk, tokens)
        pair_t = lanes([pair_ref[r].T for r in chunk])
        pair_t_ref[:, part] = pair_t
        normed = affine(unit(pair_t.astype(F32), 0), columns_ref[0], columns_ref[1], tokens)
        products = dot(proj_t_ref[0], normed, NN)
        gate_t_ref[:, part] = store_panels(
            panels, per_group, rows, chunk, tokens, products, half_lanes(mask_ref, chunk)
        )
    if by_core:
        split_panels(panels, core_ref, *outs)
    else:
        pack_panels(panels, both_ref)


def mix_kernel(per_group, rows, incoming, both_ref, product_ref):
    groups, _, tokens = both_ref.shape
    step = 2 * rows

    def matrices(side, pair):
        start = (side * per_group + 2 * pair) * rows
        block = both_ref[:, start : start + step, :].astype(F32)
        return [block[:, h * rows : (h + 1) * rows].reshape(groups * rows, tokens).astype(BF16) for h in range(2)]

    for pair in range(per_group // 2):
        lefts, rights = matrices(0, pair), matrices(1, pair)
        sums = [
            dot(left, right, TN if incoming else NT).reshape(groups, rows, tokens)
            for left, right in zip(lefts, rights)
        ]
        product_ref[:, pair * step : (pair + 1) * step, :] = jnp.concatenate(sums, axis=1).astype(BF16)


def ring_chips(count):
    return list(range(0, count, 2)) + list(range(count - 1, 0, -2))


def token_order(chips, distances, rows):
    device = lax.axis_index("row")
    chip, core = device // 2, device % 2
    place = jnp.where(chip % 2 == 0, chip // 2, chips - 1 - chip // 2)
    size = 2 * chips * rows
    lane, token = (lax.broadcasted_iota(jnp.int32, (size, size), axis) for axis in range(2))
    first = jnp.zeros((size, size), jnp.int32)
    for n, d in enumerate(distances):
        source = place - d + jnp.where(place < d, chips, 0)
        source = jnp.where(2 * source < chips, 2 * source, 2 * (chips - 1 - source) + 1)
        for piece in range(2):
            start = (2 * n + piece) * rows
            block = 2 * source + (1 - core if piece else core)
            first = jnp.where((lane >= start) & (lane < start + rows), block * rows - start, first)
    return (token == lane + first).astype(BF16)


def gathered_sums(own_ref, got_ref, rights, first_lane, c):
    _, rows, tokens = own_ref.shape
    left = jnp.concatenate([own_ref[c].astype(F32), got_ref[c].astype(F32)], axis=0).astype(BF16)
    blocks = [ref[c].astype(F32) for ref in rights]
    last = first_lane + len(blocks) * rows
    empty = [jnp.zeros((n, tokens), F32) for n in (first_lane, tokens - last)]
    blocks = [block for block in (empty[0], *blocks, empty[1]) if block.shape[0]]
    return dot(left, jnp.concatenate(blocks, axis=0).astype(BF16), NT)


def mix_early(own_ref, got_ref, *refs):
    rights, early_ref = refs[:-1], refs[-1]
    for c in range(own_ref.shape[0]):
        early_ref[c] = gathered_sums(own_ref, got_ref, rights, 0, c).astype(BF16)


def mix_late(early, order_ref, own_ref, got_ref, early_ref, *refs):
    rights, (keep_ref, send_ref) = refs[:-2], refs[-2:]
    count, rows, tokens = own_ref.shape
    order = order_ref[...]
    group = 8
    for first in range(0, count, group):
        sums = [
            (gathered_sums(own_ref, got_ref, rights, early * rows, c) + early_ref[c].astype(F32)).astype(BF16)
            for c in range(first, first + group)
        ]
        sums = dot(jnp.concatenate(sums, axis=0), order, NN).reshape(group, 2 * rows, tokens)
        keep_ref[first : first + group] = sums[:, :rows].astype(BF16)
        send_ref[first : first + group] = sums[:, rows:].astype(BF16)


def finish_rows(emit, rows, channels, tokens, load, pair_t_ref, gate_t_ref, gain, bias, outw_t, unit_scratch):
    tiles = range(tokens // LANES)
    parts = [slice(first * rows, (first + 16) * rows) for first in range(0, channels, 16)]

    def sums(part):
        return load(part).reshape(16, rows, tokens)

    average = sum(jnp.sum(sums(part), axis=0) for part in parts) * (1.0 / channels)
    spread = sum(jnp.sum(jnp.square(sums(part) - average), axis=0) for part in parts) * (1.0 / channels)
    inverse = lax.rsqrt(spread + 1e-05)
    for part in parts:
        units = ((sums(part) - average) * inverse).reshape(16 * rows, tokens)
        for t in tiles:
            unit_scratch[t, part, :] = units[:, t * LANES : (t + 1) * LANES]
    for chunk in chunks(rows, tokens, 256):
        part = span(chunk, tokens)
        units = lanes([unit_scratch[t, pl.ds(r, channels, stride=rows), :] for r in chunk for t in tiles])
        normed = affine(units, gain, bias, tokens)
        change = gate_t_ref[:, part].astype(F32) * dot(outw_t, normed, NN)
        emit(chunk, part, (pair_t_ref[:, part].astype(F32) + change).astype(BF16))


def step_kernel(per_group, by_core, *refs):
    if not by_core:
        merged_ref, refs = refs[0], refs[1:]
        return step_rows(per_group, lambda part: merged_ref[part].astype(F32), *refs)
    core_ref, keep_ref, got_ref, refs = refs[0], refs[1], refs[2], refs[3:]
    size = keep_ref.shape[0]

    def load(part):
        late = part.start >= size
        part = slice(part.start - size, part.stop - size) if late else part
        keep, got = keep_ref[part].astype(F32), got_ref[part].astype(F32)
        return jnp.where(jnp.full(keep.shape, core_ref[0]) == int(late), keep, got)

    step_rows(per_group, load, *refs)


def step_rows(
    per_group, load, pair_t_ref, gate_t_ref, mask_ref, columns_ref, outw_t_ref, proj_t_ref,
    both_ref, middle_t_ref, gate1_t_ref, unit_scratch, panels,
):
    rows, tokens = mask_ref.shape

    def emit(chunk, part, middle):
        middle_t_ref[:, part] = middle
        normed = affine(unit(middle.astype(F32), 0), columns_ref[4], columns_ref[5], tokens)
        products = dot(proj_t_ref[1], normed, NN)
        gate1_t_ref[:, part] = store_panels(
            panels, per_group, rows, chunk, tokens, products, half_lanes(mask_ref, chunk)
        )

    finish_rows(
        emit, rows, pair_t_ref.shape[0], tokens, load, pair_t_ref, gate_t_ref, columns_ref[2], columns_ref[3],
        outw_t_ref[0], unit_scratch,
    )
    pack_panels(panels, both_ref)


def finish_kernel(
    merged_ref, middle_t_ref, gate_t_ref, columns_ref, outw_t_ref, result_ref, unit_scratch, done, sems
):
    rows, tokens, _ = result_ref.shape
    copies = []

    def emit(chunk, part, result):
        for h, r in enumerate(chunk):
            done[r] = result[:, h * tokens : (h + 1) * tokens].T
            copies.append(pltpu.make_async_copy(done.at[r], result_ref.at[r], sems.at[r]))
            copies[-1].start()

    finish_rows(
        emit, rows, middle_t_ref.shape[0], tokens, lambda part: merged_ref[part].astype(F32), middle_t_ref, gate_t_ref,
        columns_ref[6], columns_ref[7], outw_t_ref[1], unit_scratch,
    )
    for copy in copies:
        copy.wait()


def on_device(*inputs):
    groups = lax.axis_size("row")
    rows, tokens, channels = inputs[0].shape
    per_group = channels // groups
    whole = pl.BlockSpec(memory_space=pltpu.VMEM)
    hbm = pl.BlockSpec(memory_space=pltpu.HBM)
    params = pltpu.CompilerParams(vmem_limit_bytes=48 * 1024 * 1024)
    shape = jax.ShapeDtypeStruct
    both_shape = shape((2 * channels * rows, tokens), BF16)
    flat_shape = shape((channels, rows * tokens), BF16)
    panels = pltpu.VMEM((tokens // LANES, 2 * channels * rows, LANES), F32)
    unit_scratch = pltpu.VMEM((tokens // LANES, channels * rows, LANES), F32)

    def exchange(array):
        return lax.all_to_all(array, "row", split_axis=0, concat_axis=0, tiled=True)

    def mix(both, incoming):
        product = pl.pallas_call(
            functools.partial(mix_kernel, per_group, rows, incoming),
            out_shape=shape((groups, per_group * rows, tokens), BF16),
            in_specs=[whole],
            out_specs=whole,
            compiler_params=params,
            name="mix",
        )(both.reshape(groups, 2 * per_group * rows, tokens))
        return product.reshape(channels * rows, tokens)

    half = channels // 2
    by_core = groups % 4 == 0 and groups * rows * tokens * half * 2 <= 4 * 2**20
    smem = pl.BlockSpec(memory_space=pltpu.SMEM)
    core = (lax.axis_index("row") % 2).astype(jnp.int32).reshape(1)
    half_shape = shape((half * rows, tokens), BF16)
    projected = (half_shape,) * 4 if by_core else (both_shape,)
    results = pl.pallas_call(
        functools.partial(project_kernel, half if by_core else per_group, by_core),
        out_shape=projected
        + (
            flat_shape,
            flat_shape,
            shape((rows, tokens), inputs[1].dtype),
            shape((8, channels, tokens), F32),
            shape((2, 5 * channels, channels), BF16),
            shape((2, channels, channels), BF16),
        ),
        in_specs=[smem] * by_core + [hbm] * 7,
        out_specs=(whole,) * (len(projected) + 6),
        scratch_shapes=[pltpu.VMEM(inputs[n].shape, inputs[n].dtype) for n in (0, 2, 3, 4, 5, 6)]
        + [panels, pltpu.SemaphoreType.DMA((7,))],
        compiler_params=params,
        name="project",
    )(*[core] * by_core, *(pltpu.with_memory_space_constraint(a, pltpu.HBM) for a in inputs))
    pair_t, gate_t, mask, columns, proj_t, outw_t = results[-6:]
    if by_core:
        left, right, other_left, other_right = results[:4]
        chips = groups // 2
        ring = ring_chips(chips)

        def along(array, step):
            pairs = [(2 * q + c, 2 * ring[(p + step) % chips] + c) for p, q in enumerate(ring) for c in range(2)]
            return lax.ppermute(array, "row", pairs)

        def rounds(array, step, count):
            arrays = [array]
            for _ in range(count):
                arrays.append(along(arrays[-1], step))
            return arrays

        swap = [(d, d ^ 1) for d in range(groups)]
        got_right = lax.ppermute(other_right, "row", swap)
        got_left = lax.ppermute(other_left, "row", swap)
        got_right, got_left = lax.optimization_barrier((got_right, got_left))
        middle = chips // 2
        ups = [rounds(right, 1, middle), rounds(got_right, 1, middle - 1)]
        downs = [rounds(right, -1, middle - 1), rounds(got_right, -1, middle)]
        distances = sorted(range(chips), key=lambda d: min(d, chips - d))
        early = 2 * (chips // 2 + 1)
        rights = [
            ups[piece][d] if d < len(ups[piece]) else downs[piece][chips - d] for d in distances for piece in range(2)
        ]
        rights = [array.reshape(half, rows, tokens) for array in rights]
        lefts = [array.reshape(half, rows, tokens) for array in (left, got_left)]
        first_sums = pl.pallas_call(
            mix_early,
            out_shape=shape((half, 2 * rows, tokens), BF16),
            in_specs=[whole] * (2 + early),
            out_specs=whole,
            compiler_params=params,
            cost_estimate=pl.CostEstimate(flops=10**9, bytes_accessed=4 * 2**20, transcendentals=0),
            name="mix_early",
        )(*lefts, *rights[:early])
        keep, send = pl.pallas_call(
            functools.partial(mix_late, early),
            out_shape=(shape((half, rows, tokens), BF16),) * 2,
            in_specs=[whole] * (4 + len(rights) - early),
            out_specs=(whole,) * 2,
            compiler_params=params,
            name="mix_late",
        )(token_order(chips, distances, rows), *lefts, first_sums, *rights[early:])
        merged = (core, keep.reshape(half * rows, tokens), lax.ppermute(send, "row", swap).reshape(half * rows, tokens))
    else:
        merged = (exchange(mix(exchange(results[0]), False)),)
    both, middle_t, gate_t = pl.pallas_call(
        functools.partial(step_kernel, per_group, by_core),
        out_shape=(both_shape, flat_shape, flat_shape),
        in_specs=[smem] * by_core + [whole] * (len(merged) - by_core + 6),
        out_specs=(whole,) * 3,
        scratch_shapes=[unit_scratch, panels],
        compiler_params=params,
        name="finish_project",
    )(*merged, pair_t, gate_t, mask, columns, outw_t, proj_t)
    merged = exchange(mix(exchange(both), True))
    return pl.pallas_call(
        finish_kernel,
        out_shape=shape((rows, tokens, channels), BF16),
        in_specs=[whole] * 5,
        out_specs=hbm,
        scratch_shapes=[unit_scratch, pltpu.VMEM((rows, tokens, channels), BF16), pltpu.SemaphoreType.DMA((rows,))],
        compiler_params=params,
        name="finish",
    )(merged, middle_t, gate_t, columns, outw_t)


def solution(mesh):
    rows = ("groups", "row")
    return jax.shard_map(
        on_device,
        mesh=mesh,
        in_specs=(P(rows, None, None), P(rows, None), P(), P(), P(), P(), P()),
        out_specs=P(rows, None, None),
        check_vma=False,
    )
```

```python
import functools

import jax
import jax.numpy as jnp
from jax import lax
from jax.experimental import pallas as pl
from jax.experimental.pallas import tpu as pltpu
from jax.sharding import PartitionSpec as P

F32 = jnp.float32
BF16 = jnp.bfloat16
LANES = 128
NT = (((1,), (1,)), ((), ()))
NN = (((1,), (0,)), ((), ()))
TN = (((0,), (0,)), ((), ()))


def dot(a, b, dims):
    return lax.dot_general(a, b, dims, preferred_element_type=F32)


def unit(values, axis):
    scale = 1.0 / values.shape[axis]
    centred = values - jnp.sum(values, axis=axis, keepdims=True) * scale
    spread = jnp.sum(centred * centred, axis=axis, keepdims=True) * scale
    return centred * lax.rsqrt(spread + 1e-05)


def chunks(rows, tokens, limit):
    wide = max(1, min(rows, limit // tokens))
    return [list(range(start, min(start + wide, rows))) for start in range(0, rows, wide)]


def span(chunk, tokens):
    return slice(chunk[0] * tokens, (chunk[-1] + 1) * tokens)


def lanes(parts):
    return parts[0] if len(parts) == 1 else jnp.concatenate(parts, axis=1)


def affine(values, gain, bias, tokens):
    parts = [values[:, n : n + tokens] * gain + bias for n in range(0, values.shape[1], tokens)]
    return lanes(parts).astype(BF16)


def store_panels(panels, per_group, rows, chunk, tokens, products, half_mask):
    channels = products.shape[0] // 5
    for side in range(2):
        base = 2 * side * channels
        gate, value = products[base : base + channels], products[base + channels : base + 2 * channels]
        gated = (jnp.tanh(gate) + 1.0) * (value * half_mask)
        for h, r in enumerate(chunk):
            for g in range(channels // per_group):
                where = pl.ds((2 * g + side) * per_group * rows + r, per_group, stride=rows)
                for t in range(tokens // LANES):
                    first = h * tokens + t * LANES
                    panels[t, where, :] = gated[g * per_group : (g + 1) * per_group, first : first + LANES]
    return (0.5 * jnp.tanh(products[4 * channels :]) + 0.5).astype(BF16)


def pack_panels(panels, both_ref):
    for t in range(both_ref.shape[1] // LANES):
        both_ref[:, t * LANES : (t + 1) * LANES] = panels[t].astype(BF16)


def split_panels(panels, core_ref, left_ref, right_ref, other_left_ref, other_right_ref):
    size = left_ref.shape[0]
    core = core_ref[0]
    for t in range(left_ref.shape[1] // LANES):
        for side, (own_ref, other_ref) in enumerate(((left_ref, other_left_ref), (right_ref, other_right_ref))):
            for group, ref in ((core, own_ref), (1 - core, other_ref)):
                start = pl.multiple_of((2 * group + side) * size, size)
                ref[:, t * LANES : (t + 1) * LANES] = panels[t, pl.ds(start, size), :].astype(BF16)


def half_lanes(mask_ref, chunk):
    return lanes([mask_ref[r : r + 1].astype(F32) * 0.5 for r in chunk])


def project_kernel(per_group, by_core, *refs):
    core_ref, refs = (refs[0], refs[1:]) if by_core else (None, refs)
    inputs, refs = refs[:7], refs[7:]
    if by_core:
        outs, refs = refs[:4], refs[4:]
        both_ref = None
    else:
        both_ref, refs = refs[0], refs[1:]
    pair_t_ref, gate_t_ref, mask_ref, columns_ref, proj_t_ref, outw_t_ref = refs[:6]
    pair_ref, gain_ref, bias_ref, proj_ref, gatew_ref, outw_ref, panels, sems = refs[6:]
    held = (pair_ref, mask_ref, gain_ref, bias_ref, proj_ref, gatew_ref, outw_ref)
    copies = [pltpu.make_async_copy(src, dst, sems.at[n]) for n, (src, dst) in enumerate(zip(inputs, held))]
    for copy in copies:
        copy.start()
    for copy in copies:
        copy.wait()
    rows, tokens, channels = pair_ref.shape
    small = jnp.concatenate([ref[which] for ref in (gain_ref, bias_ref) for which in range(2)], axis=0).T
    for n in range(4):
        for side in range(2):
            place = 4 * side + n
            columns_ref[2 * n + side] = jnp.broadcast_to(small[:, place : place + 1], (channels, tokens))
    for which in range(2):
        for part in range(4):
            block = proj_ref[which, :, part * channels : (part + 1) * channels].T
            proj_t_ref[which, part * channels : (part + 1) * channels] = block if part % 2 else block * 0.5
        proj_t_ref[which, 4 * channels :] = gatew_ref[which].T * 0.5
        outw_t_ref[which] = outw_ref[which].T
    for chunk in chunks(rows, tokens, 256):
        part = span(chunk, tokens)
        pair_t = lanes([pair_ref[r].T for r in chunk])
        pair_t_ref[:, part] = pair_t
        normed = affine(unit(pair_t.astype(F32), 0), columns_ref[0], columns_ref[1], tokens)
        products = dot(proj_t_ref[0], normed, NN)
        gate_t_ref[:, part] = store_panels(
            panels, per_group, rows, chunk, tokens, products, half_lanes(mask_ref, chunk)
        )
    if by_core:
        split_panels(panels, core_ref, *outs)
    else:
        pack_panels(panels, both_ref)


def mix_kernel(per_group, rows, incoming, both_ref, product_ref):
    groups, _, tokens = both_ref.shape
    step = 2 * rows

    def matrices(side, pair):
        start = (side * per_group + 2 * pair) * rows
        block = both_ref[:, start : start + step, :].astype(F32)
        return [block[:, h * rows : (h + 1) * rows].reshape(groups * rows, tokens).astype(BF16) for h in range(2)]

    for pair in range(per_group // 2):
        lefts, rights = matrices(0, pair), matrices(1, pair)
        sums = [
            dot(left, right, TN if incoming else NT).reshape(groups, rows, tokens)
            for left, right in zip(lefts, rights)
        ]
        product_ref[:, pair * step : (pair + 1) * step, :] = jnp.concatenate(sums, axis=1).astype(BF16)


def ring_chips(count):
    return list(range(0, count, 2)) + list(range(count - 1, 0, -2))


def token_order(chips, distances, rows):
    device = lax.axis_index("row")
    chip, core = device // 2, device % 2
    place = jnp.where(chip % 2 == 0, chip // 2, chips - 1 - chip // 2)
    size = 2 * chips * rows
    lane, token = (lax.broadcasted_iota(jnp.int32, (size, size), axis) for axis in range(2))
    first = jnp.zeros((size, size), jnp.int32)
    for n, d in enumerate(distances):
        source = place - d + jnp.where(place < d, chips, 0)
        source = jnp.where(2 * source < chips, 2 * source, 2 * (chips - 1 - source) + 1)
        for piece in range(2):
            start = (2 * n + piece) * rows
            block = 2 * source + (1 - core if piece else core)
            first = jnp.where((lane >= start) & (lane < start + rows), block * rows - start, first)
    return (token == lane + first).astype(BF16)


def gathered_sums(own_ref, got_ref, rights, first_lane, c):
    _, rows, tokens = own_ref.shape
    left = jnp.concatenate([own_ref[c].astype(F32), got_ref[c].astype(F32)], axis=0).astype(BF16)
    blocks = [ref[c].astype(F32) for ref in rights]
    last = first_lane + len(blocks) * rows
    empty = [jnp.zeros((n, tokens), F32) for n in (first_lane, tokens - last)]
    blocks = [block for block in (empty[0], *blocks, empty[1]) if block.shape[0]]
    return dot(left, jnp.concatenate(blocks, axis=0).astype(BF16), NT)


def mix_early(own_ref, got_ref, *refs):
    rights, early_ref = refs[:-1], refs[-1]
    for c in range(own_ref.shape[0]):
        early_ref[c] = gathered_sums(own_ref, got_ref, rights, 0, c).astype(BF16)


def mix_late(early, order_ref, own_ref, got_ref, early_ref, *refs):
    rights, (keep_ref, send_ref, sums_ref) = refs[:-3], refs[-3:]
    count, rows, tokens = own_ref.shape
    for c in range(count):
        sums = gathered_sums(own_ref, got_ref, rights, early * rows, c)
        sums_ref[2 * rows * c : 2 * rows * (c + 1)] = (sums + early_ref[c].astype(F32)).astype(BF16)
    order = order_ref[...]
    group = 16
    for first in range(0, count, group):
        sums = dot(sums_ref[2 * rows * first : 2 * rows * (first + group)], order, NN)
        sums = sums.reshape(group, 2 * rows, tokens)
        keep_ref[first : first + group] = sums[:, :rows].astype(BF16)
        send_ref[first : first + group] = sums[:, rows:].astype(BF16)


def finish_rows(emit, rows, channels, tokens, load, pair_t_ref, gate_t_ref, gain, bias, outw_t, unit_scratch):
    tiles = range(tokens // LANES)
    parts = [slice(first * rows, (first + 16) * rows) for first in range(0, channels, 16)]

    def sums(part):
        return load(part).reshape(16, rows, tokens)

    average = sum(jnp.sum(sums(part), axis=0) for part in parts) * (1.0 / channels)
    spread = sum(jnp.sum(jnp.square(sums(part) - average), axis=0) for part in parts) * (1.0 / channels)
    inverse = lax.rsqrt(spread + 1e-05)
    for part in parts:
        units = ((sums(part) - average) * inverse).reshape(16 * rows, tokens)
        for t in tiles:
            unit_scratch[t, part, :] = units[:, t * LANES : (t + 1) * LANES]
    for chunk in chunks(rows, tokens, 256):
        part = span(chunk, tokens)
        units = lanes([unit_scratch[t, pl.ds(r, channels, stride=rows), :] for r in chunk for t in tiles])
        normed = affine(units, gain, bias, tokens)
        change = gate_t_ref[:, part].astype(F32) * dot(outw_t, normed, NN)
        emit(chunk, part, (pair_t_ref[:, part].astype(F32) + change).astype(BF16))


def step_kernel(per_group, by_core, *refs):
    if not by_core:
        merged_ref, refs = refs[0], refs[1:]
        return step_rows(per_group, lambda part: merged_ref[part].astype(F32), *refs)
    core_ref, keep_ref, got_ref, refs = refs[0], refs[1], refs[2], refs[3:]
    size = keep_ref.shape[0]

    def load(part):
        late = part.start >= size
        part = slice(part.start - size, part.stop - size) if late else part
        keep, got = keep_ref[part].astype(F32), got_ref[part].astype(F32)
        return jnp.where(jnp.full(keep.shape, core_ref[0]) == int(late), keep, got)

    step_rows(per_group, load, *refs)


def step_rows(
    per_group, load, pair_t_ref, gate_t_ref, mask_ref, columns_ref, outw_t_ref, proj_t_ref,
    both_ref, middle_t_ref, gate1_t_ref, unit_scratch, panels,
):
    rows, tokens = mask_ref.shape

    def emit(chunk, part, middle):
        middle_t_ref[:, part] = middle
        normed = affine(unit(middle.astype(F32), 0), columns_ref[4], columns_ref[5], tokens)
        products = dot(proj_t_ref[1], normed, NN)
        gate1_t_ref[:, part] = store_panels(
            panels, per_group, rows, chunk, tokens, products, half_lanes(mask_ref, chunk)
        )

    finish_rows(
        emit, rows, pair_t_ref.shape[0], tokens, load, pair_t_ref, gate_t_ref, columns_ref[2], columns_ref[3],
        outw_t_ref[0], unit_scratch,
    )
    pack_panels(panels, both_ref)


def finish_kernel(
    merged_ref, middle_t_ref, gate_t_ref, columns_ref, outw_t_ref, result_ref, unit_scratch, done, sems
):
    rows, tokens, _ = result_ref.shape
    copies = []

    def emit(chunk, part, result):
        for h, r in enumerate(chunk):
            done[r] = result[:, h * tokens : (h + 1) * tokens].T
            copies.append(pltpu.make_async_copy(done.at[r], result_ref.at[r], sems.at[r]))
            copies[-1].start()

    finish_rows(
        emit, rows, middle_t_ref.shape[0], tokens, lambda part: merged_ref[part].astype(F32), middle_t_ref, gate_t_ref,
        columns_ref[6], columns_ref[7], outw_t_ref[1], unit_scratch,
    )
    for copy in copies:
        copy.wait()


def on_device(*inputs):
    groups = lax.axis_size("row")
    rows, tokens, channels = inputs[0].shape
    per_group = channels // groups
    whole = pl.BlockSpec(memory_space=pltpu.VMEM)
    hbm = pl.BlockSpec(memory_space=pltpu.HBM)
    params = pltpu.CompilerParams(vmem_limit_bytes=48 * 1024 * 1024)
    shape = jax.ShapeDtypeStruct
    both_shape = shape((2 * channels * rows, tokens), BF16)
    flat_shape = shape((channels, rows * tokens), BF16)
    panels = pltpu.VMEM((tokens // LANES, 2 * channels * rows, LANES), F32)
    unit_scratch = pltpu.VMEM((tokens // LANES, channels * rows, LANES), F32)

    def exchange(array):
        return lax.all_to_all(array, "row", split_axis=0, concat_axis=0, tiled=True)

    def mix(both, incoming):
        product = pl.pallas_call(
            functools.partial(mix_kernel, per_group, rows, incoming),
            out_shape=shape((groups, per_group * rows, tokens), BF16),
            in_specs=[whole],
            out_specs=whole,
            compiler_params=params,
            name="mix",
        )(both.reshape(groups, 2 * per_group * rows, tokens))
        return product.reshape(channels * rows, tokens)

    half = channels // 2
    by_core = groups % 4 == 0 and groups * rows * tokens * half * 2 <= 4 * 2**20
    smem = pl.BlockSpec(memory_space=pltpu.SMEM)
    core = (lax.axis_index("row") % 2).astype(jnp.int32).reshape(1)
    half_shape = shape((half * rows, tokens), BF16)
    projected = (half_shape,) * 4 if by_core else (both_shape,)
    results = pl.pallas_call(
        functools.partial(project_kernel, half if by_core else per_group, by_core),
        out_shape=projected
        + (
            flat_shape,
            flat_shape,
            shape((rows, tokens), inputs[1].dtype),
            shape((8, channels, tokens), F32),
            shape((2, 5 * channels, channels), BF16),
            shape((2, channels, channels), BF16),
        ),
        in_specs=[smem] * by_core + [hbm] * 7,
        out_specs=(whole,) * (len(projected) + 6),
        scratch_shapes=[pltpu.VMEM(inputs[n].shape, inputs[n].dtype) for n in (0, 2, 3, 4, 5, 6)]
        + [panels, pltpu.SemaphoreType.DMA((7,))],
        compiler_params=params,
        name="project",
    )(*[core] * by_core, *(pltpu.with_memory_space_constraint(a, pltpu.HBM) for a in inputs))
    pair_t, gate_t, mask, columns, proj_t, outw_t = results[-6:]
    if by_core:
        left, right, other_left, other_right = results[:4]
        chips = groups // 2
        ring = ring_chips(chips)

        def along(array, step):
            pairs = [(2 * q + c, 2 * ring[(p + step) % chips] + c) for p, q in enumerate(ring) for c in range(2)]
            return lax.ppermute(array, "row", pairs)

        def rounds(array, step, count):
            arrays = [array]
            for _ in range(count):
                arrays.append(along(arrays[-1], step))
            return arrays

        swap = [(d, d ^ 1) for d in range(groups)]
        got_right = lax.ppermute(other_right, "row", swap)
        got_left = lax.ppermute(other_left, "row", swap)
        middle = chips // 2
        ups = [rounds(right, 1, middle), rounds(got_right, 1, middle - 1)]
        downs = [rounds(right, -1, middle - 1), rounds(got_right, -1, middle)]
        distances = sorted(range(chips), key=lambda d: min(d, chips - d))
        early = 2 * (chips // 2 + 1)
        rights = [
            ups[piece][d] if d < len(ups[piece]) else downs[piece][chips - d] for d in distances for piece in range(2)
        ]
        rights = [array.reshape(half, rows, tokens) for array in rights]
        lefts = [array.reshape(half, rows, tokens) for array in (left, got_left)]
        first_sums = pl.pallas_call(
            mix_early,
            out_shape=shape((half, 2 * rows, tokens), BF16),
            in_specs=[whole] * (2 + early),
            out_specs=whole,
            compiler_params=params,
            cost_estimate=pl.CostEstimate(flops=10**9, bytes_accessed=4 * 2**20, transcendentals=0),
            name="mix_early",
        )(*lefts, *rights[:early])
        keep, send = pl.pallas_call(
            functools.partial(mix_late, early),
            out_shape=(shape((half, rows, tokens), BF16),) * 2,
            in_specs=[whole] * (4 + len(rights) - early),
            out_specs=(whole,) * 2,
            scratch_shapes=[pltpu.VMEM((2 * half * rows, tokens), BF16)],
            compiler_params=params,
            name="mix_late",
        )(token_order(chips, distances, rows), *lefts, first_sums, *rights[early:])
        merged = (core, keep.reshape(half * rows, tokens), lax.ppermute(send, "row", swap).reshape(half * rows, tokens))
    else:
        merged = (exchange(mix(exchange(results[0]), False)),)
    both, middle_t, gate_t = pl.pallas_call(
        functools.partial(step_kernel, per_group, by_core),
        out_shape=(both_shape, flat_shape, flat_shape),
        in_specs=[smem] * by_core + [whole] * (len(merged) - by_core + 6),
        out_specs=(whole,) * 3,
        scratch_shapes=[unit_scratch, panels],
        compiler_params=params,
        name="finish_project",
    )(*merged, pair_t, gate_t, mask, columns, outw_t, proj_t)
    merged = exchange(mix(exchange(both), True))
    return pl.pallas_call(
        finish_kernel,
        out_shape=shape((rows, tokens, channels), BF16),
        in_specs=[whole] * 5,
        out_specs=hbm,
        scratch_shapes=[unit_scratch, pltpu.VMEM((rows, tokens, channels), BF16), pltpu.SemaphoreType.DMA((rows,))],
        compiler_params=params,
        name="finish",
    )(merged, middle_t, gate_t, columns, outw_t)


def solution(mesh):
    rows = ("groups", "row")
    return jax.shard_map(
        on_device,
        mesh=mesh,
        in_specs=(P(rows, None, None), P(rows, None), P(), P(), P(), P(), P()),
        out_specs=P(rows, None, None),
        check_vma=False,
    )
```

```python
import functools

import jax
import jax.numpy as jnp
from jax import lax
from jax.experimental import pallas as pl
from jax.experimental.pallas import tpu as pltpu
from jax.sharding import PartitionSpec as P

F32 = jnp.float32
BF16 = jnp.bfloat16
LANES = 128
NT = (((1,), (1,)), ((), ()))
NN = (((1,), (0,)), ((), ()))
TN = (((0,), (0,)), ((), ()))


def dot(a, b, dims):
    return lax.dot_general(a, b, dims, preferred_element_type=F32)


def unit(values, axis):
    scale = 1.0 / values.shape[axis]
    centred = values - jnp.sum(values, axis=axis, keepdims=True) * scale
    spread = jnp.sum(centred * centred, axis=axis, keepdims=True) * scale
    return centred * lax.rsqrt(spread + 1e-05)


def chunks(rows, tokens, limit):
    wide = max(1, min(rows, limit // tokens))
    return [list(range(start, min(start + wide, rows))) for start in range(0, rows, wide)]


def span(chunk, tokens):
    return slice(chunk[0] * tokens, (chunk[-1] + 1) * tokens)


def lanes(parts):
    return parts[0] if len(parts) == 1 else jnp.concatenate(parts, axis=1)


def affine(values, gain, bias, tokens):
    parts = [values[:, n : n + tokens] * gain + bias for n in range(0, values.shape[1], tokens)]
    return lanes(parts).astype(BF16)


def store_panels(panels, per_group, rows, chunk, tokens, products, half_mask):
    channels = products.shape[0] // 5
    for side in range(2):
        base = 2 * side * channels
        gate, value = products[base : base + channels], products[base + channels : base + 2 * channels]
        gated = (jnp.tanh(gate) + 1.0) * (value * half_mask)
        for h, r in enumerate(chunk):
            for g in range(channels // per_group):
                where = pl.ds((2 * g + side) * per_group * rows + r, per_group, stride=rows)
                for t in range(tokens // LANES):
                    first = h * tokens + t * LANES
                    panels[t, where, :] = gated[g * per_group : (g + 1) * per_group, first : first + LANES]
    return (0.5 * jnp.tanh(products[4 * channels :]) + 0.5).astype(BF16)


def pack_panels(panels, both_ref):
    for t in range(both_ref.shape[1] // LANES):
        both_ref[:, t * LANES : (t + 1) * LANES] = panels[t].astype(BF16)


def split_panels(panels, core_ref, left_ref, right_ref, other_left_ref, other_right_ref):
    size = left_ref.shape[0]
    core = core_ref[0]
    for t in range(left_ref.shape[1] // LANES):
        for side, (own_ref, other_ref) in enumerate(((left_ref, other_left_ref), (right_ref, other_right_ref))):
            for group, ref in ((core, own_ref), (1 - core, other_ref)):
                start = pl.multiple_of((2 * group + side) * size, size)
                ref[:, t * LANES : (t + 1) * LANES] = panels[t, pl.ds(start, size), :].astype(BF16)


def half_lanes(mask_ref, chunk):
    return lanes([mask_ref[r : r + 1].astype(F32) * 0.5 for r in chunk])


def project_kernel(per_group, by_core, *refs):
    core_ref, refs = (refs[0], refs[1:]) if by_core else (None, refs)
    inputs, refs = refs[:7], refs[7:]
    if by_core:
        outs, refs = refs[:4], refs[4:]
        both_ref = None
    else:
        both_ref, refs = refs[0], refs[1:]
    pair_t_ref, gate_t_ref, mask_ref, columns_ref, proj_t_ref, outw_t_ref = refs[:6]
    pair_ref, gain_ref, bias_ref, proj_ref, gatew_ref, outw_ref, panels, sems = refs[6:]
    held = (pair_ref, mask_ref, gain_ref, bias_ref, proj_ref, gatew_ref, outw_ref)
    copies = [pltpu.make_async_copy(src, dst, sems.at[n]) for n, (src, dst) in enumerate(zip(inputs, held))]
    for copy in copies:
        copy.start()
    for copy in copies:
        copy.wait()
    rows, tokens, channels = pair_ref.shape
    small = jnp.concatenate([ref[which] for ref in (gain_ref, bias_ref) for which in range(2)], axis=0).T
    for n in range(4):
        for side in range(2):
            place = 4 * side + n
            columns_ref[2 * n + side] = jnp.broadcast_to(small[:, place : place + 1], (channels, tokens))
    for which in range(2):
        for part in range(4):
            block = proj_ref[which, :, part * channels : (part + 1) * channels].T
            proj_t_ref[which, part * channels : (part + 1) * channels] = block if part % 2 else block * 0.5
        proj_t_ref[which, 4 * channels :] = gatew_ref[which].T * 0.5
        outw_t_ref[which] = outw_ref[which].T
    for chunk in chunks(rows, tokens, 256):
        part = span(chunk, tokens)
        pair_t = lanes([pair_ref[r].T for r in chunk])
        pair_t_ref[:, part] = pair_t
        normed = affine(unit(pair_t.astype(F32), 0), columns_ref[0], columns_ref[1], tokens)
        products = dot(proj_t_ref[0], normed, NN)
        gate_t_ref[:, part] = store_panels(
            panels, per_group, rows, chunk, tokens, products, half_lanes(mask_ref, chunk)
        )
    if by_core:
        split_panels(panels, core_ref, *outs)
    else:
        pack_panels(panels, both_ref)


def mix_kernel(per_group, rows, incoming, both_ref, product_ref):
    groups, _, tokens = both_ref.shape
    step = 2 * rows

    def matrices(side, pair):
        start = (side * per_group + 2 * pair) * rows
        block = both_ref[:, start : start + step, :].astype(F32)
        return [block[:, h * rows : (h + 1) * rows].reshape(groups * rows, tokens).astype(BF16) for h in range(2)]

    for pair in range(per_group // 2):
        lefts, rights = matrices(0, pair), matrices(1, pair)
        sums = [
            dot(left, right, TN if incoming else NT).reshape(groups, rows, tokens)
            for left, right in zip(lefts, rights)
        ]
        product_ref[:, pair * step : (pair + 1) * step, :] = jnp.concatenate(sums, axis=1).astype(BF16)


def ring_chips(count):
    return list(range(0, count, 2)) + list(range(count - 1, 0, -2))


def token_order(chips, distances, rows):
    device = lax.axis_index("row")
    chip, core = device // 2, device % 2
    place = jnp.where(chip % 2 == 0, chip // 2, chips - 1 - chip // 2)
    size = 2 * chips * rows
    lane, token = (lax.broadcasted_iota(jnp.int32, (size, size), axis) for axis in range(2))
    first = jnp.zeros((size, size), jnp.int32)
    for n, d in enumerate(distances):
        source = place - d + jnp.where(place < d, chips, 0)
        source = jnp.where(2 * source < chips, 2 * source, 2 * (chips - 1 - source) + 1)
        for piece in range(2):
            start = (2 * n + piece) * rows
            block = 2 * source + (1 - core if piece else core)
            first = jnp.where((lane >= start) & (lane < start + rows), block * rows - start, first)
    return (token == lane + first).astype(BF16)


def gathered_sums(own_ref, got_ref, rights, first_lane, c):
    _, rows, tokens = own_ref.shape
    left = jnp.concatenate([own_ref[c].astype(F32), got_ref[c].astype(F32)], axis=0).astype(BF16)
    blocks = [ref[c].astype(F32) for ref in rights]
    last = first_lane + len(blocks) * rows
    empty = [jnp.zeros((n, tokens), F32) for n in (first_lane, tokens - last)]
    blocks = [block for block in (empty[0], *blocks, empty[1]) if block.shape[0]]
    return dot(left, jnp.concatenate(blocks, axis=0).astype(BF16), NT)


def mix_early(own_ref, got_ref, *refs):
    rights, early_ref = refs[:-1], refs[-1]
    for c in range(own_ref.shape[0]):
        early_ref[c] = gathered_sums(own_ref, got_ref, rights, 0, c).astype(BF16)


def mix_late(early, order_ref, own_ref, got_ref, early_ref, *refs):
    rights, (keep_ref, send_ref, sums_ref) = refs[:-3], refs[-3:]
    count, rows, tokens = own_ref.shape
    for c in range(count):
        sums = gathered_sums(own_ref, got_ref, rights, early * rows, c)
        sums_ref[2 * rows * c : 2 * rows * (c + 1)] = (sums + early_ref[c].astype(F32)).astype(BF16)
    order = order_ref[...]
    group = 16
    for first in range(0, count, group):
        sums = dot(sums_ref[2 * rows * first : 2 * rows * (first + group)], order, NN)
        sums = sums.reshape(group, 2 * rows, tokens)
        keep_ref[first : first + group] = sums[:, :rows].astype(BF16)
        send_ref[first : first + group] = sums[:, rows:].astype(BF16)


def finish_rows(emit, rows, channels, tokens, load, pair_t_ref, gate_t_ref, gain, bias, outw_t, unit_scratch):
    tiles = range(tokens // LANES)
    parts = [slice(first * rows, (first + 16) * rows) for first in range(0, channels, 16)]

    def sums(part):
        return load(part).reshape(16, rows, tokens)

    average = sum(jnp.sum(sums(part), axis=0) for part in parts) * (1.0 / channels)
    spread = sum(jnp.sum(jnp.square(sums(part) - average), axis=0) for part in parts) * (1.0 / channels)
    inverse = lax.rsqrt(spread + 1e-05)
    for part in parts:
        units = ((sums(part) - average) * inverse).reshape(16 * rows, tokens)
        for t in tiles:
            unit_scratch[t, part, :] = units[:, t * LANES : (t + 1) * LANES]
    for chunk in chunks(rows, tokens, 256):
        part = span(chunk, tokens)
        units = lanes([unit_scratch[t, pl.ds(r, channels, stride=rows), :] for r in chunk for t in tiles])
        normed = affine(units, gain, bias, tokens)
        change = gate_t_ref[:, part].astype(F32) * dot(outw_t, normed, NN)
        emit(chunk, part, (pair_t_ref[:, part].astype(F32) + change).astype(BF16))


def step_kernel(per_group, by_core, *refs):
    if not by_core:
        merged_ref, refs = refs[0], refs[1:]
        return step_rows(per_group, lambda part: merged_ref[part].astype(F32), *refs)
    core_ref, refs = refs[0], refs[1:]
    step_rows(per_group, core_halves(core_ref, refs[0], refs[1]), *refs[2:], core_ref=core_ref)


def core_halves(core_ref, keep_ref, got_ref):
    size = keep_ref.shape[0]

    def load(part):
        late = part.start >= size
        part = slice(part.start - size, part.stop - size) if late else part
        keep, got = keep_ref[part].astype(F32), got_ref[part].astype(F32)
        return jnp.where(jnp.full(keep.shape, core_ref[0]) == int(late), keep, got)

    return load


def step_rows(
    per_group, load, pair_t_ref, gate_t_ref, mask_ref, columns_ref, outw_t_ref, proj_t_ref, *refs, core_ref=None
):
    outs, (middle_t_ref, gate1_t_ref, unit_scratch, panels) = refs[:-4], refs[-4:]
    rows, tokens = mask_ref.shape

    def emit(chunk, part, middle):
        middle_t_ref[:, part] = middle
        normed = affine(unit(middle.astype(F32), 0), columns_ref[4], columns_ref[5], tokens)
        products = dot(proj_t_ref[1], normed, NN)
        gate1_t_ref[:, part] = store_panels(
            panels, per_group, rows, chunk, tokens, products, half_lanes(mask_ref, chunk)
        )

    finish_rows(
        emit, rows, pair_t_ref.shape[0], tokens, load, pair_t_ref, gate_t_ref, columns_ref[2], columns_ref[3],
        outw_t_ref[0], unit_scratch,
    )
    if core_ref is None:
        pack_panels(panels, *outs)
    else:
        split_panels(panels, core_ref, *outs)


def finish_kernel(by_core, *refs):
    if by_core:
        load, refs = core_halves(*refs[:3]), refs[3:]
    else:
        merged_ref, refs = refs[0], refs[1:]

        def load(part):
            return merged_ref[part].astype(F32)

    middle_t_ref, gate_t_ref, columns_ref, outw_t_ref, result_ref, unit_scratch, done, sems = refs
    rows, tokens, _ = result_ref.shape
    copies = []

    def emit(chunk, part, result):
        for h, r in enumerate(chunk):
            done[r] = result[:, h * tokens : (h + 1) * tokens].T
            copies.append(pltpu.make_async_copy(done.at[r], result_ref.at[r], sems.at[r]))
            copies[-1].start()

    finish_rows(
        emit, rows, middle_t_ref.shape[0], tokens, load, middle_t_ref, gate_t_ref,
        columns_ref[6], columns_ref[7], outw_t_ref[1], unit_scratch,
    )
    for copy in copies:
        copy.wait()


def chip_rows(chips_ref, distance, count):
    return pl.ds(pl.multiple_of(chips_ref[distance] * count, count), count)


def scatter_start(first, up, down, chips_ref, *refs):
    own_left, got_left, own_right, got_right, sums_ref, up_ref, down_ref = refs
    rows = own_left.shape[1]
    for c in range(sums_ref.shape[0]):
        left, right = [
            jnp.concatenate([own[first + c].astype(F32), got[first + c].astype(F32)], axis=0).astype(BF16)
            for own, got in ((own_left, got_left), (own_right, got_right))
        ]
        sums_ref[c] = dot(left, right, TN)
    for distance, ref in ((up, up_ref), (down, down_ref)):
        ref[...] = sums_ref[:, chip_rows(chips_ref, distance, 2 * rows), :].astype(BF16)


def scatter_add(distance, chips_ref, got_ref, sums_ref, out_ref):
    here = sums_ref[:, chip_rows(chips_ref, distance, got_ref.shape[1]), :]
    out_ref[...] = (got_ref[...].astype(F32) + here).astype(BF16)


def scatter_end(core_ref, chips_ref, *refs):
    pieces, (keep_ref, send_ref) = refs[:-2], refs[-2:]
    rows = keep_ref.shape[1]
    first = 0
    for n in range(0, len(pieces), 3):
        sums_ref, up_ref, down_ref = pieces[n : n + 3]
        count = sums_ref.shape[0]
        sums = sums_ref[:, chip_rows(chips_ref, 0, 2 * rows), :] + up_ref[...].astype(F32) + down_ref[...].astype(F32)
        halves = sums[:, :rows], sums[:, rows:]
        first_core = jnp.full(halves[0].shape, core_ref[0]) == 0
        keep_ref[first : first + count] = jnp.where(first_core, *halves).astype(BF16)
        send_ref[first : first + count] = jnp.where(first_core, *halves[::-1]).astype(BF16)
        first += count


def on_device(*inputs):
    groups = lax.axis_size("row")
    rows, tokens, channels = inputs[0].shape
    per_group = channels // groups
    whole = pl.BlockSpec(memory_space=pltpu.VMEM)
    hbm = pl.BlockSpec(memory_space=pltpu.HBM)
    params = pltpu.CompilerParams(vmem_limit_bytes=32 * 1024 * 1024)
    shape = jax.ShapeDtypeStruct
    both_shape = shape((2 * channels * rows, tokens), BF16)
    flat_shape = shape((channels, rows * tokens), BF16)
    panels = pltpu.VMEM((tokens // LANES, 2 * channels * rows, LANES), F32)
    unit_scratch = pltpu.VMEM((tokens // LANES, channels * rows, LANES), F32)

    def exchange(array):
        return lax.all_to_all(array, "row", split_axis=0, concat_axis=0, tiled=True)

    def mix(both, incoming):
        product = pl.pallas_call(
            functools.partial(mix_kernel, per_group, rows, incoming),
            out_shape=shape((groups, per_group * rows, tokens), BF16),
            in_specs=[whole],
            out_specs=whole,
            compiler_params=params,
            name="mix",
        )(both.reshape(groups, 2 * per_group * rows, tokens))
        return product.reshape(channels * rows, tokens)

    half = channels // 2
    by_core = groups % 4 == 0 and groups * rows * tokens * half * 2 <= 4 * 2**20
    smem = pl.BlockSpec(memory_space=pltpu.SMEM)
    core = (lax.axis_index("row") % 2).astype(jnp.int32).reshape(1)
    half_shape = shape((half * rows, tokens), BF16)
    projected = (half_shape,) * 4 if by_core else (both_shape,)
    results = pl.pallas_call(
        functools.partial(project_kernel, half if by_core else per_group, by_core),
        out_shape=projected
        + (
            flat_shape,
            flat_shape,
            shape((rows, tokens), inputs[1].dtype),
            shape((8, channels, tokens), F32),
            shape((2, 5 * channels, channels), BF16),
            shape((2, channels, channels), BF16),
        ),
        in_specs=[smem] * by_core + [hbm] * 7,
        out_specs=(whole,) * (len(projected) + 6),
        scratch_shapes=[pltpu.VMEM(inputs[n].shape, inputs[n].dtype) for n in (0, 2, 3, 4, 5, 6)]
        + [panels, pltpu.SemaphoreType.DMA((7,))],
        compiler_params=params,
        name="project",
    )(*[core] * by_core, *(pltpu.with_memory_space_constraint(a, pltpu.HBM) for a in inputs))
    pair_t, gate_t, mask, columns, proj_t, outw_t = results[-6:]
    if by_core:
        left, right, other_left, other_right = results[:4]
        chips = groups // 2
        ring = ring_chips(chips)

        def along(array, step):
            pairs = [(2 * q + c, 2 * ring[(p + step) % chips] + c) for p, q in enumerate(ring) for c in range(2)]
            return lax.ppermute(array, "row", pairs)

        def rounds(array, step, count):
            arrays = [array]
            for _ in range(count):
                arrays.append(along(arrays[-1], step))
            return arrays

        swap = [(d, d ^ 1) for d in range(groups)]
        got_right = lax.ppermute(other_right, "row", swap)
        got_left = lax.ppermute(other_left, "row", swap)
        middle = chips // 2
        ups = [rounds(right, 1, middle), rounds(got_right, 1, middle - 1)]
        downs = [rounds(right, -1, middle - 1), rounds(got_right, -1, middle)]
        distances = sorted(range(chips), key=lambda d: min(d, chips - d))
        early = 2 * (chips // 2 + 1)
        rights = [
            ups[piece][d] if d < len(ups[piece]) else downs[piece][chips - d] for d in distances for piece in range(2)
        ]
        rights = [array.reshape(half, rows, tokens) for array in rights]
        lefts = [array.reshape(half, rows, tokens) for array in (left, got_left)]
        first_sums = pl.pallas_call(
            mix_early,
            out_shape=shape((half, 2 * rows, tokens), BF16),
            in_specs=[whole] * (2 + early),
            out_specs=whole,
            compiler_params=params,
            cost_estimate=pl.CostEstimate(flops=10**9, bytes_accessed=4 * 2**20, transcendentals=0),
            name="mix_early",
        )(*lefts, *rights[:early])
        keep, send = pl.pallas_call(
            functools.partial(mix_late, early),
            out_shape=(shape((half, rows, tokens), BF16),) * 2,
            in_specs=[whole] * (4 + len(rights) - early),
            out_specs=(whole,) * 2,
            scratch_shapes=[pltpu.VMEM((2 * half * rows, tokens), BF16)],
            compiler_params=params,
            name="mix_late",
        )(token_order(chips, distances, rows), *lefts, first_sums, *rights[early:])
        merged = (core, keep.reshape(half * rows, tokens), lax.ppermute(send, "row", swap).reshape(half * rows, tokens))
    else:
        merged = (exchange(mix(exchange(results[0]), False)),)
    results = pl.pallas_call(
        functools.partial(step_kernel, half if by_core else per_group, by_core),
        out_shape=projected + (flat_shape, flat_shape),
        in_specs=[smem] * by_core + [whole] * (len(merged) - by_core + 6),
        out_specs=(whole,) * (len(projected) + 2),
        scratch_shapes=[unit_scratch, panels],
        compiler_params=params,
        name="finish_project",
    )(*merged, pair_t, gate_t, mask, columns, outw_t, proj_t)
    middle_t, gate_t = results[-2:]
    if by_core:
        left, right, other_left, other_right = results[:4]
        got_left = lax.ppermute(other_left, "row", swap)
        got_right = lax.ppermute(other_right, "row", swap)
        operands = [array.reshape(half, rows, tokens) for array in (left, got_left, right, got_right)]
        chip = lax.axis_index("row") // 2
        place = jnp.where(chip % 2 == 0, chip // 2, chips - 1 - chip // 2)
        spots = [place + d - jnp.where(place + d >= chips, chips, 0) for d in range(chips)]
        chips_at = jnp.stack([jnp.where(2 * p < chips, 2 * p, 2 * (chips - 1 - p) + 1) for p in spots]).astype(jnp.int32)
        size = half // 2
        part_shape = shape((size, 2 * rows, tokens), BF16)
        pieces = []
        for piece in range(2):
            hops = (middle, middle - 1) if piece == 0 else (middle - 1, middle)
            sums, *travelling = pl.pallas_call(
                functools.partial(scatter_start, piece * size, hops[0], chips - hops[1]),
                out_shape=(shape((size, tokens, tokens), F32), part_shape, part_shape),
                in_specs=[smem] + [whole] * 4,
                out_specs=(whole,) * 3,
                compiler_params=params,
                name="scatter_start",
            )(chips_at, *operands)
            for way, (step, count) in enumerate(zip((1, -1), hops)):
                for left_over in reversed(range(count)):
                    travelling[way] = along(travelling[way], step)
                    if left_over:
                        travelling[way] = pl.pallas_call(
                            functools.partial(scatter_add, step * left_over % chips),
                            out_shape=part_shape,
                            in_specs=[smem] + [whole] * 2,
                            out_specs=whole,
                            compiler_params=params,
                            name="scatter_add",
                        )(chips_at, travelling[way], sums)
            pieces += [sums, *travelling]
        keep, send = pl.pallas_call(
            scatter_end,
            out_shape=(shape((half, rows, tokens), BF16),) * 2,
            in_specs=[smem] * 2 + [whole] * len(pieces),
            out_specs=(whole,) * 2,
            compiler_params=params,
            name="scatter_end",
        )(core, chips_at, *pieces)
        merged = (core, keep.reshape(half * rows, tokens), lax.ppermute(send, "row", swap).reshape(half * rows, tokens))
    else:
        merged = (exchange(mix(exchange(results[0]), True)),)
    return pl.pallas_call(
        functools.partial(finish_kernel, by_core),
        out_shape=shape((rows, tokens, channels), BF16),
        in_specs=[smem] * by_core + [whole] * (len(merged) - by_core + 4),
        out_specs=hbm,
        scratch_shapes=[unit_scratch, pltpu.VMEM((rows, tokens, channels), BF16), pltpu.SemaphoreType.DMA((rows,))],
        compiler_params=params,
        name="finish",
    )(*merged, middle_t, gate_t, columns, outw_t)


def solution(mesh):
    rows = ("groups", "row")
    return jax.shard_map(
        on_device,
        mesh=mesh,
        in_specs=(P(rows, None, None), P(rows, None), P(), P(), P(), P(), P()),
        out_specs=P(rows, None, None),
        check_vma=False,
    )
```

```python
import functools

import jax
import jax.numpy as jnp
from jax import lax
from jax.experimental import pallas as pl
from jax.experimental.pallas import tpu as pltpu
from jax.sharding import PartitionSpec as P

F32 = jnp.float32
BF16 = jnp.bfloat16
LANES = 128
NT = (((1,), (1,)), ((), ()))
NN = (((1,), (0,)), ((), ()))
TN = (((0,), (0,)), ((), ()))


def dot(a, b, dims):
    return lax.dot_general(a, b, dims, preferred_element_type=F32)


def unit(values, axis):
    scale = 1.0 / values.shape[axis]
    centred = values - jnp.sum(values, axis=axis, keepdims=True) * scale
    spread = jnp.sum(centred * centred, axis=axis, keepdims=True) * scale
    return centred * lax.rsqrt(spread + 1e-05)


def chunks(rows, tokens, limit):
    wide = max(1, min(rows, limit // tokens))
    return [list(range(start, min(start + wide, rows))) for start in range(0, rows, wide)]


def span(chunk, tokens):
    return slice(chunk[0] * tokens, (chunk[-1] + 1) * tokens)


def lanes(parts):
    return parts[0] if len(parts) == 1 else jnp.concatenate(parts, axis=1)


def affine(values, gain, bias, tokens):
    parts = [values[:, n : n + tokens] * gain + bias for n in range(0, values.shape[1], tokens)]
    return lanes(parts).astype(BF16)


def store_panels(panels, per_group, rows, chunk, tokens, products, half_mask):
    channels = products.shape[0] // 5
    for side in range(2):
        base = 2 * side * channels
        gate, value = products[base : base + channels], products[base + channels : base + 2 * channels]
        gated = (jnp.tanh(gate) + 1.0) * (value * half_mask)
        for h, r in enumerate(chunk):
            for g in range(channels // per_group):
                where = pl.ds((2 * g + side) * per_group * rows + r, per_group, stride=rows)
                for t in range(tokens // LANES):
                    first = h * tokens + t * LANES
                    panels[t, where, :] = gated[g * per_group : (g + 1) * per_group, first : first + LANES]
    return (0.5 * jnp.tanh(products[4 * channels :]) + 0.5).astype(BF16)


def pack_panels(panels, both_ref):
    for t in range(both_ref.shape[1] // LANES):
        both_ref[:, t * LANES : (t + 1) * LANES] = panels[t].astype(BF16)


def split_panels(panels, core_ref, left_ref, right_ref, other_left_ref, other_right_ref):
    size = left_ref.shape[0]
    core = core_ref[0]
    for t in range(left_ref.shape[1] // LANES):
        for side, (own_ref, other_ref) in enumerate(((left_ref, other_left_ref), (right_ref, other_right_ref))):
            for group, ref in ((core, own_ref), (1 - core, other_ref)):
                start = pl.multiple_of((2 * group + side) * size, size)
                ref[:, t * LANES : (t + 1) * LANES] = panels[t, pl.ds(start, size), :].astype(BF16)


def half_lanes(mask_ref, chunk):
    return lanes([mask_ref[r : r + 1].astype(F32) * 0.5 for r in chunk])


def project_kernel(per_group, by_core, *refs):
    core_ref, refs = (refs[0], refs[1:]) if by_core else (None, refs)
    inputs, refs = refs[:7], refs[7:]
    if by_core:
        outs, refs = refs[:4], refs[4:]
        both_ref = None
    else:
        both_ref, refs = refs[0], refs[1:]
    pair_t_ref, gate_t_ref, mask_ref, columns_ref, proj_t_ref, outw_t_ref = refs[:6]
    pair_ref, gain_ref, bias_ref, proj_ref, gatew_ref, outw_ref, panels, sems = refs[6:]
    held = (pair_ref, mask_ref, gain_ref, bias_ref, proj_ref, gatew_ref, outw_ref)
    copies = [pltpu.make_async_copy(src, dst, sems.at[n]) for n, (src, dst) in enumerate(zip(inputs, held))]
    for copy in copies:
        copy.start()
    for copy in copies:
        copy.wait()
    rows, tokens, channels = pair_ref.shape
    small = jnp.concatenate([ref[which] for ref in (gain_ref, bias_ref) for which in range(2)], axis=0).T
    for n in range(4):
        for side in range(2):
            place = 4 * side + n
            columns_ref[2 * n + side] = jnp.broadcast_to(small[:, place : place + 1], (channels, tokens))
    for which in range(2):
        for part in range(4):
            block = proj_ref[which, :, part * channels : (part + 1) * channels].T
            proj_t_ref[which, part * channels : (part + 1) * channels] = block if part % 2 else block * 0.5
        proj_t_ref[which, 4 * channels :] = gatew_ref[which].T * 0.5
        outw_t_ref[which] = outw_ref[which].T
    for chunk in chunks(rows, tokens, 256):
        part = span(chunk, tokens)
        pair_t = lanes([pair_ref[r].T for r in chunk])
        pair_t_ref[:, part] = pair_t
        normed = affine(unit(pair_t.astype(F32), 0), columns_ref[0], columns_ref[1], tokens)
        products = dot(proj_t_ref[0], normed, NN)
        gate_t_ref[:, part] = store_panels(
            panels, per_group, rows, chunk, tokens, products, half_lanes(mask_ref, chunk)
        )
    if by_core:
        split_panels(panels, core_ref, *outs)
    else:
        pack_panels(panels, both_ref)


def mix_kernel(per_group, rows, incoming, both_ref, product_ref):
    groups, _, tokens = both_ref.shape
    step = 2 * rows

    def matrices(side, pair):
        start = (side * per_group + 2 * pair) * rows
        block = both_ref[:, start : start + step, :].astype(F32)
        return [block[:, h * rows : (h + 1) * rows].reshape(groups * rows, tokens).astype(BF16) for h in range(2)]

    for pair in range(per_group // 2):
        lefts, rights = matrices(0, pair), matrices(1, pair)
        sums = [
            dot(left, right, TN if incoming else NT).reshape(groups, rows, tokens)
            for left, right in zip(lefts, rights)
        ]
        product_ref[:, pair * step : (pair + 1) * step, :] = jnp.concatenate(sums, axis=1).astype(BF16)


def ring_chips(count):
    return list(range(0, count, 2)) + list(range(count - 1, 0, -2))


def token_order(chips, distances, rows):
    device = lax.axis_index("row")
    chip, core = device // 2, device % 2
    place = jnp.where(chip % 2 == 0, chip // 2, chips - 1 - chip // 2)
    size = 2 * chips * rows
    lane, token = (lax.broadcasted_iota(jnp.int32, (size, size), axis) for axis in range(2))
    first = jnp.zeros((size, size), jnp.int32)
    for n, d in enumerate(distances):
        source = place - d + jnp.where(place < d, chips, 0)
        source = jnp.where(2 * source < chips, 2 * source, 2 * (chips - 1 - source) + 1)
        for piece in range(2):
            start = (2 * n + piece) * rows
            block = 2 * source + (1 - core if piece else core)
            first = jnp.where((lane >= start) & (lane < start + rows), block * rows - start, first)
    return (token == lane + first).astype(BF16)


def gathered_sums(own_ref, got_ref, rights, first_lane, c):
    _, rows, tokens = own_ref.shape
    left = jnp.concatenate([own_ref[c].astype(F32), got_ref[c].astype(F32)], axis=0).astype(BF16)
    blocks = [ref[c].astype(F32) for ref in rights]
    last = first_lane + len(blocks) * rows
    empty = [jnp.zeros((n, tokens), F32) for n in (first_lane, tokens - last)]
    blocks = [block for block in (empty[0], *blocks, empty[1]) if block.shape[0]]
    return dot(left, jnp.concatenate(blocks, axis=0).astype(BF16), NT)


def mix_early(own_ref, got_ref, *refs):
    rights, early_ref = refs[:-1], refs[-1]
    for c in range(own_ref.shape[0]):
        early_ref[c] = gathered_sums(own_ref, got_ref, rights, 0, c).astype(BF16)


def mix_late(early, order_ref, own_ref, got_ref, early_ref, *refs):
    rights, (keep_ref, send_ref, sums_ref) = refs[:-3], refs[-3:]
    count, rows, tokens = own_ref.shape
    for c in range(count):
        sums = gathered_sums(own_ref, got_ref, rights, early * rows, c)
        sums_ref[2 * rows * c : 2 * rows * (c + 1)] = (sums + early_ref[c].astype(F32)).astype(BF16)
    order = order_ref[...]
    group = 16
    for first in range(0, count, group):
        sums = dot(sums_ref[2 * rows * first : 2 * rows * (first + group)], order, NN)
        sums = sums.reshape(group, 2 * rows, tokens)
        keep_ref[first : first + group] = sums[:, :rows].astype(BF16)
        send_ref[first : first + group] = sums[:, rows:].astype(BF16)


def finish_rows(emit, rows, channels, tokens, load, pair_t_ref, gate_t_ref, gain, bias, outw_t, unit_scratch):
    tiles = range(tokens // LANES)
    parts = [slice(first * rows, (first + 16) * rows) for first in range(0, channels, 16)]

    def sums(part):
        return load(part).reshape(16, rows, tokens)

    average = sum(jnp.sum(sums(part), axis=0) for part in parts) * (1.0 / channels)
    spread = sum(jnp.sum(jnp.square(sums(part) - average), axis=0) for part in parts) * (1.0 / channels)
    inverse = lax.rsqrt(spread + 1e-05)
    for part in parts:
        units = ((sums(part) - average) * inverse).reshape(16 * rows, tokens)
        for t in tiles:
            unit_scratch[t, part, :] = units[:, t * LANES : (t + 1) * LANES]
    for chunk in chunks(rows, tokens, 256):
        part = span(chunk, tokens)
        units = lanes([unit_scratch[t, pl.ds(r, channels, stride=rows), :] for r in chunk for t in tiles])
        normed = affine(units, gain, bias, tokens)
        change = gate_t_ref[:, part].astype(F32) * dot(outw_t, normed, NN)
        emit(chunk, part, (pair_t_ref[:, part].astype(F32) + change).astype(BF16))


def step_kernel(per_group, by_core, *refs):
    if not by_core:
        merged_ref, refs = refs[0], refs[1:]
        return step_rows(per_group, lambda part: merged_ref[part].astype(F32), *refs)
    core_ref, refs = refs[0], refs[1:]
    step_rows(per_group, core_halves(core_ref, refs[0], refs[1]), *refs[2:], core_ref=core_ref)


def core_halves(core_ref, keep_ref, got_ref):
    size = keep_ref.shape[0]

    def load(part):
        late = part.start >= size
        part = slice(part.start - size, part.stop - size) if late else part
        keep, got = keep_ref[part].astype(F32), got_ref[part].astype(F32)
        return jnp.where(jnp.full(keep.shape, core_ref[0]) == int(late), keep, got)

    return load


def step_rows(
    per_group, load, pair_t_ref, gate_t_ref, mask_ref, columns_ref, outw_t_ref, proj_t_ref, *refs, core_ref=None
):
    outs, (middle_t_ref, gate1_t_ref, unit_scratch, panels) = refs[:-4], refs[-4:]
    rows, tokens = mask_ref.shape

    def emit(chunk, part, middle):
        middle_t_ref[:, part] = middle
        normed = affine(unit(middle.astype(F32), 0), columns_ref[4], columns_ref[5], tokens)
        products = dot(proj_t_ref[1], normed, NN)
        gate1_t_ref[:, part] = store_panels(
            panels, per_group, rows, chunk, tokens, products, half_lanes(mask_ref, chunk)
        )

    finish_rows(
        emit, rows, pair_t_ref.shape[0], tokens, load, pair_t_ref, gate_t_ref, columns_ref[2], columns_ref[3],
        outw_t_ref[0], unit_scratch,
    )
    if core_ref is None:
        pack_panels(panels, *outs)
    else:
        split_panels(panels, core_ref, *outs)


def finish_kernel(by_core, *refs):
    if by_core:
        load, refs = core_halves(*refs[:3]), refs[3:]
    else:
        merged_ref, refs = refs[0], refs[1:]

        def load(part):
            return merged_ref[part].astype(F32)

    middle_t_ref, gate_t_ref, columns_ref, outw_t_ref, result_ref, unit_scratch, done, sems = refs
    rows, tokens, _ = result_ref.shape
    copies = []

    def emit(chunk, part, result):
        for h, r in enumerate(chunk):
            done[r] = result[:, h * tokens : (h + 1) * tokens].T
            copies.append(pltpu.make_async_copy(done.at[r], result_ref.at[r], sems.at[r]))
            copies[-1].start()

    finish_rows(
        emit, rows, middle_t_ref.shape[0], tokens, load, middle_t_ref, gate_t_ref,
        columns_ref[6], columns_ref[7], outw_t_ref[1], unit_scratch,
    )
    for copy in copies:
        copy.wait()


def scatter_start(first, up, down, order_ref, own_left, got_left, own_right, got_right, sums_ref, up_ref, down_ref):
    rows, tokens = own_left.shape[1:]
    count = sums_ref.shape[0]

    def both(own, got, c):
        return jnp.concatenate([own[first + c].astype(F32), got[first + c].astype(F32)], axis=0).astype(BF16)

    lefts = jnp.concatenate([both(own_left, got_left, c) for c in range(count)], axis=0)
    lefts = dot(lefts, order_ref[...], NT).astype(BF16).reshape(count, 2 * rows, tokens)
    for c in range(count):
        sums_ref[c] = dot(lefts[c], both(own_right, got_right, c), TN)
    for distance, ref in ((up, up_ref), (down, down_ref)):
        ref[...] = at_distance(sums_ref, distance, 2 * rows).astype(BF16)


def at_distance(sums_ref, distance, count):
    return sums_ref[:, distance * count : (distance + 1) * count, :]


def scatter_add(distance, got_ref, sums_ref, out_ref):
    out_ref[...] = (got_ref[...].astype(F32) + at_distance(sums_ref, distance, got_ref.shape[1])).astype(BF16)


def scatter_end(*refs):
    pieces, (keep_ref, send_ref) = refs[:-2], refs[-2:]
    rows = keep_ref.shape[1]
    first = 0
    for n in range(0, len(pieces), 3):
        sums_ref, up_ref, down_ref = pieces[n : n + 3]
        count = sums_ref.shape[0]
        sums = at_distance(sums_ref, 0, 2 * rows) + up_ref[...].astype(F32) + down_ref[...].astype(F32)
        keep_ref[first : first + count] = sums[:, :rows].astype(BF16)
        send_ref[first : first + count] = sums[:, rows:].astype(BF16)
        first += count


def on_device(*inputs):
    groups = lax.axis_size("row")
    rows, tokens, channels = inputs[0].shape
    per_group = channels // groups
    whole = pl.BlockSpec(memory_space=pltpu.VMEM)
    hbm = pl.BlockSpec(memory_space=pltpu.HBM)
    params = pltpu.CompilerParams(vmem_limit_bytes=32 * 1024 * 1024)
    shape = jax.ShapeDtypeStruct
    both_shape = shape((2 * channels * rows, tokens), BF16)
    flat_shape = shape((channels, rows * tokens), BF16)
    panels = pltpu.VMEM((tokens // LANES, 2 * channels * rows, LANES), F32)
    unit_scratch = pltpu.VMEM((tokens // LANES, channels * rows, LANES), F32)

    def exchange(array):
        return lax.all_to_all(array, "row", split_axis=0, concat_axis=0, tiled=True)

    def mix(both, incoming):
        product = pl.pallas_call(
            functools.partial(mix_kernel, per_group, rows, incoming),
            out_shape=shape((groups, per_group * rows, tokens), BF16),
            in_specs=[whole],
            out_specs=whole,
            compiler_params=params,
            name="mix",
        )(both.reshape(groups, 2 * per_group * rows, tokens))
        return product.reshape(channels * rows, tokens)

    half = channels // 2
    by_core = groups % 4 == 0 and groups * rows * tokens * half * 2 <= 4 * 2**20
    smem = pl.BlockSpec(memory_space=pltpu.SMEM)
    core = (lax.axis_index("row") % 2).astype(jnp.int32).reshape(1)
    half_shape = shape((half * rows, tokens), BF16)
    projected = (half_shape,) * 4 if by_core else (both_shape,)
    results = pl.pallas_call(
        functools.partial(project_kernel, half if by_core else per_group, by_core),
        out_shape=projected
        + (
            flat_shape,
            flat_shape,
            shape((rows, tokens), inputs[1].dtype),
            shape((8, channels, tokens), F32),
            shape((2, 5 * channels, channels), BF16),
            shape((2, channels, channels), BF16),
        ),
        in_specs=[smem] * by_core + [hbm] * 7,
        out_specs=(whole,) * (len(projected) + 6),
        scratch_shapes=[pltpu.VMEM(inputs[n].shape, inputs[n].dtype) for n in (0, 2, 3, 4, 5, 6)]
        + [panels, pltpu.SemaphoreType.DMA((7,))],
        compiler_params=params,
        name="project",
    )(*[core] * by_core, *(pltpu.with_memory_space_constraint(a, pltpu.HBM) for a in inputs))
    pair_t, gate_t, mask, columns, proj_t, outw_t = results[-6:]
    if by_core:
        left, right, other_left, other_right = results[:4]
        chips = groups // 2
        ring = ring_chips(chips)

        def along(array, step):
            pairs = [(2 * q + c, 2 * ring[(p + step) % chips] + c) for p, q in enumerate(ring) for c in range(2)]
            return lax.ppermute(array, "row", pairs)

        def rounds(array, step, count):
            arrays = [array]
            for _ in range(count):
                arrays.append(along(arrays[-1], step))
            return arrays

        swap = [(d, d ^ 1) for d in range(groups)]
        got_right = lax.ppermute(other_right, "row", swap)
        got_left = lax.ppermute(other_left, "row", swap)
        middle = chips // 2
        ups = [rounds(right, 1, middle), rounds(got_right, 1, middle - 1)]
        downs = [rounds(right, -1, middle - 1), rounds(got_right, -1, middle)]
        distances = sorted(range(chips), key=lambda d: min(d, chips - d))
        early = 2 * (chips // 2 + 1)
        rights = [
            ups[piece][d] if d < len(ups[piece]) else downs[piece][chips - d] for d in distances for piece in range(2)
        ]
        rights = [array.reshape(half, rows, tokens) for array in rights]
        lefts = [array.reshape(half, rows, tokens) for array in (left, got_left)]
        first_sums = pl.pallas_call(
            mix_early,
            out_shape=shape((half, 2 * rows, tokens), BF16),
            in_specs=[whole] * (2 + early),
            out_specs=whole,
            compiler_params=params,
            cost_estimate=pl.CostEstimate(flops=10**9, bytes_accessed=4 * 2**20, transcendentals=0),
            name="mix_early",
        )(*lefts, *rights[:early])
        keep, send = pl.pallas_call(
            functools.partial(mix_late, early),
            out_shape=(shape((half, rows, tokens), BF16),) * 2,
            in_specs=[whole] * (4 + len(rights) - early),
            out_specs=(whole,) * 2,
            scratch_shapes=[pltpu.VMEM((2 * half * rows, tokens), BF16)],
            compiler_params=params,
            name="mix_late",
        )(token_order(chips, distances, rows), *lefts, first_sums, *rights[early:])
        merged = (core, keep.reshape(half * rows, tokens), lax.ppermute(send, "row", swap).reshape(half * rows, tokens))
    else:
        merged = (exchange(mix(exchange(results[0]), False)),)
    results = pl.pallas_call(
        functools.partial(step_kernel, half if by_core else per_group, by_core),
        out_shape=projected + (flat_shape, flat_shape),
        in_specs=[smem] * by_core + [whole] * (len(merged) - by_core + 6),
        out_specs=(whole,) * (len(projected) + 2),
        scratch_shapes=[unit_scratch, panels],
        compiler_params=params,
        name="finish_project",
    )(*merged, pair_t, gate_t, mask, columns, outw_t, proj_t)
    middle_t, gate_t = results[-2:]
    if by_core:
        left, right, other_left, other_right = results[:4]
        got_left = lax.ppermute(other_left, "row", swap)
        got_right = lax.ppermute(other_right, "row", swap)
        operands = [array.reshape(half, rows, tokens) for array in (left, got_left, right, got_right)]
        order = token_order(chips, [-d % chips for d in range(chips)], rows)
        size = half // 2
        part_shape = shape((size, 2 * rows, tokens), BF16)
        pieces = []
        for piece in range(2):
            hops = (middle, middle - 1) if piece == 0 else (middle - 1, middle)
            sums, *travelling = pl.pallas_call(
                functools.partial(scatter_start, piece * size, hops[0], chips - hops[1]),
                out_shape=(shape((size, tokens, tokens), F32), part_shape, part_shape),
                in_specs=[whole] * 5,
                out_specs=(whole,) * 3,
                compiler_params=params,
                name="scatter_start",
            )(order, *operands)
            for way, (step, count) in enumerate(zip((1, -1), hops)):
                for left_over in reversed(range(count)):
                    travelling[way] = along(travelling[way], step)
                    if left_over:
                        travelling[way] = pl.pallas_call(
                            functools.partial(scatter_add, step * left_over % chips),
                            out_shape=part_shape,
                            in_specs=[whole] * 2,
                            out_specs=whole,
                            compiler_params=params,
                            name="scatter_add",
                        )(travelling[way], sums)
            pieces += [sums, *travelling]
        keep, send = pl.pallas_call(
            scatter_end,
            out_shape=(shape((half, rows, tokens), BF16),) * 2,
            in_specs=[whole] * len(pieces),
            out_specs=(whole,) * 2,
            compiler_params=params,
            name="scatter_end",
        )(*pieces)
        merged = (core, keep.reshape(half * rows, tokens), lax.ppermute(send, "row", swap).reshape(half * rows, tokens))
    else:
        merged = (exchange(mix(exchange(results[0]), True)),)
    return pl.pallas_call(
        functools.partial(finish_kernel, by_core),
        out_shape=shape((rows, tokens, channels), BF16),
        in_specs=[smem] * by_core + [whole] * (len(merged) - by_core + 4),
        out_specs=hbm,
        scratch_shapes=[unit_scratch, pltpu.VMEM((rows, tokens, channels), BF16), pltpu.SemaphoreType.DMA((rows,))],
        compiler_params=params,
        name="finish",
    )(*merged, middle_t, gate_t, columns, outw_t)


def solution(mesh):
    rows = ("groups", "row")
    return jax.shard_map(
        on_device,
        mesh=mesh,
        in_specs=(P(rows, None, None), P(rows, None), P(), P(), P(), P(), P()),
        out_specs=P(rows, None, None),
        check_vma=False,
    )
```

```python
import functools

import jax
import jax.numpy as jnp
from jax import lax
from jax.experimental import pallas as pl
from jax.experimental.pallas import tpu as pltpu
from jax.sharding import PartitionSpec as P

F32 = jnp.float32
BF16 = jnp.bfloat16
LANES = 128
NT = (((1,), (1,)), ((), ()))
NN = (((1,), (0,)), ((), ()))
TN = (((0,), (0,)), ((), ()))


def dot(a, b, dims):
    return lax.dot_general(a, b, dims, preferred_element_type=F32)


def unit(values, axis):
    scale = 1.0 / values.shape[axis]
    centred = values - jnp.sum(values, axis=axis, keepdims=True) * scale
    spread = jnp.sum(centred * centred, axis=axis, keepdims=True) * scale
    return centred * lax.rsqrt(spread + 1e-05)


def chunks(rows, tokens, limit):
    wide = max(1, min(rows, limit // tokens))
    return [list(range(start, min(start + wide, rows))) for start in range(0, rows, wide)]


def span(chunk, tokens):
    return slice(chunk[0] * tokens, (chunk[-1] + 1) * tokens)


def lanes(parts):
    return parts[0] if len(parts) == 1 else jnp.concatenate(parts, axis=1)


def affine(values, gain, bias, tokens):
    parts = [values[:, n : n + tokens] * gain + bias for n in range(0, values.shape[1], tokens)]
    return lanes(parts).astype(BF16)


def store_panels(panels, per_group, rows, chunk, tokens, products, half_mask):
    channels = products.shape[0] // 5
    for side in range(2):
        base = 2 * side * channels
        gate, value = products[base : base + channels], products[base + channels : base + 2 * channels]
        gated = (jnp.tanh(gate) + 1.0) * (value * half_mask)
        for h, r in enumerate(chunk):
            for g in range(channels // per_group):
                where = pl.ds((2 * g + side) * per_group * rows + r, per_group, stride=rows)
                for t in range(tokens // LANES):
                    first = h * tokens + t * LANES
                    panels[t, where, :] = gated[g * per_group : (g + 1) * per_group, first : first + LANES]
    return (0.5 * jnp.tanh(products[4 * channels :]) + 0.5).astype(BF16)


def pack_panels(panels, both_ref):
    for t in range(both_ref.shape[1] // LANES):
        both_ref[:, t * LANES : (t + 1) * LANES] = panels[t].astype(BF16)


def split_panels(panels, core_ref, left_ref, right_ref, other_left_ref, other_right_ref):
    size = left_ref.shape[0]
    core = core_ref[0]
    for t in range(left_ref.shape[1] // LANES):
        for side, (own_ref, other_ref) in enumerate(((left_ref, other_left_ref), (right_ref, other_right_ref))):
            for group, ref in ((core, own_ref), (1 - core, other_ref)):
                start = pl.multiple_of((2 * group + side) * size, size)
                ref[:, t * LANES : (t + 1) * LANES] = panels[t, pl.ds(start, size), :].astype(BF16)


def half_lanes(mask_ref, chunk):
    return lanes([mask_ref[r : r + 1].astype(F32) * 0.5 for r in chunk])


def project_kernel(per_group, by_core, *refs):
    core_ref, refs = (refs[0], refs[1:]) if by_core else (None, refs)
    inputs, refs = refs[:7], refs[7:]
    if by_core:
        outs, refs = refs[:4], refs[4:]
        both_ref = None
    else:
        both_ref, refs = refs[0], refs[1:]
    pair_t_ref, gate_t_ref, mask_ref, columns_ref, proj_t_ref, outw_t_ref = refs[:6]
    pair_ref, gain_ref, bias_ref, proj_ref, gatew_ref, outw_ref, panels, sems = refs[6:]
    held = (pair_ref, mask_ref, gain_ref, bias_ref, proj_ref, gatew_ref, outw_ref)
    copies = [pltpu.make_async_copy(src, dst, sems.at[n]) for n, (src, dst) in enumerate(zip(inputs, held))]
    for copy in copies:
        copy.start()
    for copy in copies:
        copy.wait()
    rows, tokens, channels = pair_ref.shape
    small = jnp.concatenate([ref[which] for ref in (gain_ref, bias_ref) for which in range(2)], axis=0).T
    for n in range(4):
        for side in range(2):
            place = 4 * side + n
            columns_ref[2 * n + side] = jnp.broadcast_to(small[:, place : place + 1], (channels, tokens))
    for which in range(2):
        for part in range(4):
            block = proj_ref[which, :, part * channels : (part + 1) * channels].T
            proj_t_ref[which, part * channels : (part + 1) * channels] = block if part % 2 else block * 0.5
        proj_t_ref[which, 4 * channels :] = gatew_ref[which].T * 0.5
        outw_t_ref[which] = outw_ref[which].T
    for chunk in chunks(rows, tokens, 256):
        part = span(chunk, tokens)
        pair_t = lanes([pair_ref[r].T for r in chunk])
        pair_t_ref[:, part] = pair_t
        normed = affine(unit(pair_t.astype(F32), 0), columns_ref[0], columns_ref[1], tokens)
        products = dot(proj_t_ref[0], normed, NN)
        gate_t_ref[:, part] = store_panels(
            panels, per_group, rows, chunk, tokens, products, half_lanes(mask_ref, chunk)
        )
    if by_core:
        split_panels(panels, core_ref, *outs)
    else:
        pack_panels(panels, both_ref)


def mix_kernel(per_group, rows, incoming, both_ref, product_ref):
    groups, _, tokens = both_ref.shape
    step = 2 * rows

    def matrices(side, pair):
        start = (side * per_group + 2 * pair) * rows
        block = both_ref[:, start : start + step, :].astype(F32)
        return [block[:, h * rows : (h + 1) * rows].reshape(groups * rows, tokens).astype(BF16) for h in range(2)]

    for pair in range(per_group // 2):
        lefts, rights = matrices(0, pair), matrices(1, pair)
        sums = [
            dot(left, right, TN if incoming else NT).reshape(groups, rows, tokens)
            for left, right in zip(lefts, rights)
        ]
        product_ref[:, pair * step : (pair + 1) * step, :] = jnp.concatenate(sums, axis=1).astype(BF16)


def ring_chips(count):
    return list(range(0, count, 2)) + list(range(count - 1, 0, -2))


def token_order(chips, distances, rows):
    device = lax.axis_index("row")
    chip, core = device // 2, device % 2
    place = jnp.where(chip % 2 == 0, chip // 2, chips - 1 - chip // 2)
    size = 2 * chips * rows
    lane, token = (lax.broadcasted_iota(jnp.int32, (size, size), axis) for axis in range(2))
    first = jnp.zeros((size, size), jnp.int32)
    for n, d in enumerate(distances):
        source = place - d + jnp.where(place < d, chips, 0)
        source = jnp.where(2 * source < chips, 2 * source, 2 * (chips - 1 - source) + 1)
        for piece in range(2):
            start = (2 * n + piece) * rows
            block = 2 * source + (1 - core if piece else core)
            first = jnp.where((lane >= start) & (lane < start + rows), block * rows - start, first)
    return (token == lane + first).astype(BF16)


def joined(own_ref, got_ref, c):
    return jnp.concatenate([own_ref[c].astype(F32), got_ref[c].astype(F32)], axis=0).astype(BF16)


def join_kernel(own_ref, got_ref, block_ref):
    for c in range(own_ref.shape[0]):
        block_ref[c] = joined(own_ref, got_ref, c)


def gathered_sums(left, blocks, first):
    count, tokens = blocks[0].shape
    empty = [jnp.zeros((n * count, tokens), BF16) for n in (first, tokens // count - first - len(blocks))]
    blocks = [block for block in (empty[0], *blocks, empty[1]) if block.shape[0]]
    return dot(left, jnp.concatenate(blocks, axis=0), NT)


def mix_early(own_ref, got_ref, *refs):
    rights, early_ref = refs[:-1], refs[-1]
    for c in range(own_ref.shape[0]):
        sums = gathered_sums(joined(own_ref, got_ref, c), [ref[c] for ref in rights], 0)
        early_ref[c] = sums.astype(BF16)


def mix_late(early, order_ref, own_ref, got_ref, early_ref, *refs):
    rights, halves, (keep_ref, send_ref, sums_ref) = refs[:-5], refs[-5:-3], refs[-3:]
    count, rows, tokens = own_ref.shape
    size = count // 2
    for c in range(count):
        blocks = [ref[c] for ref in rights] + [halves[c // size][c % size]]
        sums = gathered_sums(joined(own_ref, got_ref, c), blocks, early)
        sums_ref[2 * rows * c : 2 * rows * (c + 1)] = (sums + early_ref[c].astype(F32)).astype(BF16)
    order = order_ref[...]
    group = 16
    for first in range(0, count, group):
        sums = dot(sums_ref[2 * rows * first : 2 * rows * (first + group)], order, NN)
        sums = sums.reshape(group, 2 * rows, tokens)
        keep_ref[first : first + group] = sums[:, :rows].astype(BF16)
        send_ref[first : first + group] = sums[:, rows:].astype(BF16)


def finish_rows(emit, rows, channels, tokens, load, pair_t_ref, gate_t_ref, gain, bias, outw_t, unit_scratch):
    tiles = range(tokens // LANES)
    parts = [slice(first * rows, (first + 16) * rows) for first in range(0, channels, 16)]

    def sums(part):
        return load(part).reshape(16, rows, tokens)

    average = sum(jnp.sum(sums(part), axis=0) for part in parts) * (1.0 / channels)
    spread = sum(jnp.sum(jnp.square(sums(part) - average), axis=0) for part in parts) * (1.0 / channels)
    inverse = lax.rsqrt(spread + 1e-05)
    for part in parts:
        units = ((sums(part) - average) * inverse).reshape(16 * rows, tokens)
        for t in tiles:
            unit_scratch[t, part, :] = units[:, t * LANES : (t + 1) * LANES]
    for chunk in chunks(rows, tokens, 256):
        part = span(chunk, tokens)
        units = lanes([unit_scratch[t, pl.ds(r, channels, stride=rows), :] for r in chunk for t in tiles])
        normed = affine(units, gain, bias, tokens)
        change = gate_t_ref[:, part].astype(F32) * dot(outw_t, normed, NN)
        emit(chunk, part, (pair_t_ref[:, part].astype(F32) + change).astype(BF16))


def step_kernel(per_group, by_core, *refs):
    if not by_core:
        merged_ref, refs = refs[0], refs[1:]
        return step_rows(per_group, lambda part: merged_ref[part].astype(F32), *refs)
    core_ref, refs = refs[0], refs[1:]
    step_rows(per_group, core_halves(core_ref, refs[0], refs[1]), *refs[2:], core_ref=core_ref)


def core_halves(core_ref, keep_ref, got_ref):
    size = keep_ref.shape[0]

    def load(part):
        late = part.start >= size
        part = slice(part.start - size, part.stop - size) if late else part
        keep, got = keep_ref[part].astype(F32), got_ref[part].astype(F32)
        return jnp.where(jnp.full(keep.shape, core_ref[0]) == int(late), keep, got)

    return load


def step_rows(
    per_group, load, pair_t_ref, gate_t_ref, mask_ref, columns_ref, outw_t_ref, proj_t_ref, *refs, core_ref=None
):
    outs, (middle_t_ref, gate1_t_ref, unit_scratch, panels) = refs[:-4], refs[-4:]
    rows, tokens = mask_ref.shape

    def emit(chunk, part, middle):
        middle_t_ref[:, part] = middle
        normed = affine(unit(middle.astype(F32), 0), columns_ref[4], columns_ref[5], tokens)
        products = dot(proj_t_ref[1], normed, NN)
        gate1_t_ref[:, part] = store_panels(
            panels, per_group, rows, chunk, tokens, products, half_lanes(mask_ref, chunk)
        )

    finish_rows(
        emit, rows, pair_t_ref.shape[0], tokens, load, pair_t_ref, gate_t_ref, columns_ref[2], columns_ref[3],
        outw_t_ref[0], unit_scratch,
    )
    if core_ref is None:
        pack_panels(panels, *outs)
    else:
        split_panels(panels, core_ref, *outs)


def finish_kernel(by_core, *refs):
    if by_core:
        load, refs = core_halves(*refs[:3]), refs[3:]
    else:
        merged_ref, refs = refs[0], refs[1:]

        def load(part):
            return merged_ref[part].astype(F32)

    middle_t_ref, gate_t_ref, columns_ref, outw_t_ref, result_ref, unit_scratch, done, sems = refs
    rows, tokens, _ = result_ref.shape
    copies = []

    def emit(chunk, part, result):
        for h, r in enumerate(chunk):
            done[r] = result[:, h * tokens : (h + 1) * tokens].T
            copies.append(pltpu.make_async_copy(done.at[r], result_ref.at[r], sems.at[r]))
            copies[-1].start()

    finish_rows(
        emit, rows, middle_t_ref.shape[0], tokens, load, middle_t_ref, gate_t_ref,
        columns_ref[6], columns_ref[7], outw_t_ref[1], unit_scratch,
    )
    for copy in copies:
        copy.wait()


def scatter_start(first, distance, order_ref, own_left, got_left, own_right, got_right, sums_ref, far_ref):
    rows, tokens = own_left.shape[1:]
    count = sums_ref.shape[0]
    lefts = jnp.concatenate([joined(own_left, got_left, first + c) for c in range(count)], axis=0)
    lefts = dot(lefts, order_ref[...], NT).astype(BF16).reshape(count, 2 * rows, tokens)
    for c in range(count):
        sums_ref[c] = dot(lefts[c], joined(own_right, got_right, first + c), TN)
    far_ref[...] = at_distance(sums_ref, distance, 2 * rows).astype(BF16)


def at_distance(sums_ref, distance, count):
    return sums_ref[:, distance * count : (distance + 1) * count, :]


def scatter_add(distance, half, got_ref, *refs):
    sums_refs, out_ref = refs[:-1], refs[-1]
    size = sums_refs[0].shape[0]
    for n, sums_ref in enumerate(sums_refs):
        sums = at_distance(sums_ref, distance, out_ref.shape[1])
        if half is None:
            sums = sums + got_ref[n * size : (n + 1) * size].astype(F32)
        elif half == n:
            sums = sums + got_ref[...].astype(F32)
        out_ref[n * size : (n + 1) * size] = sums.astype(BF16)


def scatter_end(up_ref, down_ref, *refs):
    sums_refs, (keep_ref, send_ref) = refs[:-2], refs[-2:]
    rows = keep_ref.shape[1]
    size = sums_refs[0].shape[0]
    for n, sums_ref in enumerate(sums_refs):
        part = slice(n * size, (n + 1) * size)
        sums = at_distance(sums_ref, 0, 2 * rows) + up_ref[part].astype(F32) + down_ref[part].astype(F32)
        keep_ref[part] = sums[:, :rows].astype(BF16)
        send_ref[part] = sums[:, rows:].astype(BF16)


def on_device(*inputs):
    groups = lax.axis_size("row")
    rows, tokens, channels = inputs[0].shape
    per_group = channels // groups
    whole = pl.BlockSpec(memory_space=pltpu.VMEM)
    hbm = pl.BlockSpec(memory_space=pltpu.HBM)
    params = pltpu.CompilerParams(vmem_limit_bytes=32 * 1024 * 1024)
    shape = jax.ShapeDtypeStruct
    both_shape = shape((2 * channels * rows, tokens), BF16)
    flat_shape = shape((channels, rows * tokens), BF16)
    panels = pltpu.VMEM((tokens // LANES, 2 * channels * rows, LANES), F32)
    unit_scratch = pltpu.VMEM((tokens // LANES, channels * rows, LANES), F32)

    def exchange(array):
        return lax.all_to_all(array, "row", split_axis=0, concat_axis=0, tiled=True)

    def mix(both, incoming):
        product = pl.pallas_call(
            functools.partial(mix_kernel, per_group, rows, incoming),
            out_shape=shape((groups, per_group * rows, tokens), BF16),
            in_specs=[whole],
            out_specs=whole,
            compiler_params=params,
            name="mix",
        )(both.reshape(groups, 2 * per_group * rows, tokens))
        return product.reshape(channels * rows, tokens)

    half = channels // 2
    by_core = groups % 4 == 0 and groups * rows * tokens * half * 2 <= 4 * 2**20
    smem = pl.BlockSpec(memory_space=pltpu.SMEM)
    core = (lax.axis_index("row") % 2).astype(jnp.int32).reshape(1)
    half_shape = shape((half * rows, tokens), BF16)
    projected = (half_shape,) * 4 if by_core else (both_shape,)
    results = pl.pallas_call(
        functools.partial(project_kernel, half if by_core else per_group, by_core),
        out_shape=projected
        + (
            flat_shape,
            flat_shape,
            shape((rows, tokens), inputs[1].dtype),
            shape((8, channels, tokens), F32),
            shape((2, 5 * channels, channels), BF16),
            shape((2, channels, channels), BF16),
        ),
        in_specs=[smem] * by_core + [hbm] * 7,
        out_specs=(whole,) * (len(projected) + 6),
        scratch_shapes=[pltpu.VMEM(inputs[n].shape, inputs[n].dtype) for n in (0, 2, 3, 4, 5, 6)]
        + [panels, pltpu.SemaphoreType.DMA((7,))],
        compiler_params=params,
        name="project",
    )(*[core] * by_core, *(pltpu.with_memory_space_constraint(a, pltpu.HBM) for a in inputs))
    pair_t, gate_t, mask, columns, proj_t, outw_t = results[-6:]
    if by_core:
        left, right, other_left, other_right = results[:4]
        chips = groups // 2
        ring = ring_chips(chips)

        def along(array, step):
            pairs = [(2 * q + c, 2 * ring[(p + step) % chips] + c) for p, q in enumerate(ring) for c in range(2)]
            return lax.ppermute(array, "row", pairs)

        def rounds(array, step, count):
            arrays = [array]
            for _ in range(count):
                arrays.append(along(arrays[-1], step))
            return arrays

        swap = [(d, d ^ 1) for d in range(groups)]
        got_right = lax.ppermute(other_right, "row", swap)
        got_left = lax.ppermute(other_left, "row", swap)
        middle = chips // 2
        size = half // 2
        block_shape = shape((half, 2 * rows, tokens), BF16)
        lefts = [array.reshape(half, rows, tokens) for array in (left, got_left)]
        block = pl.pallas_call(
            join_kernel,
            out_shape=block_shape,
            in_specs=[whole] * 2,
            out_specs=whole,
            compiler_params=params,
            name="join",
        )(right.reshape(half, rows, tokens), got_right.reshape(half, rows, tokens))
        ups, downs = rounds(block, 1, middle - 1), rounds(block, -1, middle - 1)
        halves = [along(ups[-1][:size], 1), along(downs[-1][size:], -1)]
        distances = sorted(range(chips), key=lambda d: min(d, chips - d))
        early = middle + 1
        rights = [ups[d] if d < middle else downs[chips - d] for d in distances[:-1]]
        first_sums = pl.pallas_call(
            mix_early,
            out_shape=block_shape,
            in_specs=[whole] * (2 + early),
            out_specs=whole,
            compiler_params=params,
            cost_estimate=pl.CostEstimate(flops=10**9, bytes_accessed=4 * 2**20, transcendentals=0),
            name="mix_early",
        )(*lefts, *rights[:early])
        keep, send = pl.pallas_call(
            functools.partial(mix_late, early),
            out_shape=(shape((half, rows, tokens), BF16),) * 2,
            in_specs=[whole] * (6 + len(rights) - early),
            out_specs=(whole,) * 2,
            scratch_shapes=[pltpu.VMEM((2 * half * rows, tokens), BF16)],
            compiler_params=params,
            name="mix_late",
        )(token_order(chips, distances, rows), *lefts, first_sums, *rights[early:], *halves)
        merged = (core, keep.reshape(half * rows, tokens), lax.ppermute(send, "row", swap).reshape(half * rows, tokens))
    else:
        merged = (exchange(mix(exchange(results[0]), False)),)
    results = pl.pallas_call(
        functools.partial(step_kernel, half if by_core else per_group, by_core),
        out_shape=projected + (flat_shape, flat_shape),
        in_specs=[smem] * by_core + [whole] * (len(merged) - by_core + 6),
        out_specs=(whole,) * (len(projected) + 2),
        scratch_shapes=[unit_scratch, panels],
        compiler_params=params,
        name="finish_project",
    )(*merged, pair_t, gate_t, mask, columns, outw_t, proj_t)
    middle_t, gate_t = results[-2:]
    if by_core:
        left, right, other_left, other_right = results[:4]
        got_left = lax.ppermute(other_left, "row", swap)
        got_right = lax.ppermute(other_right, "row", swap)
        operands = [array.reshape(half, rows, tokens) for array in (left, got_left, right, got_right)]
        order = token_order(chips, [-d % chips for d in range(chips)], rows)
        sums, far = [], []
        for piece in range(2):
            part = pl.pallas_call(
                functools.partial(scatter_start, piece * size, middle),
                out_shape=(shape((size, tokens, tokens), F32), shape((size, 2 * rows, tokens), BF16)),
                in_specs=[whole] * 5,
                out_specs=(whole,) * 2,
                compiler_params=params,
                name="scatter_start",
            )(order, *operands)
            sums.append(part[0])
            far.append(part[1])
        for piece, step in enumerate((1, -1)):
            for left_over in reversed(range(middle)):
                far[piece] = along(far[piece], step)
                if left_over:
                    far[piece] = pl.pallas_call(
                        functools.partial(
                            scatter_add, step * left_over % chips, piece if left_over == middle - 1 else None
                        ),
                        out_shape=block_shape,
                        in_specs=[whole] * 3,
                        out_specs=whole,
                        compiler_params=params,
                        name="scatter_add",
                    )(far[piece], *sums)
        pieces = (*far, *sums)
        keep, send = pl.pallas_call(
            scatter_end,
            out_shape=(shape((half, rows, tokens), BF16),) * 2,
            in_specs=[whole] * len(pieces),
            out_specs=(whole,) * 2,
            compiler_params=params,
            name="scatter_end",
        )(*pieces)
        merged = (core, keep.reshape(half * rows, tokens), lax.ppermute(send, "row", swap).reshape(half * rows, tokens))
    else:
        merged = (exchange(mix(exchange(results[0]), True)),)
    return pl.pallas_call(
        functools.partial(finish_kernel, by_core),
        out_shape=shape((rows, tokens, channels), BF16),
        in_specs=[smem] * by_core + [whole] * (len(merged) - by_core + 4),
        out_specs=hbm,
        scratch_shapes=[unit_scratch, pltpu.VMEM((rows, tokens, channels), BF16), pltpu.SemaphoreType.DMA((rows,))],
        compiler_params=params,
        name="finish",
    )(*merged, middle_t, gate_t, columns, outw_t)


def solution(mesh):
    rows = ("groups", "row")
    return jax.shard_map(
        on_device,
        mesh=mesh,
        in_specs=(P(rows, None, None), P(rows, None), P(), P(), P(), P(), P()),
        out_specs=P(rows, None, None),
        check_vma=False,
    )
```

```python
import functools

import jax
import jax.numpy as jnp
from jax import lax
from jax.experimental import pallas as pl
from jax.experimental.pallas import tpu as pltpu
from jax.sharding import PartitionSpec as P

F32 = jnp.float32
BF16 = jnp.bfloat16
LANES = 128
NT = (((1,), (1,)), ((), ()))
NN = (((1,), (0,)), ((), ()))
TN = (((0,), (0,)), ((), ()))


def dot(a, b, dims):
    return lax.dot_general(a, b, dims, preferred_element_type=F32)


def unit(values, axis):
    scale = 1.0 / values.shape[axis]
    centred = values - jnp.sum(values, axis=axis, keepdims=True) * scale
    spread = jnp.sum(centred * centred, axis=axis, keepdims=True) * scale
    return centred * lax.rsqrt(spread + 1e-05)


def chunks(rows, tokens, limit):
    wide = max(1, min(rows, limit // tokens))
    return [list(range(start, min(start + wide, rows))) for start in range(0, rows, wide)]


def span(chunk, tokens):
    return slice(chunk[0] * tokens, (chunk[-1] + 1) * tokens)


def lanes(parts):
    return parts[0] if len(parts) == 1 else jnp.concatenate(parts, axis=1)


def affine(values, gain, bias, tokens):
    parts = [values[:, n : n + tokens] * gain + bias for n in range(0, values.shape[1], tokens)]
    return lanes(parts).astype(BF16)


def store_panels(panels, per_group, rows, chunk, tokens, products, half_mask):
    channels = products.shape[0] // 5
    for side in range(2):
        base = 2 * side * channels
        gate, value = products[base : base + channels], products[base + channels : base + 2 * channels]
        gated = (jnp.tanh(gate) + 1.0) * (value * half_mask)
        for h, r in enumerate(chunk):
            for g in range(channels // per_group):
                where = pl.ds((2 * g + side) * per_group * rows + r, per_group, stride=rows)
                for t in range(tokens // LANES):
                    first = h * tokens + t * LANES
                    panels[t, where, :] = gated[g * per_group : (g + 1) * per_group, first : first + LANES]
    return (0.5 * jnp.tanh(products[4 * channels :]) + 0.5).astype(BF16)


def pack_panels(panels, both_ref):
    for t in range(both_ref.shape[1] // LANES):
        both_ref[:, t * LANES : (t + 1) * LANES] = panels[t].astype(BF16)


def split_panels(panels, core_ref, left_ref, right_ref, other_left_ref, other_right_ref):
    size = left_ref.shape[0]
    core = core_ref[0]
    for t in range(left_ref.shape[1] // LANES):
        for side, (own_ref, other_ref) in enumerate(((left_ref, other_left_ref), (right_ref, other_right_ref))):
            for group, ref in ((core, own_ref), (1 - core, other_ref)):
                start = pl.multiple_of((2 * group + side) * size, size)
                ref[:, t * LANES : (t + 1) * LANES] = panels[t, pl.ds(start, size), :].astype(BF16)


def half_lanes(mask_ref, chunk):
    return lanes([mask_ref[r : r + 1].astype(F32) * 0.5 for r in chunk])


def project_kernel(per_group, by_core, *refs):
    core_ref, refs = (refs[0], refs[1:]) if by_core else (None, refs)
    inputs, refs = refs[:7], refs[7:]
    if by_core:
        outs, refs = refs[:4], refs[4:]
        both_ref = None
    else:
        both_ref, refs = refs[0], refs[1:]
    pair_t_ref, gate_t_ref, mask_ref, columns_ref, proj_t_ref, outw_t_ref = refs[:6]
    pair_ref, gain_ref, bias_ref, proj_ref, gatew_ref, outw_ref, panels, sems = refs[6:]
    held = (pair_ref, mask_ref, gain_ref, bias_ref, proj_ref, gatew_ref, outw_ref)
    copies = [pltpu.make_async_copy(src, dst, sems.at[n]) for n, (src, dst) in enumerate(zip(inputs, held))]
    for copy in copies:
        copy.start()
    for copy in copies:
        copy.wait()
    rows, tokens, channels = pair_ref.shape
    small = jnp.concatenate([ref[which] for ref in (gain_ref, bias_ref) for which in range(2)], axis=0).T
    for n in range(4):
        for side in range(2):
            place = 4 * side + n
            columns_ref[2 * n + side] = jnp.broadcast_to(small[:, place : place + 1], (channels, tokens))
    for which in range(2):
        for part in range(4):
            block = proj_ref[which, :, part * channels : (part + 1) * channels].T
            proj_t_ref[which, part * channels : (part + 1) * channels] = block if part % 2 else block * 0.5
        proj_t_ref[which, 4 * channels :] = gatew_ref[which].T * 0.5
        outw_t_ref[which] = outw_ref[which].T
    for chunk in chunks(rows, tokens, 256):
        part = span(chunk, tokens)
        pair_t = lanes([pair_ref[r].T for r in chunk])
        pair_t_ref[:, part] = pair_t
        normed = affine(unit(pair_t.astype(F32), 0), columns_ref[0], columns_ref[1], tokens)
        products = dot(proj_t_ref[0], normed, NN)
        gate_t_ref[:, part] = store_panels(
            panels, per_group, rows, chunk, tokens, products, half_lanes(mask_ref, chunk)
        )
    if by_core:
        split_panels(panels, core_ref, *outs)
    else:
        pack_panels(panels, both_ref)


def mix_kernel(per_group, rows, incoming, both_ref, product_ref):
    groups, _, tokens = both_ref.shape
    step = 2 * rows

    def matrices(side, pair):
        start = (side * per_group + 2 * pair) * rows
        block = both_ref[:, start : start + step, :].astype(F32)
        return [block[:, h * rows : (h + 1) * rows].reshape(groups * rows, tokens).astype(BF16) for h in range(2)]

    for pair in range(per_group // 2):
        lefts, rights = matrices(0, pair), matrices(1, pair)
        sums = [
            dot(left, right, TN if incoming else NT).reshape(groups, rows, tokens)
            for left, right in zip(lefts, rights)
        ]
        product_ref[:, pair * step : (pair + 1) * step, :] = jnp.concatenate(sums, axis=1).astype(BF16)


def ring_chips(count):
    return list(range(0, count, 2)) + list(range(count - 1, 0, -2))


def token_order(chips, distances, rows):
    device = lax.axis_index("row")
    chip, core = device // 2, device % 2
    place = jnp.where(chip % 2 == 0, chip // 2, chips - 1 - chip // 2)
    extent = (2 * len(distances) * rows, 2 * chips * rows)
    lane, token = (lax.broadcasted_iota(jnp.int32, extent, axis) for axis in range(2))
    first = jnp.zeros(extent, jnp.int32)
    for n, d in enumerate(distances):
        source = place - d + jnp.where(place < d, chips, 0)
        source = jnp.where(2 * source < chips, 2 * source, 2 * (chips - 1 - source) + 1)
        for piece in range(2):
            start = (2 * n + piece) * rows
            block = 2 * source + (1 - core if piece else core)
            first = jnp.where((lane >= start) & (lane < start + rows), block * rows - start, first)
    return (token == lane + first).astype(BF16)


def gathered_sums(order_ref, own_ref, got_ref, rights, sums_ref):
    count, rows, tokens = own_ref.shape
    for c in range(count):
        left = jnp.concatenate([own_ref[c].astype(F32), got_ref[c].astype(F32)], axis=0).astype(BF16)
        right = jnp.concatenate([ref[c].astype(F32) for ref in rights], axis=0).astype(BF16)
        sums_ref[2 * rows * c : 2 * rows * (c + 1)] = dot(left, right, NT).astype(BF16)
    order = order_ref[...]
    group = 16
    for first in range(0, count, group):
        sums = dot(sums_ref[2 * rows * first : 2 * rows * (first + group)], order, NN)
        yield slice(first, first + group), sums.reshape(group, 2 * rows, tokens)


def mix_early(order_ref, own_ref, got_ref, *refs):
    rights, (early_ref, sums_ref) = refs[:-2], refs[-2:]
    for part, sums in gathered_sums(order_ref, own_ref, got_ref, rights, sums_ref):
        early_ref[part] = sums.astype(BF16)


def mix_late(order_ref, own_ref, got_ref, early_ref, *refs):
    rights, (keep_ref, send_ref, sums_ref) = refs[:-3], refs[-3:]
    rows = own_ref.shape[1]
    for part, sums in gathered_sums(order_ref, own_ref, got_ref, rights, sums_ref):
        sums = sums + early_ref[part].astype(F32)
        keep_ref[part] = sums[:, :rows].astype(BF16)
        send_ref[part] = sums[:, rows:].astype(BF16)


def finish_rows(emit, rows, channels, tokens, load, pair_t_ref, gate_t_ref, gain, bias, outw_t, unit_scratch):
    tiles = range(tokens // LANES)
    parts = [slice(first * rows, (first + 16) * rows) for first in range(0, channels, 16)]

    def sums(part):
        return load(part).reshape(16, rows, tokens)

    average = sum(jnp.sum(sums(part), axis=0) for part in parts) * (1.0 / channels)
    spread = sum(jnp.sum(jnp.square(sums(part) - average), axis=0) for part in parts) * (1.0 / channels)
    inverse = lax.rsqrt(spread + 1e-05)
    for part in parts:
        units = ((sums(part) - average) * inverse).reshape(16 * rows, tokens)
        for t in tiles:
            unit_scratch[t, part, :] = units[:, t * LANES : (t + 1) * LANES]
    for chunk in chunks(rows, tokens, 256):
        part = span(chunk, tokens)
        units = lanes([unit_scratch[t, pl.ds(r, channels, stride=rows), :] for r in chunk for t in tiles])
        normed = affine(units, gain, bias, tokens)
        change = gate_t_ref[:, part].astype(F32) * dot(outw_t, normed, NN)
        emit(chunk, part, (pair_t_ref[:, part].astype(F32) + change).astype(BF16))


def step_kernel(per_group, by_core, *refs):
    if not by_core:
        merged_ref, refs = refs[0], refs[1:]
        return step_rows(per_group, lambda part: merged_ref[part].astype(F32), *refs)
    core_ref, refs = refs[0], refs[1:]
    step_rows(per_group, core_halves(core_ref, refs[0], refs[1]), *refs[2:], core_ref=core_ref)


def core_halves(core_ref, keep_ref, got_ref):
    size = keep_ref.shape[0]

    def load(part):
        late = part.start >= size
        part = slice(part.start - size, part.stop - size) if late else part
        keep, got = keep_ref[part].astype(F32), got_ref[part].astype(F32)
        return jnp.where(jnp.full(keep.shape, core_ref[0]) == int(late), keep, got)

    return load


def step_rows(
    per_group, load, pair_t_ref, gate_t_ref, mask_ref, columns_ref, outw_t_ref, proj_t_ref, *refs, core_ref=None
):
    outs, (middle_t_ref, gate1_t_ref, unit_scratch, panels) = refs[:-4], refs[-4:]
    rows, tokens = mask_ref.shape

    def emit(chunk, part, middle):
        middle_t_ref[:, part] = middle
        normed = affine(unit(middle.astype(F32), 0), columns_ref[4], columns_ref[5], tokens)
        products = dot(proj_t_ref[1], normed, NN)
        gate1_t_ref[:, part] = store_panels(
            panels, per_group, rows, chunk, tokens, products, half_lanes(mask_ref, chunk)
        )

    finish_rows(
        emit, rows, pair_t_ref.shape[0], tokens, load, pair_t_ref, gate_t_ref, columns_ref[2], columns_ref[3],
        outw_t_ref[0], unit_scratch,
    )
    if core_ref is None:
        pack_panels(panels, *outs)
    else:
        split_panels(panels, core_ref, *outs)


def finish_kernel(by_core, *refs):
    if by_core:
        load, refs = core_halves(*refs[:3]), refs[3:]
    else:
        merged_ref, refs = refs[0], refs[1:]

        def load(part):
            return merged_ref[part].astype(F32)

    middle_t_ref, gate_t_ref, columns_ref, outw_t_ref, result_ref, unit_scratch, done, sems = refs
    rows, tokens, _ = result_ref.shape
    copies = []

    def emit(chunk, part, result):
        for h, r in enumerate(chunk):
            done[r] = result[:, h * tokens : (h + 1) * tokens].T
            copies.append(pltpu.make_async_copy(done.at[r], result_ref.at[r], sems.at[r]))
            copies[-1].start()

    finish_rows(
        emit, rows, middle_t_ref.shape[0], tokens, load, middle_t_ref, gate_t_ref,
        columns_ref[6], columns_ref[7], outw_t_ref[1], unit_scratch,
    )
    for copy in copies:
        copy.wait()


def scatter_start(first, up, down, order_ref, own_left, got_left, own_right, got_right, sums_ref, up_ref, down_ref):
    rows, tokens = own_left.shape[1:]
    count = sums_ref.shape[0]

    def both(own, got, c):
        return jnp.concatenate([own[first + c].astype(F32), got[first + c].astype(F32)], axis=0).astype(BF16)

    lefts = jnp.concatenate([both(own_left, got_left, c) for c in range(count)], axis=0)
    lefts = dot(lefts, order_ref[...], NT).astype(BF16).reshape(count, 2 * rows, tokens)
    for c in range(count):
        sums_ref[c] = dot(lefts[c], both(own_right, got_right, c), TN)
    for distance, ref in ((up, up_ref), (down, down_ref)):
        ref[...] = at_distance(sums_ref, distance, 2 * rows).astype(BF16)


def at_distance(sums_ref, distance, count):
    return sums_ref[:, distance * count : (distance + 1) * count, :]


def scatter_add(distance, got_ref, sums_ref, out_ref):
    out_ref[...] = (got_ref[...].astype(F32) + at_distance(sums_ref, distance, got_ref.shape[1])).astype(BF16)


def scatter_end(*refs):
    pieces, (keep_ref, send_ref) = refs[:-2], refs[-2:]
    rows = keep_ref.shape[1]
    first = 0
    for n in range(0, len(pieces), 3):
        sums_ref, up_ref, down_ref = pieces[n : n + 3]
        count = sums_ref.shape[0]
        sums = at_distance(sums_ref, 0, 2 * rows) + up_ref[...].astype(F32) + down_ref[...].astype(F32)
        keep_ref[first : first + count] = sums[:, :rows].astype(BF16)
        send_ref[first : first + count] = sums[:, rows:].astype(BF16)
        first += count


def on_device(*inputs):
    groups = lax.axis_size("row")
    rows, tokens, channels = inputs[0].shape
    per_group = channels // groups
    whole = pl.BlockSpec(memory_space=pltpu.VMEM)
    hbm = pl.BlockSpec(memory_space=pltpu.HBM)
    params = pltpu.CompilerParams(vmem_limit_bytes=32 * 1024 * 1024)
    shape = jax.ShapeDtypeStruct
    both_shape = shape((2 * channels * rows, tokens), BF16)
    flat_shape = shape((channels, rows * tokens), BF16)
    panels = pltpu.VMEM((tokens // LANES, 2 * channels * rows, LANES), F32)
    unit_scratch = pltpu.VMEM((tokens // LANES, channels * rows, LANES), F32)

    def exchange(array):
        return lax.all_to_all(array, "row", split_axis=0, concat_axis=0, tiled=True)

    def mix(both, incoming):
        product = pl.pallas_call(
            functools.partial(mix_kernel, per_group, rows, incoming),
            out_shape=shape((groups, per_group * rows, tokens), BF16),
            in_specs=[whole],
            out_specs=whole,
            compiler_params=params,
            name="mix",
        )(both.reshape(groups, 2 * per_group * rows, tokens))
        return product.reshape(channels * rows, tokens)

    half = channels // 2
    by_core = groups % 4 == 0 and groups * rows * tokens * half * 2 <= 4 * 2**20
    smem = pl.BlockSpec(memory_space=pltpu.SMEM)
    core = (lax.axis_index("row") % 2).astype(jnp.int32).reshape(1)
    half_shape = shape((half * rows, tokens), BF16)
    projected = (half_shape,) * 4 if by_core else (both_shape,)
    results = pl.pallas_call(
        functools.partial(project_kernel, half if by_core else per_group, by_core),
        out_shape=projected
        + (
            flat_shape,
            flat_shape,
            shape((rows, tokens), inputs[1].dtype),
            shape((8, channels, tokens), F32),
            shape((2, 5 * channels, channels), BF16),
            shape((2, channels, channels), BF16),
        ),
        in_specs=[smem] * by_core + [hbm] * 7,
        out_specs=(whole,) * (len(projected) + 6),
        scratch_shapes=[pltpu.VMEM(inputs[n].shape, inputs[n].dtype) for n in (0, 2, 3, 4, 5, 6)]
        + [panels, pltpu.SemaphoreType.DMA((7,))],
        compiler_params=params,
        name="project",
    )(*[core] * by_core, *(pltpu.with_memory_space_constraint(a, pltpu.HBM) for a in inputs))
    pair_t, gate_t, mask, columns, proj_t, outw_t = results[-6:]
    if by_core:
        left, right, other_left, other_right = results[:4]
        chips = groups // 2
        ring = ring_chips(chips)

        def along(array, step):
            pairs = [(2 * q + c, 2 * ring[(p + step) % chips] + c) for p, q in enumerate(ring) for c in range(2)]
            return lax.ppermute(array, "row", pairs)

        def rounds(array, step, count):
            arrays = [array]
            for _ in range(count):
                arrays.append(along(arrays[-1], step))
            return arrays

        swap = [(d, d ^ 1) for d in range(groups)]
        got_right = lax.ppermute(other_right, "row", swap)
        got_left = lax.ppermute(other_left, "row", swap)
        middle = chips // 2
        ups = [rounds(right, 1, middle), rounds(got_right, 1, middle - 1)]
        downs = [rounds(right, -1, middle - 1), rounds(got_right, -1, middle)]
        distances = sorted(range(chips), key=lambda d: min(d, chips - d))
        early = 2 * (chips // 2 + 1)
        rights = [
            ups[piece][d] if d < len(ups[piece]) else downs[piece][chips - d] for d in distances for piece in range(2)
        ]
        rights = [array.reshape(half, rows, tokens) for array in rights]
        lefts = [array.reshape(half, rows, tokens) for array in (left, got_left)]
        first_sums = pl.pallas_call(
            mix_early,
            out_shape=shape((half, 2 * rows, tokens), BF16),
            in_specs=[whole] * (3 + early),
            out_specs=whole,
            scratch_shapes=[pltpu.VMEM((2 * half * rows, early * rows), BF16)],
            compiler_params=params,
            cost_estimate=pl.CostEstimate(flops=10**9, bytes_accessed=4 * 2**20, transcendentals=0),
            name="mix_early",
        )(token_order(chips, distances[: early // 2], rows), *lefts, *rights[:early])
        keep, send = pl.pallas_call(
            mix_late,
            out_shape=(shape((half, rows, tokens), BF16),) * 2,
            in_specs=[whole] * (4 + len(rights) - early),
            out_specs=(whole,) * 2,
            scratch_shapes=[pltpu.VMEM((2 * half * rows, (len(rights) - early) * rows), BF16)],
            compiler_params=params,
            name="mix_late",
        )(token_order(chips, distances[early // 2 :], rows), *lefts, first_sums, *rights[early:])
        merged = (core, keep.reshape(half * rows, tokens), lax.ppermute(send, "row", swap).reshape(half * rows, tokens))
    else:
        merged = (exchange(mix(exchange(results[0]), False)),)
    results = pl.pallas_call(
        functools.partial(step_kernel, half if by_core else per_group, by_core),
        out_shape=projected + (flat_shape, flat_shape),
        in_specs=[smem] * by_core + [whole] * (len(merged) - by_core + 6),
        out_specs=(whole,) * (len(projected) + 2),
        scratch_shapes=[unit_scratch, panels],
        compiler_params=params,
        name="finish_project",
    )(*merged, pair_t, gate_t, mask, columns, outw_t, proj_t)
    middle_t, gate_t = results[-2:]
    if by_core:
        left, right, other_left, other_right = results[:4]
        got_left = lax.ppermute(other_left, "row", swap)
        got_right = lax.ppermute(other_right, "row", swap)
        operands = [array.reshape(half, rows, tokens) for array in (left, got_left, right, got_right)]
        order = token_order(chips, [-d % chips for d in range(chips)], rows)
        size = half // 2
        part_shape = shape((size, 2 * rows, tokens), BF16)
        pieces = []
        for piece in range(2):
            hops = (middle, middle - 1) if piece == 0 else (middle - 1, middle)
            sums, *travelling = pl.pallas_call(
                functools.partial(scatter_start, piece * size, hops[0], chips - hops[1]),
                out_shape=(shape((size, tokens, tokens), F32), part_shape, part_shape),
                in_specs=[whole] * 5,
                out_specs=(whole,) * 3,
                compiler_params=params,
                name="scatter_start",
            )(order, *operands)
            for way, (step, count) in enumerate(zip((1, -1), hops)):
                for left_over in reversed(range(count)):
                    travelling[way] = along(travelling[way], step)
                    if left_over:
                        travelling[way] = pl.pallas_call(
                            functools.partial(scatter_add, step * left_over % chips),
                            out_shape=part_shape,
                            in_specs=[whole] * 2,
                            out_specs=whole,
                            compiler_params=params,
                            name="scatter_add",
                        )(travelling[way], sums)
            pieces += [sums, *travelling]
        keep, send = pl.pallas_call(
            scatter_end,
            out_shape=(shape((half, rows, tokens), BF16),) * 2,
            in_specs=[whole] * len(pieces),
            out_specs=(whole,) * 2,
            compiler_params=params,
            name="scatter_end",
        )(*pieces)
        merged = (core, keep.reshape(half * rows, tokens), lax.ppermute(send, "row", swap).reshape(half * rows, tokens))
    else:
        merged = (exchange(mix(exchange(results[0]), True)),)
    return pl.pallas_call(
        functools.partial(finish_kernel, by_core),
        out_shape=shape((rows, tokens, channels), BF16),
        in_specs=[smem] * by_core + [whole] * (len(merged) - by_core + 4),
        out_specs=hbm,
        scratch_shapes=[unit_scratch, pltpu.VMEM((rows, tokens, channels), BF16), pltpu.SemaphoreType.DMA((rows,))],
        compiler_params=params,
        name="finish",
    )(*merged, middle_t, gate_t, columns, outw_t)


def solution(mesh):
    rows = ("groups", "row")
    return jax.shard_map(
        on_device,
        mesh=mesh,
        in_specs=(P(rows, None, None), P(rows, None), P(), P(), P(), P(), P()),
        out_specs=P(rows, None, None),
        check_vma=False,
    )
```

```python
import functools

import jax
import jax.numpy as jnp
from jax import lax
from jax.experimental import pallas as pl
from jax.experimental.pallas import tpu as pltpu
from jax.sharding import PartitionSpec as P

F32 = jnp.float32
BF16 = jnp.bfloat16
LANES = 128
NT = (((1,), (1,)), ((), ()))
NN = (((1,), (0,)), ((), ()))
TN = (((0,), (0,)), ((), ()))


def dot(a, b, dims):
    return lax.dot_general(a, b, dims, preferred_element_type=F32)


def unit(values, axis):
    scale = 1.0 / values.shape[axis]
    centred = values - jnp.sum(values, axis=axis, keepdims=True) * scale
    spread = jnp.sum(centred * centred, axis=axis, keepdims=True) * scale
    return centred * lax.rsqrt(spread + 1e-05)


def chunks(rows, tokens, limit):
    wide = max(1, min(rows, limit // tokens))
    return [list(range(start, min(start + wide, rows))) for start in range(0, rows, wide)]


def span(chunk, tokens):
    return slice(chunk[0] * tokens, (chunk[-1] + 1) * tokens)


def lanes(parts):
    return parts[0] if len(parts) == 1 else jnp.concatenate(parts, axis=1)


def affine(values, gain, bias, tokens):
    parts = [values[:, n : n + tokens] * gain + bias for n in range(0, values.shape[1], tokens)]
    return lanes(parts).astype(BF16)


def store_panels(panels, per_group, rows, chunk, tokens, products, half_mask):
    channels = products.shape[0] // 5
    for side in range(2):
        base = 2 * side * channels
        gate, value = products[base : base + channels], products[base + channels : base + 2 * channels]
        gated = (jnp.tanh(gate) + 1.0) * (value * half_mask)
        for h, r in enumerate(chunk):
            for g in range(channels // per_group):
                where = pl.ds((2 * g + side) * per_group * rows + r, per_group, stride=rows)
                for t in range(tokens // LANES):
                    first = h * tokens + t * LANES
                    panels[t, where, :] = gated[g * per_group : (g + 1) * per_group, first : first + LANES]
    return (0.5 * jnp.tanh(products[4 * channels :]) + 0.5).astype(BF16)


def pack_panels(panels, both_ref):
    for t in range(both_ref.shape[1] // LANES):
        both_ref[:, t * LANES : (t + 1) * LANES] = panels[t].astype(BF16)


def split_panels(panels, core_ref, left_ref, right_ref, other_left_ref, other_right_ref):
    size = left_ref.shape[0]
    core = core_ref[0]
    for t in range(left_ref.shape[1] // LANES):
        for side, (own_ref, other_ref) in enumerate(((left_ref, other_left_ref), (right_ref, other_right_ref))):
            for group, ref in ((core, own_ref), (1 - core, other_ref)):
                start = pl.multiple_of((2 * group + side) * size, size)
                ref[:, t * LANES : (t + 1) * LANES] = panels[t, pl.ds(start, size), :].astype(BF16)


def half_lanes(mask_ref, chunk):
    return lanes([mask_ref[r : r + 1].astype(F32) * 0.5 for r in chunk])


def project_kernel(per_group, by_core, *refs):
    core_ref, refs = (refs[0], refs[1:]) if by_core else (None, refs)
    inputs, refs = refs[:7], refs[7:]
    if by_core:
        outs, refs = refs[:4], refs[4:]
        both_ref = None
    else:
        both_ref, refs = refs[0], refs[1:]
    pair_t_ref, gate_t_ref, mask_ref, columns_ref, proj_t_ref, outw_t_ref = refs[:6]
    pair_ref, gain_ref, bias_ref, proj_ref, gatew_ref, outw_ref, panels, sems = refs[6:]
    held = (pair_ref, mask_ref, gain_ref, bias_ref, proj_ref, gatew_ref, outw_ref)
    copies = [pltpu.make_async_copy(src, dst, sems.at[n]) for n, (src, dst) in enumerate(zip(inputs, held))]
    for copy in copies:
        copy.start()
    for copy in copies:
        copy.wait()
    rows, tokens, channels = pair_ref.shape
    small = jnp.concatenate([ref[which] for ref in (gain_ref, bias_ref) for which in range(2)], axis=0).T
    for n in range(4):
        for side in range(2):
            place = 4 * side + n
            columns_ref[2 * n + side] = jnp.broadcast_to(small[:, place : place + 1], (channels, tokens))
    for which in range(2):
        for part in range(4):
            block = proj_ref[which, :, part * channels : (part + 1) * channels].T
            proj_t_ref[which, part * channels : (part + 1) * channels] = block if part % 2 else block * 0.5
        proj_t_ref[which, 4 * channels :] = gatew_ref[which].T * 0.5
        outw_t_ref[which] = outw_ref[which].T
    for chunk in chunks(rows, tokens, 256):
        part = span(chunk, tokens)
        pair_t = lanes([pair_ref[r].T for r in chunk])
        pair_t_ref[:, part] = pair_t
        normed = affine(unit(pair_t.astype(F32), 0), columns_ref[0], columns_ref[1], tokens)
        products = dot(proj_t_ref[0], normed, NN)
        gate_t_ref[:, part] = store_panels(
            panels, per_group, rows, chunk, tokens, products, half_lanes(mask_ref, chunk)
        )
    if by_core:
        split_panels(panels, core_ref, *outs)
    else:
        pack_panels(panels, both_ref)


def gated_side(panels, rows, chunk, tokens, products, half_mask):
    channels = products.shape[0] // 2
    gated = (jnp.tanh(products[:channels]) + 1.0) * (products[channels:] * half_mask)
    for h, r in enumerate(chunk):
        for c in range(0, channels, 8):
            for t in range(tokens // LANES):
                first = h * tokens + t * LANES
                panels[t, pl.ds(c * rows + r, 8, stride=rows), :] = gated[c : c + 8, first : first + LANES]


def split_side(panels, core_ref, own_ref, other_ref):
    size = own_ref.shape[0]
    for t in range(own_ref.shape[1] // LANES):
        for half, ref in ((core_ref[0], own_ref), (1 - core_ref[0], other_ref)):
            start = pl.multiple_of(half * size, size)
            ref[:, t * LANES : (t + 1) * LANES] = panels[t, pl.ds(start, size), :].astype(BF16)


def side_weights(proj_ref, side, channels):
    gate, value = [proj_ref[0, :, (2 * side + n) * channels : (2 * side + n + 1) * channels].T for n in range(2)]
    return jnp.concatenate([gate * 0.5, value], axis=0)


def fetch(pairs, sems):
    copies = [pltpu.make_async_copy(src, dst, sems.at[n]) for n, (src, dst) in enumerate(pairs)]
    for copy in copies:
        copy.start()
    for copy in copies:
        copy.wait()


def right_kernel(core_ref, pair_hbm, mask_hbm, gain_hbm, bias_hbm, proj_hbm, *refs):
    own_ref, other_ref, pair_t_ref, normed_t_ref, mask_ref, columns_ref = refs[:6]
    pair_ref, gain_ref, bias_ref, proj_ref, panels, sems = refs[6:]
    held = (pair_ref, mask_ref, gain_ref, bias_ref, proj_ref)
    fetch(zip((pair_hbm, mask_hbm, gain_hbm, bias_hbm, proj_hbm), held), sems)
    rows, tokens, channels = pair_ref.shape
    small = jnp.concatenate([ref[which] for ref in (gain_ref, bias_ref) for which in range(2)], axis=0).T
    for n in range(4):
        for side in range(2):
            place = 4 * side + n
            columns_ref[2 * n + side] = jnp.broadcast_to(small[:, place : place + 1], (channels, tokens))
    weights = side_weights(proj_ref, 1, channels)
    for chunk in chunks(rows, tokens, 256):
        part = span(chunk, tokens)
        pair_t = lanes([pair_ref[r].T for r in chunk])
        pair_t_ref[:, part] = pair_t
        normed = affine(unit(pair_t.astype(F32), 0), columns_ref[0], columns_ref[1], tokens)
        normed_t_ref[:, part] = normed
        gated_side(panels, rows, chunk, tokens, dot(weights, normed, NN), half_lanes(mask_ref, chunk))
    split_side(panels, core_ref, own_ref, other_ref)


def left_kernel(core_ref, normed_t_ref, mask_ref, proj_hbm, gatew_hbm, outw_hbm, *refs):
    own_ref, other_ref, gate_t_ref, proj_t_ref, outw_t_ref, proj_ref, gatew_ref, outw_ref, panels, sems = refs
    fetch(zip((proj_hbm, gatew_hbm, outw_hbm), (proj_ref, gatew_ref, outw_ref)), sems)
    rows, tokens = mask_ref.shape
    channels = normed_t_ref.shape[0]
    weights = side_weights(proj_ref, 0, channels)
    gate_weights = gatew_ref[0].T * 0.5
    for chunk in chunks(rows, tokens, 256):
        part = span(chunk, tokens)
        normed = normed_t_ref[:, part]
        gated_side(panels, rows, chunk, tokens, dot(weights, normed, NN), half_lanes(mask_ref, chunk))
        gate_t_ref[:, part] = (0.5 * jnp.tanh(dot(gate_weights, normed, NN)) + 0.5).astype(BF16)
    split_side(panels, core_ref, own_ref, other_ref)
    for part in range(4):
        block = proj_ref[1, :, part * channels : (part + 1) * channels].T
        proj_t_ref[1, part * channels : (part + 1) * channels] = block if part % 2 else block * 0.5
    proj_t_ref[1, 4 * channels :] = gatew_ref[1].T * 0.5
    for which in range(2):
        outw_t_ref[which] = outw_ref[which].T


def mix_kernel(per_group, rows, incoming, both_ref, product_ref):
    groups, _, tokens = both_ref.shape
    step = 2 * rows

    def matrices(side, pair):
        start = (side * per_group + 2 * pair) * rows
        block = both_ref[:, start : start + step, :].astype(F32)
        return [block[:, h * rows : (h + 1) * rows].reshape(groups * rows, tokens).astype(BF16) for h in range(2)]

    for pair in range(per_group // 2):
        lefts, rights = matrices(0, pair), matrices(1, pair)
        sums = [
            dot(left, right, TN if incoming else NT).reshape(groups, rows, tokens)
            for left, right in zip(lefts, rights)
        ]
        product_ref[:, pair * step : (pair + 1) * step, :] = jnp.concatenate(sums, axis=1).astype(BF16)


def ring_chips(count):
    return list(range(0, count, 2)) + list(range(count - 1, 0, -2))


def token_order(chips, distances, rows):
    device = lax.axis_index("row")
    chip, core = device // 2, device % 2
    place = jnp.where(chip % 2 == 0, chip // 2, chips - 1 - chip // 2)
    extent = (2 * len(distances) * rows, 2 * chips * rows)
    lane, token = (lax.broadcasted_iota(jnp.int32, extent, axis) for axis in range(2))
    first = jnp.zeros(extent, jnp.int32)
    for n, d in enumerate(distances):
        source = place - d + jnp.where(place < d, chips, 0)
        source = jnp.where(2 * source < chips, 2 * source, 2 * (chips - 1 - source) + 1)
        for piece in range(2):
            start = (2 * n + piece) * rows
            block = 2 * source + (1 - core if piece else core)
            first = jnp.where((lane >= start) & (lane < start + rows), block * rows - start, first)
    return (token == lane + first).astype(BF16)


def gathered_sums(order_ref, own_ref, got_ref, rights, sums_ref):
    count, rows, tokens = own_ref.shape
    for c in range(count):
        left = jnp.concatenate([own_ref[c].astype(F32), got_ref[c].astype(F32)], axis=0).astype(BF16)
        right = jnp.concatenate([ref[c].astype(F32) for ref in rights], axis=0).astype(BF16)
        sums_ref[2 * rows * c : 2 * rows * (c + 1)] = dot(left, right, NT).astype(BF16)
    order = order_ref[...]
    group = 16
    for first in range(0, count, group):
        sums = dot(sums_ref[2 * rows * first : 2 * rows * (first + group)], order, NN)
        yield slice(first, first + group), sums.reshape(group, 2 * rows, tokens)


def mix_early(order_ref, own_ref, got_ref, *refs):
    rights, (early_ref, sums_ref) = refs[:-2], refs[-2:]
    for part, sums in gathered_sums(order_ref, own_ref, got_ref, rights, sums_ref):
        early_ref[part] = sums.astype(BF16)


def mix_late(order_ref, own_ref, got_ref, early_ref, *refs):
    rights, (keep_ref, send_ref, sums_ref) = refs[:-3], refs[-3:]
    rows = own_ref.shape[1]
    for part, sums in gathered_sums(order_ref, own_ref, got_ref, rights, sums_ref):
        sums = sums + early_ref[part].astype(F32)
        keep_ref[part] = sums[:, :rows].astype(BF16)
        send_ref[part] = sums[:, rows:].astype(BF16)


def finish_rows(emit, rows, channels, tokens, load, pair_t_ref, gate_t_ref, gain, bias, outw_t, unit_scratch):
    tiles = range(tokens // LANES)
    parts = [slice(first * rows, (first + 16) * rows) for first in range(0, channels, 16)]

    def sums(part):
        return load(part).reshape(16, rows, tokens)

    average = sum(jnp.sum(sums(part), axis=0) for part in parts) * (1.0 / channels)
    spread = sum(jnp.sum(jnp.square(sums(part) - average), axis=0) for part in parts) * (1.0 / channels)
    inverse = lax.rsqrt(spread + 1e-05)
    for part in parts:
        units = ((sums(part) - average) * inverse).reshape(16 * rows, tokens)
        for t in tiles:
            unit_scratch[t, part, :] = units[:, t * LANES : (t + 1) * LANES]
    for chunk in chunks(rows, tokens, 256):
        part = span(chunk, tokens)
        units = lanes([unit_scratch[t, pl.ds(r, channels, stride=rows), :] for r in chunk for t in tiles])
        normed = affine(units, gain, bias, tokens)
        change = gate_t_ref[:, part].astype(F32) * dot(outw_t, normed, NN)
        emit(chunk, part, (pair_t_ref[:, part].astype(F32) + change).astype(BF16))


def step_kernel(per_group, by_core, *refs):
    if not by_core:
        merged_ref, refs = refs[0], refs[1:]
        return step_rows(per_group, lambda part: merged_ref[part].astype(F32), *refs)
    core_ref, refs = refs[0], refs[1:]
    step_rows(per_group, core_halves(core_ref, refs[0], refs[1]), *refs[2:], core_ref=core_ref)


def core_halves(core_ref, keep_ref, got_ref):
    size = keep_ref.shape[0]

    def load(part):
        late = part.start >= size
        part = slice(part.start - size, part.stop - size) if late else part
        keep, got = keep_ref[part].astype(F32), got_ref[part].astype(F32)
        return jnp.where(jnp.full(keep.shape, core_ref[0]) == int(late), keep, got)

    return load


def step_rows(
    per_group, load, pair_t_ref, gate_t_ref, mask_ref, columns_ref, outw_t_ref, proj_t_ref, *refs, core_ref=None
):
    outs, (middle_t_ref, gate1_t_ref, unit_scratch, panels) = refs[:-4], refs[-4:]
    rows, tokens = mask_ref.shape

    def emit(chunk, part, middle):
        middle_t_ref[:, part] = middle
        normed = affine(unit(middle.astype(F32), 0), columns_ref[4], columns_ref[5], tokens)
        products = dot(proj_t_ref[1], normed, NN)
        gate1_t_ref[:, part] = store_panels(
            panels, per_group, rows, chunk, tokens, products, half_lanes(mask_ref, chunk)
        )

    finish_rows(
        emit, rows, pair_t_ref.shape[0], tokens, load, pair_t_ref, gate_t_ref, columns_ref[2], columns_ref[3],
        outw_t_ref[0], unit_scratch,
    )
    if core_ref is None:
        pack_panels(panels, *outs)
    else:
        split_panels(panels, core_ref, *outs)


def finish_kernel(by_core, *refs):
    if by_core:
        load, refs = core_halves(*refs[:3]), refs[3:]
    else:
        merged_ref, refs = refs[0], refs[1:]

        def load(part):
            return merged_ref[part].astype(F32)

    middle_t_ref, gate_t_ref, columns_ref, outw_t_ref, result_ref, unit_scratch, done, sems = refs
    rows, tokens, _ = result_ref.shape
    copies = []

    def emit(chunk, part, result):
        for h, r in enumerate(chunk):
            done[r] = result[:, h * tokens : (h + 1) * tokens].T
            copies.append(pltpu.make_async_copy(done.at[r], result_ref.at[r], sems.at[r]))
            copies[-1].start()

    finish_rows(
        emit, rows, middle_t_ref.shape[0], tokens, load, middle_t_ref, gate_t_ref,
        columns_ref[6], columns_ref[7], outw_t_ref[1], unit_scratch,
    )
    for copy in copies:
        copy.wait()


def scatter_start(first, up, down, order_ref, own_left, got_left, own_right, got_right, sums_ref, up_ref, down_ref):
    rows, tokens = own_left.shape[1:]
    count = sums_ref.shape[0]

    def both(own, got, c):
        return jnp.concatenate([own[first + c].astype(F32), got[first + c].astype(F32)], axis=0).astype(BF16)

    lefts = jnp.concatenate([both(own_left, got_left, c) for c in range(count)], axis=0)
    lefts = dot(lefts, order_ref[...], NT).astype(BF16).reshape(count, 2 * rows, tokens)
    for c in range(count):
        sums_ref[c] = dot(lefts[c], both(own_right, got_right, c), TN)
    for distance, ref in ((up, up_ref), (down, down_ref)):
        ref[...] = at_distance(sums_ref, distance, 2 * rows).astype(BF16)


def at_distance(sums_ref, distance, count):
    return sums_ref[:, distance * count : (distance + 1) * count, :]


def scatter_add(distance, got_ref, sums_ref, out_ref):
    out_ref[...] = (got_ref[...].astype(F32) + at_distance(sums_ref, distance, got_ref.shape[1])).astype(BF16)


def scatter_end(*refs):
    pieces, (keep_ref, send_ref) = refs[:-2], refs[-2:]
    rows = keep_ref.shape[1]
    first = 0
    for n in range(0, len(pieces), 3):
        sums_ref, up_ref, down_ref = pieces[n : n + 3]
        count = sums_ref.shape[0]
        sums = at_distance(sums_ref, 0, 2 * rows) + up_ref[...].astype(F32) + down_ref[...].astype(F32)
        keep_ref[first : first + count] = sums[:, :rows].astype(BF16)
        send_ref[first : first + count] = sums[:, rows:].astype(BF16)
        first += count


def on_device(*inputs):
    groups = lax.axis_size("row")
    rows, tokens, channels = inputs[0].shape
    per_group = channels // groups
    whole = pl.BlockSpec(memory_space=pltpu.VMEM)
    hbm = pl.BlockSpec(memory_space=pltpu.HBM)
    params = pltpu.CompilerParams(vmem_limit_bytes=32 * 1024 * 1024)
    shape = jax.ShapeDtypeStruct
    both_shape = shape((2 * channels * rows, tokens), BF16)
    flat_shape = shape((channels, rows * tokens), BF16)
    panels = pltpu.VMEM((tokens // LANES, 2 * channels * rows, LANES), F32)
    unit_scratch = pltpu.VMEM((tokens // LANES, channels * rows, LANES), F32)

    def exchange(array):
        return lax.all_to_all(array, "row", split_axis=0, concat_axis=0, tiled=True)

    def mix(both, incoming):
        product = pl.pallas_call(
            functools.partial(mix_kernel, per_group, rows, incoming),
            out_shape=shape((groups, per_group * rows, tokens), BF16),
            in_specs=[whole],
            out_specs=whole,
            compiler_params=params,
            name="mix",
        )(both.reshape(groups, 2 * per_group * rows, tokens))
        return product.reshape(channels * rows, tokens)

    half = channels // 2
    by_core = groups % 4 == 0 and groups * rows * tokens * half * 2 <= 4 * 2**20
    smem = pl.BlockSpec(memory_space=pltpu.SMEM)
    core = (lax.axis_index("row") % 2).astype(jnp.int32).reshape(1)
    half_shape = shape((half * rows, tokens), BF16)
    projected = (half_shape,) * 4 if by_core else (both_shape,)
    columns_shape = shape((8, channels, tokens), F32)
    proj_t_shape = shape((2, 5 * channels, channels), BF16)
    if by_core:
        pair, mask, gains, biases, proj, gatew, outw = (
            pltpu.with_memory_space_constraint(a, pltpu.HBM) for a in inputs
        )
        side_panels = pltpu.VMEM((tokens // LANES, channels * rows, LANES), F32)

        def held(*arrays):
            return [pltpu.VMEM(a.shape, a.dtype) for a in arrays] + [side_panels, pltpu.SemaphoreType.DMA((len(arrays) + 1,))]

        right, other_right, pair_t, normed_t, mask, columns = pl.pallas_call(
            right_kernel,
            out_shape=(half_shape, half_shape, flat_shape, flat_shape, shape(mask.shape, mask.dtype), columns_shape),
            in_specs=[smem] + [hbm] * 5,
            out_specs=(whole,) * 6,
            scratch_shapes=held(pair, gains, biases, proj),
            compiler_params=params,
            name="project_right",
        )(core, pair, mask, gains, biases, proj)
        left, other_left, gate_t, proj_t, outw_t = pl.pallas_call(
            left_kernel,
            out_shape=(half_shape, half_shape, flat_shape, proj_t_shape, shape(outw.shape, BF16)),
            in_specs=[smem] + [whole] * 2 + [hbm] * 3,
            out_specs=(whole,) * 5,
            scratch_shapes=held(proj, gatew, outw),
            compiler_params=params,
            cost_estimate=pl.CostEstimate(flops=10**9, bytes_accessed=4 * 2**20, transcendentals=0),
            name="project_left",
        )(core, normed_t, mask, proj, gatew, outw)
    else:
        results = pl.pallas_call(
            functools.partial(project_kernel, half if by_core else per_group, by_core),
            out_shape=projected
            + (
                flat_shape,
                flat_shape,
                shape((rows, tokens), inputs[1].dtype),
                shape((8, channels, tokens), F32),
                shape((2, 5 * channels, channels), BF16),
                shape((2, channels, channels), BF16),
            ),
            in_specs=[smem] * by_core + [hbm] * 7,
            out_specs=(whole,) * (len(projected) + 6),
            scratch_shapes=[pltpu.VMEM(inputs[n].shape, inputs[n].dtype) for n in (0, 2, 3, 4, 5, 6)]
            + [panels, pltpu.SemaphoreType.DMA((7,))],
            compiler_params=params,
            name="project",
        )(*[core] * by_core, *(pltpu.with_memory_space_constraint(a, pltpu.HBM) for a in inputs))
        pair_t, gate_t, mask, columns, proj_t, outw_t = results[-6:]
    if by_core:
        chips = groups // 2
        ring = ring_chips(chips)

        def along(array, step):
            pairs = [(2 * q + c, 2 * ring[(p + step) % chips] + c) for p, q in enumerate(ring) for c in range(2)]
            return lax.ppermute(array, "row", pairs)

        def rounds(array, step, count):
            arrays = [array]
            for _ in range(count):
                arrays.append(along(arrays[-1], step))
            return arrays

        swap = [(d, d ^ 1) for d in range(groups)]
        got_right = lax.ppermute(other_right, "row", swap)
        got_left = lax.ppermute(other_left, "row", swap)
        middle = chips // 2
        ups = [rounds(right, 1, middle), rounds(got_right, 1, middle - 1)]
        downs = [rounds(right, -1, middle - 1), rounds(got_right, -1, middle)]
        distances = sorted(range(chips), key=lambda d: min(d, chips - d))
        early = 2 * (chips // 2 + 1)
        rights = [
            ups[piece][d] if d < len(ups[piece]) else downs[piece][chips - d] for d in distances for piece in range(2)
        ]
        rights = [array.reshape(half, rows, tokens) for array in rights]
        lefts = [array.reshape(half, rows, tokens) for array in (left, got_left)]
        first_sums = pl.pallas_call(
            mix_early,
            out_shape=shape((half, 2 * rows, tokens), BF16),
            in_specs=[whole] * (3 + early),
            out_specs=whole,
            scratch_shapes=[pltpu.VMEM((2 * half * rows, early * rows), BF16)],
            compiler_params=params,
            cost_estimate=pl.CostEstimate(flops=10**9, bytes_accessed=4 * 2**20, transcendentals=0),
            name="mix_early",
        )(token_order(chips, distances[: early // 2], rows), *lefts, *rights[:early])
        keep, send = pl.pallas_call(
            mix_late,
            out_shape=(shape((half, rows, tokens), BF16),) * 2,
            in_specs=[whole] * (4 + len(rights) - early),
            out_specs=(whole,) * 2,
            scratch_shapes=[pltpu.VMEM((2 * half * rows, (len(rights) - early) * rows), BF16)],
            compiler_params=params,
            name="mix_late",
        )(token_order(chips, distances[early // 2 :], rows), *lefts, first_sums, *rights[early:])
        merged = (core, keep.reshape(half * rows, tokens), lax.ppermute(send, "row", swap).reshape(half * rows, tokens))
    else:
        merged = (exchange(mix(exchange(results[0]), False)),)
    results = pl.pallas_call(
        functools.partial(step_kernel, half if by_core else per_group, by_core),
        out_shape=projected + (flat_shape, flat_shape),
        in_specs=[smem] * by_core + [whole] * (len(merged) - by_core + 6),
        out_specs=(whole,) * (len(projected) + 2),
        scratch_shapes=[unit_scratch, panels],
        compiler_params=params,
        name="finish_project",
    )(*merged, pair_t, gate_t, mask, columns, outw_t, proj_t)
    middle_t, gate_t = results[-2:]
    if by_core:
        left, right, other_left, other_right = results[:4]
        got_left = lax.ppermute(other_left, "row", swap)
        got_right = lax.ppermute(other_right, "row", swap)
        operands = [array.reshape(half, rows, tokens) for array in (left, got_left, right, got_right)]
        order = token_order(chips, [-d % chips for d in range(chips)], rows)
        size = half // 2
        part_shape = shape((size, 2 * rows, tokens), BF16)
        pieces = []
        for piece in range(2):
            hops = (middle, middle - 1) if piece == 0 else (middle - 1, middle)
            sums, *travelling = pl.pallas_call(
                functools.partial(scatter_start, piece * size, hops[0], chips - hops[1]),
                out_shape=(shape((size, tokens, tokens), F32), part_shape, part_shape),
                in_specs=[whole] * 5,
                out_specs=(whole,) * 3,
                compiler_params=params,
                name="scatter_start",
            )(order, *operands)
            for way, (step, count) in enumerate(zip((1, -1), hops)):
                for left_over in reversed(range(count)):
                    travelling[way] = along(travelling[way], step)
                    if left_over:
                        travelling[way] = pl.pallas_call(
                            functools.partial(scatter_add, step * left_over % chips),
                            out_shape=part_shape,
                            in_specs=[whole] * 2,
                            out_specs=whole,
                            compiler_params=params,
                            name="scatter_add",
                        )(travelling[way], sums)
            pieces += [sums, *travelling]
        keep, send = pl.pallas_call(
            scatter_end,
            out_shape=(shape((half, rows, tokens), BF16),) * 2,
            in_specs=[whole] * len(pieces),
            out_specs=(whole,) * 2,
            compiler_params=params,
            name="scatter_end",
        )(*pieces)
        merged = (core, keep.reshape(half * rows, tokens), lax.ppermute(send, "row", swap).reshape(half * rows, tokens))
    else:
        merged = (exchange(mix(exchange(results[0]), True)),)
    return pl.pallas_call(
        functools.partial(finish_kernel, by_core),
        out_shape=shape((rows, tokens, channels), BF16),
        in_specs=[smem] * by_core + [whole] * (len(merged) - by_core + 4),
        out_specs=hbm,
        scratch_shapes=[unit_scratch, pltpu.VMEM((rows, tokens, channels), BF16), pltpu.SemaphoreType.DMA((rows,))],
        compiler_params=params,
        name="finish",
    )(*merged, middle_t, gate_t, columns, outw_t)


def solution(mesh):
    rows = ("groups", "row")
    return jax.shard_map(
        on_device,
        mesh=mesh,
        in_specs=(P(rows, None, None), P(rows, None), P(), P(), P(), P(), P()),
        out_specs=P(rows, None, None),
        check_vma=False,
    )
```

```python
import functools

import jax
import jax.numpy as jnp
from jax import lax
from jax.experimental import pallas as pl
from jax.experimental.pallas import tpu as pltpu
from jax.sharding import PartitionSpec as P

F32 = jnp.float32
BF16 = jnp.bfloat16
LANES = 128
NT = (((1,), (1,)), ((), ()))
NN = (((1,), (0,)), ((), ()))
TN = (((0,), (0,)), ((), ()))


def dot(a, b, dims):
    return lax.dot_general(a, b, dims, preferred_element_type=F32)


def unit(values, axis):
    scale = 1.0 / values.shape[axis]
    centred = values - jnp.sum(values, axis=axis, keepdims=True) * scale
    spread = jnp.sum(centred * centred, axis=axis, keepdims=True) * scale
    return centred * lax.rsqrt(spread + 1e-05)


def chunks(rows, tokens, limit):
    wide = max(1, min(rows, limit // tokens))
    return [list(range(start, min(start + wide, rows))) for start in range(0, rows, wide)]


def span(chunk, tokens):
    return slice(chunk[0] * tokens, (chunk[-1] + 1) * tokens)


def lanes(parts):
    return parts[0] if len(parts) == 1 else jnp.concatenate(parts, axis=1)


def affine(values, gain, bias, tokens):
    parts = [values[:, n : n + tokens] * gain + bias for n in range(0, values.shape[1], tokens)]
    return lanes(parts).astype(BF16)


def store_panels(panels, per_group, rows, chunk, tokens, products, half_mask):
    channels = products.shape[0] // 5
    for side in range(2):
        base = 2 * side * channels
        gate, value = products[base : base + channels], products[base + channels : base + 2 * channels]
        gated = (jnp.tanh(gate) + 1.0) * (value * half_mask)
        for h, r in enumerate(chunk):
            for g in range(channels // per_group):
                where = pl.ds((2 * g + side) * per_group * rows + r, per_group, stride=rows)
                for t in range(tokens // LANES):
                    first = h * tokens + t * LANES
                    panels[t, where, :] = gated[g * per_group : (g + 1) * per_group, first : first + LANES]
    return (0.5 * jnp.tanh(products[4 * channels :]) + 0.5).astype(BF16)


def pack_panels(panels, both_ref):
    for t in range(both_ref.shape[1] // LANES):
        both_ref[:, t * LANES : (t + 1) * LANES] = panels[t].astype(BF16)


def split_panels(panels, core_ref, left_ref, right_ref, other_left_ref, other_right_ref):
    size = left_ref.shape[0]
    core = core_ref[0]
    for t in range(left_ref.shape[1] // LANES):
        for side, (own_ref, other_ref) in enumerate(((left_ref, other_left_ref), (right_ref, other_right_ref))):
            for group, ref in ((core, own_ref), (1 - core, other_ref)):
                start = pl.multiple_of((2 * group + side) * size, size)
                ref[:, t * LANES : (t + 1) * LANES] = panels[t, pl.ds(start, size), :].astype(BF16)


def half_lanes(mask_ref, chunk):
    return lanes([mask_ref[r : r + 1].astype(F32) * 0.5 for r in chunk])


def project_kernel(per_group, by_core, *refs):
    core_ref, refs = (refs[0], refs[1:]) if by_core else (None, refs)
    inputs, refs = refs[:7], refs[7:]
    if by_core:
        outs, refs = refs[:4], refs[4:]
        both_ref = None
    else:
        both_ref, refs = refs[0], refs[1:]
    pair_t_ref, gate_t_ref, mask_ref, columns_ref, proj_t_ref, outw_t_ref = refs[:6]
    pair_ref, gain_ref, bias_ref, proj_ref, gatew_ref, outw_ref, panels, sems = refs[6:]
    held = (pair_ref, mask_ref, gain_ref, bias_ref, proj_ref, gatew_ref, outw_ref)
    copies = [pltpu.make_async_copy(src, dst, sems.at[n]) for n, (src, dst) in enumerate(zip(inputs, held))]
    for copy in copies:
        copy.start()
    for copy in copies:
        copy.wait()
    rows, tokens, channels = pair_ref.shape
    small = jnp.concatenate([ref[which] for ref in (gain_ref, bias_ref) for which in range(2)], axis=0).T
    for n in range(4):
        for side in range(2):
            place = 4 * side + n
            columns_ref[2 * n + side] = jnp.broadcast_to(small[:, place : place + 1], (channels, tokens))
    for which in range(2):
        for part in range(4):
            block = proj_ref[which, :, part * channels : (part + 1) * channels].T
            proj_t_ref[which, part * channels : (part + 1) * channels] = block if part % 2 else block * 0.5
        proj_t_ref[which, 4 * channels :] = gatew_ref[which].T * 0.5
        outw_t_ref[which] = outw_ref[which].T
    for chunk in chunks(rows, tokens, 256):
        part = span(chunk, tokens)
        pair_t = lanes([pair_ref[r].T for r in chunk])
        pair_t_ref[:, part] = pair_t
        normed = affine(unit(pair_t.astype(F32), 0), columns_ref[0], columns_ref[1], tokens)
        products = dot(proj_t_ref[0], normed, NN)
        gate_t_ref[:, part] = store_panels(
            panels, per_group, rows, chunk, tokens, products, half_lanes(mask_ref, chunk)
        )
    if by_core:
        split_panels(panels, core_ref, *outs)
    else:
        pack_panels(panels, both_ref)


def gated_side(panels, rows, chunk, tokens, products, half_mask):
    channels = products.shape[0] // 2
    gated = (jnp.tanh(products[:channels]) + 1.0) * (products[channels:] * half_mask)
    for h, r in enumerate(chunk):
        for c in range(0, channels, 8):
            for t in range(tokens // LANES):
                first = h * tokens + t * LANES
                panels[t, pl.ds(c * rows + r, 8, stride=rows), :] = gated[c : c + 8, first : first + LANES]


def split_side(panels, core_ref, own_ref, other_ref):
    size = own_ref.shape[0]
    for t in range(own_ref.shape[1] // LANES):
        for half, ref in ((core_ref[0], own_ref), (1 - core_ref[0], other_ref)):
            start = pl.multiple_of(half * size, size)
            ref[:, t * LANES : (t + 1) * LANES] = panels[t, pl.ds(start, size), :].astype(BF16)


def side_weights(proj_ref, side, channels):
    gate, value = [proj_ref[0, :, (2 * side + n) * channels : (2 * side + n + 1) * channels].T for n in range(2)]
    return jnp.concatenate([gate * 0.5, value], axis=0)


def fetch(pairs, sems):
    copies = [pltpu.make_async_copy(src, dst, sems.at[n]) for n, (src, dst) in enumerate(pairs)]
    for copy in copies:
        copy.start()
    for copy in copies:
        copy.wait()


def right_kernel(core_ref, pair_hbm, mask_hbm, gain_hbm, bias_hbm, proj_hbm, gatew_hbm, outw_hbm, *refs):
    own_ref, other_ref, pair_t_ref, normed_t_ref, mask_ref, columns_ref, proj_ref, gatew_ref, outw_ref = refs[:9]
    pair_ref, gain_ref, bias_ref, panels, sems = refs[9:]
    held = (pair_ref, mask_ref, gain_ref, bias_ref, proj_ref, gatew_ref, outw_ref)
    fetch(zip((pair_hbm, mask_hbm, gain_hbm, bias_hbm, proj_hbm, gatew_hbm, outw_hbm), held), sems)
    rows, tokens, channels = pair_ref.shape
    small = jnp.concatenate([ref[which] for ref in (gain_ref, bias_ref) for which in range(2)], axis=0).T
    for n in range(4):
        for side in range(2):
            place = 4 * side + n
            columns_ref[2 * n + side] = jnp.broadcast_to(small[:, place : place + 1], (channels, tokens))
    weights = side_weights(proj_ref, 1, channels)
    for chunk in chunks(rows, tokens, 256):
        part = span(chunk, tokens)
        pair_t = lanes([pair_ref[r].T for r in chunk])
        pair_t_ref[:, part] = pair_t
        normed = affine(unit(pair_t.astype(F32), 0), columns_ref[0], columns_ref[1], tokens)
        normed_t_ref[:, part] = normed
        gated_side(panels, rows, chunk, tokens, dot(weights, normed, NN), half_lanes(mask_ref, chunk))
    split_side(panels, core_ref, own_ref, other_ref)


def left_kernel(core_ref, normed_t_ref, mask_ref, proj_ref, gatew_ref, outw_ref, *refs):
    own_ref, other_ref, gate_t_ref, proj_t_ref, outw_t_ref, panels = refs
    rows, tokens = mask_ref.shape
    channels = normed_t_ref.shape[0]
    weights = side_weights(proj_ref, 0, channels)
    gate_weights = gatew_ref[0].T * 0.5
    for chunk in chunks(rows, tokens, 256):
        part = span(chunk, tokens)
        normed = normed_t_ref[:, part]
        gated_side(panels, rows, chunk, tokens, dot(weights, normed, NN), half_lanes(mask_ref, chunk))
        gate_t_ref[:, part] = (0.5 * jnp.tanh(dot(gate_weights, normed, NN)) + 0.5).astype(BF16)
    split_side(panels, core_ref, own_ref, other_ref)
    for part in range(4):
        block = proj_ref[1, :, part * channels : (part + 1) * channels].T
        proj_t_ref[1, part * channels : (part + 1) * channels] = block if part % 2 else block * 0.5
    proj_t_ref[1, 4 * channels :] = gatew_ref[1].T * 0.5
    for which in range(2):
        outw_t_ref[which] = outw_ref[which].T


def mix_kernel(per_group, rows, incoming, both_ref, product_ref):
    groups, _, tokens = both_ref.shape
    step = 2 * rows

    def matrices(side, pair):
        start = (side * per_group + 2 * pair) * rows
        block = both_ref[:, start : start + step, :].astype(F32)
        return [block[:, h * rows : (h + 1) * rows].reshape(groups * rows, tokens).astype(BF16) for h in range(2)]

    for pair in range(per_group // 2):
        lefts, rights = matrices(0, pair), matrices(1, pair)
        sums = [
            dot(left, right, TN if incoming else NT).reshape(groups, rows, tokens)
            for left, right in zip(lefts, rights)
        ]
        product_ref[:, pair * step : (pair + 1) * step, :] = jnp.concatenate(sums, axis=1).astype(BF16)


def ring_chips(count):
    return list(range(0, count, 2)) + list(range(count - 1, 0, -2))


def token_order(chips, distances, rows):
    device = lax.axis_index("row")
    chip, core = device // 2, device % 2
    place = jnp.where(chip % 2 == 0, chip // 2, chips - 1 - chip // 2)
    extent = (2 * len(distances) * rows, 2 * chips * rows)
    lane, token = (lax.broadcasted_iota(jnp.int32, extent, axis) for axis in range(2))
    first = jnp.zeros(extent, jnp.int32)
    for n, d in enumerate(distances):
        source = place - d + jnp.where(place < d, chips, 0)
        source = jnp.where(2 * source < chips, 2 * source, 2 * (chips - 1 - source) + 1)
        for piece in range(2):
            start = (2 * n + piece) * rows
            block = 2 * source + (1 - core if piece else core)
            first = jnp.where((lane >= start) & (lane < start + rows), block * rows - start, first)
    return (token == lane + first).astype(BF16)


def gathered_sums(order_ref, own_ref, got_ref, rights, sums_ref):
    count, rows, tokens = own_ref.shape
    for c in range(count):
        left = jnp.concatenate([own_ref[c].astype(F32), got_ref[c].astype(F32)], axis=0).astype(BF16)
        right = jnp.concatenate([ref[c].astype(F32) for ref in rights], axis=0).astype(BF16)
        sums_ref[2 * rows * c : 2 * rows * (c + 1)] = dot(left, right, NT).astype(BF16)
    order = order_ref[...]
    group = 16
    for first in range(0, count, group):
        sums = dot(sums_ref[2 * rows * first : 2 * rows * (first + group)], order, NN)
        yield slice(first, first + group), sums.reshape(group, 2 * rows, tokens)


def mix_early(order_ref, own_ref, got_ref, *refs):
    rights, (early_ref, sums_ref) = refs[:-2], refs[-2:]
    for part, sums in gathered_sums(order_ref, own_ref, got_ref, rights, sums_ref):
        early_ref[part] = sums.astype(BF16)


def mix_late(order_ref, own_ref, got_ref, early_ref, *refs):
    rights, (keep_ref, send_ref, sums_ref) = refs[:-3], refs[-3:]
    rows = own_ref.shape[1]
    for part, sums in gathered_sums(order_ref, own_ref, got_ref, rights, sums_ref):
        sums = sums + early_ref[part].astype(F32)
        keep_ref[part] = sums[:, :rows].astype(BF16)
        send_ref[part] = sums[:, rows:].astype(BF16)


def finish_rows(emit, rows, channels, tokens, load, pair_t_ref, gate_t_ref, gain, bias, outw_t, unit_scratch):
    tiles = range(tokens // LANES)
    parts = [slice(first * rows, (first + 16) * rows) for first in range(0, channels, 16)]

    def sums(part):
        return load(part).reshape(16, rows, tokens)

    average = sum(jnp.sum(sums(part), axis=0) for part in parts) * (1.0 / channels)
    spread = sum(jnp.sum(jnp.square(sums(part) - average), axis=0) for part in parts) * (1.0 / channels)
    inverse = lax.rsqrt(spread + 1e-05)
    for part in parts:
        units = ((sums(part) - average) * inverse).reshape(16 * rows, tokens)
        for t in tiles:
            unit_scratch[t, part, :] = units[:, t * LANES : (t + 1) * LANES]
    for chunk in chunks(rows, tokens, 256):
        part = span(chunk, tokens)
        units = lanes([unit_scratch[t, pl.ds(r, channels, stride=rows), :] for r in chunk for t in tiles])
        normed = affine(units, gain, bias, tokens)
        change = gate_t_ref[:, part].astype(F32) * dot(outw_t, normed, NN)
        emit(chunk, part, (pair_t_ref[:, part].astype(F32) + change).astype(BF16))


def step_kernel(per_group, by_core, *refs):
    if not by_core:
        merged_ref, refs = refs[0], refs[1:]
        return step_rows(per_group, lambda part: merged_ref[part].astype(F32), *refs)
    core_ref, refs = refs[0], refs[1:]
    step_rows(per_group, core_halves(core_ref, refs[0], refs[1]), *refs[2:], core_ref=core_ref)


def core_halves(core_ref, keep_ref, got_ref):
    size = keep_ref.shape[0]

    def load(part):
        late = part.start >= size
        part = slice(part.start - size, part.stop - size) if late else part
        keep, got = keep_ref[part].astype(F32), got_ref[part].astype(F32)
        return jnp.where(jnp.full(keep.shape, core_ref[0]) == int(late), keep, got)

    return load


def step_rows(
    per_group, load, pair_t_ref, gate_t_ref, mask_ref, columns_ref, outw_t_ref, proj_t_ref, *refs, core_ref=None
):
    outs, (middle_t_ref, gate1_t_ref, unit_scratch, panels) = refs[:-4], refs[-4:]
    rows, tokens = mask_ref.shape

    def emit(chunk, part, middle):
        middle_t_ref[:, part] = middle
        normed = affine(unit(middle.astype(F32), 0), columns_ref[4], columns_ref[5], tokens)
        products = dot(proj_t_ref[1], normed, NN)
        gate1_t_ref[:, part] = store_panels(
            panels, per_group, rows, chunk, tokens, products, half_lanes(mask_ref, chunk)
        )

    finish_rows(
        emit, rows, pair_t_ref.shape[0], tokens, load, pair_t_ref, gate_t_ref, columns_ref[2], columns_ref[3],
        outw_t_ref[0], unit_scratch,
    )
    if core_ref is None:
        pack_panels(panels, *outs)
    else:
        split_panels(panels, core_ref, *outs)


def finish_kernel(by_core, *refs):
    if by_core:
        load, refs = core_halves(*refs[:3]), refs[3:]
    else:
        merged_ref, refs = refs[0], refs[1:]

        def load(part):
            return merged_ref[part].astype(F32)

    middle_t_ref, gate_t_ref, columns_ref, outw_t_ref, result_ref, unit_scratch, done, sems = refs
    rows, tokens, _ = result_ref.shape
    copies = []

    def emit(chunk, part, result):
        for h, r in enumerate(chunk):
            done[r] = result[:, h * tokens : (h + 1) * tokens].T
            copies.append(pltpu.make_async_copy(done.at[r], result_ref.at[r], sems.at[r]))
            copies[-1].start()

    finish_rows(
        emit, rows, middle_t_ref.shape[0], tokens, load, middle_t_ref, gate_t_ref,
        columns_ref[6], columns_ref[7], outw_t_ref[1], unit_scratch,
    )
    for copy in copies:
        copy.wait()


def scatter_start(first, up, down, order_ref, own_left, got_left, own_right, got_right, sums_ref, up_ref, down_ref):
    rows, tokens = own_left.shape[1:]
    count = sums_ref.shape[0]

    def both(own, got, c):
        return jnp.concatenate([own[first + c].astype(F32), got[first + c].astype(F32)], axis=0).astype(BF16)

    lefts = jnp.concatenate([both(own_left, got_left, c) for c in range(count)], axis=0)
    lefts = dot(lefts, order_ref[...], NT).astype(BF16).reshape(count, 2 * rows, tokens)
    for c in range(count):
        sums_ref[c] = dot(lefts[c], both(own_right, got_right, c), TN)
    for distance, ref in ((up, up_ref), (down, down_ref)):
        ref[...] = at_distance(sums_ref, distance, 2 * rows).astype(BF16)


def at_distance(sums_ref, distance, count):
    return sums_ref[:, distance * count : (distance + 1) * count, :]


def scatter_add(distance, got_ref, sums_ref, out_ref):
    out_ref[...] = (got_ref[...].astype(F32) + at_distance(sums_ref, distance, got_ref.shape[1])).astype(BF16)


def scatter_end(*refs):
    pieces, (keep_ref, send_ref) = refs[:-2], refs[-2:]
    rows = keep_ref.shape[1]
    first = 0
    for n in range(0, len(pieces), 3):
        sums_ref, up_ref, down_ref = pieces[n : n + 3]
        count = sums_ref.shape[0]
        sums = at_distance(sums_ref, 0, 2 * rows) + up_ref[...].astype(F32) + down_ref[...].astype(F32)
        keep_ref[first : first + count] = sums[:, :rows].astype(BF16)
        send_ref[first : first + count] = sums[:, rows:].astype(BF16)
        first += count


def on_device(*inputs):
    groups = lax.axis_size("row")
    rows, tokens, channels = inputs[0].shape
    per_group = channels // groups
    whole = pl.BlockSpec(memory_space=pltpu.VMEM)
    hbm = pl.BlockSpec(memory_space=pltpu.HBM)
    params = pltpu.CompilerParams(vmem_limit_bytes=32 * 1024 * 1024)
    shape = jax.ShapeDtypeStruct
    both_shape = shape((2 * channels * rows, tokens), BF16)
    flat_shape = shape((channels, rows * tokens), BF16)
    panels = pltpu.VMEM((tokens // LANES, 2 * channels * rows, LANES), F32)
    unit_scratch = pltpu.VMEM((tokens // LANES, channels * rows, LANES), F32)

    def exchange(array):
        return lax.all_to_all(array, "row", split_axis=0, concat_axis=0, tiled=True)

    def mix(both, incoming):
        product = pl.pallas_call(
            functools.partial(mix_kernel, per_group, rows, incoming),
            out_shape=shape((groups, per_group * rows, tokens), BF16),
            in_specs=[whole],
            out_specs=whole,
            compiler_params=params,
            name="mix",
        )(both.reshape(groups, 2 * per_group * rows, tokens))
        return product.reshape(channels * rows, tokens)

    half = channels // 2
    by_core = groups % 4 == 0 and groups * rows * tokens * half * 2 <= 4 * 2**20
    smem = pl.BlockSpec(memory_space=pltpu.SMEM)
    core = (lax.axis_index("row") % 2).astype(jnp.int32).reshape(1)
    half_shape = shape((half * rows, tokens), BF16)
    projected = (half_shape,) * 4 if by_core else (both_shape,)
    columns_shape = shape((8, channels, tokens), F32)
    proj_t_shape = shape((2, 5 * channels, channels), BF16)
    if by_core:
        pair, mask, gains, biases, proj, gatew, outw = (
            pltpu.with_memory_space_constraint(a, pltpu.HBM) for a in inputs
        )
        side_panels = pltpu.VMEM((tokens // LANES, channels * rows, LANES), F32)

        def like(array):
            return shape(array.shape, array.dtype)

        right, other_right, pair_t, normed_t, mask, columns, proj, gatew, outw = pl.pallas_call(
            right_kernel,
            out_shape=(half_shape, half_shape, flat_shape, flat_shape, like(mask), columns_shape)
            + (like(proj), like(gatew), like(outw)),
            in_specs=[smem] + [hbm] * 7,
            out_specs=(whole,) * 9,
            scratch_shapes=[pltpu.VMEM(a.shape, a.dtype) for a in (pair, gains, biases)]
            + [side_panels, pltpu.SemaphoreType.DMA((7,))],
            compiler_params=params,
            name="project_right",
        )(core, pair, mask, gains, biases, proj, gatew, outw)
        left, other_left, gate_t, proj_t, outw_t = pl.pallas_call(
            left_kernel,
            out_shape=(half_shape, half_shape, flat_shape, proj_t_shape, shape(outw.shape, BF16)),
            in_specs=[smem] + [whole] * 5,
            out_specs=(whole,) * 5,
            scratch_shapes=[side_panels],
            compiler_params=params,
            cost_estimate=pl.CostEstimate(flops=10**9, bytes_accessed=4 * 2**20, transcendentals=0),
            name="project_left",
        )(core, normed_t, mask, proj, gatew, outw)
    else:
        results = pl.pallas_call(
            functools.partial(project_kernel, half if by_core else per_group, by_core),
            out_shape=projected
            + (
                flat_shape,
                flat_shape,
                shape((rows, tokens), inputs[1].dtype),
                shape((8, channels, tokens), F32),
                shape((2, 5 * channels, channels), BF16),
                shape((2, channels, channels), BF16),
            ),
            in_specs=[smem] * by_core + [hbm] * 7,
            out_specs=(whole,) * (len(projected) + 6),
            scratch_shapes=[pltpu.VMEM(inputs[n].shape, inputs[n].dtype) for n in (0, 2, 3, 4, 5, 6)]
            + [panels, pltpu.SemaphoreType.DMA((7,))],
            compiler_params=params,
            name="project",
        )(*[core] * by_core, *(pltpu.with_memory_space_constraint(a, pltpu.HBM) for a in inputs))
        pair_t, gate_t, mask, columns, proj_t, outw_t = results[-6:]
    if by_core:
        chips = groups // 2
        ring = ring_chips(chips)

        def along(array, step):
            pairs = [(2 * q + c, 2 * ring[(p + step) % chips] + c) for p, q in enumerate(ring) for c in range(2)]
            return lax.ppermute(array, "row", pairs)

        def rounds(array, step, count):
            arrays = [array]
            for _ in range(count):
                arrays.append(along(arrays[-1], step))
            return arrays

        swap = [(d, d ^ 1) for d in range(groups)]
        got_right = lax.ppermute(other_right, "row", swap)
        got_left = lax.ppermute(other_left, "row", swap)
        middle = chips // 2
        ups = [rounds(right, 1, middle), rounds(got_right, 1, middle - 1)]
        downs = [rounds(right, -1, middle - 1), rounds(got_right, -1, middle)]
        distances = sorted(range(chips), key=lambda d: min(d, chips - d))
        early = 2 * (chips // 2 + 1)
        rights = [
            ups[piece][d] if d < len(ups[piece]) else downs[piece][chips - d] for d in distances for piece in range(2)
        ]
        rights = [array.reshape(half, rows, tokens) for array in rights]
        lefts = [array.reshape(half, rows, tokens) for array in (left, got_left)]
        first_sums = pl.pallas_call(
            mix_early,
            out_shape=shape((half, 2 * rows, tokens), BF16),
            in_specs=[whole] * (3 + early),
            out_specs=whole,
            scratch_shapes=[pltpu.VMEM((2 * half * rows, early * rows), BF16)],
            compiler_params=params,
            cost_estimate=pl.CostEstimate(flops=10**9, bytes_accessed=4 * 2**20, transcendentals=0),
            name="mix_early",
        )(token_order(chips, distances[: early // 2], rows), *lefts, *rights[:early])
        keep, send = pl.pallas_call(
            mix_late,
            out_shape=(shape((half, rows, tokens), BF16),) * 2,
            in_specs=[whole] * (4 + len(rights) - early),
            out_specs=(whole,) * 2,
            scratch_shapes=[pltpu.VMEM((2 * half * rows, (len(rights) - early) * rows), BF16)],
            compiler_params=params,
            name="mix_late",
        )(token_order(chips, distances[early // 2 :], rows), *lefts, first_sums, *rights[early:])
        merged = (core, keep.reshape(half * rows, tokens), lax.ppermute(send, "row", swap).reshape(half * rows, tokens))
    else:
        merged = (exchange(mix(exchange(results[0]), False)),)
    results = pl.pallas_call(
        functools.partial(step_kernel, half if by_core else per_group, by_core),
        out_shape=projected + (flat_shape, flat_shape),
        in_specs=[smem] * by_core + [whole] * (len(merged) - by_core + 6),
        out_specs=(whole,) * (len(projected) + 2),
        scratch_shapes=[unit_scratch, panels],
        compiler_params=params,
        name="finish_project",
    )(*merged, pair_t, gate_t, mask, columns, outw_t, proj_t)
    middle_t, gate_t = results[-2:]
    if by_core:
        left, right, other_left, other_right = results[:4]
        got_left = lax.ppermute(other_left, "row", swap)
        got_right = lax.ppermute(other_right, "row", swap)
        operands = [array.reshape(half, rows, tokens) for array in (left, got_left, right, got_right)]
        order = token_order(chips, [-d % chips for d in range(chips)], rows)
        size = half // 2
        part_shape = shape((size, 2 * rows, tokens), BF16)
        pieces = []
        for piece in range(2):
            hops = (middle, middle - 1) if piece == 0 else (middle - 1, middle)
            sums, *travelling = pl.pallas_call(
                functools.partial(scatter_start, piece * size, hops[0], chips - hops[1]),
                out_shape=(shape((size, tokens, tokens), F32), part_shape, part_shape),
                in_specs=[whole] * 5,
                out_specs=(whole,) * 3,
                compiler_params=params,
                name="scatter_start",
            )(order, *operands)
            for way, (step, count) in enumerate(zip((1, -1), hops)):
                for left_over in reversed(range(count)):
                    travelling[way] = along(travelling[way], step)
                    if left_over:
                        travelling[way] = pl.pallas_call(
                            functools.partial(scatter_add, step * left_over % chips),
                            out_shape=part_shape,
                            in_specs=[whole] * 2,
                            out_specs=whole,
                            compiler_params=params,
                            name="scatter_add",
                        )(travelling[way], sums)
            pieces += [sums, *travelling]
        keep, send = pl.pallas_call(
            scatter_end,
            out_shape=(shape((half, rows, tokens), BF16),) * 2,
            in_specs=[whole] * len(pieces),
            out_specs=(whole,) * 2,
            compiler_params=params,
            name="scatter_end",
        )(*pieces)
        merged = (core, keep.reshape(half * rows, tokens), lax.ppermute(send, "row", swap).reshape(half * rows, tokens))
    else:
        merged = (exchange(mix(exchange(results[0]), True)),)
    return pl.pallas_call(
        functools.partial(finish_kernel, by_core),
        out_shape=shape((rows, tokens, channels), BF16),
        in_specs=[smem] * by_core + [whole] * (len(merged) - by_core + 4),
        out_specs=hbm,
        scratch_shapes=[unit_scratch, pltpu.VMEM((rows, tokens, channels), BF16), pltpu.SemaphoreType.DMA((rows,))],
        compiler_params=params,
        name="finish",
    )(*merged, middle_t, gate_t, columns, outw_t)


def solution(mesh):
    rows = ("groups", "row")
    return jax.shard_map(
        on_device,
        mesh=mesh,
        in_specs=(P(rows, None, None), P(rows, None), P(), P(), P(), P(), P()),
        out_specs=P(rows, None, None),
        check_vma=False,
    )
```

```python
import functools

import jax
import jax.numpy as jnp
from jax import lax
from jax.experimental import pallas as pl
from jax.experimental.pallas import tpu as pltpu
from jax.sharding import PartitionSpec as P

F32 = jnp.float32
BF16 = jnp.bfloat16
LANES = 128
NT = (((1,), (1,)), ((), ()))
NN = (((1,), (0,)), ((), ()))
TN = (((0,), (0,)), ((), ()))


def dot(a, b, dims):
    return lax.dot_general(a, b, dims, preferred_element_type=F32)


def unit(values, axis):
    scale = 1.0 / values.shape[axis]
    centred = values - jnp.sum(values, axis=axis, keepdims=True) * scale
    spread = jnp.sum(centred * centred, axis=axis, keepdims=True) * scale
    return centred * lax.rsqrt(spread + 1e-05)


def chunks(rows, tokens, limit):
    wide = max(1, min(rows, limit // tokens))
    return [list(range(start, min(start + wide, rows))) for start in range(0, rows, wide)]


def span(chunk, tokens):
    return slice(chunk[0] * tokens, (chunk[-1] + 1) * tokens)


def lanes(parts):
    return parts[0] if len(parts) == 1 else jnp.concatenate(parts, axis=1)


def affine(values, gain, bias, tokens):
    parts = [values[:, n : n + tokens] * gain + bias for n in range(0, values.shape[1], tokens)]
    return lanes(parts).astype(BF16)


def store_panels(panels, per_group, rows, chunk, tokens, products, half_mask):
    channels = products.shape[0] // 5
    for side in range(2):
        base = 2 * side * channels
        gate, value = products[base : base + channels], products[base + channels : base + 2 * channels]
        gated = (jnp.tanh(gate) + 1.0) * (value * half_mask)
        for h, r in enumerate(chunk):
            for g in range(channels // per_group):
                where = pl.ds((2 * g + side) * per_group * rows + r, per_group, stride=rows)
                for t in range(tokens // LANES):
                    first = h * tokens + t * LANES
                    panels[t, where, :] = gated[g * per_group : (g + 1) * per_group, first : first + LANES]
    return (0.5 * jnp.tanh(products[4 * channels :]) + 0.5).astype(BF16)


def pack_panels(panels, both_ref):
    for t in range(both_ref.shape[1] // LANES):
        both_ref[:, t * LANES : (t + 1) * LANES] = panels[t].astype(BF16)


def split_panels(panels, core_ref, left_ref, right_ref, other_left_ref, other_right_ref):
    size = left_ref.shape[0]
    core = core_ref[0]
    for t in range(left_ref.shape[1] // LANES):
        for side, (own_ref, other_ref) in enumerate(((left_ref, other_left_ref), (right_ref, other_right_ref))):
            for group, ref in ((core, own_ref), (1 - core, other_ref)):
                start = pl.multiple_of((2 * group + side) * size, size)
                ref[:, t * LANES : (t + 1) * LANES] = panels[t, pl.ds(start, size), :].astype(BF16)


def half_lanes(mask_ref, chunk):
    return lanes([mask_ref[r : r + 1].astype(F32) * 0.5 for r in chunk])


def project_kernel(per_group, by_core, *refs):
    core_ref, refs = (refs[0], refs[1:]) if by_core else (None, refs)
    inputs, refs = refs[:7], refs[7:]
    if by_core:
        outs, refs = refs[:4], refs[4:]
        both_ref = None
    else:
        both_ref, refs = refs[0], refs[1:]
    pair_t_ref, gate_t_ref, mask_ref, columns_ref, proj_t_ref, outw_t_ref = refs[:6]
    pair_ref, gain_ref, bias_ref, proj_ref, gatew_ref, outw_ref, panels, sems = refs[6:]
    held = (pair_ref, mask_ref, gain_ref, bias_ref, proj_ref, gatew_ref, outw_ref)
    copies = [pltpu.make_async_copy(src, dst, sems.at[n]) for n, (src, dst) in enumerate(zip(inputs, held))]
    for copy in copies:
        copy.start()
    for copy in copies:
        copy.wait()
    rows, tokens, channels = pair_ref.shape
    small = jnp.concatenate([ref[which] for ref in (gain_ref, bias_ref) for which in range(2)], axis=0).T
    for n in range(4):
        for side in range(2):
            place = 4 * side + n
            columns_ref[2 * n + side] = jnp.broadcast_to(small[:, place : place + 1], (channels, tokens))
    for which in range(2):
        for part in range(4):
            block = proj_ref[which, :, part * channels : (part + 1) * channels].T
            proj_t_ref[which, part * channels : (part + 1) * channels] = block if part % 2 else block * 0.5
        proj_t_ref[which, 4 * channels :] = gatew_ref[which].T * 0.5
        outw_t_ref[which] = outw_ref[which].T
    for chunk in chunks(rows, tokens, 256):
        part = span(chunk, tokens)
        pair_t = lanes([pair_ref[r].T for r in chunk])
        pair_t_ref[:, part] = pair_t
        normed = affine(unit(pair_t.astype(F32), 0), columns_ref[0], columns_ref[1], tokens)
        products = dot(proj_t_ref[0], normed, NN)
        gate_t_ref[:, part] = store_panels(
            panels, per_group, rows, chunk, tokens, products, half_lanes(mask_ref, chunk)
        )
    if by_core:
        split_panels(panels, core_ref, *outs)
    else:
        pack_panels(panels, both_ref)


def gated_side(panels, rows, chunk, tokens, products, half_mask):
    channels = products.shape[0] // 2
    gated = (jnp.tanh(products[:channels]) + 1.0) * (products[channels:] * half_mask)
    for h, r in enumerate(chunk):
        for c in range(0, channels, 8):
            for t in range(tokens // LANES):
                first = h * tokens + t * LANES
                panels[t, pl.ds(c * rows + r, 8, stride=rows), :] = gated[c : c + 8, first : first + LANES]


def split_side(panels, core_ref, own_ref, other_ref):
    size = own_ref.shape[0]
    for t in range(own_ref.shape[1] // LANES):
        for half, ref in ((core_ref[0], own_ref), (1 - core_ref[0], other_ref)):
            start = pl.multiple_of(half * size, size)
            ref[:, t * LANES : (t + 1) * LANES] = panels[t, pl.ds(start, size), :].astype(BF16)


def side_weights(proj_ref, side, channels):
    gate, value = [proj_ref[0, :, (2 * side + n) * channels : (2 * side + n + 1) * channels].T for n in range(2)]
    return jnp.concatenate([gate * 0.5, value], axis=0)


def fetch(pairs, sems):
    copies = [pltpu.make_async_copy(src, dst, sems.at[n]) for n, (src, dst) in enumerate(pairs)]
    for copy in copies:
        copy.start()
    for copy in copies:
        copy.wait()


def right_kernel(core_ref, pair_hbm, mask_hbm, gain_hbm, bias_hbm, proj_hbm, gatew_hbm, outw_hbm, *refs):
    own_ref, other_ref, pair_t_ref, normed_t_ref, mask_ref, columns_ref, proj_ref, gatew_ref, outw_ref = refs[:9]
    pair_ref, gain_ref, bias_ref, panels, sems = refs[9:]
    held = (pair_ref, mask_ref, gain_ref, bias_ref, proj_ref, gatew_ref, outw_ref)
    fetch(zip((pair_hbm, mask_hbm, gain_hbm, bias_hbm, proj_hbm, gatew_hbm, outw_hbm), held), sems)
    rows, tokens, channels = pair_ref.shape
    small = jnp.concatenate([ref[which] for ref in (gain_ref, bias_ref) for which in range(2)], axis=0).T
    for n in range(4):
        for side in range(2):
            place = 4 * side + n
            columns_ref[2 * n + side] = jnp.broadcast_to(small[:, place : place + 1], (channels, tokens))
    weights = side_weights(proj_ref, 1, channels)
    for chunk in chunks(rows, tokens, 256):
        part = span(chunk, tokens)
        pair_t = lanes([pair_ref[r].T for r in chunk])
        pair_t_ref[:, part] = pair_t
        normed = affine(unit(pair_t.astype(F32), 0), columns_ref[0], columns_ref[1], tokens)
        normed_t_ref[:, part] = normed
        gated_side(panels, rows, chunk, tokens, dot(weights, normed, NN), half_lanes(mask_ref, chunk))
    split_side(panels, core_ref, own_ref, other_ref)


def left_kernel(core_ref, normed_t_ref, mask_ref, proj_ref, gatew_ref, outw_ref, *refs):
    own_ref, other_ref, gate_t_ref, proj_t_ref, outw_t_ref, panels = refs
    rows, tokens = mask_ref.shape
    channels = normed_t_ref.shape[0]
    weights = side_weights(proj_ref, 0, channels)
    gate_weights = gatew_ref[0].T * 0.5
    for chunk in chunks(rows, tokens, 256):
        part = span(chunk, tokens)
        normed = normed_t_ref[:, part]
        gated_side(panels, rows, chunk, tokens, dot(weights, normed, NN), half_lanes(mask_ref, chunk))
        gate_t_ref[:, part] = (0.5 * jnp.tanh(dot(gate_weights, normed, NN)) + 0.5).astype(BF16)
    split_side(panels, core_ref, own_ref, other_ref)
    for part in range(4):
        block = proj_ref[1, :, part * channels : (part + 1) * channels].T
        proj_t_ref[1, part * channels : (part + 1) * channels] = block if part % 2 else block * 0.5
    proj_t_ref[1, 4 * channels :] = gatew_ref[1].T * 0.5
    for which in range(2):
        outw_t_ref[which] = outw_ref[which].T


def mix_kernel(per_group, rows, incoming, both_ref, product_ref):
    groups, _, tokens = both_ref.shape
    step = 2 * rows

    def matrices(side, pair):
        start = (side * per_group + 2 * pair) * rows
        block = both_ref[:, start : start + step, :].astype(F32)
        return [block[:, h * rows : (h + 1) * rows].reshape(groups * rows, tokens).astype(BF16) for h in range(2)]

    for pair in range(per_group // 2):
        lefts, rights = matrices(0, pair), matrices(1, pair)
        sums = [
            dot(left, right, TN if incoming else NT).reshape(groups, rows, tokens)
            for left, right in zip(lefts, rights)
        ]
        product_ref[:, pair * step : (pair + 1) * step, :] = jnp.concatenate(sums, axis=1).astype(BF16)


def ring_chips(count):
    return list(range(0, count, 2)) + list(range(count - 1, 0, -2))


def token_order(chips, distances, rows):
    device = lax.axis_index("row")
    chip, core = device // 2, device % 2
    place = jnp.where(chip % 2 == 0, chip // 2, chips - 1 - chip // 2)
    extent = (2 * len(distances) * rows, 2 * chips * rows)
    lane, token = (lax.broadcasted_iota(jnp.int32, extent, axis) for axis in range(2))
    first = jnp.zeros(extent, jnp.int32)
    for n, d in enumerate(distances):
        source = place - d + jnp.where(place < d, chips, 0)
        source = jnp.where(2 * source < chips, 2 * source, 2 * (chips - 1 - source) + 1)
        for piece in range(2):
            start = (2 * n + piece) * rows
            block = 2 * source + (1 - core if piece else core)
            first = jnp.where((lane >= start) & (lane < start + rows), block * rows - start, first)
    return (token == lane + first).astype(BF16)


def gathered_sums(order_ref, own_ref, got_ref, rights, sums_ref):
    count, rows, tokens = own_ref.shape
    for c in range(count):
        left = jnp.concatenate([own_ref[c].astype(F32), got_ref[c].astype(F32)], axis=0).astype(BF16)
        right = jnp.concatenate([ref[c].astype(F32) for ref in rights], axis=0).astype(BF16)
        sums_ref[2 * rows * c : 2 * rows * (c + 1)] = dot(left, right, NT).astype(BF16)
    order = order_ref[...]
    group = 16
    for first in range(0, count, group):
        sums = dot(sums_ref[2 * rows * first : 2 * rows * (first + group)], order, NN)
        yield slice(first, first + group), sums.reshape(group, 2 * rows, tokens)


def mix_early(order_ref, own_ref, got_ref, *refs):
    rights, (early_ref, sums_ref) = refs[:-2], refs[-2:]
    for part, sums in gathered_sums(order_ref, own_ref, got_ref, rights, sums_ref):
        early_ref[part] = sums.astype(BF16)


def mix_late(order_ref, own_ref, got_ref, early_ref, *refs):
    rights, (keep_ref, send_ref, sums_ref) = refs[:-3], refs[-3:]
    rows = own_ref.shape[1]
    for part, sums in gathered_sums(order_ref, own_ref, got_ref, rights, sums_ref):
        sums = sums + early_ref[part].astype(F32)
        keep_ref[part] = sums[:, :rows].astype(BF16)
        send_ref[part] = sums[:, rows:].astype(BF16)


def finish_rows(emit, rows, channels, tokens, load, pair_t_ref, gate_t_ref, gain, bias, outw_t, unit_scratch):
    tiles = range(tokens // LANES)
    parts = [slice(first * rows, (first + 16) * rows) for first in range(0, channels, 16)]

    def sums(part):
        return load(part).reshape(16, rows, tokens)

    average = sum(jnp.sum(sums(part), axis=0) for part in parts) * (1.0 / channels)
    spread = sum(jnp.sum(jnp.square(sums(part) - average), axis=0) for part in parts) * (1.0 / channels)
    inverse = lax.rsqrt(spread + 1e-05)
    for part in parts:
        units = ((sums(part) - average) * inverse).reshape(16 * rows, tokens)
        for t in tiles:
            unit_scratch[t, part, :] = units[:, t * LANES : (t + 1) * LANES]
    for chunk in chunks(rows, tokens, 256):
        part = span(chunk, tokens)
        units = lanes([unit_scratch[t, pl.ds(r, channels, stride=rows), :] for r in chunk for t in tiles])
        normed = affine(units, gain, bias, tokens)
        change = gate_t_ref[:, part].astype(F32) * dot(outw_t, normed, NN)
        emit(chunk, part, (pair_t_ref[:, part].astype(F32) + change).astype(BF16))


def step_kernel(per_group, by_core, *refs):
    if not by_core:
        merged_ref, refs = refs[0], refs[1:]
        return step_rows(per_group, lambda part: merged_ref[part].astype(F32), *refs)
    core_ref, refs = refs[0], refs[1:]
    step_rows(per_group, core_halves(core_ref, refs[0], refs[1]), *refs[2:], core_ref=core_ref)


def core_halves(core_ref, keep_ref, got_ref):
    size = keep_ref.shape[0]

    def load(part):
        late = part.start >= size
        part = slice(part.start - size, part.stop - size) if late else part
        keep, got = keep_ref[part].astype(F32), got_ref[part].astype(F32)
        return jnp.where(jnp.full(keep.shape, core_ref[0]) == int(late), keep, got)

    return load


def step_rows(
    per_group, load, pair_t_ref, gate_t_ref, mask_ref, columns_ref, outw_t_ref, proj_t_ref, *refs, core_ref=None
):
    outs, (middle_t_ref, gate1_t_ref, unit_scratch, panels) = refs[:-4], refs[-4:]
    rows, tokens = mask_ref.shape

    def emit(chunk, part, middle):
        middle_t_ref[:, part] = middle
        normed = affine(unit(middle.astype(F32), 0), columns_ref[4], columns_ref[5], tokens)
        products = dot(proj_t_ref[1], normed, NN)
        gate1_t_ref[:, part] = store_panels(
            panels, per_group, rows, chunk, tokens, products, half_lanes(mask_ref, chunk)
        )

    finish_rows(
        emit, rows, pair_t_ref.shape[0], tokens, load, pair_t_ref, gate_t_ref, columns_ref[2], columns_ref[3],
        outw_t_ref[0], unit_scratch,
    )
    if core_ref is None:
        pack_panels(panels, *outs)
    else:
        split_panels(panels, core_ref, *outs)


def finish_kernel(by_core, *refs):
    if by_core:
        load, refs = core_halves(*refs[:3]), refs[3:]
    else:
        merged_ref, refs = refs[0], refs[1:]

        def load(part):
            return merged_ref[part].astype(F32)

    middle_t_ref, gate_t_ref, columns_ref, outw_t_ref, result_ref, unit_scratch, done, sems = refs
    rows, tokens, _ = result_ref.shape
    copies = []

    def emit(chunk, part, result):
        for h, r in enumerate(chunk):
            done[r] = result[:, h * tokens : (h + 1) * tokens].T
            copies.append(pltpu.make_async_copy(done.at[r], result_ref.at[r], sems.at[r]))
            copies[-1].start()

    finish_rows(
        emit, rows, middle_t_ref.shape[0], tokens, load, middle_t_ref, gate_t_ref,
        columns_ref[6], columns_ref[7], outw_t_ref[1], unit_scratch,
    )
    for copy in copies:
        copy.wait()


def scatter_start(first, up, down, order_ref, own_left, got_left, own_right, got_right, sums_ref, up_ref, down_ref):
    rows, tokens = own_left.shape[1:]
    count = sums_ref.shape[0]

    def both(own, got, c):
        return jnp.concatenate([own[first + c].astype(F32), got[first + c].astype(F32)], axis=0).astype(BF16)

    lefts = jnp.concatenate([both(own_left, got_left, c) for c in range(count)], axis=0)
    lefts = dot(lefts, order_ref[...], NT).astype(BF16).reshape(count, 2 * rows, tokens)
    for c in range(count):
        sums_ref[c] = dot(lefts[c], both(own_right, got_right, c), TN)
    for distance, ref in ((up, up_ref), (down, down_ref)):
        ref[...] = at_distance(sums_ref, distance, 2 * rows).astype(BF16)


def at_distance(sums_ref, distance, count):
    return sums_ref[:, distance * count : (distance + 1) * count, :]


def scatter_add(distance, got_ref, sums_ref, out_ref):
    out_ref[...] = (got_ref[...].astype(F32) + at_distance(sums_ref, distance, got_ref.shape[1])).astype(BF16)


def scatter_end(*refs):
    pieces, (keep_ref, send_ref) = refs[:-2], refs[-2:]
    rows = keep_ref.shape[1]
    first = 0
    for n in range(0, len(pieces), 3):
        sums_ref, up_ref, down_ref = pieces[n : n + 3]
        count = sums_ref.shape[0]
        sums = at_distance(sums_ref, 0, 2 * rows) + up_ref[...].astype(F32) + down_ref[...].astype(F32)
        keep_ref[first : first + count] = sums[:, :rows].astype(BF16)
        send_ref[first : first + count] = sums[:, rows:].astype(BF16)
        first += count


def on_device(*inputs):
    groups = lax.axis_size("row")
    rows, tokens, channels = inputs[0].shape
    per_group = channels // groups
    whole = pl.BlockSpec(memory_space=pltpu.VMEM)
    hbm = pl.BlockSpec(memory_space=pltpu.HBM)
    params = pltpu.CompilerParams(vmem_limit_bytes=32 * 1024 * 1024)
    shape = jax.ShapeDtypeStruct
    both_shape = shape((2 * channels * rows, tokens), BF16)
    flat_shape = shape((channels, rows * tokens), BF16)
    panels = pltpu.VMEM((tokens // LANES, 2 * channels * rows, LANES), F32)
    unit_scratch = pltpu.VMEM((tokens // LANES, channels * rows, LANES), F32)

    def exchange(array):
        return lax.all_to_all(array, "row", split_axis=0, concat_axis=0, tiled=True)

    def mix(both, incoming):
        product = pl.pallas_call(
            functools.partial(mix_kernel, per_group, rows, incoming),
            out_shape=shape((groups, per_group * rows, tokens), BF16),
            in_specs=[whole],
            out_specs=whole,
            compiler_params=params,
            name="mix",
        )(both.reshape(groups, 2 * per_group * rows, tokens))
        return product.reshape(channels * rows, tokens)

    half = channels // 2
    by_core = groups % 4 == 0 and groups * rows * tokens * half * 2 <= 4 * 2**20
    smem = pl.BlockSpec(memory_space=pltpu.SMEM)
    core = (lax.axis_index("row") % 2).astype(jnp.int32).reshape(1)
    half_shape = shape((half * rows, tokens), BF16)
    projected = (half_shape,) * 4 if by_core else (both_shape,)
    columns_shape = shape((8, channels, tokens), F32)
    proj_t_shape = shape((2, 5 * channels, channels), BF16)
    if by_core:
        pair, mask, gains, biases, proj, gatew, outw = (
            pltpu.with_memory_space_constraint(a, pltpu.HBM) for a in inputs
        )
        side_panels = pltpu.VMEM((tokens // LANES, channels * rows, LANES), F32)

        def like(array):
            return shape(array.shape, array.dtype)

        right, other_right, pair_t, normed_t, mask, columns, proj, gatew, outw = pl.pallas_call(
            right_kernel,
            out_shape=(half_shape, half_shape, flat_shape, flat_shape, like(mask), columns_shape)
            + (like(proj), like(gatew), like(outw)),
            in_specs=[smem] + [hbm] * 7,
            out_specs=(whole,) * 9,
            scratch_shapes=[pltpu.VMEM(a.shape, a.dtype) for a in (pair, gains, biases)]
            + [side_panels, pltpu.SemaphoreType.DMA((7,))],
            compiler_params=params,
            name="project_right",
        )(core, pair, mask, gains, biases, proj, gatew, outw)
        left, other_left, gate_t, proj_t, outw_t = pl.pallas_call(
            left_kernel,
            out_shape=(half_shape, half_shape, flat_shape, proj_t_shape, shape(outw.shape, BF16)),
            in_specs=[smem] + [whole] * 5,
            out_specs=(whole,) * 5,
            scratch_shapes=[side_panels],
            compiler_params=params,
            cost_estimate=pl.CostEstimate(flops=10**9, bytes_accessed=4 * 2**20, transcendentals=0),
            name="project_left",
        )(core, normed_t, mask, proj, gatew, outw)
    else:
        results = pl.pallas_call(
            functools.partial(project_kernel, half if by_core else per_group, by_core),
            out_shape=projected
            + (
                flat_shape,
                flat_shape,
                shape((rows, tokens), inputs[1].dtype),
                shape((8, channels, tokens), F32),
                shape((2, 5 * channels, channels), BF16),
                shape((2, channels, channels), BF16),
            ),
            in_specs=[smem] * by_core + [hbm] * 7,
            out_specs=(whole,) * (len(projected) + 6),
            scratch_shapes=[pltpu.VMEM(inputs[n].shape, inputs[n].dtype) for n in (0, 2, 3, 4, 5, 6)]
            + [panels, pltpu.SemaphoreType.DMA((7,))],
            compiler_params=params,
            name="project",
        )(*[core] * by_core, *(pltpu.with_memory_space_constraint(a, pltpu.HBM) for a in inputs))
        pair_t, gate_t, mask, columns, proj_t, outw_t = results[-6:]
    if by_core:
        chips = groups // 2
        ring = ring_chips(chips)

        def along(array, step):
            pairs = [(2 * q + c, 2 * ring[(p + step) % chips] + c) for p, q in enumerate(ring) for c in range(2)]
            return lax.ppermute(array, "row", pairs)

        def rounds(array, step, count):
            arrays = [array]
            for _ in range(count):
                arrays.append(along(arrays[-1], step))
            return arrays

        swap = [(d, d ^ 1) for d in range(groups)]
        got_right = lax.ppermute(other_right, "row", swap)
        got_left = lax.ppermute(other_left, "row", swap)
        middle = chips // 2
        ups = [rounds(right, 1, middle), rounds(got_right, 1, middle - 1)]
        downs = [rounds(right, -1, middle - 1), rounds(got_right, -1, middle)]
        distances = sorted(range(chips), key=lambda d: min(d, chips - d))
        early = 2 * (chips - 1)
        rights = [
            ups[piece][d] if d < len(ups[piece]) else downs[piece][chips - d] for d in distances for piece in range(2)
        ]
        rights = [array.reshape(half, rows, tokens) for array in rights]
        lefts = [array.reshape(half, rows, tokens) for array in (left, got_left)]
        first_sums = pl.pallas_call(
            mix_early,
            out_shape=shape((half, 2 * rows, tokens), BF16),
            in_specs=[whole] * (3 + early),
            out_specs=whole,
            scratch_shapes=[pltpu.VMEM((2 * half * rows, early * rows), BF16)],
            compiler_params=params,
            cost_estimate=pl.CostEstimate(flops=10**9, bytes_accessed=4 * 2**20, transcendentals=0),
            name="mix_early",
        )(token_order(chips, distances[: early // 2], rows), *lefts, *rights[:early])
        keep, send = pl.pallas_call(
            mix_late,
            out_shape=(shape((half, rows, tokens), BF16),) * 2,
            in_specs=[whole] * (4 + len(rights) - early),
            out_specs=(whole,) * 2,
            scratch_shapes=[pltpu.VMEM((2 * half * rows, (len(rights) - early) * rows), BF16)],
            compiler_params=params,
            name="mix_late",
        )(token_order(chips, distances[early // 2 :], rows), *lefts, first_sums, *rights[early:])
        merged = (core, keep.reshape(half * rows, tokens), lax.ppermute(send, "row", swap).reshape(half * rows, tokens))
    else:
        merged = (exchange(mix(exchange(results[0]), False)),)
    results = pl.pallas_call(
        functools.partial(step_kernel, half if by_core else per_group, by_core),
        out_shape=projected + (flat_shape, flat_shape),
        in_specs=[smem] * by_core + [whole] * (len(merged) - by_core + 6),
        out_specs=(whole,) * (len(projected) + 2),
        scratch_shapes=[unit_scratch, panels],
        compiler_params=params,
        name="finish_project",
    )(*merged, pair_t, gate_t, mask, columns, outw_t, proj_t)
    middle_t, gate_t = results[-2:]
    if by_core:
        left, right, other_left, other_right = results[:4]
        got_left = lax.ppermute(other_left, "row", swap)
        got_right = lax.ppermute(other_right, "row", swap)
        operands = [array.reshape(half, rows, tokens) for array in (left, got_left, right, got_right)]
        order = token_order(chips, [-d % chips for d in range(chips)], rows)
        size = half // 2
        part_shape = shape((size, 2 * rows, tokens), BF16)
        pieces = []
        for piece in range(2):
            hops = (middle, middle - 1) if piece == 0 else (middle - 1, middle)
            sums, *travelling = pl.pallas_call(
                functools.partial(scatter_start, piece * size, hops[0], chips - hops[1]),
                out_shape=(shape((size, tokens, tokens), F32), part_shape, part_shape),
                in_specs=[whole] * 5,
                out_specs=(whole,) * 3,
                compiler_params=params,
                name="scatter_start",
            )(order, *operands)
            for way, (step, count) in enumerate(zip((1, -1), hops)):
                for left_over in reversed(range(count)):
                    travelling[way] = along(travelling[way], step)
                    if left_over:
                        travelling[way] = pl.pallas_call(
                            functools.partial(scatter_add, step * left_over % chips),
                            out_shape=part_shape,
                            in_specs=[whole] * 2,
                            out_specs=whole,
                            compiler_params=params,
                            name="scatter_add",
                        )(travelling[way], sums)
            pieces += [sums, *travelling]
        keep, send = pl.pallas_call(
            scatter_end,
            out_shape=(shape((half, rows, tokens), BF16),) * 2,
            in_specs=[whole] * len(pieces),
            out_specs=(whole,) * 2,
            compiler_params=params,
            name="scatter_end",
        )(*pieces)
        merged = (core, keep.reshape(half * rows, tokens), lax.ppermute(send, "row", swap).reshape(half * rows, tokens))
    else:
        merged = (exchange(mix(exchange(results[0]), True)),)
    return pl.pallas_call(
        functools.partial(finish_kernel, by_core),
        out_shape=shape((rows, tokens, channels), BF16),
        in_specs=[smem] * by_core + [whole] * (len(merged) - by_core + 4),
        out_specs=hbm,
        scratch_shapes=[unit_scratch, pltpu.VMEM((rows, tokens, channels), BF16), pltpu.SemaphoreType.DMA((rows,))],
        compiler_params=params,
        name="finish",
    )(*merged, middle_t, gate_t, columns, outw_t)


def solution(mesh):
    rows = ("groups", "row")
    return jax.shard_map(
        on_device,
        mesh=mesh,
        in_specs=(P(rows, None, None), P(rows, None), P(), P(), P(), P(), P()),
        out_specs=P(rows, None, None),
        check_vma=False,
    )
```

```python
import functools

import jax
import jax.numpy as jnp
from jax import lax
from jax.experimental import pallas as pl
from jax.experimental.pallas import tpu as pltpu
from jax.sharding import PartitionSpec as P

F32 = jnp.float32
BF16 = jnp.bfloat16
LANES = 128
NT = (((1,), (1,)), ((), ()))
NN = (((1,), (0,)), ((), ()))
TN = (((0,), (0,)), ((), ()))


def dot(a, b, dims):
    return lax.dot_general(a, b, dims, preferred_element_type=F32)


def unit(values, axis):
    scale = 1.0 / values.shape[axis]
    centred = values - jnp.sum(values, axis=axis, keepdims=True) * scale
    spread = jnp.sum(centred * centred, axis=axis, keepdims=True) * scale
    return centred * lax.rsqrt(spread + 1e-05)


def chunks(rows, tokens, limit):
    wide = max(1, min(rows, limit // tokens))
    return [list(range(start, min(start + wide, rows))) for start in range(0, rows, wide)]


def span(chunk, tokens):
    return slice(chunk[0] * tokens, (chunk[-1] + 1) * tokens)


def lanes(parts):
    return parts[0] if len(parts) == 1 else jnp.concatenate(parts, axis=1)


def affine(values, gain, bias, tokens):
    parts = [values[:, n : n + tokens] * gain + bias for n in range(0, values.shape[1], tokens)]
    return lanes(parts).astype(BF16)


def store_panels(panels, per_group, rows, chunk, tokens, products, half_mask):
    channels = products.shape[0] // 5
    for side in range(2):
        base = 2 * side * channels
        gate, value = products[base : base + channels], products[base + channels : base + 2 * channels]
        gated = (jnp.tanh(gate) + 1.0) * (value * half_mask)
        for h, r in enumerate(chunk):
            for g in range(channels // per_group):
                where = pl.ds((2 * g + side) * per_group * rows + r, per_group, stride=rows)
                for t in range(tokens // LANES):
                    first = h * tokens + t * LANES
                    panels[t, where, :] = gated[g * per_group : (g + 1) * per_group, first : first + LANES]
    return (0.5 * jnp.tanh(products[4 * channels :]) + 0.5).astype(BF16)


def pack_panels(panels, both_ref):
    for t in range(both_ref.shape[1] // LANES):
        both_ref[:, t * LANES : (t + 1) * LANES] = panels[t].astype(BF16)


def split_panels(panels, core_ref, left_ref, right_ref, other_left_ref, other_right_ref):
    size = left_ref.shape[0]
    core = core_ref[0]
    for t in range(left_ref.shape[1] // LANES):
        for side, (own_ref, other_ref) in enumerate(((left_ref, other_left_ref), (right_ref, other_right_ref))):
            for group, ref in ((core, own_ref), (1 - core, other_ref)):
                start = pl.multiple_of((2 * group + side) * size, size)
                ref[:, t * LANES : (t + 1) * LANES] = panels[t, pl.ds(start, size), :].astype(BF16)


def half_lanes(mask_ref, chunk):
    return lanes([mask_ref[r : r + 1].astype(F32) * 0.5 for r in chunk])


def project_kernel(per_group, by_core, *refs):
    core_ref, refs = (refs[0], refs[1:]) if by_core else (None, refs)
    inputs, refs = refs[:7], refs[7:]
    if by_core:
        outs, refs = refs[:4], refs[4:]
        both_ref = None
    else:
        both_ref, refs = refs[0], refs[1:]
    pair_t_ref, gate_t_ref, mask_ref, columns_ref, proj_t_ref, outw_t_ref = refs[:6]
    pair_ref, gain_ref, bias_ref, proj_ref, gatew_ref, outw_ref, panels, sems = refs[6:]
    held = (pair_ref, mask_ref, gain_ref, bias_ref, proj_ref, gatew_ref, outw_ref)
    copies = [pltpu.make_async_copy(src, dst, sems.at[n]) for n, (src, dst) in enumerate(zip(inputs, held))]
    for copy in copies:
        copy.start()
    for copy in copies:
        copy.wait()
    rows, tokens, channels = pair_ref.shape
    small = jnp.concatenate([ref[which] for ref in (gain_ref, bias_ref) for which in range(2)], axis=0).T
    for n in range(4):
        for side in range(2):
            place = 4 * side + n
            columns_ref[2 * n + side] = jnp.broadcast_to(small[:, place : place + 1], (channels, tokens))
    for which in range(2):
        for part in range(4):
            block = proj_ref[which, :, part * channels : (part + 1) * channels].T
            proj_t_ref[which, part * channels : (part + 1) * channels] = block if part % 2 else block * 0.5
        proj_t_ref[which, 4 * channels :] = gatew_ref[which].T * 0.5
        outw_t_ref[which] = outw_ref[which].T
    for chunk in chunks(rows, tokens, 256):
        part = span(chunk, tokens)
        pair_t = lanes([pair_ref[r].T for r in chunk])
        pair_t_ref[:, part] = pair_t
        normed = affine(unit(pair_t.astype(F32), 0), columns_ref[0], columns_ref[1], tokens)
        products = dot(proj_t_ref[0], normed, NN)
        gate_t_ref[:, part] = store_panels(
            panels, per_group, rows, chunk, tokens, products, half_lanes(mask_ref, chunk)
        )
    if by_core:
        split_panels(panels, core_ref, *outs)
    else:
        pack_panels(panels, both_ref)


def gated_side(panels, rows, chunk, tokens, products, half_mask):
    channels = products.shape[0] // 2
    gated = (jnp.tanh(products[:channels]) + 1.0) * (products[channels:] * half_mask)
    for h, r in enumerate(chunk):
        for c in range(0, channels, 8):
            for t in range(tokens // LANES):
                first = h * tokens + t * LANES
                panels[t, pl.ds(c * rows + r, 8, stride=rows), :] = gated[c : c + 8, first : first + LANES]


def split_side(panels, core_ref, own_ref, other_ref):
    size = own_ref.shape[0]
    for t in range(own_ref.shape[1] // LANES):
        for half, ref in ((core_ref[0], own_ref), (1 - core_ref[0], other_ref)):
            start = pl.multiple_of(half * size, size)
            ref[:, t * LANES : (t + 1) * LANES] = panels[t, pl.ds(start, size), :].astype(BF16)


def side_weights(proj_ref, side, channels):
    gate, value = [proj_ref[0, :, (2 * side + n) * channels : (2 * side + n + 1) * channels].T for n in range(2)]
    return jnp.concatenate([gate * 0.5, value], axis=0)


def fetch(pairs, sems):
    copies = [pltpu.make_async_copy(src, dst, sems.at[n]) for n, (src, dst) in enumerate(pairs)]
    for copy in copies:
        copy.start()
    for copy in copies:
        copy.wait()


def right_kernel(core_ref, pair_hbm, mask_hbm, gain_hbm, bias_hbm, proj_hbm, gatew_hbm, outw_hbm, *refs):
    own_ref, other_ref, pair_t_ref, normed_t_ref, mask_ref, columns_ref, proj_ref, gatew_ref, outw_ref = refs[:9]
    pair_ref, gain_ref, bias_ref, panels, sems = refs[9:]
    held = (pair_ref, mask_ref, gain_ref, bias_ref, proj_ref, gatew_ref, outw_ref)
    fetch(zip((pair_hbm, mask_hbm, gain_hbm, bias_hbm, proj_hbm, gatew_hbm, outw_hbm), held), sems)
    rows, tokens, channels = pair_ref.shape
    small = jnp.concatenate([ref[which] for ref in (gain_ref, bias_ref) for which in range(2)], axis=0).T
    for n in range(4):
        for side in range(2):
            place = 4 * side + n
            columns_ref[2 * n + side] = jnp.broadcast_to(small[:, place : place + 1], (channels, tokens))
    weights = side_weights(proj_ref, 1, channels)
    for chunk in chunks(rows, tokens, 256):
        part = span(chunk, tokens)
        pair_t = lanes([pair_ref[r].T for r in chunk])
        pair_t_ref[:, part] = pair_t
        normed = affine(unit(pair_t.astype(F32), 0), columns_ref[0], columns_ref[1], tokens)
        normed_t_ref[:, part] = normed
        gated_side(panels, rows, chunk, tokens, dot(weights, normed, NN), half_lanes(mask_ref, chunk))
    split_side(panels, core_ref, own_ref, other_ref)


def left_kernel(core_ref, normed_t_ref, mask_ref, proj_ref, gatew_ref, outw_ref, *refs):
    own_ref, other_ref, gate_t_ref, proj_t_ref, outw_t_ref, panels = refs
    rows, tokens = mask_ref.shape
    channels = normed_t_ref.shape[0]
    weights = side_weights(proj_ref, 0, channels)
    gate_weights = gatew_ref[0].T * 0.5
    for chunk in chunks(rows, tokens, 256):
        part = span(chunk, tokens)
        normed = normed_t_ref[:, part]
        gated_side(panels, rows, chunk, tokens, dot(weights, normed, NN), half_lanes(mask_ref, chunk))
        gate_t_ref[:, part] = (0.5 * jnp.tanh(dot(gate_weights, normed, NN)) + 0.5).astype(BF16)
    split_side(panels, core_ref, own_ref, other_ref)
    for part in range(4):
        block = proj_ref[1, :, part * channels : (part + 1) * channels].T
        proj_t_ref[1, part * channels : (part + 1) * channels] = block if part % 2 else block * 0.5
    proj_t_ref[1, 4 * channels :] = gatew_ref[1].T * 0.5
    for which in range(2):
        outw_t_ref[which] = outw_ref[which].T


def mix_kernel(per_group, rows, incoming, both_ref, product_ref):
    groups, _, tokens = both_ref.shape
    step = 2 * rows

    def matrices(side, pair):
        start = (side * per_group + 2 * pair) * rows
        block = both_ref[:, start : start + step, :].astype(F32)
        return [block[:, h * rows : (h + 1) * rows].reshape(groups * rows, tokens).astype(BF16) for h in range(2)]

    for pair in range(per_group // 2):
        lefts, rights = matrices(0, pair), matrices(1, pair)
        sums = [
            dot(left, right, TN if incoming else NT).reshape(groups, rows, tokens)
            for left, right in zip(lefts, rights)
        ]
        product_ref[:, pair * step : (pair + 1) * step, :] = jnp.concatenate(sums, axis=1).astype(BF16)


def ring_chips(count):
    return list(range(0, count, 2)) + list(range(count - 1, 0, -2))


def token_order(chips, distances, rows):
    device = lax.axis_index("row")
    chip, core = device // 2, device % 2
    place = jnp.where(chip % 2 == 0, chip // 2, chips - 1 - chip // 2)
    extent = (2 * len(distances) * rows, 2 * chips * rows)
    lane, token = (lax.broadcasted_iota(jnp.int32, extent, axis) for axis in range(2))
    first = jnp.zeros(extent, jnp.int32)
    for n, d in enumerate(distances):
        source = place - d + jnp.where(place < d, chips, 0)
        source = jnp.where(2 * source < chips, 2 * source, 2 * (chips - 1 - source) + 1)
        for piece in range(2):
            start = (2 * n + piece) * rows
            block = 2 * source + (1 - core if piece else core)
            first = jnp.where((lane >= start) & (lane < start + rows), block * rows - start, first)
    return (token == lane + first).astype(BF16)


def gathered_sums(order_ref, own_ref, got_ref, rights, sums_ref):
    count, rows, tokens = own_ref.shape
    for c in range(count):
        left = jnp.concatenate([own_ref[c].astype(F32), got_ref[c].astype(F32)], axis=0).astype(BF16)
        right = jnp.concatenate([ref[c].astype(F32) for ref in rights], axis=0).astype(BF16)
        sums_ref[2 * rows * c : 2 * rows * (c + 1)] = dot(left, right, NT).astype(BF16)
    order = order_ref[...]
    group = 16
    for first in range(0, count, group):
        sums = dot(sums_ref[2 * rows * first : 2 * rows * (first + group)], order, NN)
        yield slice(first, first + group), sums.reshape(group, 2 * rows, tokens)


def mix_early(order_ref, own_ref, got_ref, *refs):
    rights, (early_ref, sums_ref) = refs[:-2], refs[-2:]
    for part, sums in gathered_sums(order_ref, own_ref, got_ref, rights, sums_ref):
        early_ref[part] = sums.astype(BF16)


def mix_late(order_ref, own_ref, got_ref, early_ref, *refs):
    rights, (keep_ref, send_ref, sums_ref) = refs[:-3], refs[-3:]
    rows = own_ref.shape[1]
    for part, sums in gathered_sums(order_ref, own_ref, got_ref, rights, sums_ref):
        sums = sums + early_ref[part].astype(F32)
        keep_ref[part] = sums[:, :rows].astype(BF16)
        send_ref[part] = sums[:, rows:].astype(BF16)


def finish_rows(emit, rows, channels, tokens, load, pair_t_ref, gate_t_ref, gain, bias, outw_t, unit_scratch):
    tiles = range(tokens // LANES)
    parts = [slice(first * rows, (first + 16) * rows) for first in range(0, channels, 16)]

    def sums(part):
        return load(part).reshape(16, rows, tokens)

    average = sum(jnp.sum(sums(part), axis=0) for part in parts) * (1.0 / channels)
    spread = sum(jnp.sum(jnp.square(sums(part) - average), axis=0) for part in parts) * (1.0 / channels)
    inverse = lax.rsqrt(spread + 1e-05)
    for part in parts:
        units = ((sums(part) - average) * inverse).reshape(16 * rows, tokens)
        for t in tiles:
            unit_scratch[t, part, :] = units[:, t * LANES : (t + 1) * LANES]
    for chunk in chunks(rows, tokens, 512):
        part = span(chunk, tokens)
        units = lanes([unit_scratch[t, pl.ds(r, channels, stride=rows), :] for r in chunk for t in tiles])
        normed = affine(units, gain, bias, tokens)
        change = gate_t_ref[:, part].astype(F32) * dot(outw_t, normed, NN)
        emit(chunk, part, (pair_t_ref[:, part].astype(F32) + change).astype(BF16))


def step_kernel(per_group, by_core, *refs):
    if not by_core:
        merged_ref, refs = refs[0], refs[1:]
        return step_rows(per_group, lambda part: merged_ref[part].astype(F32), *refs)
    core_ref, refs = refs[0], refs[1:]
    step_rows(per_group, core_halves(core_ref, refs[0], refs[1]), *refs[2:], core_ref=core_ref)


def core_halves(core_ref, keep_ref, got_ref):
    size = keep_ref.shape[0]

    def load(part):
        late = part.start >= size
        part = slice(part.start - size, part.stop - size) if late else part
        keep, got = keep_ref[part].astype(F32), got_ref[part].astype(F32)
        return jnp.where(jnp.full(keep.shape, core_ref[0]) == int(late), keep, got)

    return load


def step_rows(
    per_group, load, pair_t_ref, gate_t_ref, mask_ref, columns_ref, outw_t_ref, proj_t_ref, *refs, core_ref=None
):
    outs, (middle_t_ref, gate1_t_ref, unit_scratch, panels) = refs[:-4], refs[-4:]
    rows, tokens = mask_ref.shape

    def emit(chunk, part, middle):
        middle_t_ref[:, part] = middle
        normed = affine(unit(middle.astype(F32), 0), columns_ref[4], columns_ref[5], tokens)
        products = dot(proj_t_ref[1], normed, NN)
        gate1_t_ref[:, part] = store_panels(
            panels, per_group, rows, chunk, tokens, products, half_lanes(mask_ref, chunk)
        )

    finish_rows(
        emit, rows, pair_t_ref.shape[0], tokens, load, pair_t_ref, gate_t_ref, columns_ref[2], columns_ref[3],
        outw_t_ref[0], unit_scratch,
    )
    if core_ref is None:
        pack_panels(panels, *outs)
    else:
        split_panels(panels, core_ref, *outs)


def finish_kernel(by_core, *refs):
    if by_core:
        load, refs = core_halves(*refs[:3]), refs[3:]
    else:
        merged_ref, refs = refs[0], refs[1:]

        def load(part):
            return merged_ref[part].astype(F32)

    middle_t_ref, gate_t_ref, columns_ref, outw_t_ref, result_ref, unit_scratch, done, sems = refs
    rows, tokens, _ = result_ref.shape
    copies = []

    def emit(chunk, part, result):
        for h, r in enumerate(chunk):
            done[r] = result[:, h * tokens : (h + 1) * tokens].T
            copies.append(pltpu.make_async_copy(done.at[r], result_ref.at[r], sems.at[r]))
            copies[-1].start()

    finish_rows(
        emit, rows, middle_t_ref.shape[0], tokens, load, middle_t_ref, gate_t_ref,
        columns_ref[6], columns_ref[7], outw_t_ref[1], unit_scratch,
    )
    for copy in copies:
        copy.wait()


def scatter_start(first, up, down, order_ref, own_left, got_left, own_right, got_right, sums_ref, up_ref, down_ref):
    rows, tokens = own_left.shape[1:]
    count = sums_ref.shape[0]

    def both(own, got, c):
        return jnp.concatenate([own[first + c].astype(F32), got[first + c].astype(F32)], axis=0).astype(BF16)

    lefts = jnp.concatenate([both(own_left, got_left, c) for c in range(count)], axis=0)
    lefts = dot(lefts, order_ref[...], NT).astype(BF16).reshape(count, 2 * rows, tokens)
    for c in range(count):
        sums_ref[c] = dot(lefts[c], both(own_right, got_right, c), TN)
    for distance, ref in ((up, up_ref), (down, down_ref)):
        ref[...] = at_distance(sums_ref, distance, 2 * rows).astype(BF16)


def at_distance(sums_ref, distance, count):
    return sums_ref[:, distance * count : (distance + 1) * count, :]


def scatter_add(distance, got_ref, sums_ref, out_ref):
    out_ref[...] = (got_ref[...].astype(F32) + at_distance(sums_ref, distance, got_ref.shape[1])).astype(BF16)


def scatter_end(*refs):
    pieces, (keep_ref, send_ref) = refs[:-2], refs[-2:]
    rows = keep_ref.shape[1]
    first = 0
    for n in range(0, len(pieces), 3):
        sums_ref, up_ref, down_ref = pieces[n : n + 3]
        count = sums_ref.shape[0]
        sums = at_distance(sums_ref, 0, 2 * rows) + up_ref[...].astype(F32) + down_ref[...].astype(F32)
        keep_ref[first : first + count] = sums[:, :rows].astype(BF16)
        send_ref[first : first + count] = sums[:, rows:].astype(BF16)
        first += count


def on_device(*inputs):
    groups = lax.axis_size("row")
    rows, tokens, channels = inputs[0].shape
    per_group = channels // groups
    whole = pl.BlockSpec(memory_space=pltpu.VMEM)
    hbm = pl.BlockSpec(memory_space=pltpu.HBM)
    params = pltpu.CompilerParams(vmem_limit_bytes=32 * 1024 * 1024)
    shape = jax.ShapeDtypeStruct
    both_shape = shape((2 * channels * rows, tokens), BF16)
    flat_shape = shape((channels, rows * tokens), BF16)
    panels = pltpu.VMEM((tokens // LANES, 2 * channels * rows, LANES), F32)
    unit_scratch = pltpu.VMEM((tokens // LANES, channels * rows, LANES), F32)

    def exchange(array):
        return lax.all_to_all(array, "row", split_axis=0, concat_axis=0, tiled=True)

    def mix(both, incoming):
        product = pl.pallas_call(
            functools.partial(mix_kernel, per_group, rows, incoming),
            out_shape=shape((groups, per_group * rows, tokens), BF16),
            in_specs=[whole],
            out_specs=whole,
            compiler_params=params,
            name="mix",
        )(both.reshape(groups, 2 * per_group * rows, tokens))
        return product.reshape(channels * rows, tokens)

    half = channels // 2
    by_core = groups % 4 == 0 and groups * rows * tokens * half * 2 <= 4 * 2**20
    smem = pl.BlockSpec(memory_space=pltpu.SMEM)
    core = (lax.axis_index("row") % 2).astype(jnp.int32).reshape(1)
    half_shape = shape((half * rows, tokens), BF16)
    projected = (half_shape,) * 4 if by_core else (both_shape,)
    columns_shape = shape((8, channels, tokens), F32)
    proj_t_shape = shape((2, 5 * channels, channels), BF16)
    if by_core:
        pair, mask, gains, biases, proj, gatew, outw = (
            pltpu.with_memory_space_constraint(a, pltpu.HBM) for a in inputs
        )
        side_panels = pltpu.VMEM((tokens // LANES, channels * rows, LANES), F32)

        def like(array):
            return shape(array.shape, array.dtype)

        right, other_right, pair_t, normed_t, mask, columns, proj, gatew, outw = pl.pallas_call(
            right_kernel,
            out_shape=(half_shape, half_shape, flat_shape, flat_shape, like(mask), columns_shape)
            + (like(proj), like(gatew), like(outw)),
            in_specs=[smem] + [hbm] * 7,
            out_specs=(whole,) * 9,
            scratch_shapes=[pltpu.VMEM(a.shape, a.dtype) for a in (pair, gains, biases)]
            + [side_panels, pltpu.SemaphoreType.DMA((7,))],
            compiler_params=params,
            name="project_right",
        )(core, pair, mask, gains, biases, proj, gatew, outw)
        left, other_left, gate_t, proj_t, outw_t = pl.pallas_call(
            left_kernel,
            out_shape=(half_shape, half_shape, flat_shape, proj_t_shape, shape(outw.shape, BF16)),
            in_specs=[smem] + [whole] * 5,
            out_specs=(whole,) * 5,
            scratch_shapes=[side_panels],
            compiler_params=params,
            cost_estimate=pl.CostEstimate(flops=10**9, bytes_accessed=4 * 2**20, transcendentals=0),
            name="project_left",
        )(core, normed_t, mask, proj, gatew, outw)
    else:
        results = pl.pallas_call(
            functools.partial(project_kernel, half if by_core else per_group, by_core),
            out_shape=projected
            + (
                flat_shape,
                flat_shape,
                shape((rows, tokens), inputs[1].dtype),
                shape((8, channels, tokens), F32),
                shape((2, 5 * channels, channels), BF16),
                shape((2, channels, channels), BF16),
            ),
            in_specs=[smem] * by_core + [hbm] * 7,
            out_specs=(whole,) * (len(projected) + 6),
            scratch_shapes=[pltpu.VMEM(inputs[n].shape, inputs[n].dtype) for n in (0, 2, 3, 4, 5, 6)]
            + [panels, pltpu.SemaphoreType.DMA((7,))],
            compiler_params=params,
            name="project",
        )(*[core] * by_core, *(pltpu.with_memory_space_constraint(a, pltpu.HBM) for a in inputs))
        pair_t, gate_t, mask, columns, proj_t, outw_t = results[-6:]
    if by_core:
        chips = groups // 2
        ring = ring_chips(chips)

        def along(array, step):
            pairs = [(2 * q + c, 2 * ring[(p + step) % chips] + c) for p, q in enumerate(ring) for c in range(2)]
            return lax.ppermute(array, "row", pairs)

        def rounds(array, step, count):
            arrays = [array]
            for _ in range(count):
                arrays.append(along(arrays[-1], step))
            return arrays

        swap = [(d, d ^ 1) for d in range(groups)]
        got_right = lax.ppermute(other_right, "row", swap)
        got_left = lax.ppermute(other_left, "row", swap)
        middle = chips // 2
        ups = [rounds(right, 1, middle), rounds(got_right, 1, middle - 1)]
        downs = [rounds(right, -1, middle - 1), rounds(got_right, -1, middle)]
        distances = sorted(range(chips), key=lambda d: min(d, chips - d))
        early = 2 * (chips - 1)
        rights = [
            ups[piece][d] if d < len(ups[piece]) else downs[piece][chips - d] for d in distances for piece in range(2)
        ]
        rights = [array.reshape(half, rows, tokens) for array in rights]
        lefts = [array.reshape(half, rows, tokens) for array in (left, got_left)]
        first_sums = pl.pallas_call(
            mix_early,
            out_shape=shape((half, 2 * rows, tokens), BF16),
            in_specs=[whole] * (3 + early),
            out_specs=whole,
            scratch_shapes=[pltpu.VMEM((2 * half * rows, early * rows), BF16)],
            compiler_params=params,
            cost_estimate=pl.CostEstimate(flops=10**9, bytes_accessed=4 * 2**20, transcendentals=0),
            name="mix_early",
        )(token_order(chips, distances[: early // 2], rows), *lefts, *rights[:early])
        keep, send = pl.pallas_call(
            mix_late,
            out_shape=(shape((half, rows, tokens), BF16),) * 2,
            in_specs=[whole] * (4 + len(rights) - early),
            out_specs=(whole,) * 2,
            scratch_shapes=[pltpu.VMEM((2 * half * rows, (len(rights) - early) * rows), BF16)],
            compiler_params=params,
            name="mix_late",
        )(token_order(chips, distances[early // 2 :], rows), *lefts, first_sums, *rights[early:])
        merged = (core, keep.reshape(half * rows, tokens), lax.ppermute(send, "row", swap).reshape(half * rows, tokens))
    else:
        merged = (exchange(mix(exchange(results[0]), False)),)
    results = pl.pallas_call(
        functools.partial(step_kernel, half if by_core else per_group, by_core),
        out_shape=projected + (flat_shape, flat_shape),
        in_specs=[smem] * by_core + [whole] * (len(merged) - by_core + 6),
        out_specs=(whole,) * (len(projected) + 2),
        scratch_shapes=[unit_scratch, panels],
        compiler_params=params,
        name="finish_project",
    )(*merged, pair_t, gate_t, mask, columns, outw_t, proj_t)
    middle_t, gate_t = results[-2:]
    if by_core:
        left, right, other_left, other_right = results[:4]
        got_left = lax.ppermute(other_left, "row", swap)
        got_right = lax.ppermute(other_right, "row", swap)
        operands = [array.reshape(half, rows, tokens) for array in (left, got_left, right, got_right)]
        order = token_order(chips, [-d % chips for d in range(chips)], rows)
        size = half // 2
        part_shape = shape((size, 2 * rows, tokens), BF16)
        pieces = []
        for piece in range(2):
            hops = (middle, middle - 1) if piece == 0 else (middle - 1, middle)
            sums, *travelling = pl.pallas_call(
                functools.partial(scatter_start, piece * size, hops[0], chips - hops[1]),
                out_shape=(shape((size, tokens, tokens), F32), part_shape, part_shape),
                in_specs=[whole] * 5,
                out_specs=(whole,) * 3,
                compiler_params=params,
                name="scatter_start",
            )(order, *operands)
            for way, (step, count) in enumerate(zip((1, -1), hops)):
                for left_over in reversed(range(count)):
                    travelling[way] = along(travelling[way], step)
                    if left_over:
                        travelling[way] = pl.pallas_call(
                            functools.partial(scatter_add, step * left_over % chips),
                            out_shape=part_shape,
                            in_specs=[whole] * 2,
                            out_specs=whole,
                            compiler_params=params,
                            name="scatter_add",
                        )(travelling[way], sums)
            pieces += [sums, *travelling]
        keep, send = pl.pallas_call(
            scatter_end,
            out_shape=(shape((half, rows, tokens), BF16),) * 2,
            in_specs=[whole] * len(pieces),
            out_specs=(whole,) * 2,
            compiler_params=params,
            name="scatter_end",
        )(*pieces)
        merged = (core, keep.reshape(half * rows, tokens), lax.ppermute(send, "row", swap).reshape(half * rows, tokens))
    else:
        merged = (exchange(mix(exchange(results[0]), True)),)
    return pl.pallas_call(
        functools.partial(finish_kernel, by_core),
        out_shape=shape((rows, tokens, channels), BF16),
        in_specs=[smem] * by_core + [whole] * (len(merged) - by_core + 4),
        out_specs=hbm,
        scratch_shapes=[unit_scratch, pltpu.VMEM((rows, tokens, channels), BF16), pltpu.SemaphoreType.DMA((rows,))],
        compiler_params=params,
        name="finish",
    )(*merged, middle_t, gate_t, columns, outw_t)


def solution(mesh):
    rows = ("groups", "row")
    return jax.shard_map(
        on_device,
        mesh=mesh,
        in_specs=(P(rows, None, None), P(rows, None), P(), P(), P(), P(), P()),
        out_specs=P(rows, None, None),
        check_vma=False,
    )
```
